32 devices in a mesh: page: 8 (over y, x, core), row: 4 (over z).
Axes of the slice: x: 2, y: 2, z: 4, core: 2. Of those that a mesh axis runs over, the one named last changes fastest.
Arguments:
- page_tokens: bfloat16 [8, 40, 60, 512], P('page', 'row'), may hold values from -6 to 6
- blank_mask: int32 [8, 4, 6], P('page', 'row'), may hold values 0 or 1
- cotangent: float32 [8, 40, 60, 512], P('page', 'row'), may hold values from -6 to 6
- ln_gain: float32 [2, 1024], replicated, may hold values from 0.25 to 1.75
- ln_bias: float32 [2, 1024], replicated, may hold values from -2 to 2
- qv_bias: float32 [2, 1024], replicated, may hold values from -2 to 2
- rel_table: float32 [2, 16, 361], replicated, may hold values from -4 to 4
- w_qkv: bfloat16 [2, 512, 1536], replicated, may hold values from -0.25 to 0.25
- w_proj: bfloat16 [2, 512, 512], replicated, may hold values from -1 to 1
- proj_bias: float32 [2, 512], replicated, may hold values from -2 to 2
- w_fc1: bfloat16 [2, 512, 2048], replicated, may hold values from -0.25 to 0.25
- fc1_bias: float32 [2, 2048], replicated, may hold values from -2 to 2
- w_fc2: bfloat16 [2, 2048, 512], replicated, may hold values from -0.125 to 0.125
- fc2_bias: float32 [2, 512], replicated, may hold values from -2 to 2
Outputs:
- out_tokens: float32 [8, 40, 60, 512], P('page', 'row')
- grad_tokens: float32 [8, 40, 60, 512], P('page', 'row')
- grad_ln_gain: float32 [2, 1024], P(None, 'row')
- grad_ln_bias: float32 [2, 1024], P(None, 'row')
- grad_qv_bias: float32 [2, 1024], P(None, 'row')
- grad_rel_table: float32 [2, 16, 361], replicated
- grad_w_qkv: float32 [2, 512, 1536], P(None, 'row')
- grad_w_proj: float32 [2, 512, 512], P(None, 'row')
- grad_proj_bias: float32 [2, 512], P(None, 'row')
- grad_w_fc1: float32 [2, 512, 2048], P(None, 'row')
- grad_fc1_bias: float32 [2, 2048], P(None, 'row')
- grad_w_fc2: float32 [2, 2048, 512], P(None, 'row')
- grad_fc2_bias: float32 [2, 512], P(None, 'row')
The draws below stay inside these ranges and needn't reach their ends.
All inputs are finite; a program needn't handle non-finite values. No bound on the sum of `blank_mask` on one device may be relied on, other than what follows from the above.
Results may differ from the reference program's by a relative error of at most 0.015.
Values sent between devices are 32-bit elements; how exact they have to be, the bound alone decides.
A program may use at most 192 MiB of HBM per device.

```python
import jax
import jax.numpy as jnp
from jax import lax

D = 512
HEADS = 16
HEAD_DIM = 32
FF = 2048
WIN = 10
WCOLS = 6
SHIFT = 5
TABLE = 361
PAGES = 8
IMG_H = 40
IMG_W = 60
N_ROW = 4


def place_ends(drawn, rng, least, largest):
    spot = [jax.random.randint(jax.random.fold_in(rng, axis), (), 0, length) for axis, length in enumerate(drawn.shape)]
    main_axis = drawn.shape.index(max(drawn.shape))
    next_to = spot[:main_axis] + [(spot[main_axis] + 1) % drawn.shape[main_axis]] + spot[main_axis + 1:]
    return drawn.at[tuple(spot)].set(least).at[tuple(next_to)].set(largest)


def steps_of(own_key, extent, cuts, least, top_value):
    def one(position, shards_of):
        heights = jax.random.uniform(jax.random.fold_in(jax.random.fold_in(own_key, 6), position), (shards_of,), jnp.float32, least / len(cuts), top_value / len(cuts))
        return jnp.repeat(jnp.exp(heights), extent[position] // shards_of).reshape((-1,) + (1,) * (len(extent) - position - 1))

    factor_of = one(*cuts[0])
    for cut in cuts[1:]:
        factor_of = factor_of * one(*cut)
    return factor_of


def scatter_about(rng, extent, scale, limit, split=(), kind=jnp.bfloat16):
    values = jax.random.normal(rng, extent, jnp.float32) * scale
    if len(split) > 0:
        values = steps_of(rng, extent, split, -0.22, 0.18) * values
    return jnp.clip(values, min=-limit, max=limit).astype(kind)


def setup_inputs(seed: int = 0) -> dict:
    streams_of = jax.random.split(jax.random.key(seed), 15)
    page_tokens = scatter_about(streams_of[0], (PAGES, IMG_H, IMG_W, D), 1.0, 6.0, ((0, 8), (1, 4)))
    blank_mask = place_ends((jax.random.randint(streams_of[1], (PAGES, N_ROW, WCOLS), 0, 4) < 1).astype(jnp.int32), jax.random.fold_in(streams_of[1], 1), 0, 1)
    cotangent = scatter_about(streams_of[2], (PAGES, IMG_H, IMG_W, D), 1.0, 6.0, ((0, 8), (1, 4)), jnp.float32)
    ln_gain = jnp.clip(1.0 + 0.15 * jax.random.normal(streams_of[3], (2, 2 * D), jnp.float32), 0.25, 1.75)
    ln_bias = scatter_about(streams_of[4], (2, 2 * D), 0.3, 2.0, (), jnp.float32)
    qv_bias = scatter_about(streams_of[5], (2, 2 * D), 0.3, 2.0, (), jnp.float32)
    rel_table = scatter_about(streams_of[6], (2, HEADS, TABLE), 1.0, 4.0, (), jnp.float32)
    w_qkv = scatter_about(streams_of[7], (2, D, 3 * D), D ** -0.5, 0.25)
    w_proj = scatter_about(streams_of[8], (2, D, D), (D // 16) ** -0.5, 1.0)
    proj_bias = scatter_about(streams_of[9], (2, D), 0.3, 2.0, (), jnp.float32)
    w_fc1 = scatter_about(streams_of[10], (2, D, FF), D ** -0.5, 0.25)
    fc1_bias = scatter_about(streams_of[11], (2, FF), 0.3, 2.0, (), jnp.float32)
    w_fc2 = scatter_about(streams_of[12], (2, FF, D), FF ** -0.5, 0.125)
    fc2_bias = scatter_about(streams_of[13], (2, D), 0.3, 2.0, (), jnp.float32)
    return {"page_tokens": page_tokens, "blank_mask": blank_mask, "cotangent": cotangent, "ln_gain": ln_gain, "ln_bias": ln_bias, "qv_bias": qv_bias, "rel_table": rel_table, "w_qkv": w_qkv, "w_proj": w_proj, "proj_bias": proj_bias, "w_fc1": w_fc1, "fc1_bias": fc1_bias, "w_fc2": w_fc2, "fc2_bias": fc2_bias}


@jax.custom_vjp
def low(v):
    return lax.optimization_barrier(v.astype(jnp.bfloat16)).astype(jnp.float32)

@jax.custom_vjp
def low_back(v):
    return v

def low_keep(v):
    return (low(v), None)

def low_pass(kept, grad):
    return (grad,)

def back_keep(v):
    return (v, None)

def back_low(kept, grad):
    return (low(grad),)
low.defvjp(low_keep, low_pass)
low_back.defvjp(back_keep, back_low)
EPSILON = 1e-05
MASK_VALUE = -100.0
PRECISE = lax.Precision.HIGHEST

def layer_norm(values, norm_gain, norm_shift):
    center = values - lax.optimization_barrier(jnp.mean(values, axis=-1, keepdims=True))
    spread = lax.optimization_barrier(jnp.mean(center * center, axis=-1, keepdims=True))
    return center * lax.rsqrt(spread + EPSILON) * norm_gain + norm_shift

def product(left, right):
    return jnp.dot(left, right, precision=PRECISE, preferred_element_type=jnp.float32)

def to_windows(values):
    row_count = values.shape[0] // WIN
    col_count = values.shape[1] // WIN
    trailing = values.shape[2:]
    values = values.reshape((row_count, WIN, col_count, WIN) + trailing)
    values = jnp.moveaxis(values, 2, 1)
    return values.reshape((row_count, col_count, WIN * WIN) + trailing)

def from_windows(values):
    row_count, col_count = (values.shape[0], values.shape[1])
    trailing = values.shape[3:]
    values = values.reshape((row_count, col_count, WIN, WIN) + trailing)
    values = jnp.moveaxis(values, 1, 2)
    return values.reshape((row_count * WIN, col_count * WIN) + trailing)

def relative_index():
    places = jnp.arange(WIN * WIN)
    vertical = places // WIN
    horizontal = places % WIN
    row_offset = vertical[:, None] - vertical[None, :] + WIN - 1
    col_offset = horizontal[:, None] - horizontal[None, :] + WIN - 1
    return row_offset * (2 * WIN - 1) + col_offset

def region_map(height, col_width):
    row_ids = jnp.arange(height)
    col_ids = jnp.arange(col_width)
    row_part = (row_ids >= height - WIN).astype(jnp.int32) + (row_ids >= height - SHIFT).astype(jnp.int32)
    col_part = (col_ids >= col_width - WIN).astype(jnp.int32) + (col_ids >= col_width - SHIFT).astype(jnp.int32)
    return row_part[:, None] * 3 + col_part[None, :]

def window_attention(queries, key_rows, value_rows, live_keys, regions, rel_bias):
    scores = jnp.einsum('wihd,wjhd->whij', queries, key_rows, precision=PRECISE) * HEAD_DIM ** (-0.5)
    differ = (regions[:, :, None] != regions[:, None, :]).astype(jnp.float32)
    masked = MASK_VALUE * differ + MASK_VALUE * (1.0 - live_keys)[:, None, :]
    scores = low_back(scores + rel_bias[None] + masked[:, None])
    row_max = lax.optimization_barrier(jnp.max(scores, axis=-1, keepdims=True))
    exponent = jnp.exp(scores - row_max)
    soft_weights = exponent / lax.optimization_barrier(jnp.sum(exponent, axis=-1, keepdims=True))
    return jnp.einsum('whij,wjhd->wihd', low(soft_weights), value_rows, precision=PRECISE)

def run_block(block_in, live_map, params, block_index, shifted):
    norm_gain, norm_shift, qv_bias, rel_table, w_qkv, w_proj, proj_bias, w_fc1, fc1_bias, w_fc2, fc2_bias = [item[block_index] for item in params]
    height, col_width = (block_in.shape[0], block_in.shape[1])
    if shifted:
        block_in = jnp.roll(block_in, (-SHIFT, -SHIFT), (0, 1))
        live_map = jnp.roll(live_map, (-SHIFT, -SHIFT), (0, 1))
        regions = region_map(height, col_width)
    else:
        regions = jnp.zeros((height, col_width), jnp.int32)
    flat_in = block_in.reshape(height * col_width, D)
    normed = low(layer_norm(flat_in, norm_gain[:D], norm_shift[:D]))
    projected = product(normed, w_qkv)
    queries = low(low_back(projected[:, :D] + qv_bias[:D]))
    key_rows = low(low_back(projected[:, D:2 * D]))
    value_rows = low(low_back(projected[:, 2 * D:] + qv_bias[D:]))

    def windowed(rows_in):
        return to_windows(rows_in.reshape(height, col_width, HEADS, HEAD_DIM))
    rel_bias = rel_table[:, relative_index()]
    row_count = height // WIN
    tiled_bias = jnp.broadcast_to(rel_bias, (row_count,) + rel_bias.shape)
    attend = jax.checkpoint(lambda pieces: window_attention(*pieces))
    attended = lax.map(attend, (windowed(queries), windowed(key_rows), windowed(value_rows), to_windows(live_map), to_windows(regions), tiled_bias))
    merged = low(low_back(from_windows(attended).reshape(height * col_width, D)))
    branch = low_back(product(merged, w_proj) + proj_bias)
    hidden = flat_in + live_map.reshape(-1, 1) * branch
    second = low(layer_norm(hidden, norm_gain[D:], norm_shift[D:]))
    inner_rows = low_back(product(second, w_fc1) + fc1_bias)
    activated = low(jax.nn.gelu(inner_rows, approximate=False))
    block_out = hidden + low_back(product(activated, w_fc2) + fc2_bias)
    block_out = block_out.reshape(height, col_width, D)
    if shifted:
        block_out = jnp.roll(block_out, (SHIFT, SHIFT), (0, 1))
    return block_out

def run_page(page_in, blank_page, params):
    live_map = jnp.repeat(jnp.repeat(1.0 - blank_page.astype(jnp.float32), WIN, axis=0), WIN, axis=1)
    first_out = run_block(page_in, live_map, params, 0, False)
    return run_block(first_out, live_map, params, 1, True)

def reference(page_tokens, blank_mask, cotangent, ln_gain, ln_bias, qv_bias, rel_table, w_qkv, w_proj, proj_bias, w_fc1, fc1_bias, w_fc2, fc2_bias):
    params = (ln_gain, ln_bias, qv_bias, rel_table, w_qkv.astype(jnp.float32), w_proj.astype(jnp.float32), proj_bias, w_fc1.astype(jnp.float32), fc1_bias, w_fc2.astype(jnp.float32), fc2_bias)
    totals = jax.tree.map(jnp.zeros_like, params)

    def one_page(carried, pieces):
        page_in, blank_page, page_grad = pieces
        page_out, pull_back = jax.vjp(lambda tokens_in, weights_in: run_page(tokens_in, blank_page, weights_in), page_in.astype(jnp.float32), params)
        grad_in, grad_params = pull_back(page_grad)
        return (jax.tree.map(jnp.add, carried, grad_params), (page_out, grad_in))
    totals, (outputs, grad_tokens) = lax.scan(one_page, totals, (page_tokens, blank_mask, cotangent))
    return (outputs, grad_tokens) + tuple(totals)
```

```python
import functools

import jax
import jax.numpy as jnp
import numpy as np
from jax import lax
from jax.experimental import pallas as pl
from jax.experimental.pallas import tpu as pltpu
from jax.sharding import PartitionSpec as P

WIN = 10
SHIFT = 5
AREA = WIN * WIN
LANES = 128
SPAN = 64
D = 512
HEADS = 16
HEAD_DIM = 32
FF = 2048
CHUNK = 512
EPSILON = 1e-05
MASK_VALUE = -100.0
NEVER = -1e30
SCORE_SCALE = HEAD_DIM ** (-0.5)
VMEM_LIMIT = 60 * 1024 * 1024
BF = jnp.bfloat16
F32 = jnp.float32
G1, B1, G2, B2, QB, VB, PB, F2B, F1B, NONE = 0, 1, 2, 3, 4, 5, 6, 7, 8, 12
VECTORS = 12


def mm(left, right, left_dim, right_dim):
    return lax.dot_general(
        left, right, (((left_dim,), (right_dim,)), ((), ())), preferred_element_type=F32
    )


def split(values):
    high = values.astype(BF)
    return high, (values - high.astype(F32)).astype(BF)


def lane_tile(index):
    return pl.ds(pl.multiple_of(index * LANES, LANES), LANES)


def chunk_of(index):
    return pl.ds(pl.multiple_of(index * CHUNK, CHUNK), CHUNK)


def wide(column, count):
    return jnp.concatenate([column] * count, axis=1)


def fold(values):
    total = values[:, :LANES]
    for start in range(LANES, values.shape[1], LANES):
        total = total + values[:, start : start + LANES]
    return total


def norm_parts(values):
    center = values - jnp.sum(values, axis=0, keepdims=True) * (1.0 / D)
    spread = jnp.sum(center * center, axis=0, keepdims=True) * (1.0 / D)
    scale = lax.rsqrt(spread + EPSILON)
    return center * scale, scale


def norm_pull(grad, gain, hat, scale):
    scaled = grad * gain
    mean_one = jnp.sum(scaled, axis=0, keepdims=True) * (1.0 / D)
    mean_two = jnp.sum(scaled * hat, axis=0, keepdims=True) * (1.0 / D)
    return scale * (scaled - mean_one - hat * mean_two)


def gelu_parts(inner):
    step = 1.0 / (1.0 + (0.3275911 * 0.7071067811865476) * jnp.abs(inner))
    bell = jnp.exp(inner * inner * -0.5)
    poly = 0.5 * 1.061405429
    for factor in (-1.453152027, 1.421413741, -0.284496736, 0.254829592):
        poly = poly * step + 0.5 * factor
    tail = poly * step * bell
    below = jnp.where(inner >= 0, 1.0 - tail, tail)
    return inner * below, below + inner * bell * 0.3989422804014327


def to_channels(upper_ref, lower_ref, place_ref, out_ref):
    half = upper_ref.shape[0]

    def step(index, carry):
        lanes = pl.ds(pl.multiple_of(index * 256, 256), 256)
        rows = pl.ds(pl.multiple_of(index * 256, 256), 256)
        total = None
        for part, start in ((upper_ref, 0), (lower_ref, half)):
            for piece in split(part[:, lanes]):
                term = mm(piece, place_ref[start : start + half, :], 0, 0)
                total = term if total is None else total + term
        out_ref[rows, :] = total
        return carry

    lax.fori_loop(0, D // 256, step, 0)


def to_page(values_ref, place_ref, out_ref):
    def step(index, carry):
        rows = pl.ds(pl.multiple_of(index * 256, 256), 256)
        high, low = split(values_ref[rows, :])
        out_ref[:, rows] = mm(place_ref[...], high, 1, 1) + mm(place_ref[...], low, 1, 1)
        return carry

    lax.fori_loop(0, D // 256, step, 0)


def spread_columns(vec_ref, cols_ref):
    for index in range(VECTORS):
        cols_ref[index] = jnp.broadcast_to(vec_ref[:, index : index + 1], (D, LANES))
    cols_ref[NONE] = jnp.zeros((D, LANES), F32)


def spread_bias(table_ref, rows_ref, bias_ref):
    rows_ref[...] = jnp.zeros(rows_ref.shape, F32)
    source = table_ref[...].reshape(WIN * HEADS, 2 * LANES)
    for row in range(WIN):
        shift = (WIN - 1 - row) * WIN
        moved = source if shift == 0 else pltpu.roll(source, 2 * LANES - shift, axis=1)
        rows_ref[pl.ds(row * WIN * HEADS, WIN * HEADS), :] = moved[:, :LANES]
    for head in range(HEADS):
        bias_ref[head] = rows_ref[pl.ds(head, LANES, stride=HEADS), :]


def gather_bias(grad_ref, rows_ref, out_ref):
    for head in range(HEADS):
        rows_ref[pl.ds(head, LANES, stride=HEADS), :] = grad_ref[head]
    total = jnp.zeros((WIN * HEADS, 2 * LANES), F32)
    for row in range(WIN):
        shift = (WIN - 1 - row) * WIN
        piece = rows_ref[pl.ds(row * WIN * HEADS, WIN * HEADS), :]
        piece = jnp.concatenate([piece, jnp.zeros_like(piece)], axis=1)
        total = total + (piece if shift == 0 else pltpu.roll(piece, shift, axis=1))
    out_ref[...] = total.reshape(WIN, HEADS, 2 * LANES)


def head_rows(head, base=0):
    return pl.ds(base + head * HEAD_DIM, HEAD_DIM)


def forward(s):
    windows = s.x.shape[1] // LANES

    def norm_one(index, carry):
        lanes = lane_tile(index)
        hat, _ = norm_parts(s.x[:, lanes])
        s.normed[:, lanes] = (hat * s.cols[G1] + s.cols[B1]).astype(BF)
        return carry

    lax.fori_loop(0, windows, norm_one, 0)

    def project(index, carry):
        which = jnp.where(index == 0, QB, jnp.where(index == 1, NONE, VB))
        rows = chunk_of(index)
        out = mm(s.w_qkv[:, rows], s.normed[...], 0, 0)
        s.qkv[rows, :] = (out + wide(s.cols[which], windows)).astype(BF)
        return carry

    lax.fori_loop(0, 3, project, 0)

    def attend(index, carry):
        lanes = lane_tile(index)
        masked = s.mask[index]
        for head in range(HEADS):
            query = s.qkv[head_rows(head), lanes]
            key = s.qkv[head_rows(head, D), lanes]
            value = s.qkv[head_rows(head, 2 * D), lanes]
            scores = mm(key, query, 0, 0) * SCORE_SCALE + (s.bias[head] + masked)
            exponent = jnp.exp(scores - jnp.max(scores, axis=0, keepdims=True))
            total = jnp.sum(exponent, axis=0, keepdims=True)
            soft = (exponent * (1.0 / total)).astype(BF)
            s.soft[index * HEADS + head] = soft
            s.merged[head_rows(head), lanes] = mm(value, soft, 1, 0).astype(BF)
        return carry

    lax.fori_loop(0, windows, attend, 0)

    s.work[...] = mm(s.w_proj[...], s.merged[...], 0, 0)

    def norm_two(index, carry):
        lanes = lane_tile(index)
        hidden = s.x[:, lanes] + s.live[:, lanes] * (s.work[:, lanes] + s.cols[PB])
        s.hidden[:, lanes] = hidden
        s.work[:, lanes] = hidden + s.cols[F2B]
        hat, _ = norm_parts(hidden)
        s.second[:, lanes] = (hat * s.cols[G2] + s.cols[B2]).astype(BF)
        return carry

    lax.fori_loop(0, windows, norm_two, 0)

    def feed(index, carry):
        rows = chunk_of(index)
        inner = mm(s.w_fc1[:, rows], s.second[...], 0, 0) + wide(s.cols[F1B + index], windows)
        active, slope = gelu_parts(inner)
        active = active.astype(BF)
        s.active[rows, :] = active
        s.slope[rows, :] = slope.astype(BF)
        s.work[...] += mm(s.w_fc2[rows, :], active, 0, 0)
        return carry

    lax.fori_loop(0, FF // CHUNK, feed, 0)


def backward(s):
    windows = s.x.shape[1] // LANES
    s.sums[...] = jnp.zeros(s.sums.shape, F32)
    s.grad_bias[...] = jnp.zeros(s.grad_bias.shape, F32)
    lowered = s.grad[...].astype(BF)
    s.low[...] = lowered
    s.sums[F2B] = fold(lowered.astype(F32))
    s.work[...] = jnp.zeros(s.work.shape, F32)

    def feed(index, carry):
        rows = chunk_of(index)
        s.grad_w_fc2[rows, :] = mm(s.active[rows, :], s.low[...], 1, 1)
        grad_inner = mm(s.w_fc2[rows, :], s.low[...], 1, 0) * s.slope[rows, :].astype(F32)
        grad_inner = grad_inner.astype(BF)
        s.sums[F1B + index] = fold(grad_inner.astype(F32))
        s.grad_w_fc1[:, rows] = mm(s.second[...], grad_inner, 1, 1)
        s.work[...] += mm(s.w_fc1[:, rows], grad_inner, 1, 0)
        return carry

    lax.fori_loop(0, FF // CHUNK, feed, 0)

    def norm_two(index, carry):
        lanes = lane_tile(index)
        hat, scale = norm_parts(s.hidden[:, lanes])
        grad = s.work[:, lanes]
        s.sums[G2] += grad * hat
        s.sums[B2] += grad
        grad = s.grad[:, lanes] + norm_pull(grad, s.cols[G2], hat, scale)
        s.grad[:, lanes] = grad
        grad_low = (grad * s.live[:, lanes]).astype(BF)
        s.low[:, lanes] = grad_low
        s.sums[PB] += grad_low.astype(F32)
        return carry

    lax.fori_loop(0, windows, norm_two, 0)

    s.grad_w_proj[...] = mm(s.merged[...], s.low[...], 1, 1)
    s.grad_merged[...] = mm(s.w_proj[...], s.low[...], 1, 0).astype(BF)

    def attend(index, carry):
        lanes = lane_tile(index)
        for head in range(HEADS):
            query = s.qkv[head_rows(head), lanes]
            key = s.qkv[head_rows(head, D), lanes]
            value = s.qkv[head_rows(head, 2 * D), lanes]
            grad_out = s.grad_merged[head_rows(head), lanes]
            soft_low = s.soft[index * HEADS + head]
            soft = soft_low.astype(F32)
            grad_soft = mm(value, grad_out, 0, 0)
            inner = jnp.sum(soft * grad_soft, axis=0, keepdims=True)
            grad_scores = (soft * (grad_soft - inner)).astype(BF)
            s.grad_bias[head] += grad_scores.astype(F32)
            grad_query = (mm(key, grad_scores, 1, 0) * SCORE_SCALE).astype(BF)
            grad_key = (mm(query, grad_scores, 1, 1) * SCORE_SCALE).astype(BF)
            grad_value = mm(grad_out, soft_low, 1, 1).astype(BF)
            s.grad_qkv[head_rows(head), lanes] = grad_query
            s.grad_qkv[head_rows(head, D), lanes] = grad_key
            s.grad_qkv[head_rows(head, 2 * D), lanes] = grad_value
            s.sums[QB, head_rows(head), :] += grad_query.astype(F32)
            s.sums[VB, head_rows(head), :] += grad_value.astype(F32)
        return carry

    lax.fori_loop(0, windows, attend, 0)
    s.work[...] = jnp.zeros(s.work.shape, F32)

    def project(index, carry):
        rows = chunk_of(index)
        s.grad_w_qkv[:, rows] = mm(s.normed[...], s.grad_qkv[rows, :], 1, 1)
        s.work[...] += mm(s.w_qkv[:, rows], s.grad_qkv[rows, :], 1, 0)
        return carry

    lax.fori_loop(0, 3, project, 0)

    def norm_one(index, carry):
        lanes = lane_tile(index)
        hat, scale = norm_parts(s.x[:, lanes])
        grad = s.work[:, lanes]
        s.sums[G1] += grad * hat
        s.sums[B1] += grad
        s.grad[:, lanes] += norm_pull(grad, s.cols[G1], hat, scale)
        return carry

    lax.fori_loop(0, windows, norm_one, 0)


def pack_sums(sums_ref, out_ref):
    places = lax.broadcasted_iota(jnp.int32, (D, LANES), 1)
    packed = jnp.zeros((D, LANES), F32)
    for index in range(VECTORS):
        packed = jnp.where(places == index, jnp.sum(sums_ref[index], axis=1, keepdims=True), packed)
    out_ref[...] = packed.T[: out_ref.shape[0]]


class Refs:
    def __init__(self, names, refs):
        for name, ref in zip(names, refs, strict=True):
            setattr(self, name, ref)


WEIGHTS = ("w_qkv", "w_proj", "w_fc1", "w_fc2")


def saved_shapes(lanes):
    windows = lanes // LANES
    return {
        "x": ((D, lanes), F32),
        "normed": ((D, lanes), BF),
        "qkv": ((3 * D, lanes), BF),
        "soft": ((windows * HEADS, LANES, LANES), BF),
        "merged": ((D, lanes), BF),
        "hidden": ((D, lanes), F32),
        "second": ((D, lanes), BF),
        "active": ((FF, lanes), BF),
        "slope": ((FF, lanes), BF),
    }


def grad_shapes(rows):
    return {
        "grad_page": ((rows, D), F32),
        "grad_w_qkv": ((D, 3 * D), F32),
        "grad_w_proj": ((D, D), F32),
        "grad_w_fc1": ((D, FF), F32),
        "grad_w_fc2": ((FF, D), F32),
        "grad_vectors": ((16, D), F32),
        "grad_table": ((WIN, HEADS, 2 * LANES), F32),
    }


def forward_scratch(lanes):
    return {
        "work": ((D, lanes), F32),
        "cols": ((VECTORS + 1, D, LANES), F32),
        "bias": ((HEADS, LANES, LANES), F32),
        "bias_rows": ((HEADS * LANES, LANES), F32),
    }


def backward_scratch(lanes):
    return {
        "work": ((D, lanes), F32),
        "cols": ((VECTORS + 1, D, LANES), F32),
        "grad": ((D, lanes), F32),
        "low": ((D, lanes), BF),
        "grad_merged": ((D, lanes), BF),
        "grad_qkv": ((3 * D, lanes), BF),
        "grad_bias": ((HEADS, LANES, LANES), F32),
        "bias_rows": ((HEADS * LANES, LANES), F32),
        "sums": ((VECTORS, D, LANES), F32),
    }


def run_forward(names, *refs):
    s = Refs(names, refs)
    spread_columns(s.vectors, s.cols)
    spread_bias(s.table, s.bias_rows, s.bias)
    to_channels(s.upper, s.lower, s.place, s.x)
    forward(s)
    to_page(s.work, s.place, s.out_page)


def run_backward(names, *refs):
    s = Refs(names, refs)
    spread_columns(s.vectors, s.cols)
    to_channels(s.grad_upper, s.grad_lower, s.place, s.grad)
    backward(s)
    to_page(s.grad, s.place, s.grad_page)
    gather_bias(s.grad_bias, s.bias_rows, s.grad_table)
    pack_sums(s.sums, s.grad_vectors)


def run_both(names, *refs):
    s = Refs(names, refs)
    spread_columns(s.vectors, s.cols)
    spread_bias(s.table, s.bias_rows, s.bias)
    to_channels(s.upper, s.lower, s.place, s.x)
    forward(s)
    to_page(s.work, s.place, s.out_page)
    to_channels(s.grad_upper, s.grad_lower, s.place, s.grad)
    backward(s)
    to_page(s.grad, s.place, s.grad_page)
    gather_bias(s.grad_bias, s.bias_rows, s.grad_table)
    pack_sums(s.sums, s.grad_vectors)


def call(body, name, inputs, outputs, scratch, flops):
    names = tuple(inputs) + tuple(outputs) + tuple(scratch)
    in_vmem = pl.BlockSpec(memory_space=pltpu.VMEM)
    moved = sum(value.size * value.dtype.itemsize for value in inputs.values())
    results = pl.pallas_call(
        functools.partial(body, names),
        out_shape=[jax.ShapeDtypeStruct(*shape) for shape in outputs.values()],
        in_specs=[in_vmem] * len(inputs),
        out_specs=[in_vmem] * len(outputs),
        scratch_shapes=[pltpu.VMEM(*shape) for shape in scratch.values()],
        compiler_params=pltpu.CompilerParams(vmem_limit_bytes=VMEM_LIMIT),
        cost_estimate=pl.CostEstimate(flops=flops, bytes_accessed=moved, transcendentals=0),
        name=name,
    )(*inputs.values())
    return dict(zip(outputs, results))


def placements(cols):
    windows = cols // WIN
    plain = np.zeros((WIN * SPAN, windows * LANES), np.float32)
    moved = np.zeros((WIN * SPAN, windows * LANES), np.float32)
    for row in range(WIN):
        for col in range(cols):
            source = row * SPAN + col
            plain[source, (col // WIN) * LANES + row * WIN + col % WIN] = 1
            new_row, new_col = (row - SHIFT) % WIN, (col - SHIFT) % cols
            moved[source, (new_col // WIN) * LANES + new_row * WIN + new_col % WIN] = 1
    return plain.astype(jnp.bfloat16), moved.astype(jnp.bfloat16)


def table_spread():
    size = 2 * WIN - 1
    spread = np.zeros((size * size, WIN, 2 * LANES), np.float32)
    for key_col in range(WIN):
        for offset in range(size):
            for col in range(WIN):
                spread[offset * size + col - key_col + WIN - 1, key_col, offset * WIN + col] = 1
    return spread


def window_masks(live_windows, regions):
    windows = live_windows.shape[0]
    differ = (regions[:, :, None] != regions[:, None, :]).astype(F32)
    masked = MASK_VALUE * differ + MASK_VALUE * (1.0 - live_windows)[:, :, None]
    wide_mask = jnp.full((windows, LANES, LANES), NEVER, F32)
    masked = jnp.pad(masked, ((0, 0), (0, 0), (0, LANES - AREA)))
    return wide_mask.at[:, :AREA, :].set(masked)


def to_windows(values):
    windows = values.shape[1] // WIN
    return values.reshape(WIN, windows, WIN).swapaxes(0, 1).reshape(windows, AREA)


def live_lanes(live_windows):
    return jnp.pad(live_windows, ((0, 0), (0, LANES - AREA))).reshape(1, -1)


def shifted_regions(row_index, row_count, col_width):
    row_ids = WIN * row_index + jnp.arange(WIN)
    height = WIN * row_count
    row_part = (row_ids >= height - WIN).astype(jnp.int32) + (row_ids >= height - SHIFT).astype(jnp.int32)
    col_ids = jnp.arange(col_width)
    col_part = (col_ids >= col_width - WIN).astype(jnp.int32) + (col_ids >= col_width - SHIFT).astype(jnp.int32)
    return row_part[:, None] * 3 + col_part[None, :]


def shifted(value, axis, steps):
    count = lax.axis_size(axis)
    pairs = [(source, (source + steps) % count) for source in range(count)]
    return lax.ppermute(value, axis, pairs)


def page_rows(values):
    rows, cols, width = values.shape
    return jnp.pad(values, ((0, 0), (0, SPAN - cols), (0, 0))).reshape(rows * SPAN, width)


def from_page_rows(values, cols):
    return values.reshape(-1, SPAN, values.shape[-1])[:, :cols]


def reduce_weight(part):
    pages = lax.axis_size("page")
    pairs = [[2 * index, 2 * index + 1] for index in range(pages // 2)]
    same = [[2 * index + core for index in range(pages // 2)] for core in range(2)]
    part = lax.psum_scatter(part, "page", scatter_dimension=1, axis_index_groups=pairs, tiled=True)
    part = lax.psum_scatter(part, "row", scatter_dimension=0, tiled=True)
    part = lax.psum_scatter(part, "page", scatter_dimension=1, axis_index_groups=same, tiled=True)
    part = lax.all_gather(part, "page", axis=1, axis_index_groups=same, tiled=True)
    return lax.all_gather(part, "page", axis=1, axis_index_groups=pairs, tiled=True)


def per_device(
    page_tokens,
    blank_mask,
    cotangent,
    ln_gain,
    ln_bias,
    qv_bias,
    rel_table,
    w_qkv,
    w_proj,
    proj_bias,
    w_fc1,
    fc1_bias,
    w_fc2,
    fc2_bias,
):
    cols = page_tokens.shape[2]
    lanes = cols // WIN * LANES
    half = SHIFT * SPAN
    plain, moved = placements(cols)
    vectors = jnp.concatenate(
        [
            jnp.stack([ln_gain[:, :D], ln_bias[:, :D], ln_gain[:, D:], ln_bias[:, D:]], axis=1),
            jnp.stack([qv_bias[:, :D], qv_bias[:, D:], proj_bias, fc2_bias], axis=1),
            fc1_bias.reshape(2, FF // D, D),
            jnp.zeros((2, 4, D), F32),
        ],
        axis=1,
    ).swapaxes(1, 2)
    spread = table_spread()
    tables = jnp.einsum("lht,txj->lxhj", rel_table, spread, precision=lax.Precision.HIGHEST)

    live_own = 1.0 - blank_mask[0, 0].astype(F32)
    live_own = jnp.repeat(live_own, WIN)
    tokens = page_rows(page_tokens[0].astype(F32))
    grad_end = page_rows(cotangent[0])
    grad_upper, live_upper = shifted((grad_end[:half], live_own), "row", -1)

    live_one = to_windows(jnp.broadcast_to(live_own, (WIN, cols)))
    live_two = jnp.concatenate(
        [jnp.broadcast_to(live_own, (WIN - SHIFT, cols)), jnp.broadcast_to(live_upper, (SHIFT, cols))]
    )
    live_two = to_windows(jnp.roll(live_two, -SHIFT, axis=1))
    regions_two = to_windows(shifted_regions(lax.axis_index("row"), lax.axis_size("row"), cols))
    masks = (window_masks(live_one, jnp.zeros_like(regions_two)), window_masks(live_two, regions_two))
    lives = (live_lanes(live_one), live_lanes(live_two))

    def common(layer):
        return {
            "place": (jnp.asarray(plain), jnp.asarray(moved))[layer],
            "live": lives[layer],
            "vectors": vectors[layer],
            "w_qkv": w_qkv[layer],
            "w_proj": w_proj[layer],
            "w_fc1": w_fc1[layer],
            "w_fc2": w_fc2[layer],
        }

    def extra(layer):
        return {"mask": masks[layer], "table": tables[layer]}

    page_out = {"out_page": ((WIN * SPAN, D), F32)}
    first = call(
        run_forward,
        "layer0_forward",
        {"upper": tokens[:half], "lower": tokens[half:], **common(0), **extra(0)},
        {**page_out, **saved_shapes(lanes)},
        forward_scratch(lanes),
        6 * 10**9,
    )
    first_out = first.pop("out_page")
    upper_in = shifted(first_out[:half], "row", -1)
    second = call(
        run_both,
        "layer1_both",
        {
            "upper": upper_in,
            "lower": first_out[half:],
            "grad_upper": grad_upper,
            "grad_lower": grad_end[half:],
            **common(1),
            **extra(1),
        },
        {**page_out, **grad_shapes(WIN * SPAN)},
        {**saved_shapes(lanes), **forward_scratch(lanes), **backward_scratch(lanes)},
        18 * 10**9,
    )
    lower_grad = shifted(second["grad_page"][:half], "row", 1)
    third = call(
        run_backward,
        "layer0_backward",
        {"grad_upper": lower_grad, "grad_lower": second["grad_page"][half:], **common(0), **first},
        grad_shapes(WIN * SPAN),
        backward_scratch(lanes),
        12 * 10**9,
    )
    lower_out = shifted(second["out_page"][:half], "row", 1)
    final_out = jnp.concatenate(
        [from_page_rows(lower_out, cols), from_page_rows(second["out_page"][half:], cols)]
    )
    grad_first = from_page_rows(third["grad_page"], cols)

    weights = []
    for name in ("grad_w_qkv", "grad_w_proj", "grad_w_fc1", "grad_w_fc2"):
        weights.append(jnp.stack([reduce_weight(part[name]) for part in (third, second)]))
    tables_grad = jnp.stack([third["grad_table"], second["grad_table"]])
    tables_grad = jnp.einsum("lxhj,txj->lht", tables_grad, spread, precision=lax.Precision.HIGHEST)
    vectors_grad = jnp.stack([third["grad_vectors"], second["grad_vectors"]])
    tables_grad, vectors_grad = lax.psum((tables_grad, vectors_grad), ("page", "row"))

    def share(*indices):
        joined = jnp.concatenate([vectors_grad[:, index] for index in indices], axis=1)
        size = joined.shape[1] // lax.axis_size("row")
        return lax.dynamic_slice_in_dim(joined, lax.axis_index("row") * size, size, axis=1)

    return (
        final_out[None],
        grad_first[None],
        share(G1, G2),
        share(B1, B2),
        share(QB, VB),
        tables_grad,
        weights[0],
        weights[1],
        share(PB),
        weights[2],
        share(*range(F1B, F1B + FF // D)),
        weights[3],
        share(F2B),
    )


def solution(mesh):
    split_rows = P("page", "row", None, None)
    return jax.shard_map(
        per_device,
        mesh=mesh,
        in_specs=(split_rows, P("page", "row", None), split_rows) + (P(),) * 11,
        out_specs=(
            split_rows,
            split_rows,
            P(None, "row"),
            P(None, "row"),
            P(None, "row"),
            P(),
            P(None, "row", None),
            P(None, "row", None),
            P(None, "row"),
            P(None, "row", None),
            P(None, "row"),
            P(None, "row", None),
            P(None, "row"),
        ),
        check_vma=False,
    )
```

```python
import functools

import jax
import jax.numpy as jnp
import numpy as np
from jax import lax
from jax.experimental import pallas as pl
from jax.experimental.pallas import tpu as pltpu
from jax.sharding import PartitionSpec as P

WIN = 10
SHIFT = 5
AREA = WIN * WIN
LANES = 128
SPAN = 64
D = 512
HEADS = 16
HEAD_DIM = 32
FF = 2048
CHUNK = 512
EPSILON = 1e-05
MASK_VALUE = -100.0
NEVER = -1e30
SCORE_SCALE = HEAD_DIM ** (-0.5)
VMEM_LIMIT = 60 * 1024 * 1024
BF = jnp.bfloat16
F32 = jnp.float32
G1, B1, G2, B2, QB, VB, PB, F2B, F1B, NONE = 0, 1, 2, 3, 4, 5, 6, 7, 8, 12
VECTORS = 12
UNIT_QKV, UNIT_PROJ, UNIT_FC1, UNIT_FC2, UNITS = 0, 3, 4, 8, 12
SKEW = 2


def mm(left, right, left_dim, right_dim):
    return lax.dot_general(
        left, right, (((left_dim,), (right_dim,)), ((), ())), preferred_element_type=F32
    )


def split(values):
    high = values.astype(BF)
    return high, (values - high.astype(F32)).astype(BF)


def lane_tile(index):
    return pl.ds(pl.multiple_of(index * LANES, LANES), LANES)


def chunk_of(index):
    return pl.ds(pl.multiple_of(index * CHUNK, CHUNK), CHUNK)


def wide(column, count):
    return jnp.concatenate([column] * count, axis=1)


def fold(values):
    total = values[:, :LANES]
    for start in range(LANES, values.shape[1], LANES):
        total = total + values[:, start : start + LANES]
    return total


def norm_parts(values):
    center = values - jnp.sum(values, axis=0, keepdims=True) * (1.0 / D)
    spread = jnp.sum(center * center, axis=0, keepdims=True) * (1.0 / D)
    scale = lax.rsqrt(spread + EPSILON)
    return center * scale, scale


def norm_pull(grad, gain, hat, scale):
    scaled = grad * gain
    mean_one = jnp.sum(scaled, axis=0, keepdims=True) * (1.0 / D)
    mean_two = jnp.sum(scaled * hat, axis=0, keepdims=True) * (1.0 / D)
    return scale * (scaled - mean_one - hat * mean_two)


def gelu_parts(inner):
    step = 1.0 / (1.0 + (0.3275911 * 0.7071067811865476) * jnp.abs(inner))
    bell = jnp.exp(inner * inner * -0.5)
    poly = 0.5 * 1.061405429
    for factor in (-1.453152027, 1.421413741, -0.284496736, 0.254829592):
        poly = poly * step + 0.5 * factor
    tail = poly * step * bell
    below = jnp.where(inner >= 0, 1.0 - tail, tail)
    return inner * below, below + inner * bell * 0.3989422804014327


def to_channels(upper_ref, lower_ref, place_ref, out_ref):
    half = upper_ref.shape[0]

    def step(index, carry):
        lanes = pl.ds(pl.multiple_of(index * 256, 256), 256)
        rows = pl.ds(pl.multiple_of(index * 256, 256), 256)
        total = None
        for part, start in ((upper_ref, 0), (lower_ref, half)):
            for piece in split(part[:, lanes]):
                term = mm(piece, place_ref[start : start + half, :], 0, 0)
                total = term if total is None else total + term
        out_ref[rows, :] = total
        return carry

    lax.fori_loop(0, D // 256, step, 0)


def to_page(values_ref, place_ref, out_ref):
    def step(index, carry):
        rows = pl.ds(pl.multiple_of(index * 256, 256), 256)
        high, low = split(values_ref[rows, :])
        out_ref[:, rows] = mm(place_ref[...], high, 1, 1) + mm(place_ref[...], low, 1, 1)
        return carry

    lax.fori_loop(0, D // 256, step, 0)


def spread_columns(vec_ref, cols_ref):
    for index in range(VECTORS):
        cols_ref[index] = jnp.broadcast_to(vec_ref[:, index : index + 1], (D, LANES))
    cols_ref[NONE] = jnp.zeros((D, LANES), F32)


def spread_bias(table_ref, rows_ref, bias_ref):
    rows_ref[...] = jnp.zeros(rows_ref.shape, F32)
    source = table_ref[...].reshape(WIN * HEADS, 2 * LANES)
    for row in range(WIN):
        shift = (WIN - 1 - row) * WIN
        moved = source if shift == 0 else pltpu.roll(source, 2 * LANES - shift, axis=1)
        rows_ref[pl.ds(row * WIN * HEADS, WIN * HEADS), :] = moved[:, :LANES]
    for head in range(HEADS):
        bias_ref[head] = rows_ref[pl.ds(head, LANES, stride=HEADS), :]


def gather_bias(grad_ref, rows_ref, out_ref):
    for head in range(HEADS):
        rows_ref[pl.ds(head, LANES, stride=HEADS), :] = grad_ref[head]
    total = jnp.zeros((WIN * HEADS, 2 * LANES), F32)
    for row in range(WIN):
        shift = (WIN - 1 - row) * WIN
        piece = rows_ref[pl.ds(row * WIN * HEADS, WIN * HEADS), :]
        piece = jnp.concatenate([piece, jnp.zeros_like(piece)], axis=1)
        total = total + (piece if shift == 0 else pltpu.roll(piece, shift, axis=1))
    out_ref[...] = total.reshape(WIN, HEADS, 2 * LANES)


def head_rows(head, base=0):
    return pl.ds(base + head * HEAD_DIM, HEAD_DIM)


def reversed_bits(value, count):
    turned = 0
    for bit in range(count):
        turned = turned * 2 + (value // 2**bit) % 2
    return turned


def put_shares(units_ref, unit, grad):
    shares, rows = units_ref.shape[1:3]
    for share in range(shares):
        place = reversed_bits(share, shares.bit_length() - 1)
        units_ref[unit, place] = grad[share * rows : (share + 1) * rows]


def put_feed_rows(units_ref, index, grad):
    shares, rows = units_ref.shape[1:3]
    count = shares.bit_length() - 1
    parts = FF // CHUNK
    for share in range(shares // parts):
        place = reversed_bits(index * (shares // parts) + share, count)
        for part in range(parts):
            start = (share * parts + part) * rows
            units_ref[UNIT_FC2 + part, place] = grad[start : start + rows]


def forward(s):
    windows = s.x.shape[1] // LANES

    def norm_one(index, carry):
        lanes = lane_tile(index)
        hat, _ = norm_parts(s.x[:, lanes])
        s.normed[:, lanes] = (hat * s.cols[G1] + s.cols[B1]).astype(BF)
        return carry

    lax.fori_loop(0, windows, norm_one, 0)

    def project(index, carry):
        which = jnp.where(index == 0, QB, jnp.where(index == 1, NONE, VB))
        rows = chunk_of(index)
        out = mm(s.w_qkv[:, rows], s.normed[...], 0, 0)
        s.qkv[rows, :] = (out + wide(s.cols[which], windows)).astype(BF)
        return carry

    lax.fori_loop(0, 3, project, 0)

    def attend(index, carry):
        lanes = lane_tile(index)
        masked = s.mask[index]
        for head in range(HEADS):
            query = s.qkv[head_rows(head), lanes]
            key = s.qkv[head_rows(head, D), lanes]
            value = s.qkv[head_rows(head, 2 * D), lanes]
            scores = mm(key, query, 0, 0) * SCORE_SCALE + (s.bias[head] + masked)
            exponent = jnp.exp(scores - jnp.max(scores, axis=0, keepdims=True))
            total = jnp.sum(exponent, axis=0, keepdims=True)
            soft = (exponent * (1.0 / total)).astype(BF)
            s.soft[index * HEADS + head] = soft
            s.merged[head_rows(head), lanes] = mm(value, soft, 1, 0).astype(BF)
        return carry

    lax.fori_loop(0, windows, attend, 0)

    s.work[...] = mm(s.w_proj[...], s.merged[...], 0, 0)

    def norm_two(index, carry):
        lanes = lane_tile(index)
        hidden = s.x[:, lanes] + s.live[:, lanes] * (s.work[:, lanes] + s.cols[PB])
        s.hidden[:, lanes] = hidden
        s.work[:, lanes] = hidden + s.cols[F2B]
        hat, _ = norm_parts(hidden)
        s.second[:, lanes] = (hat * s.cols[G2] + s.cols[B2]).astype(BF)
        return carry

    lax.fori_loop(0, windows, norm_two, 0)

    def feed(index, carry):
        rows = chunk_of(index)
        inner = mm(s.w_fc1[:, rows], s.second[...], 0, 0) + wide(s.cols[F1B + index], windows)
        active, slope = gelu_parts(inner)
        active = active.astype(BF)
        s.active[rows, :] = active
        s.slope[rows, :] = slope.astype(BF)
        s.work[...] += mm(s.w_fc2[rows, :], active, 0, 0)
        return carry

    lax.fori_loop(0, FF // CHUNK, feed, 0)


def backward(s):
    windows = s.x.shape[1] // LANES
    s.sums[...] = jnp.zeros(s.sums.shape, F32)
    s.grad_bias[...] = jnp.zeros(s.grad_bias.shape, F32)
    lowered = s.grad[...].astype(BF)
    s.low[...] = lowered
    s.sums[F2B] = fold(lowered.astype(F32))
    s.work[...] = jnp.zeros(s.work.shape, F32)

    def feed(index, carry):
        rows = chunk_of(index)
        put_feed_rows(s.units, index, mm(s.active[rows, :], s.low[...], 1, 1))
        grad_inner = mm(s.w_fc2[rows, :], s.low[...], 1, 0) * s.slope[rows, :].astype(F32)
        grad_inner = grad_inner.astype(BF)
        s.sums[F1B + index] = fold(grad_inner.astype(F32))
        put_shares(s.units, UNIT_FC1 + index, mm(s.second[...], grad_inner, 1, 1))
        s.work[...] += mm(s.w_fc1[:, rows], grad_inner, 1, 0)
        return carry

    lax.fori_loop(0, FF // CHUNK, feed, 0)

    def norm_two(index, carry):
        lanes = lane_tile(index)
        hat, scale = norm_parts(s.hidden[:, lanes])
        grad = s.work[:, lanes]
        s.sums[G2] += grad * hat
        s.sums[B2] += grad
        grad = s.grad[:, lanes] + norm_pull(grad, s.cols[G2], hat, scale)
        s.grad[:, lanes] = grad
        grad_low = (grad * s.live[:, lanes]).astype(BF)
        s.low[:, lanes] = grad_low
        s.sums[PB] += grad_low.astype(F32)
        return carry

    lax.fori_loop(0, windows, norm_two, 0)

    put_shares(s.units, UNIT_PROJ, mm(s.merged[...], s.low[...], 1, 1))
    s.grad_merged[...] = mm(s.w_proj[...], s.low[...], 1, 0).astype(BF)

    def attend(index, carry):
        lanes = lane_tile(index)
        for head in range(HEADS):
            query = s.qkv[head_rows(head), lanes]
            key = s.qkv[head_rows(head, D), lanes]
            value = s.qkv[head_rows(head, 2 * D), lanes]
            grad_out = s.grad_merged[head_rows(head), lanes]
            soft_low = s.soft[index * HEADS + head]
            soft = soft_low.astype(F32)
            grad_soft = mm(value, grad_out, 0, 0)
            inner = jnp.sum(soft * grad_soft, axis=0, keepdims=True)
            grad_scores = (soft * (grad_soft - inner)).astype(BF)
            s.grad_bias[head] += grad_scores.astype(F32)
            grad_query = (mm(key, grad_scores, 1, 0) * SCORE_SCALE).astype(BF)
            grad_key = (mm(query, grad_scores, 1, 1) * SCORE_SCALE).astype(BF)
            grad_value = mm(grad_out, soft_low, 1, 1).astype(BF)
            s.grad_qkv[head_rows(head), lanes] = grad_query
            s.grad_qkv[head_rows(head, D), lanes] = grad_key
            s.grad_qkv[head_rows(head, 2 * D), lanes] = grad_value
            s.sums[QB, head_rows(head), :] += grad_query.astype(F32)
            s.sums[VB, head_rows(head), :] += grad_value.astype(F32)
        return carry

    lax.fori_loop(0, windows, attend, 0)
    s.work[...] = jnp.zeros(s.work.shape, F32)

    def project(index, carry):
        rows = chunk_of(index)
        put_shares(s.units, UNIT_QKV + index, mm(s.normed[...], s.grad_qkv[rows, :], 1, 1))
        s.work[...] += mm(s.w_qkv[:, rows], s.grad_qkv[rows, :], 1, 0)
        return carry

    lax.fori_loop(0, 3, project, 0)

    def norm_one(index, carry):
        lanes = lane_tile(index)
        hat, scale = norm_parts(s.x[:, lanes])
        grad = s.work[:, lanes]
        s.sums[G1] += grad * hat
        s.sums[B1] += grad
        s.grad[:, lanes] += norm_pull(grad, s.cols[G1], hat, scale)
        return carry

    lax.fori_loop(0, windows, norm_one, 0)


def pack_sums(sums_ref, out_ref):
    places = lax.broadcasted_iota(jnp.int32, (D, LANES), 1)
    packed = jnp.zeros((D, LANES), F32)
    for index in range(VECTORS):
        packed = jnp.where(places == index, jnp.sum(sums_ref[index], axis=1, keepdims=True), packed)
    out_ref[...] = packed.T[: out_ref.shape[0]]


class Refs:
    def __init__(self, names, refs):
        for name, ref in zip(names, refs, strict=True):
            setattr(self, name, ref)


WEIGHTS = ("w_qkv", "w_proj", "w_fc1", "w_fc2")


def saved_shapes(lanes):
    windows = lanes // LANES
    return {
        "x": ((D, lanes), F32),
        "normed": ((D, lanes), BF),
        "qkv": ((3 * D, lanes), BF),
        "soft": ((windows * HEADS, LANES, LANES), BF),
        "merged": ((D, lanes), BF),
        "hidden": ((D, lanes), F32),
        "second": ((D, lanes), BF),
        "active": ((FF, lanes), BF),
        "slope": ((FF, lanes), BF),
    }


def grad_shapes(rows, shares):
    return {
        "grad_page": ((rows, D), F32),
        "units": ((UNITS, shares, D // shares, CHUNK), F32),
        "grad_vectors": ((16, D), F32),
        "grad_table": ((WIN, HEADS, 2 * LANES), F32),
    }


def forward_scratch(lanes):
    return {
        "work": ((D, lanes), F32),
        "cols": ((VECTORS + 1, D, LANES), F32),
        "bias": ((HEADS, LANES, LANES), F32),
        "bias_rows": ((HEADS * LANES, LANES), F32),
    }


def backward_scratch(lanes):
    return {
        "work": ((D, lanes), F32),
        "cols": ((VECTORS + 1, D, LANES), F32),
        "grad": ((D, lanes), F32),
        "low": ((D, lanes), BF),
        "grad_merged": ((D, lanes), BF),
        "grad_qkv": ((3 * D, lanes), BF),
        "grad_bias": ((HEADS, LANES, LANES), F32),
        "bias_rows": ((HEADS * LANES, LANES), F32),
        "sums": ((VECTORS, D, LANES), F32),
    }


def run_forward(names, *refs):
    s = Refs(names, refs)
    spread_columns(s.vectors, s.cols)
    spread_bias(s.table, s.bias_rows, s.bias)
    to_channels(s.upper, s.lower, s.place, s.x)
    forward(s)
    to_page(s.work, s.place, s.out_page)


def run_backward(names, *refs):
    s = Refs(names, refs)
    spread_columns(s.vectors, s.cols)
    to_channels(s.grad_upper, s.grad_lower, s.place, s.grad)
    backward(s)
    to_page(s.grad, s.place, s.grad_page)
    gather_bias(s.grad_bias, s.bias_rows, s.grad_table)
    pack_sums(s.sums, s.grad_vectors)


def run_both(names, *refs):
    s = Refs(names, refs)
    spread_columns(s.vectors, s.cols)
    spread_bias(s.table, s.bias_rows, s.bias)
    to_channels(s.upper, s.lower, s.place, s.x)
    forward(s)
    to_page(s.work, s.place, s.out_page)
    to_channels(s.grad_upper, s.grad_lower, s.place, s.grad)
    backward(s)
    to_page(s.grad, s.place, s.grad_page)
    gather_bias(s.grad_bias, s.bias_rows, s.grad_table)
    pack_sums(s.sums, s.grad_vectors)


def call(body, name, inputs, outputs, scratch, flops):
    names = tuple(inputs) + tuple(outputs) + tuple(scratch)
    in_vmem = pl.BlockSpec(memory_space=pltpu.VMEM)
    moved = sum(value.size * value.dtype.itemsize for value in inputs.values())
    results = pl.pallas_call(
        functools.partial(body, names),
        out_shape=[jax.ShapeDtypeStruct(*shape) for shape in outputs.values()],
        in_specs=[in_vmem] * len(inputs),
        out_specs=[in_vmem] * len(outputs),
        scratch_shapes=[pltpu.VMEM(*shape) for shape in scratch.values()],
        compiler_params=pltpu.CompilerParams(vmem_limit_bytes=VMEM_LIMIT),
        cost_estimate=pl.CostEstimate(flops=flops, bytes_accessed=moved, transcendentals=0),
        name=name,
    )(*inputs.values())
    return dict(zip(outputs, results))


def placements(cols):
    windows = cols // WIN
    plain = np.zeros((WIN * SPAN, windows * LANES), np.float32)
    moved = np.zeros((WIN * SPAN, windows * LANES), np.float32)
    for row in range(WIN):
        for col in range(cols):
            source = row * SPAN + col
            plain[source, (col // WIN) * LANES + row * WIN + col % WIN] = 1
            new_row, new_col = (row - SHIFT) % WIN, (col - SHIFT) % cols
            moved[source, (new_col // WIN) * LANES + new_row * WIN + new_col % WIN] = 1
    return plain.astype(jnp.bfloat16), moved.astype(jnp.bfloat16)


def table_spread():
    size = 2 * WIN - 1
    spread = np.zeros((size * size, WIN, 2 * LANES), np.float32)
    for key_col in range(WIN):
        for offset in range(size):
            for col in range(WIN):
                spread[offset * size + col - key_col + WIN - 1, key_col, offset * WIN + col] = 1
    return spread


def window_masks(live_windows, regions):
    windows = live_windows.shape[0]
    differ = (regions[:, :, None] != regions[:, None, :]).astype(F32)
    masked = MASK_VALUE * differ + MASK_VALUE * (1.0 - live_windows)[:, :, None]
    wide_mask = jnp.full((windows, LANES, LANES), NEVER, F32)
    masked = jnp.pad(masked, ((0, 0), (0, 0), (0, LANES - AREA)))
    return wide_mask.at[:, :AREA, :].set(masked)


def to_windows(values):
    windows = values.shape[1] // WIN
    return values.reshape(WIN, windows, WIN).swapaxes(0, 1).reshape(windows, AREA)


def live_lanes(live_windows):
    return jnp.pad(live_windows, ((0, 0), (0, LANES - AREA))).reshape(1, -1)


def shifted_regions(row_index, row_count, col_width):
    row_ids = WIN * row_index + jnp.arange(WIN)
    height = WIN * row_count
    row_part = (row_ids >= height - WIN).astype(jnp.int32) + (row_ids >= height - SHIFT).astype(jnp.int32)
    col_ids = jnp.arange(col_width)
    col_part = (col_ids >= col_width - WIN).astype(jnp.int32) + (col_ids >= col_width - SHIFT).astype(jnp.int32)
    return row_part[:, None] * 3 + col_part[None, :]


def shifted(value, axis, steps):
    count = lax.axis_size(axis)
    pairs = [(source, (source + steps) % count) for source in range(count)]
    return lax.ppermute(value, axis, pairs)


def page_rows(values):
    rows, cols, width = values.shape
    return jnp.pad(values, ((0, 0), (0, SPAN - cols), (0, 0))).reshape(rows * SPAN, width)


def from_page_rows(values, cols):
    return values.reshape(-1, SPAN, values.shape[-1])[:, :cols]


class Butterfly:
    def __init__(self, pages, shares):
        self.page_bits = pages.bit_length() - 1
        self.row_bits = shares.bit_length() - 1
        self.sizes = [(shares, D // shares, CHUNK)]
        for level in range(self.page_bits):
            count, rows, cols = self.sizes[-1]
            self.sizes.append((count, rows, cols // 2) if level < 2 else (count, rows // 2, cols))
        for _ in range(self.row_bits):
            count, rows, cols = self.sizes[-1]
            self.sizes.append((count // 2, rows, cols))
        self.halvings = self.page_bits + self.row_bits
        self.phases = self.halvings + self.page_bits

    def weight(self, level, order):
        if level == 0:
            return 1
        return 2 ** (1 + (level - 1 + order) % (self.page_bits - 1))

    def partner(self, level, order):
        page, row = lax.axis_index("page"), lax.axis_index("row")
        if level < self.page_bits:
            stride = self.weight(level, order)
            bit = (page // stride) % 2
            return bit, (page + (1 - 2 * bit) * stride, row)
        stride = 2 ** (level - self.page_bits)
        bit = (row // stride) % 2
        return bit, (page, row + (1 - 2 * bit) * stride)

    def half(self, level, which):
        count, rows, cols = self.sizes[level + 1]
        if level >= self.page_bits:
            return (pl.ds(which * count, count), slice(None), slice(None))
        if level < 2:
            return (slice(None), slice(None), pl.ds(pl.multiple_of(which * cols, LANES), cols))
        return (slice(None), pl.ds(pl.multiple_of(which * rows, 8), rows), slice(None))

    def place(self, level, order):
        _, rows, cols = self.sizes[level + 1]
        row_start, col_start = 0, 0
        for bits in range(level + 1):
            bit, _ = self.partner(bits, order)
            if bits < 2:
                col_start = col_start + bit * self.sizes[bits + 1][2]
            else:
                row_start = row_start + bit * self.sizes[bits + 1][1]
        return (
            pl.ds(pl.multiple_of(row_start, 8), rows),
            pl.ds(pl.multiple_of(col_start, LANES), cols),
        )


def reduce_body(plan, *refs):
    halvings, phases = plan.halvings, plan.phases
    units_refs, small_ref, done_ref, small_out = refs[:2], refs[2], refs[3], refs[4]
    parts = refs[5 : 5 + halvings]
    small_parts, send_sems, recv_sems, small_send, small_recv = refs[5 + halvings :]
    pairs = UNITS

    barrier = pltpu.get_barrier_semaphore()
    for level in range(halvings):
        _, device = plan.partner(level, 0)
        pl.semaphore_signal(barrier, inc=1, device_id=device, device_id_type=pl.DeviceIdType.MESH)
    pl.semaphore_wait(barrier, halvings)

    def copy(phase, unit, order, source_ref):
        if phase < halvings:
            bit, device = plan.partner(phase, order)
            source = source_ref.at[plan.half(phase, 1 - bit)]
            target = parts[phase].at[unit]
        else:
            level = phases - 1 - phase
            _, device = plan.partner(level, order)
            source = target = done_ref.at[(unit,) + plan.place(level, order)]
        return pltpu.make_async_remote_copy(
            src_ref=source,
            dst_ref=target,
            send_sem=send_sems.at[unit, phase],
            recv_sem=recv_sems.at[unit, phase],
            device_id=device,
            device_id_type=pl.DeviceIdType.MESH,
        )

    def held(phase, unit, layer, index):
        return units_refs[layer].at[index] if phase == 0 else parts[phase - 1].at[unit]

    def finish(phase, unit, order, layer, index):
        source = held(min(phase, halvings), unit, layer, index)
        copy(phase, unit, order, source).wait()
        if phase < halvings:
            bit, _ = plan.partner(phase, order)
            target = parts[phase].at[unit]
            mine = source.at[plan.half(phase, bit)]
            for share in range(target.shape[0]):
                target[share] += mine[share]
        if phase == halvings - 1:
            done_ref[(unit,) + plan.place(plan.page_bits - 1, order)] = parts[phase][unit, 0]

    def small_copy(phase):
        _, device = plan.partner(phase, 0)
        source = small_ref if phase == 0 else small_parts.at[phase - 1]
        return pltpu.make_async_remote_copy(
            src_ref=source,
            dst_ref=small_parts.at[phase],
            send_sem=small_send.at[phase],
            recv_sem=small_recv.at[phase],
            device_id=device,
            device_id_type=pl.DeviceIdType.MESH,
        )

    small_copy(0).start()

    def run_layer(pair, stage, layer):
        for order in range(2):
            index = 2 * (pair % (UNITS // 2)) + order
            unit = 2 * pair + order
            if stage > 0:
                finish(stage - 1, unit, order, layer, index)
            if stage < phases:
                copy(stage, unit, order, held(min(stage, halvings), unit, layer, index)).start()

    def step(time, carry):
        for stage in range(phases, -1, -1):
            pair = time - SKEW * stage
            if stage > 1:

                @pl.when((pair >= 0) & (pair < pairs))
                def _():
                    run_layer(pair, stage, 0)

            else:
                for layer in range(2):

                    @pl.when((pair >= layer * (UNITS // 2)) & (pair < (layer + 1) * (UNITS // 2)))
                    def _():
                        run_layer(pair, stage, layer)

        for phase in range(halvings):

            @pl.when(time == phase + 1)
            def _():
                small_copy(phase).wait()
                small_parts[phase] += small_ref[...] if phase == 0 else small_parts[phase - 1]
                if phase + 1 < halvings:
                    small_copy(phase + 1).start()

        return carry

    lax.fori_loop(0, pairs + SKEW * phases, step, 0)
    small_out[...] = small_parts[halvings - 1]


def reduce_all(units, small):
    pages, shares = lax.axis_size("page"), lax.axis_size("row")
    plan = Butterfly(pages, shares)
    total = 2 * UNITS
    in_vmem = pl.BlockSpec(memory_space=pltpu.VMEM)
    return pl.pallas_call(
        functools.partial(reduce_body, plan),
        out_shape=[
            jax.ShapeDtypeStruct((total, D // shares, CHUNK), F32),
            jax.ShapeDtypeStruct(small.shape, F32),
        ],
        in_specs=[in_vmem] * 3,
        out_specs=[in_vmem] * 2,
        scratch_shapes=[pltpu.VMEM((total,) + size, F32) for size in plan.sizes[1:]]
        + [pltpu.VMEM((plan.halvings,) + small.shape, F32)]
        + [pltpu.SemaphoreType.DMA((total, plan.phases))] * 2
        + [pltpu.SemaphoreType.DMA((plan.halvings,))] * 2,
        compiler_params=pltpu.CompilerParams(
            vmem_limit_bytes=VMEM_LIMIT, collective_id=0, has_side_effects=True
        ),
        name="reduce_gradients",
    )(*units, small)


def per_device(
    page_tokens,
    blank_mask,
    cotangent,
    ln_gain,
    ln_bias,
    qv_bias,
    rel_table,
    w_qkv,
    w_proj,
    proj_bias,
    w_fc1,
    fc1_bias,
    w_fc2,
    fc2_bias,
):
    cols = page_tokens.shape[2]
    lanes = cols // WIN * LANES
    half = SHIFT * SPAN
    plain, moved = placements(cols)
    vectors = jnp.concatenate(
        [
            jnp.stack([ln_gain[:, :D], ln_bias[:, :D], ln_gain[:, D:], ln_bias[:, D:]], axis=1),
            jnp.stack([qv_bias[:, :D], qv_bias[:, D:], proj_bias, fc2_bias], axis=1),
            fc1_bias.reshape(2, FF // D, D),
            jnp.zeros((2, 4, D), F32),
        ],
        axis=1,
    ).swapaxes(1, 2)
    spread = table_spread()
    tables = jnp.einsum("lht,txj->lxhj", rel_table, spread, precision=lax.Precision.HIGHEST)

    live_own = 1.0 - blank_mask[0, 0].astype(F32)
    live_own = jnp.repeat(live_own, WIN)
    tokens = page_rows(page_tokens[0].astype(F32))
    grad_end = page_rows(cotangent[0])
    grad_upper, live_upper = shifted((grad_end[:half], live_own), "row", -1)

    live_one = to_windows(jnp.broadcast_to(live_own, (WIN, cols)))
    live_two = jnp.concatenate(
        [jnp.broadcast_to(live_own, (WIN - SHIFT, cols)), jnp.broadcast_to(live_upper, (SHIFT, cols))]
    )
    live_two = to_windows(jnp.roll(live_two, -SHIFT, axis=1))
    regions_two = to_windows(shifted_regions(lax.axis_index("row"), lax.axis_size("row"), cols))
    masks = (window_masks(live_one, jnp.zeros_like(regions_two)), window_masks(live_two, regions_two))
    lives = (live_lanes(live_one), live_lanes(live_two))

    def common(layer):
        return {
            "place": (jnp.asarray(plain), jnp.asarray(moved))[layer],
            "live": lives[layer],
            "vectors": vectors[layer],
            "w_qkv": w_qkv[layer],
            "w_proj": w_proj[layer],
            "w_fc1": w_fc1[layer],
            "w_fc2": w_fc2[layer],
        }

    def extra(layer):
        return {"mask": masks[layer], "table": tables[layer]}

    page_out = {"out_page": ((WIN * SPAN, D), F32)}
    first = call(
        run_forward,
        "layer0_forward",
        {"upper": tokens[:half], "lower": tokens[half:], **common(0), **extra(0)},
        {**page_out, **saved_shapes(lanes)},
        forward_scratch(lanes),
        6 * 10**9,
    )
    first_out = first.pop("out_page")
    upper_in = shifted(first_out[:half], "row", -1)
    second = call(
        run_both,
        "layer1_both",
        {
            "upper": upper_in,
            "lower": first_out[half:],
            "grad_upper": grad_upper,
            "grad_lower": grad_end[half:],
            **common(1),
            **extra(1),
        },
        {**page_out, **grad_shapes(WIN * SPAN, lax.axis_size("row"))},
        {**saved_shapes(lanes), **forward_scratch(lanes), **backward_scratch(lanes)},
        18 * 10**9,
    )
    lower_grad = shifted(second["grad_page"][:half], "row", 1)
    third = call(
        run_backward,
        "layer0_backward",
        {"grad_upper": lower_grad, "grad_lower": second["grad_page"][half:], **common(0), **first},
        grad_shapes(WIN * SPAN, lax.axis_size("row")),
        backward_scratch(lanes),
        12 * 10**9,
    )
    lower_out = shifted(second["out_page"][:half], "row", 1)
    final_out = jnp.concatenate(
        [from_page_rows(lower_out, cols), from_page_rows(second["out_page"][half:], cols)]
    )
    grad_first = from_page_rows(third["grad_page"], cols)

    tables_grad = jnp.stack([third["grad_table"], second["grad_table"]])
    tables_grad = jnp.einsum("lxhj,txj->lht", tables_grad, spread, precision=lax.Precision.HIGHEST)
    tables_grad = jnp.pad(tables_grad, ((0, 0), (0, 0), (0, D - tables_grad.shape[-1])))
    vectors_grad = jnp.stack([third["grad_vectors"], second["grad_vectors"]])
    small = jnp.concatenate([vectors_grad.reshape(-1, D), tables_grad.reshape(-1, D)])
    done, small = reduce_all((third["units"], second["units"]), small)
    vectors_grad = small[: 2 * 16].reshape(2, 16, D)
    tables_grad = small[2 * 16 :].reshape(2, HEADS, D)[:, :, : rel_table.shape[-1]]
    done = done.reshape((2, UNITS) + done.shape[1:])

    def side_by_side(start, stop):
        return jnp.concatenate([done[:, index] for index in range(start, stop)], axis=-1)

    def share(*indices):
        joined = jnp.concatenate([vectors_grad[:, index] for index in indices], axis=1)
        size = joined.shape[1] // lax.axis_size("row")
        return lax.dynamic_slice_in_dim(joined, lax.axis_index("row") * size, size, axis=1)

    return (
        final_out[None],
        grad_first[None],
        share(G1, G2),
        share(B1, B2),
        share(QB, VB),
        tables_grad,
        side_by_side(UNIT_QKV, UNIT_PROJ),
        done[:, UNIT_PROJ],
        share(PB),
        side_by_side(UNIT_FC1, UNIT_FC2),
        share(*range(F1B, F1B + FF // D)),
        done[:, UNIT_FC2:].reshape(2, -1, D),
        share(F2B),
    )


def solution(mesh):
    split_rows = P("page", "row", None, None)
    return jax.shard_map(
        per_device,
        mesh=mesh,
        in_specs=(split_rows, P("page", "row", None), split_rows) + (P(),) * 11,
        out_specs=(
            split_rows,
            split_rows,
            P(None, "row"),
            P(None, "row"),
            P(None, "row"),
            P(),
            P(None, "row", None),
            P(None, "row", None),
            P(None, "row"),
            P(None, "row", None),
            P(None, "row"),
            P(None, "row", None),
            P(None, "row"),
        ),
        check_vma=False,
    )
```

```python
import functools

import jax
import jax.numpy as jnp
import numpy as np
from jax import lax
from jax.experimental import pallas as pl
from jax.experimental.pallas import tpu as pltpu
from jax.sharding import PartitionSpec as P

WIN = 10
SHIFT = 5
AREA = WIN * WIN
LANES = 128
SPAN = 64
D = 512
HEADS = 16
HEAD_DIM = 32
FF = 2048
CHUNK = 512
EPSILON = 1e-05
MASK_VALUE = -100.0
NEVER = -1e30
SCORE_SCALE = HEAD_DIM ** (-0.5)
VMEM_LIMIT = 63 * 1024 * 1024
BF = jnp.bfloat16
F32 = jnp.float32
G1, B1, G2, B2, QB, VB, PB, F2B, F1B, NONE = 0, 1, 2, 3, 4, 5, 6, 7, 8, 12
VECTORS = 12
UNIT_FC1, UNIT_FC2, UNIT_PROJ, UNIT_QKV, UNITS = 0, 4, 8, 9, 12
CLASSES = 3
TRIPLES = 2 * UNITS // CLASSES
SKEW = 2
RING = 3
OFFSETS = (2 * WIN - 1) ** 2
TABLE = 384
SMALL = 32


def mm(left, right, left_dim, right_dim):
    return lax.dot_general(
        left, right, (((left_dim,), (right_dim,)), ((), ())), preferred_element_type=F32
    )


def split(values):
    high = values.astype(BF)
    return high, (values - high.astype(F32)).astype(BF)


def lane_tile(index):
    return pl.ds(pl.multiple_of(index * LANES, LANES), LANES)


def chunk_of(index):
    return pl.ds(pl.multiple_of(index * CHUNK, CHUNK), CHUNK)


def wide(column, count):
    return jnp.concatenate([column] * count, axis=1)


def fold(values):
    total = values[:, :LANES]
    for start in range(LANES, values.shape[1], LANES):
        total = total + values[:, start : start + LANES]
    return total


def norm_parts(values):
    center = values - jnp.sum(values, axis=0, keepdims=True) * (1.0 / D)
    spread = jnp.sum(center * center, axis=0, keepdims=True) * (1.0 / D)
    scale = lax.rsqrt(spread + EPSILON)
    return center * scale, scale


def norm_pull(grad, gain, hat, scale):
    scaled = grad * gain
    mean_one = jnp.sum(scaled, axis=0, keepdims=True) * (1.0 / D)
    mean_two = jnp.sum(scaled * hat, axis=0, keepdims=True) * (1.0 / D)
    return scale * (scaled - mean_one - hat * mean_two)


def gelu_parts(inner):
    step = 1.0 / (1.0 + (0.3275911 * 0.7071067811865476) * jnp.abs(inner))
    bell = jnp.exp(inner * inner * -0.5)
    poly = 0.5 * 1.061405429
    for factor in (-1.453152027, 1.421413741, -0.284496736, 0.254829592):
        poly = poly * step + 0.5 * factor
    tail = poly * step * bell
    below = jnp.where(inner >= 0, 1.0 - tail, tail)
    return inner * below, below + inner * bell * 0.3989422804014327


def to_channels(page_ref, place_ref, out_ref):
    def step(index, carry):
        channels = pl.ds(pl.multiple_of(index * 256, 256), 256)
        values = page_ref[:, channels]
        pieces = (values,) if values.dtype == BF else split(values)
        total = None
        for piece in pieces:
            term = mm(piece, place_ref[...], 0, 0)
            total = term if total is None else total + term
        out_ref[channels, :] = total
        return carry

    lax.fori_loop(0, D // 256, step, 0)


def to_page(values_ref, place_ref, out_ref):
    def step(index, carry):
        rows = pl.ds(pl.multiple_of(index * 256, 256), 256)
        high, low = split(values_ref[rows, :])
        out_ref[:, rows] = mm(place_ref[...], high, 1, 1) + mm(place_ref[...], low, 1, 1)
        return carry

    lax.fori_loop(0, D // 256, step, 0)


def to_rows(patches_ref, page_ref, start=0):
    for row in range(patches_ref.shape[0]):
        page_ref[pl.ds((start + row) * SPAN, patches_ref.shape[1]), :] = patches_ref[row]


def from_rows(page_ref, patches_ref):
    for row in range(patches_ref.shape[0]):
        patches_ref[row] = page_ref[pl.ds(row * SPAN, patches_ref.shape[1]), :]


def spread_columns(s, layer, wanted):
    rows = s.vector_rows
    halves = ((G1, s.ln_gain, 0), (B1, s.ln_bias, 0), (G2, s.ln_gain, 1), (B2, s.ln_bias, 1))
    halves += ((QB, s.qv_bias, 0), (VB, s.qv_bias, 1), (PB, s.proj_bias, 0), (F2B, s.fc2_bias, 0))
    halves += tuple((F1B + part, s.fc1_bias, part) for part in range(FF // D))
    for index, source, part in halves:
        rows[index : index + 1, :] = source[layer : layer + 1, part * D : (part + 1) * D]
    rows[VECTORS:, :] = jnp.zeros((rows.shape[0] - VECTORS, D), F32)
    columns = rows[...].T
    for index in wanted:
        s.cols[index] = jnp.broadcast_to(columns[:, index : index + 1], (D, LANES))


def spread_part(col):
    rows, lanes = (col // 2) * 2 * LANES, (col % 2) * TABLE
    return slice(rows, rows + 2 * LANES), slice(lanes, lanes + TABLE)


def spread_bias(table_ref, spread_ref, rows_ref, bias_ref):
    table = split(table_ref[...])
    parts = []
    for col in range(WIN):
        chosen = spread_ref[spread_part(col)]
        parts.append(mm(table[0], chosen, 1, 1) + mm(table[1], chosen, 1, 1))
    source = jnp.concatenate(parts, axis=0)
    rows_ref[...] = jnp.zeros(rows_ref.shape, F32)
    for row in range(WIN):
        shift = (WIN - 1 - row) * WIN
        moved = source if shift == 0 else pltpu.roll(source, 2 * LANES - shift, axis=1)
        rows_ref[pl.ds(row * WIN * HEADS, WIN * HEADS), :] = moved[:, :LANES]
    for head in range(HEADS):
        bias_ref[head] = rows_ref[pl.ds(head, LANES, stride=HEADS), :]


def gather_bias(grad_ref, spread_ref, rows_ref, out_ref):
    for head in range(HEADS):
        rows_ref[pl.ds(head, LANES, stride=HEADS), :] = grad_ref[head]
    total = jnp.zeros((WIN * HEADS, 2 * LANES), F32)
    for row in range(WIN):
        shift = (WIN - 1 - row) * WIN
        piece = rows_ref[pl.ds(row * WIN * HEADS, WIN * HEADS), :]
        piece = jnp.concatenate([piece, jnp.zeros_like(piece)], axis=1)
        total = total + (piece if shift == 0 else pltpu.roll(piece, shift, axis=1))
    table = jnp.zeros((HEADS, TABLE), F32)
    for col in range(WIN):
        for part in split(total[col * HEADS : (col + 1) * HEADS]):
            table = table + mm(part, spread_ref[spread_part(col)], 1, 0)
    out_ref[...] = jnp.concatenate([table, jnp.zeros((HEADS, D - TABLE), F32)], axis=1)


def region_masks(shifted_layer, out_ref):
    key = lax.broadcasted_iota(jnp.int32, (LANES, LANES), 0)
    query = lax.broadcasted_iota(jnp.int32, (LANES, LANES), 1)
    padding = jnp.where(key < AREA, 0.0, NEVER)
    out_ref[0] = padding
    out_ref[1] = padding
    if shifted_layer:
        last = lax.axis_index("row") == lax.axis_size("row") - 1
        rows_differ = ((key >= AREA // 2) != (query >= AREA // 2)) & last
        cols_differ = (key % WIN >= SHIFT) != (query % WIN >= SHIFT)
        out_ref[0] += jnp.where(rows_differ, MASK_VALUE, 0.0)
        out_ref[1] += jnp.where(rows_differ | cols_differ, MASK_VALUE, 0.0)


def head_rows(head, base=0):
    return pl.ds(base + head * HEAD_DIM, HEAD_DIM)


def reversed_bits(value, count):
    turned = 0
    for bit in range(count):
        turned = turned * 2 + (value // 2**bit) % 2
    return turned


def row_pieces(unit, shares):
    rows, count = CHUNK // shares, shares.bit_length() - 1
    return [(share * rows, unit, reversed_bits(share, count)) for share in range(shares)]


def feed_pieces(index, shares):
    rows, count, parts = CHUNK // shares, shares.bit_length() - 1, FF // CHUNK
    pieces = []
    for share in range(shares // parts):
        place = reversed_bits(index * (shares // parts) + share, count)
        for part in range(parts):
            pieces.append(((share * parts + part) * rows, UNIT_FC2 + part, place))
    return pieces


class Units:
    def __init__(self, s):
        self.s = s
        self.shares = s.units.shape[1]

    def stage_copies(self, slot, pieces):
        rows = CHUNK // self.shares
        return [
            pltpu.make_async_copy(
                self.s.staged.at[slot, pl.ds(start, rows)],
                self.s.units.at[unit, place],
                self.s.stage_sems.at[slot, number],
            )
            for number, (start, unit, place) in enumerate(pieces)
        ]

    def put(self, slot, grad, pieces, first):
        if first is not True:

            @pl.when(jnp.logical_not(first))
            def _():
                self.settle(slot)

        self.s.staged[slot] = grad
        for copy in self.stage_copies(slot, pieces):
            copy.start()

    def settle(self, slot):
        for copy in self.stage_copies(slot, row_pieces(0, self.shares)):
            copy.wait()

    def pump(self, point, index=0):
        pass


def forward(s):
    windows = s.x.shape[1] // LANES
    s.save("x")

    def norm_one(index, carry):
        lanes = lane_tile(index)
        hat, _ = norm_parts(s.x[:, lanes])
        s.normed[:, lanes] = (hat * s.cols[G1] + s.cols[B1]).astype(BF)
        return carry

    lax.fori_loop(0, windows, norm_one, 0)
    s.save("normed")
    s.need("w_qkv")

    def project(index, carry):
        which = jnp.where(index == 0, QB, jnp.where(index == 1, NONE, VB))
        rows = chunk_of(index)
        out = mm(s.w_qkv[:, rows], s.normed[...], 0, 0)
        s.qkv[rows, :] = (out + wide(s.cols[which], windows)).astype(BF)
        return carry

    lax.fori_loop(0, 3, project, 0)
    s.save("qkv")

    def attend(index, carry):
        lanes = lane_tile(index)
        live = jnp.broadcast_to(s.live[pl.ds(index, 1), :], (LANES, LANES)).T
        masked = s.regions[jnp.where(index == windows - 1, 1, 0)] + MASK_VALUE * (1.0 - live)
        for head in range(HEADS):
            query = s.qkv[head_rows(head), lanes]
            key = s.qkv[head_rows(head, D), lanes]
            value = s.qkv[head_rows(head, 2 * D), lanes]
            scores = mm(key, query, 0, 0) * SCORE_SCALE + (s.bias[head] + masked)
            exponent = jnp.exp(scores - jnp.max(scores, axis=0, keepdims=True))
            total = jnp.sum(exponent, axis=0, keepdims=True)
            soft = (exponent * (1.0 / total)).astype(BF)
            s.soft[index * HEADS + head] = soft
            s.merged[head_rows(head), lanes] = mm(value, soft, 1, 0).astype(BF)
        return carry

    lax.fori_loop(0, windows, attend, 0)
    s.save("soft", "merged")
    s.need("w_proj")
    s.work[...] = mm(s.w_proj[...], s.merged[...], 0, 0)

    def norm_two(index, carry):
        lanes = lane_tile(index)
        hidden = s.x[:, lanes] + s.live[pl.ds(index, 1), :] * (s.work[:, lanes] + s.cols[PB])
        s.hidden[:, lanes] = hidden
        s.work[:, lanes] = hidden + s.cols[F2B]
        hat, _ = norm_parts(hidden)
        s.second[:, lanes] = (hat * s.cols[G2] + s.cols[B2]).astype(BF)
        return carry

    lax.fori_loop(0, windows, norm_two, 0)
    s.save("hidden", "second")
    s.need("w_fc1", "w_fc2")

    def feed(index, carry):
        rows = chunk_of(index)
        inner = mm(s.w_fc1[:, rows], s.second[...], 0, 0) + wide(s.cols[F1B + index], windows)
        active, slope = gelu_parts(inner)
        active = active.astype(BF)
        s.active[rows, :] = active
        s.slope[rows, :] = slope.astype(BF)
        s.work[...] += mm(s.w_fc2[rows, :], active, 0, 0)
        return carry

    lax.fori_loop(0, FF // CHUNK, feed, 0)
    s.save("active", "slope")


def backward(s, sink):
    windows = s.grad.shape[1] // LANES
    put, shares = sink.put, sink.shares
    s.sums[...] = jnp.zeros(s.sums.shape, F32)
    s.grad_bias[...] = jnp.zeros(s.grad_bias.shape, F32)
    lowered = s.grad[...].astype(BF)
    s.low[...] = lowered
    s.sums[F2B] = fold(lowered.astype(F32))
    s.work[...] = jnp.zeros(s.work.shape, F32)
    sink.pump("feed")
    s.need("active", "w_fc2", "slope", "second", "w_fc1")

    def feed(index, carry):
        rows = chunk_of(index)
        put(0, mm(s.active[rows, :], s.low[...], 1, 1), feed_pieces(index, shares), index == 0)
        grad_inner = mm(s.w_fc2[rows, :], s.low[...], 1, 0) * s.slope[rows, :].astype(F32)
        grad_inner = grad_inner.astype(BF)
        s.sums[F1B + index] = fold(grad_inner.astype(F32))
        put(1, mm(s.second[...], grad_inner, 1, 1), row_pieces(UNIT_FC1 + index, shares), index == 0)
        s.work[...] += mm(s.w_fc1[:, rows], grad_inner, 1, 0)
        return carry

    lax.fori_loop(0, FF // CHUNK, feed, 0)
    sink.settle(0)
    sink.settle(1)
    s.fetch("normed", "w_qkv", "spread")
    sink.pump("norm_two")
    s.need("hidden", "live")

    def norm_two(index, carry):
        lanes = lane_tile(index)
        hat, scale = norm_parts(s.hidden[:, lanes])
        grad = s.work[:, lanes]
        s.sums[G2] += grad * hat
        s.sums[B2] += grad
        grad = s.grad[:, lanes] + norm_pull(grad, s.cols[G2], hat, scale)
        s.grad[:, lanes] = grad
        grad_low = (grad * s.live[pl.ds(index, 1), :]).astype(BF)
        s.low[:, lanes] = grad_low
        s.sums[PB] += grad_low.astype(F32)
        return carry

    lax.fori_loop(0, windows, norm_two, 0)
    s.fetch("x")
    s.need("merged", "w_proj")
    put(0, mm(s.merged[...], s.low[...], 1, 1), row_pieces(UNIT_PROJ, shares), True)
    s.grad_merged[...] = mm(s.w_proj[...], s.low[...], 1, 0).astype(BF)

    def attend(index, carry):
        lanes = lane_tile(index)
        for head in range(HEADS):
            query = s.qkv[head_rows(head), lanes]
            key = s.qkv[head_rows(head, D), lanes]
            value = s.qkv[head_rows(head, 2 * D), lanes]
            grad_out = s.grad_merged[head_rows(head), lanes]
            soft_low = s.soft[index * HEADS + head]
            soft = soft_low.astype(F32)
            grad_soft = mm(value, grad_out, 0, 0)
            inner = jnp.sum(soft * grad_soft, axis=0, keepdims=True)
            grad_scores = (soft * (grad_soft - inner)).astype(BF)
            s.grad_bias[head] += grad_scores.astype(F32)
            grad_query = (mm(key, grad_scores, 1, 0) * SCORE_SCALE).astype(BF)
            grad_key = (mm(query, grad_scores, 1, 1) * SCORE_SCALE).astype(BF)
            grad_value = mm(grad_out, soft_low, 1, 1).astype(BF)
            s.grad_qkv[head_rows(head), lanes] = grad_query
            s.grad_qkv[head_rows(head, D), lanes] = grad_key
            s.grad_qkv[head_rows(head, 2 * D), lanes] = grad_value
            s.sums[QB, head_rows(head), :] += grad_query.astype(F32)
            s.sums[VB, head_rows(head), :] += grad_value.astype(F32)
        sink.pump("attended", index)
        return carry

    s.need("qkv", "soft")
    lax.fori_loop(0, windows, attend, 0)
    sink.settle(0)
    s.need("normed", "w_qkv")
    s.work[...] = jnp.zeros(s.work.shape, F32)

    def project(index, carry):
        rows = chunk_of(index)
        put(1, mm(s.normed[...], s.grad_qkv[rows, :], 1, 1), row_pieces(UNIT_QKV + index, shares), index == 0)
        s.work[...] += mm(s.w_qkv[:, rows], s.grad_qkv[rows, :], 1, 0)
        return carry

    lax.fori_loop(0, 3, project, 0)
    sink.settle(1)
    s.need("x")

    def norm_one(index, carry):
        lanes = lane_tile(index)
        hat, scale = norm_parts(s.x[:, lanes])
        grad = s.work[:, lanes]
        s.sums[G1] += grad * hat
        s.sums[B1] += grad
        s.grad[:, lanes] += norm_pull(grad, s.cols[G1], hat, scale)
        return carry

    lax.fori_loop(0, windows, norm_one, 0)


def pack_sums(sums_ref, out_ref):
    places = lax.broadcasted_iota(jnp.int32, (D, LANES), 1)
    packed = jnp.zeros((D, LANES), F32)
    for index in range(VECTORS):
        packed = jnp.where(places == index, jnp.sum(sums_ref[index], axis=1, keepdims=True), packed)
    out_ref[...] = packed.T[: out_ref.shape[0]]


class Kernel:
    def __init__(self, layout, refs):
        self.layout = layout
        hbm = {}
        for name, ref in zip(layout["order"], refs, strict=True):
            if name.startswith("hbm_"):
                hbm[name[4:]] = ref
            else:
                setattr(self, name, ref)
        self.loads, self.saves = {}, {}
        for number, (name, (target, part, layer)) in enumerate(layout["loads"].items()):
            source = hbm[name] if layer is None else hbm[name].at[layer]
            target = getattr(self, target)
            target = target if part is None else target.at[part]
            self.loads[name] = functools.partial(pltpu.make_async_copy, source, target, self.load_sems.at[number])
        for number, (name, (source, part)) in enumerate(layout["saves"].items()):
            source = getattr(self, source)
            source = source if part is None else source.at[part]
            self.saves[name] = functools.partial(pltpu.make_async_copy, source, hbm[name], self.save_sems.at[number])
        self.waiting, self.late = [], set(layout["late"])
        for name, target in layout["late"].items():
            setattr(self, name, getattr(self, target))
        for name in self.loads:
            if name not in self.late:
                self.loads[name]().start()

    def fetch(self, *names):
        for name in names:
            if name in self.late:
                self.loads[name]().start()

    def need(self, *names):
        for name in names:
            if name in self.loads:
                self.loads.pop(name)().wait()

    def save(self, *names):
        for name in names:
            if name in self.saves:
                copy = self.saves.pop(name)
                copy().start()
                self.waiting.append(copy)

    def close(self):
        assert not self.loads and not self.saves
        for copy in self.waiting:
            copy().wait()


def launch(body, name, inputs, outputs, vmem, semaphores, flops, saves=(), loads=(), raw=(), late=(), **params):
    loads, saves = dict(loads), dict(saves)
    vmem = dict(vmem)
    order = []
    for key, value in inputs.items():
        if key in raw:
            order.append(key)
            continue
        order.append("hbm_" + key)
        target, part, layer = loads.get(key, (key, None, None))
        target = dict(late).get(key, target)
        loads[key] = (target, part, layer)
        if target not in vmem:
            vmem[target] = (value.shape if layer is None else value.shape[1:], value.dtype)
    loads = {key: loads[key] for key in inputs if key not in raw}
    for key, shape in outputs.items():
        order.append("hbm_" + key if key in saves else key)
    semaphores = {
        **semaphores,
        "load_sems": pltpu.SemaphoreType.DMA((len(loads),)),
        "save_sems": pltpu.SemaphoreType.DMA((max(len(saves), 1),)),
    }
    order += list(vmem) + list(semaphores)
    late = dict(late)
    layout = {"order": order, "loads": loads, "saves": saves, "late": late}
    anywhere = pl.BlockSpec(memory_space=pl.ANY)
    moved = sum(value.size * value.dtype.itemsize for value in inputs.values())
    results = pl.pallas_call(
        lambda *refs: body(Kernel(layout, refs)),
        out_shape=[jax.ShapeDtypeStruct(*shape) for shape in outputs.values()],
        in_specs=[anywhere] * len(inputs),
        out_specs=[anywhere] * len(outputs),
        scratch_shapes=[pltpu.VMEM(*shape) for shape in vmem.values()] + list(semaphores.values()),
        compiler_params=pltpu.CompilerParams(vmem_limit_bytes=VMEM_LIMIT, **params),
        cost_estimate=pl.CostEstimate(flops=flops, bytes_accessed=moved, transcendentals=0),
        name=name,
    )(*inputs.values())
    return dict(zip(outputs, results))


VECTOR_NAMES = ("ln_gain", "ln_bias", "qv_bias", "proj_bias", "fc1_bias", "fc2_bias")
WEIGHTS = ("w_qkv", "w_proj", "w_fc1", "w_fc2")


def saved_shapes(lanes):
    windows = lanes // LANES
    return {
        "x": ((D, lanes), F32),
        "normed": ((D, lanes), BF),
        "qkv": ((3 * D, lanes), BF),
        "soft": ((windows * HEADS, LANES, LANES), BF),
        "merged": ((D, lanes), BF),
        "hidden": ((D, lanes), F32),
        "second": ((D, lanes), BF),
        "active": ((FF, lanes), BF),
        "slope": ((FF, lanes), BF),
    }


def shared_scratch(lanes):
    return {
        "work": ((D, lanes), F32),
        "vector_rows": ((16, D), F32),
        "bias_rows": ((HEADS * LANES, LANES), F32),
    }


def forward_scratch():
    return {
        "cols": ((VECTORS + 1, D, LANES), F32),
        "bias": ((HEADS, LANES, LANES), F32),
        "regions": ((2, LANES, LANES), F32),
    }


def backward_scratch(lanes):
    return {
        "grad": ((D, lanes), F32),
        "low": ((D, lanes), BF),
        "grad_merged": ((D, lanes), BF),
        "grad_qkv": ((3 * D, lanes), BF),
        "grad_bias": ((HEADS, LANES, LANES), F32),
        "sums": ((VECTORS, D, LANES), F32),
        "staged": ((2, CHUNK, CHUNK), F32),
    }


def units_shape(shares):
    return (UNITS, shares, CHUNK // shares, CHUNK), F32


def prepare_forward(s, layer):
    s.need(*VECTOR_NAMES)
    spread_columns(s, layer, range(VECTORS))
    s.cols[NONE] = jnp.zeros((D, LANES), F32)
    s.need("table", "spread", "live")
    spread_bias(s.table, s.spread, s.bias_rows, s.bias)
    region_masks(layer == 1, s.regions)


def run_first(s):
    s.page[...] = jnp.zeros(s.page.shape, s.page.dtype)
    s.need("tokens", "place")
    to_rows(s.tokens, s.page)
    to_channels(s.page, s.place, s.x)
    prepare_forward(s, 0)
    forward(s)
    to_page(s.work, s.place, s.page_out)
    s.save("out_upper", "out_lower")
    s.close()


def small_gradients(s, small_ref):
    gather_bias(s.grad_bias, s.spread, s.bias_rows, small_ref.at[pl.ds(16, HEADS)])
    pack_sums(s.sums, small_ref.at[pl.ds(0, 16)])


def run_second(s):
    s.need("upper", "lower", "place")
    to_channels(s.page, s.place, s.x)
    prepare_forward(s, 1)
    forward(s)
    to_page(s.work, s.place, s.page)
    from_rows(s.page, s.patches)
    s.save("out_patches")
    s.need("grad_upper", "grad_lower")
    to_rows(s.grad_upper, s.page)
    to_rows(s.grad_lower, s.page, SHIFT)
    to_channels(s.page, s.place, s.grad)
    backward(s, Units(s))
    to_page(s.grad, s.place, s.page)
    s.save("next_upper", "next_lower")
    small_gradients(s, s.small)
    s.save("small_out")
    s.close()


class Plan:
    def __init__(self, pages, shares):
        self.shares, self.rows = shares, CHUNK // shares
        page_bits, row_bits = pages.bit_length() - 1, shares.bit_length() - 1
        others = page_bits - 1
        self.steps = []
        for kind in range(CLASSES):
            turn = kind % 2 if others > 1 else 0
            page = [("page", 2 ** (1 + (bit + turn) % others)) for bit in range(others)]
            row = [("row", 2**bit) for bit in range(row_bits)]
            self.steps.append([("page", 1)] + (row + page if kind == 2 else page + row))
        self.page_steps = [[0] + [at for at, step in enumerate(steps) if at and step[0] == "page"] for steps in self.steps]
        self.halvings = page_bits + row_bits
        self.phases = self.halvings + page_bits
        self.sizes = []
        for kind in range(CLASSES):
            size = [shares, self.rows, CHUNK // 2]
            sizes = [tuple(size)]
            for level in range(1, self.halvings):
                axis = self.split_axis(kind, level)
                size[axis] //= 2
                sizes.append(tuple(size))
            self.sizes.append(sizes)

    def split_axis(self, kind, level):
        if self.steps[kind][level][0] == "row":
            return 0
        return 2 if self.page_steps[kind].index(level) < 2 else 1

    def partner(self, kind, level):
        axis, stride = self.steps[kind][level]
        page, row = lax.axis_index("page"), lax.axis_index("row")
        mine = page if axis == "page" else row
        bit = (mine // stride) % 2
        other = mine + (1 - 2 * bit) * stride
        return bit, ((other, row) if axis == "page" else (page, other))

    def part(self, kind, level, sent=False):
        starts, sizes = [0, 0, 0], [self.shares, self.rows, CHUNK // 2]
        for at in range(1, level + 1):
            axis = self.split_axis(kind, at)
            sizes[axis] //= 2
            bit, _ = self.partner(kind, at)
            which = 1 - bit if sent and at == level else bit
            starts[axis] = starts[axis] + which * sizes[axis]
        return (
            pl.ds(starts[0], sizes[0]),
            pl.ds(pl.multiple_of(starts[1], 8), sizes[1]),
            pl.ds(pl.multiple_of(starts[2], LANES), sizes[2]),
        )

    def place(self, kind, count):
        starts, sizes = [0, 0], [self.rows, CHUNK]
        for at in self.page_steps[kind][:count]:
            axis = self.split_axis(kind, at) - 1 if at else 1
            sizes[axis] //= 2
            bit, _ = self.partner(kind, at)
            starts[axis] = starts[axis] + bit * sizes[axis]
        return starts, sizes


TARGETS = (
    (("fc1", 0, 0), ("fc1", 0, 1), ("fc1", 0, 2)),
    (("fc1", 0, 3), ("fc2", 0, 0), ("fc2", 1, 0)),
    (("fc2", 2, 0), ("fc2", 3, 0), ("proj", 0, 0)),
    (("qkv", 0, 0), ("qkv", 0, 1), ("qkv", 0, 2)),
)


class Reducer(Units):
    def __init__(self, plan, s):
        super().__init__(s)
        self.plan = plan

    def barrier(self):
        plan = self.plan
        semaphore = pltpu.get_barrier_semaphore()
        for level in range(plan.halvings):
            _, device = plan.partner(0, level)
            pl.semaphore_signal(semaphore, inc=1, device_id=device, device_id_type=pl.DeviceIdType.MESH)
        pl.semaphore_wait(semaphore, plan.halvings)

    def remote(self, source, target, unit, phase, device):
        return pltpu.make_async_remote_copy(
            src_ref=source,
            dst_ref=target,
            send_sem=self.s.send_sems.at[unit, phase],
            recv_sem=self.s.recv_sems.at[unit, phase],
            device_id=device,
            device_id_type=pl.DeviceIdType.MESH,
        )

    def halving(self, triple, kind, level, layer):
        plan, s = self.plan, self.s
        unit = CLASSES * triple + kind
        bit, device = plan.partner(kind, level)
        target = s.landing[kind][level].at[triple % RING]
        if level == 0:
            half = CHUNK // 2
            source = (s.first_units, s.units)[layer].at[unit - layer * UNITS]
            source = source.at[:, :, pl.ds(pl.multiple_of((1 - bit) * half, half), half)]
        else:
            source = s.held.at[(unit,) + plan.part(kind, level, True)]
        return self.remote(source, target, unit, level, device)

    def own_half(self, triple, kind, layer):
        s, half = self.s, CHUNK // 2
        unit = CLASSES * triple + kind
        bit, _ = self.plan.partner(kind, 0)
        source = (s.first_units, s.units)[layer].at[unit - layer * UNITS]
        source = source.at[:, :, pl.ds(pl.multiple_of(bit * half, half), half)]
        return pltpu.make_async_copy(source, s.held.at[unit], s.own_sems.at[unit, 0])

    def result(self, triple, kind, group, count):
        name, row_block, col_block = TARGETS[group][kind]
        starts, sizes = self.plan.place(kind, count)
        layer = 1 - triple // (TRIPLES // 2)
        return self.s.results[name].at[
            layer,
            pl.ds(pl.multiple_of(row_block * self.plan.rows + starts[0], 8), sizes[0]),
            pl.ds(pl.multiple_of(col_block * CHUNK + starts[1], LANES), sizes[1]),
        ]

    def finished(self, triple, kind):
        return self.s.held.at[(CLASSES * triple + kind,) + self.plan.part(kind, self.plan.halvings - 1)].at[0]

    def keep(self, triple, kind, group):
        plan = self.plan
        target = self.result(triple, kind, group, len(plan.page_steps[kind]))
        return pltpu.make_async_copy(
            self.finished(triple, kind), target, self.s.own_sems.at[CLASSES * triple + kind, 1]
        )

    def gathering(self, triple, kind, group, phase):
        plan = self.plan
        count = len(plan.page_steps[kind]) - (phase - plan.halvings)
        target = self.result(triple, kind, group, count)
        source = self.finished(triple, kind) if phase == plan.halvings else target
        _, device = plan.partner(kind, plan.page_steps[kind][count - 1])
        return self.remote(source, target, CLASSES * triple + kind, phase, device)

    def credit(self, kind, level):
        return self.s.free_sems.at[kind, level]

    def start(self, triple, kind, phase, layer, group):
        plan = self.plan
        if phase < plan.halvings:

            @pl.when(triple >= RING)
            def _():
                pl.semaphore_wait(self.credit(kind, phase), 1)

            self.halving(triple, kind, phase, layer).start()
            if phase == 0:
                self.own_half(triple, kind, layer).start()
        elif phase < plan.phases:
            if phase == plan.halvings:
                self.keep(triple, kind, group).start()
            self.gathering(triple, kind, group, phase).start()

    def finish(self, triple, kind, phase, layer, group):
        plan, s = self.plan, self.s
        if phase < plan.halvings:
            self.halving(triple, kind, phase, layer).wait()
            if phase == 0:
                self.own_half(triple, kind, layer).wait()
            landed = s.landing[kind][phase].at[triple % RING]
            kept = s.held.at[(CLASSES * triple + kind,) + plan.part(kind, phase)]
            for share in range(landed.shape[0]):
                kept[share] += landed[share]
            _, device = plan.partner(kind, phase)

            @pl.when(triple < TRIPLES - RING)
            def _():
                pl.semaphore_signal(
                    self.credit(kind, phase), inc=1, device_id=device, device_id_type=pl.DeviceIdType.MESH
                )

        else:
            if phase == plan.halvings:
                self.keep(triple, kind, group).wait()
            self.gathering(triple, kind, group, phase).wait()

    def advance(self, time, stages):
        halvings, phases, groups = self.plan.halvings, self.plan.phases, TRIPLES // 2
        for stage in reversed(stages):
            triple = time - SKEW * stage
            if stage <= 1:
                cases = [(layer * groups, (layer + 1) * groups, layer, None) for layer in range(2)]
            elif stage < halvings:
                cases = [(0, TRIPLES, None, None)]
            else:
                cases = [(0, TRIPLES, None, group) for group in range(groups)]
            for low, high, layer, group in cases:
                active = (triple >= low) & (triple < high)
                if group is not None:
                    active = active & (triple % groups == group)

                @pl.when(active)
                def _(stage=stage, triple=triple, layer=layer, group=group):
                    for kind in range(CLASSES):
                        if stage > 0:
                            self.finish(triple, kind, stage - 1, layer, group)
                        self.start(triple, kind, stage, layer, group)

    def small_copy(self, phase):
        s = self.s
        _, device = self.plan.partner(0, phase)
        return pltpu.make_async_remote_copy(
            src_ref=s.small_own if phase == 0 else s.small_parts.at[phase - 1],
            dst_ref=s.small_parts.at[phase],
            send_sem=s.small_sems.at[0, phase],
            recv_sem=s.small_sems.at[1, phase],
            device_id=device,
            device_id_type=pl.DeviceIdType.MESH,
        )

    def small_step(self, phase):
        s = self.s
        if phase >= 0:
            self.small_copy(phase).wait()
            s.small_parts[phase] += s.small_own[...] if phase == 0 else s.small_parts[phase - 1]
        if phase + 1 < self.plan.halvings:
            self.small_copy(phase + 1).start()

    def pump(self, point, index=0):
        if point == "feed":
            self.advance(0, range(1))
        elif point == "norm_two":
            self.advance(1, range(1))
        elif point == "attended":

            @pl.when(index % 2 == 1)
            def _():
                self.advance(2 + index // 2, range(3))

    def drain(self):
        first, last = 5, TRIPLES + SKEW * self.plan.phases

        def step(time, carry):
            self.advance(time, range(self.plan.phases + 1))
            for phase in range(-1, self.plan.halvings):

                @pl.when(time == first + 1 + phase)
                def _(phase=phase):
                    self.small_step(phase)

            return carry

        lax.fori_loop(first, last, step, 0)


def run_last(plan, s):
    s.landing = [[getattr(s, f"landing_{kind}_{level}") for level in range(plan.halvings)] for kind in range(CLASSES)]
    s.results = {name: getattr(s, f"sum_{name}") for name in ("qkv", "proj", "fc1", "fc2")}
    reducer = Reducer(plan, s)
    reducer.barrier()
    s.need("upper", "lower", "place")
    to_channels(s.page, s.place, s.grad)
    s.need(*VECTOR_NAMES)
    spread_columns(s, 0, (G1, G2))
    backward(s, reducer)
    to_page(s.grad, s.place, s.page)
    from_rows(s.page, s.patches)
    s.save("grad_tokens")
    s.need("spread", "first_small")
    small_gradients(s, s.small_own.at[0])
    s.small_own[1] = s.first_small[...]
    reducer.drain()
    s.small_done[...] = s.small_parts[plan.halvings - 1]
    s.save("small_sum")
    s.close()


def last_call(inputs, loads, lanes, cols):
    pages, shares = lax.axis_size("page"), lax.axis_size("row")
    plan = Plan(pages, shares)
    small = (2, SMALL, D)
    outputs = {
        "grad_tokens": ((WIN, cols, D), F32),
        "small_sum": (small, F32),
        "sum_qkv": ((2, D // shares, 3 * D), F32),
        "sum_proj": ((2, D // shares, D), F32),
        "sum_fc1": ((2, D // shares, FF), F32),
        "sum_fc2": ((2, FF // shares, D), F32),
        "units": units_shape(shares),
    }
    vmem = {
        **shared_scratch(lanes),
        **backward_scratch(lanes),
        "cols": ((G2 + 1, D, LANES), F32),
        "page": ((WIN * SPAN, D), F32),
        "patches": ((WIN, cols, D), F32),
        "held": ((2 * UNITS, shares, CHUNK // shares, CHUNK // 2), F32),
        "small_own": (small, F32),
        "small_done": (small, F32),
        "small_parts": ((plan.halvings,) + small, F32),
    }
    for kind in range(CLASSES):
        for level, size in enumerate(plan.sizes[kind]):
            vmem[f"landing_{kind}_{level}"] = ((RING,) + size, F32)
    semaphores = {
        "send_sems": pltpu.SemaphoreType.DMA((2 * UNITS, plan.phases)),
        "recv_sems": pltpu.SemaphoreType.DMA((2 * UNITS, plan.phases)),
        "own_sems": pltpu.SemaphoreType.DMA((2 * UNITS, 2)),
        "stage_sems": pltpu.SemaphoreType.DMA((2, shares)),
        "small_sems": pltpu.SemaphoreType.DMA((2, plan.halvings)),
        "free_sems": pltpu.SemaphoreType.REGULAR((CLASSES, plan.halvings)),
    }
    return launch(
        functools.partial(run_last, plan),
        "layer0_backward_and_sums",
        inputs,
        outputs,
        vmem,
        semaphores,
        12 * 10**9,
        saves={"grad_tokens": ("patches", None), "small_sum": ("small_done", None)},
        loads=loads,
        raw=("first_units",),
        late={"normed": "second", "w_qkv": "w_fc1", "spread": "active", "x": "hidden"},
        collective_id=0,
        has_side_effects=True,
    )


def placements(cols):
    windows = cols // WIN
    plain = np.zeros((WIN * SPAN, windows * LANES), np.float32)
    moved = np.zeros((WIN * SPAN, windows * LANES), np.float32)
    for row in range(WIN):
        for col in range(cols):
            source = row * SPAN + col
            plain[source, (col // WIN) * LANES + row * WIN + col % WIN] = 1
            new_row, new_col = (row - SHIFT) % WIN, (col - SHIFT) % cols
            moved[source, (new_col // WIN) * LANES + new_row * WIN + new_col % WIN] = 1
    return plain.astype(jnp.bfloat16), moved.astype(jnp.bfloat16)


def table_spread():
    size = 2 * WIN - 1
    spread = np.zeros((WIN, 2 * LANES, TABLE), np.float32)
    for key_col in range(WIN):
        for offset in range(size):
            for col in range(WIN):
                spread[key_col, offset * WIN + col, offset * size + col - key_col + WIN - 1] = 1
    spread = spread.reshape(WIN // 2, 2, 2 * LANES, TABLE).swapaxes(1, 2)
    return spread.reshape(WIN * LANES, 2 * TABLE).astype(jnp.bfloat16)


def shifted(value, axis, steps):
    count = lax.axis_size(axis)
    pairs = [(source, (source + steps) % count) for source in range(count)]
    return lax.ppermute(value, axis, pairs)


def shifted_live(own, upper):
    place = np.arange(LANES)
    from_upper = place >= AREA // 2
    from_next = place % WIN >= SHIFT
    own, upper = (jnp.where(from_next, jnp.roll(row, -1)[:, None], row[:, None]) for row in (own, upper))
    return jnp.where(from_upper, upper, own)


def per_device(
    page_tokens,
    blank_mask,
    cotangent,
    ln_gain,
    ln_bias,
    qv_bias,
    rel_table,
    w_qkv,
    w_proj,
    proj_bias,
    w_fc1,
    fc1_bias,
    w_fc2,
    fc2_bias,
):
    cols = page_tokens.shape[2]
    lanes = cols // WIN * LANES
    half = SHIFT * SPAN
    shares = lax.axis_size("row")
    plain, moved = placements(cols)
    vectors = dict(zip(VECTOR_NAMES, (ln_gain, ln_bias, qv_bias, proj_bias, fc1_bias, fc2_bias)))
    weights = dict(zip(WEIGHTS, (w_qkv, w_proj, w_fc1, w_fc2)))
    tables = jnp.pad(rel_table, ((0, 0), (0, 0), (0, TABLE - OFFSETS)))
    spread = jnp.asarray(table_spread())

    live_own = 1.0 - blank_mask[0, 0].astype(F32)
    grad_upper, live_upper = shifted((cotangent[0, :SHIFT], live_own), "row", -1)
    lives = (
        jnp.broadcast_to(live_own[:, None], (cols // WIN, LANES)),
        shifted_live(live_own, live_upper),
    )
    page = ((WIN * SPAN, D), F32)
    half_page = ((half, D), F32)

    def layer_loads(layer):
        return {name: (name, None, layer) for name in WEIGHTS + ("table",)}

    saved = saved_shapes(lanes)
    first = launch(
        run_first,
        "layer0_forward",
        {
            "tokens": page_tokens[0],
            "place": jnp.asarray(plain),
            **vectors,
            "table": tables,
            "spread": spread,
            "live": lives[0],
            **weights,
        },
        {"out_upper": half_page, "out_lower": half_page, **saved},
        {**saved, **shared_scratch(lanes), **forward_scratch(), "page": (page[0], BF), "page_out": page},
        {},
        6 * 10**9,
        saves={
            "out_upper": ("page_out", pl.ds(0, half)),
            "out_lower": ("page_out", pl.ds(half, half)),
            **{name: (name, None) for name in saved},
        },
        loads=layer_loads(0),
    )
    upper_in = shifted(first.pop("out_upper"), "row", -1)
    second = launch(
        run_second,
        "layer1_both",
        {
            "upper": upper_in,
            "lower": first.pop("out_lower"),
            "place": jnp.asarray(moved),
            **vectors,
            "table": tables,
            "spread": spread,
            "live": lives[1],
            **weights,
            "grad_upper": grad_upper,
            "grad_lower": cotangent[0],
        },
        {
            "out_patches": ((WIN, cols, D), F32),
            "next_upper": half_page,
            "next_lower": half_page,
            "small_out": ((SMALL, D), F32),
            "units": units_shape(shares),
        },
        {
            **saved,
            **shared_scratch(lanes),
            **forward_scratch(),
            **backward_scratch(lanes),
            "page": page,
            "patches": ((WIN, cols, D), F32),
            "small": ((SMALL, D), F32),
            "grad_lower": ((SHIFT, cols, D), F32),
        },
        {"stage_sems": pltpu.SemaphoreType.DMA((2, shares))},
        18 * 10**9,
        saves={
            "out_patches": ("patches", None),
            "next_upper": ("page", pl.ds(0, half)),
            "next_lower": ("page", pl.ds(half, half)),
            "small_out": ("small", None),
        },
        loads={
            **layer_loads(1),
            "upper": ("page", pl.ds(0, half), None),
            "lower": ("page", pl.ds(half, half), None),
            "grad_lower": ("grad_lower", None, pl.ds(SHIFT, SHIFT)),
        },
    )
    lower_grad = shifted(second["next_upper"], "row", 1)
    last = last_call(
        {
            "upper": lower_grad,
            "lower": second["next_lower"],
            "place": jnp.asarray(plain),
            "active": first["active"],
            "w_fc2": w_fc2,
            "slope": first["slope"],
            "second": first["second"],
            "w_fc1": w_fc1,
            **vectors,
            "hidden": first["hidden"],
            "live": lives[0],
            "merged": first["merged"],
            "w_proj": w_proj,
            "qkv": first["qkv"],
            "soft": first["soft"],
            "normed": first["normed"],
            "w_qkv": w_qkv,
            "x": first["x"],
            "spread": spread,
            "first_small": second["small_out"],
            "first_units": second["units"],
        },
        {
            **{name: (name, None, 0) for name in WEIGHTS},
            "upper": ("page", pl.ds(0, half), None),
            "lower": ("page", pl.ds(half, half), None),
            "w_qkv": ("w_fc1", (slice(None), pl.ds(0, 3 * D)), 0),
            "spread": ("active", pl.ds(0, WIN * LANES), None),
        },
        lanes,
        cols,
    )
    lower_out = shifted(second["out_patches"][:SHIFT], "row", 1)
    final_out = second["out_patches"].at[:SHIFT].set(lower_out)
    small = last["small_sum"]

    def share(*indices):
        joined = jnp.concatenate([small[:, index] for index in indices], axis=1)
        size = joined.shape[1] // shares
        return lax.dynamic_slice_in_dim(joined, lax.axis_index("row") * size, size, axis=1)

    return (
        final_out[None],
        last["grad_tokens"][None],
        share(G1, G2),
        share(B1, B2),
        share(QB, VB),
        small[:, 16:, :OFFSETS],
        last["sum_qkv"],
        last["sum_proj"],
        share(PB),
        last["sum_fc1"],
        share(*range(F1B, F1B + FF // D)),
        last["sum_fc2"],
        share(F2B),
    )


def solution(mesh):
    split_rows = P("page", "row", None, None)
    return jax.shard_map(
        per_device,
        mesh=mesh,
        in_specs=(split_rows, P("page", "row", None), split_rows) + (P(),) * 11,
        out_specs=(
            split_rows,
            split_rows,
            P(None, "row"),
            P(None, "row"),
            P(None, "row"),
            P(),
            P(None, "row", None),
            P(None, "row", None),
            P(None, "row"),
            P(None, "row", None),
            P(None, "row"),
            P(None, "row", None),
            P(None, "row"),
        ),
        check_vma=False,
    )
```

```python
import functools

import jax
import jax.numpy as jnp
import numpy as np
from jax import lax
from jax.experimental import pallas as pl
from jax.experimental.pallas import tpu as pltpu
from jax.sharding import PartitionSpec as P

WIN = 10
SHIFT = 5
AREA = WIN * WIN
LANES = 128
D = 512
HEADS = 16
HEAD_DIM = 32
FF = 2048
CHUNK = 512
FEEDS = FF // CHUNK
SPLITS = D // LANES
EPSILON = 1e-05
MASK_VALUE = -100.0
NEVER = -1e30
SCORE_SCALE = HEAD_DIM ** (-0.5)
VMEM_LIMIT = 63 * 1024 * 1024 + 512 * 1024
BF = jnp.bfloat16
F32 = jnp.float32
MESH = pl.DeviceIdType.MESH
PAGE, ROW = "page", "row"

G1, B1, G2, B2, QB, VB, PB, F2B, F1B, VECTORS = 0, 1, 2, 3, 4, 5, 6, 7, 8, 12
VECTOR_ROWS = 16
SMALL = VECTOR_ROWS + HEADS
OFFSETS = (2 * WIN - 1) ** 2
TABLE = 384

UNIT_FC1, UNIT_FC2, UNIT_PROJ, UNIT_QKV, UNITS = 0, 4, 8, 9, 12
CLASSES = 3
GROUPS = UNITS // CLASSES
TRIPLES = 2 * GROUPS
HELD = 4
RING = 3
QKV, PROJ, FC1, FC2 = range(4)
TARGETS = (
    ((FC1, 0, 0), (FC1, 0, 1), (FC1, 0, 2)),
    ((FC1, 0, 3), (FC2, 0, 0), (FC2, 1, 0)),
    ((FC2, 2, 0), (FC2, 3, 0), (PROJ, 0, 0)),
    ((QKV, 0, 0), (QKV, 0, 1), (QKV, 0, 2)),
)


def mm(left, right, left_dim, right_dim):
    return lax.dot_general(
        left, right, (((left_dim,), (right_dim,)), ((), ())), preferred_element_type=F32
    )


def split(values):
    high = values.astype(BF)
    return high, (values - high.astype(F32)).astype(BF)


def lane_tile(index):
    return pl.ds(pl.multiple_of(index * LANES, LANES), LANES)


def chunk_of(index):
    return pl.ds(pl.multiple_of(index * CHUNK, CHUNK), CHUNK)


def wide(column, count):
    return jnp.concatenate([column] * count, axis=1)


def fold(values):
    total = values[:, :LANES]
    for start in range(LANES, values.shape[1], LANES):
        total = total + values[:, start : start + LANES]
    return total


def norm_parts(values):
    center = values - jnp.sum(values, axis=0, keepdims=True) * (1.0 / D)
    spread = jnp.sum(center * center, axis=0, keepdims=True) * (1.0 / D)
    scale = lax.rsqrt(spread + EPSILON)
    return center * scale, scale


def norm_pull(grad, gain, hat, scale):
    scaled = grad * gain
    mean_one = jnp.sum(scaled, axis=0, keepdims=True) * (1.0 / D)
    mean_two = jnp.sum(scaled * hat, axis=0, keepdims=True) * (1.0 / D)
    return scale * (scaled - mean_one - hat * mean_two)


def gelu_parts(inner):
    step = 1.0 / (1.0 + (0.3275911 * 0.7071067811865476) * jnp.abs(inner))
    bell = jnp.exp(inner * inner * -0.5)
    poly = 0.5 * 1.061405429
    for factor in (-1.453152027, 1.421413741, -0.284496736, 0.254829592):
        poly = poly * step + 0.5 * factor
    tail = poly * step * bell
    below = jnp.where(inner >= 0, 1.0 - tail, tail)
    return inner * below, below + inner * bell * 0.3989422804014327


def to_channels(page_ref, place_ref, out_ref, exact=False):
    def step(index, carry):
        channels = pl.ds(pl.multiple_of(index * 256, 256), 256)
        values = page_ref[:, channels]
        if exact:
            out_ref[channels, :] = mm(values.astype(BF), place_ref[...], 0, 0)
        else:
            high, low = split(values)
            out_ref[channels, :] = mm(high, place_ref[...], 0, 0) + mm(low, place_ref[...], 0, 0)
        return carry

    lax.fori_loop(0, D // 256, step, 0)


def to_dense(values_ref, place_ref, dense_ref):
    count = dense_ref.shape[0] // SPLITS
    for index in range(D // 256):
        high, low = split(values_ref[index * 256 : (index + 1) * 256, :])
        page = mm(place_ref[...], high, 1, 1) + mm(place_ref[...], low, 1, 1)
        for part in range(2):
            rows = pl.ds(2 * index + part, count, stride=SPLITS)
            dense_ref[rows, :] = page[:count, part * LANES : (part + 1) * LANES]


def from_dense(dense_ref, start, page_ref, row, count):
    for part in range(SPLITS):
        rows = pl.ds(start * SPLITS + part, count, stride=SPLITS)
        page_ref[pl.ds(row, count), part * LANES : (part + 1) * LANES] = dense_ref[rows, :]


def vector_rows(s, layer):
    rows = s.vector_rows
    sources = ((G1, s.ln_gain, 0), (B1, s.ln_bias, 0), (G2, s.ln_gain, 1), (B2, s.ln_bias, 1))
    sources += ((QB, s.qv_bias, 0), (VB, s.qv_bias, 1), (PB, s.proj_bias, 0), (F2B, s.fc2_bias, 0))
    sources += tuple((F1B + part, s.fc1_bias, part) for part in range(FEEDS))
    for index, source, part in sources:
        rows[index : index + 1, :] = source[layer : layer + 1, part * D : (part + 1) * D]
    rows[VECTORS:, :] = jnp.zeros((VECTOR_ROWS - VECTORS, D), F32)
    return rows[...].T


def spread_columns(s, layer):
    columns = vector_rows(s, layer)
    for index in range(VECTORS):
        s.sums[index] = jnp.broadcast_to(columns[:, index : index + 1], (D, LANES))


def spread_gains(s, layer):
    columns = vector_rows(s, layer)
    for index, vector in enumerate((G1, G2)):
        s.gains[index] = jnp.broadcast_to(columns[:, vector : vector + 1], (D, LANES))


def spread_part(col):
    rows, lanes = (col // 2) * 2 * LANES, (col % 2) * TABLE
    return slice(rows, rows + 2 * LANES), slice(lanes, lanes + TABLE)


def spread_bias(table, spread_ref, rows_ref, bias_ref):
    high, low = split(table)
    parts = []
    for col in range(WIN):
        chosen = spread_ref[spread_part(col)]
        parts.append(mm(high, chosen, 1, 1) + mm(low, chosen, 1, 1))
    source = jnp.concatenate(parts, axis=0)
    rows_ref[...] = jnp.zeros(rows_ref.shape, F32)
    for row in range(WIN):
        shift = (WIN - 1 - row) * WIN
        moved = source if shift == 0 else pltpu.roll(source, 2 * LANES - shift, axis=1)
        rows_ref[pl.ds(row * WIN * HEADS, WIN * HEADS), :] = moved[:, :LANES]
    for head in range(HEADS):
        bias_ref[head] = rows_ref[pl.ds(head, LANES, stride=HEADS), :]


def gather_bias(grad_ref, spread_ref, rows_ref):
    for head in range(HEADS):
        rows_ref[pl.ds(head, LANES, stride=HEADS), :] = grad_ref[head]
    total = jnp.zeros((WIN * HEADS, 2 * LANES), F32)
    for row in range(WIN):
        shift = (WIN - 1 - row) * WIN
        piece = rows_ref[pl.ds(row * WIN * HEADS, WIN * HEADS), :]
        piece = jnp.concatenate([piece, jnp.zeros_like(piece)], axis=1)
        total = total + (piece if shift == 0 else pltpu.roll(piece, shift, axis=1))
    table = jnp.zeros((HEADS, TABLE), F32)
    for col in range(WIN):
        for part in split(total[col * HEADS : (col + 1) * HEADS]):
            table = table + mm(part, spread_ref[spread_part(col)], 1, 0)
    return table


def region_masks(shifted_layer, out_ref):
    key = lax.broadcasted_iota(jnp.int32, (LANES, LANES), 0)
    query = lax.broadcasted_iota(jnp.int32, (LANES, LANES), 1)
    padding = jnp.where(key < AREA, 0.0, NEVER)
    out_ref[0] = padding
    out_ref[1] = padding
    if shifted_layer:
        last = lax.axis_index(ROW) == lax.axis_size(ROW) - 1
        rows_differ = ((key >= AREA // 2) != (query >= AREA // 2)) & last
        cols_differ = (key % WIN >= SHIFT) != (query % WIN >= SHIFT)
        out_ref[0] += jnp.where(rows_differ, MASK_VALUE, 0.0)
        out_ref[1] += jnp.where(rows_differ | cols_differ, MASK_VALUE, 0.0)


def shifted_live(s, windows):
    place = lax.broadcasted_iota(jnp.int32, (1, LANES), 1)
    for window in range(windows):
        here, after = slice(window, window + 1), slice((window + 1) % windows, (window + 1) % windows + 1)
        beyond = place % WIN >= SHIFT
        own = jnp.where(beyond, s.live[after, :], s.live[here, :])
        upper = jnp.where(beyond, s.live_upper[after, :], s.live_upper[here, :])
        s.live_two[here, :] = jnp.where(place >= AREA // 2, upper, own)


def head_rows(head, base=0):
    return pl.ds(base + head * HEAD_DIM, HEAD_DIM)


def norm_one_forward(s, windows):
    def step(index, carry):
        lanes = lane_tile(index)
        hat, _ = norm_parts(s.x[:, lanes])
        s.normed[:, lanes] = (hat * s.sums[G1] + s.sums[B1]).astype(BF)
        return carry

    lax.fori_loop(0, windows, step, 0)


def project_forward(s, windows):
    def step(index, carry):
        rows = chunk_of(index)
        bias = s.sums[jnp.where(index == 0, QB, VB)] * jnp.where(index == 1, 0.0, 1.0)
        out = mm(s.w_qkv[:, rows], s.normed[...], 0, 0)
        s.qkv[rows, :] = (out + wide(bias, windows)).astype(BF)
        return carry

    lax.fori_loop(0, 3, step, 0)


def attend_forward(s, windows, live_ref):
    def step(index, carry):
        lanes = lane_tile(index)
        live = jnp.broadcast_to(live_ref[pl.ds(index, 1), :], (LANES, LANES)).T
        masked = s.regions[jnp.where(index == windows - 1, 1, 0)] + MASK_VALUE * (1.0 - live)
        for head in range(HEADS):
            query = s.qkv[head_rows(head), lanes]
            key = s.qkv[head_rows(head, D), lanes]
            value = s.qkv[head_rows(head, 2 * D), lanes]
            scores = mm(key, query, 0, 0) * SCORE_SCALE + (s.bias[head] + masked)
            exponent = jnp.exp(scores - jnp.max(scores, axis=0, keepdims=True))
            total = jnp.sum(exponent, axis=0, keepdims=True)
            soft = (exponent * (1.0 / total)).astype(BF)
            s.soft[index * HEADS + head] = soft
            s.merged[head_rows(head), lanes] = mm(value, soft, 1, 0).astype(BF)
        return carry

    lax.fori_loop(0, windows, step, 0)


def norm_two_forward(s, windows, live_ref):
    def step(index, carry):
        lanes = lane_tile(index)
        hidden = s.x[:, lanes] + live_ref[pl.ds(index, 1), :] * (s.work[:, lanes] + s.sums[PB])
        s.hidden[:, lanes] = hidden
        s.work[:, lanes] = hidden + s.sums[F2B]
        hat, _ = norm_parts(hidden)
        s.second[:, lanes] = (hat * s.sums[G2] + s.sums[B2]).astype(BF)
        return carry

    lax.fori_loop(0, windows, step, 0)


def feed_forward(s, windows):
    def step(index, carry):
        rows = chunk_of(index)
        inner = mm(s.w_fc1[:, rows], s.second[...], 0, 0) + wide(s.sums[F1B + index], windows)
        active, slope = gelu_parts(inner)
        active = active.astype(BF)
        s.active[rows, :] = active
        s.slope[rows, :] = slope.astype(BF)
        s.work[...] += mm(s.w_fc2[rows, :], active, 0, 0)
        return carry

    lax.fori_loop(0, FEEDS, step, 0)


def feed_backward(s, sink, times):
    s.sums[...] = jnp.zeros(s.sums.shape, F32)
    s.bias[...] = jnp.zeros(s.bias.shape, F32)
    lowered = s.grad[...].astype(BF)
    s.low[...] = lowered
    s.sums[F2B] = fold(lowered.astype(F32))
    s.work[...] = jnp.zeros(s.work.shape, F32)

    def step(index, carry):
        rows = chunk_of(index)
        sink.put(0, mm(s.active[rows, :], s.low[...], 1, 1), feed_pieces(index, sink.shares), index == 0)
        grad_inner = mm(s.w_fc2[rows, :], s.low[...], 1, 0) * s.slope[rows, :].astype(F32)
        grad_inner = grad_inner.astype(BF)
        s.sums[F1B + index] = fold(grad_inner.astype(F32))
        sink.put(1, mm(s.second[...], grad_inner, 1, 1), row_pieces(UNIT_FC1 + index, sink.shares), index == 0)
        s.work[...] += mm(s.w_fc1[:, rows], grad_inner, 1, 0)
        sink.advance_at(index, times)
        return carry

    lax.fori_loop(0, FEEDS, step, 0)
    sink.settle(0)
    sink.settle(1)


def norm_two_backward(s, windows, live_ref):
    def step(index, carry):
        lanes = lane_tile(index)
        hat, scale = norm_parts(s.hidden[:, lanes])
        grad = s.work[:, lanes]
        s.sums[G2] += grad * hat
        s.sums[B2] += grad
        grad = s.grad[:, lanes] + norm_pull(grad, s.gains[1], hat, scale)
        s.grad[:, lanes] = grad
        grad_low = (grad * live_ref[pl.ds(index, 1), :]).astype(BF)
        s.low[:, lanes] = grad_low
        s.sums[PB] += grad_low.astype(F32)
        return carry

    lax.fori_loop(0, windows, step, 0)


def merge_backward(s, sink):
    sink.put(0, mm(s.merged[...], s.low[...], 1, 1), row_pieces(UNIT_PROJ, sink.shares), True)
    s.merged[...] = mm(s.w_proj[...], s.low[...], 1, 0).astype(BF)
    sink.settle(0)


def attend_backward(s, windows, sink, times):
    def step(index, carry):
        lanes = lane_tile(index)
        for head in range(HEADS):
            query = s.qkv[head_rows(head), lanes]
            key = s.qkv[head_rows(head, D), lanes]
            value = s.qkv[head_rows(head, 2 * D), lanes]
            grad_out = s.merged[head_rows(head), lanes]
            soft_low = s.soft[index * HEADS + head]
            soft = soft_low.astype(F32)
            grad_soft = mm(value, grad_out, 0, 0)
            inner = jnp.sum(soft * grad_soft, axis=0, keepdims=True)
            grad_scores = (soft * (grad_soft - inner)).astype(BF)
            s.bias[head] += grad_scores.astype(F32)
            grad_query = (mm(key, grad_scores, 1, 0) * SCORE_SCALE).astype(BF)
            grad_key = (mm(query, grad_scores, 1, 1) * SCORE_SCALE).astype(BF)
            grad_value = mm(grad_out, soft_low, 1, 1).astype(BF)
            s.qkv[head_rows(head), lanes] = grad_query
            s.qkv[head_rows(head, D), lanes] = grad_key
            s.qkv[head_rows(head, 2 * D), lanes] = grad_value
            s.sums[QB, head_rows(head), :] += grad_query.astype(F32)
            s.sums[VB, head_rows(head), :] += grad_value.astype(F32)
        sink.advance_at(index, times)
        return carry

    lax.fori_loop(0, windows, step, 0)


def project_backward(s, sink):
    s.work[...] = jnp.zeros(s.work.shape, F32)

    def step(index, carry):
        rows = chunk_of(index)
        sink.put(1, mm(s.normed[...], s.qkv[rows, :], 1, 1), row_pieces(UNIT_QKV + index, sink.shares), index == 0)
        s.work[...] += mm(s.w_qkv[:, rows], s.qkv[rows, :], 1, 0)
        return carry

    lax.fori_loop(0, 3, step, 0)


def norm_one_backward(s, windows):
    def step(index, carry):
        lanes = lane_tile(index)
        hat, scale = norm_parts(s.x[:, lanes])
        grad = s.work[:, lanes]
        s.sums[G1] += grad * hat
        s.sums[B1] += grad
        s.grad[:, lanes] += norm_pull(grad, s.gains[0], hat, scale)
        return carry

    lax.fori_loop(0, windows, step, 0)


def small_gradients(s, small_ref):
    places = lax.broadcasted_iota(jnp.int32, (D, LANES), 1)
    packed = jnp.zeros((D, LANES), F32)
    for index in range(VECTORS):
        packed = jnp.where(places == index, jnp.sum(s.sums[index], axis=1, keepdims=True), packed)
    small_ref[:VECTOR_ROWS, :] = packed.T[:VECTOR_ROWS]
    table = gather_bias(s.bias, s.spread, s.bias_rows)
    small_ref[VECTOR_ROWS:, :] = jnp.concatenate([table, jnp.zeros((HEADS, D - TABLE), F32)], axis=1)


def reversed_bits(value, count):
    turned = 0
    for bit in range(count):
        turned = turned * 2 + (value // 2**bit) % 2
    return turned


def row_pieces(unit, shares):
    rows, count = CHUNK // shares, shares.bit_length() - 1
    return [(share * rows, unit, reversed_bits(share, count)) for share in range(shares)]


def feed_pieces(index, shares):
    rows, count = CHUNK // shares, shares.bit_length() - 1
    pieces = []
    for share in range(shares // FEEDS):
        place = reversed_bits(index * (shares // FEEDS) + share, count)
        for part in range(FEEDS):
            pieces.append(((share * FEEDS + part) * rows, UNIT_FC2 + part, place))
    return pieces


class Plan:
    def __init__(self, pages, shares):
        self.shares, self.rows = shares, CHUNK // shares
        page_bits, row_bits = pages.bit_length() - 1, shares.bit_length() - 1
        others = page_bits - 1
        self.steps = []
        for kind in range(CLASSES):
            turn = kind % 2
            page = [(PAGE, 2 ** (1 + (bit + turn) % others)) for bit in range(others)]
            row = [(ROW, 2**bit) for bit in range(row_bits)]
            self.steps.append([(PAGE, 1)] + (row + page if kind == 2 else page + row))
        self.page_steps = [[0] + [at for at, step in enumerate(steps) if at and step[0] == PAGE] for steps in self.steps]
        self.halvings = page_bits + row_bits
        self.phases = self.halvings + page_bits
        self.sizes = []
        for kind in range(CLASSES):
            size = [shares, self.rows, CHUNK // 2]
            sizes = [tuple(size)]
            for level in range(1, self.halvings):
                size[self.split_axis(kind, level)] //= 2
                sizes.append(tuple(size))
            self.sizes.append(sizes)
        self.times = self.schedule()

    def schedule(self):
        times = []
        for triple, entry in enumerate(ENTRIES):
            gaps = [3, 3] if triple < TRIPLES - 1 else []
            gaps += [2] * (self.phases - len(gaps))
            now = entry if triple < HELD else max(entry, times[triple - HELD][self.halvings + 1] + 1)
            stages = []
            for stage in range(self.phases + 1):
                if triple >= RING and stage < self.halvings:
                    now = max(now, times[triple - RING][stage + 1] + 1)
                stages.append(now)
                now += gaps[stage] if stage < self.phases else 0
            times.append(stages)
        return times

    def split_axis(self, kind, level):
        if self.steps[kind][level][0] == ROW:
            return 0
        return 2 if self.page_steps[kind].index(level) < 2 else 1

    def partner(self, kind, level):
        axis, stride = self.steps[kind][level]
        page, row = lax.axis_index(PAGE), lax.axis_index(ROW)
        mine = page if axis == PAGE else row
        bit = (mine // stride) % 2
        other = mine + (1 - 2 * bit) * stride
        return bit, ((other, row) if axis == PAGE else (page, other))

    def part(self, kind, level, sent=False):
        starts, sizes = [0, 0, 0], [self.shares, self.rows, CHUNK // 2]
        for at in range(1, level + 1):
            axis = self.split_axis(kind, at)
            sizes[axis] //= 2
            bit, _ = self.partner(kind, at)
            which = 1 - bit if sent and at == level else bit
            starts[axis] = starts[axis] + which * sizes[axis]
        return (
            pl.ds(starts[0], sizes[0]),
            pl.ds(pl.multiple_of(starts[1], 8), sizes[1]),
            pl.ds(pl.multiple_of(starts[2], LANES), sizes[2]),
        )

    def place(self, kind, count):
        starts, sizes = [0, 0], [self.rows, CHUNK]
        for at in self.page_steps[kind][:count]:
            axis = self.split_axis(kind, at) - 1 if at else 1
            sizes[axis] //= 2
            bit, _ = self.partner(kind, at)
            starts[axis] = starts[axis] + bit * sizes[axis]
        return starts, sizes


class Reducer:
    def __init__(self, plan, s):
        self.plan, self.s = plan, s
        self.shares = plan.shares
        self.layer = 1

    def stage_copies(self, slot, pieces):
        return [
            pltpu.make_async_copy(
                self.s.staged.at[slot, pl.ds(start, self.plan.rows)],
                self.s.units[self.layer].at[unit, place],
                self.s.stage_sems.at[slot, number],
            )
            for number, (start, unit, place) in enumerate(pieces)
        ]

    def put(self, slot, grad, pieces, first):
        if first is not True:

            @pl.when(jnp.logical_not(first))
            def _():
                self.settle(slot)

        self.s.staged[slot] = grad
        for copy in self.stage_copies(slot, pieces):
            copy.start()

    def settle(self, slot):
        for copy in self.stage_copies(slot, row_pieces(0, self.shares)):
            copy.wait()

    def remote(self, source, target, unit, phase, device):
        return pltpu.make_async_remote_copy(
            src_ref=source,
            dst_ref=target,
            send_sem=self.s.send_sems.at[unit, phase],
            recv_sem=self.s.recv_sems.at[unit, phase],
            device_id=device,
            device_id_type=MESH,
        )

    def unit_half(self, triple, kind, which):
        layer, half = 1 - triple // GROUPS, CHUNK // 2
        unit = CLASSES * (triple % GROUPS) + kind
        return self.s.units[layer].at[unit, :, :, pl.ds(pl.multiple_of(which * half, half), half)]

    def held(self, triple, kind):
        return self.s.held.at[CLASSES * (triple % HELD) + kind]

    def halving(self, triple, kind, level):
        plan = self.plan
        bit, device = plan.partner(kind, level)
        target = self.s.landing[kind][level].at[triple % RING]
        if level == 0:
            source = self.unit_half(triple, kind, 1 - bit)
        else:
            source = self.held(triple, kind).at[plan.part(kind, level, True)]
        return self.remote(source, target, CLASSES * triple + kind, level, device)

    def own_half(self, triple, kind):
        bit, _ = self.plan.partner(kind, 0)
        sem = self.s.own_sems.at[CLASSES * triple + kind, 0]
        return pltpu.make_async_copy(self.unit_half(triple, kind, bit), self.held(triple, kind), sem)

    def result(self, triple, kind, count):
        which, row_block, col_block = TARGETS[triple % GROUPS][kind]
        starts, sizes = self.plan.place(kind, count)
        return self.s.results[which].at[
            1 - triple // GROUPS,
            pl.ds(pl.multiple_of(row_block * self.plan.rows + starts[0], 8), sizes[0]),
            pl.ds(pl.multiple_of(col_block * CHUNK + starts[1], LANES), sizes[1]),
        ]

    def finished(self, triple, kind):
        return self.held(triple, kind).at[self.plan.part(kind, self.plan.halvings - 1)].at[0]

    def keep(self, triple, kind):
        target = self.result(triple, kind, len(self.plan.page_steps[kind]))
        sem = self.s.own_sems.at[CLASSES * triple + kind, 1]
        return pltpu.make_async_copy(self.finished(triple, kind), target, sem)

    def gathering(self, triple, kind, phase):
        plan = self.plan
        count = len(plan.page_steps[kind]) - (phase - plan.halvings)
        target = self.result(triple, kind, count)
        source = self.finished(triple, kind) if phase == plan.halvings else target
        _, device = plan.partner(kind, plan.page_steps[kind][count - 1])
        return self.remote(source, target, CLASSES * triple + kind, phase, device)

    def start(self, triple, kind, phase):
        plan = self.plan
        if phase < plan.halvings:
            if triple >= RING:
                pl.semaphore_wait(self.s.free_sems.at[kind, phase], 1)
            self.halving(triple, kind, phase).start()
            if phase == 0:
                self.own_half(triple, kind).start()
        elif phase < plan.phases:
            if phase == plan.halvings:
                self.keep(triple, kind).start()
            self.gathering(triple, kind, phase).start()

    def finish(self, triple, kind, phase):
        plan, s = self.plan, self.s
        if phase < plan.halvings:
            self.halving(triple, kind, phase).wait()
            if phase == 0:
                self.own_half(triple, kind).wait()
            landed = s.landing[kind][phase].at[triple % RING]
            kept = self.held(triple, kind).at[plan.part(kind, phase)]
            for share in range(landed.shape[0]):
                kept[share] += landed[share]
            if triple < TRIPLES - RING:
                _, device = plan.partner(kind, phase)
                pl.semaphore_signal(s.free_sems.at[kind, phase], inc=1, device_id=device, device_id_type=MESH)
        else:
            if phase == plan.halvings:
                self.keep(triple, kind).wait()
            self.gathering(triple, kind, phase).wait()

    def advance(self, time):
        for stage in range(self.plan.phases, -1, -1):
            for triple, stages in enumerate(self.plan.times):
                if stages[stage] == time:
                    for kind in range(CLASSES):
                        if stage > 0:
                            self.finish(triple, kind, stage - 1)
                        self.start(triple, kind, stage)

    def advance_at(self, index, times):
        for number, time in enumerate(times):
            if any(time in stages for stages in self.plan.times):

                @pl.when(index == number)
                def _(time=time):
                    self.advance(time)

    def small_copy(self, phase):
        s = self.s
        _, device = self.plan.partner(0, phase)
        return pltpu.make_async_remote_copy(
            src_ref=s.small_own if phase == 0 else s.small_parts.at[phase - 1],
            dst_ref=s.small_parts.at[phase],
            send_sem=s.small_sems.at[0, phase],
            recv_sem=s.small_sems.at[1, phase],
            device_id=device,
            device_id_type=MESH,
        )

    def small_step(self, phase):
        s = self.s
        if phase >= 0:
            self.small_copy(phase).wait()
            s.small_parts[phase] += s.small_own[...] if phase == 0 else s.small_parts[phase - 1]
        if phase + 1 < self.plan.halvings:
            self.small_copy(phase + 1).start()


ENTRIES = (0, 2, 5, 9, 17, 18, 20, 26)
FEED_STEPS = ((), (13, 14, 15, 16))
AFTER_FEED = (0, 17)
AFTER_NORM = (1, 18)
AFTER_MERGE = (2, 19)
ATTEND_STEPS = (range(3, 9), range(20, 26))
AFTER_PROJECT = (9, 26)


class Moves:
    def __init__(self, sems):
        self.sems, self.used = sems, 0

    def __call__(self, source, target):
        number, self.used = self.used, self.used + 1
        make = functools.partial(pltpu.make_async_copy, source, target, self.sems.at[number])
        make().start()
        return lambda: make().wait()


class Refs:
    pass


def run(plan, layout, *refs):
    s = Refs()
    for name, ref in zip(layout, refs):
        setattr(s, name, ref)
    rest = list(refs[len(layout) :])
    s.landing = [[rest.pop(0) for _ in range(plan.halvings)] for _ in range(CLASSES)]
    s.results = (s.sum_qkv, s.sum_proj, s.sum_fc1, s.sum_fc2)
    s.units = (s.units_zero, s.units_one)
    windows = s.x.shape[1] // LANES
    patches = s.dense.shape[0] // SPLITS
    half, half_rows = patches // 2, s.dense.shape[0] // 2
    upper, lower = pl.ds(0, half_rows), pl.ds(half_rows, half_rows)
    reducer = Reducer(plan, s)
    move = Moves(s.move_sems)
    page, row = lax.axis_index(PAGE), lax.axis_index(ROW)
    count = lax.axis_size(ROW)
    above, below = (page, (row + count - 1) % count), (page, (row + 1) % count)

    def halo(number, source, target, device):
        make = functools.partial(
            pltpu.make_async_remote_copy,
            src_ref=source,
            dst_ref=target,
            send_sem=s.halo_sems.at[0, number],
            recv_sem=s.halo_sems.at[1, number],
            device_id=device,
            device_id_type=MESH,
        )
        make().start()
        return lambda: make().wait()

    tokens_there = move(s.in_tokens, s.tokens)
    places_there = (move(s.in_plain, s.plain), move(s.in_moved, s.moved))
    spread_there = move(s.in_spread, s.spread)
    weights = ((s.in_qkv, s.w_qkv), (s.in_proj, s.w_proj), (s.in_fc1, s.w_fc1), (s.in_fc2, s.w_fc2))

    def fetch_weight(which, layer):
        source, target = weights[which]
        return move(source.at[layer], target)

    there = [fetch_weight(which, 0) for which in range(4)]

    barrier = pltpu.get_barrier_semaphore()
    devices = [plan.partner(0, level)[1] for level in range(plan.halvings)] + [above, below]
    for device in devices:
        pl.semaphore_signal(barrier, inc=1, device_id=device, device_id_type=MESH)
    pl.semaphore_wait(barrier, len(devices))

    live_there = halo(0, s.live, s.live_upper, above)
    grad_there = halo(1, s.in_grad.at[upper], s.grad_upper, above)
    s.page[...] = jnp.zeros(s.page.shape, F32)
    tokens_there()
    cols = s.tokens.shape[1]
    for line in range(WIN):
        s.page[pl.ds(line * cols, cols), :] = s.tokens[line].astype(F32)
    places_there[0]()
    to_channels(s.page, s.plain, s.x, True)
    saves = [move(s.x, s.kept_x)]
    spread_columns(s, 0)
    spread_there()
    spread_bias(s.table[0], s.spread, s.bias_rows, s.bias)
    region_masks(False, s.regions)
    norm_one_forward(s, windows)
    saves.append(move(s.normed, s.kept_normed))
    there[QKV]()
    project_forward(s, windows)
    saves.append(move(s.qkv, s.kept_qkv))
    there[QKV] = fetch_weight(QKV, 1)
    attend_forward(s, windows, s.live)
    saves.append(move(s.soft, s.kept_soft))
    saves.append(move(s.merged, s.kept_merged))
    there[PROJ]()
    s.work[...] = mm(s.w_proj[...], s.merged[...], 0, 0)
    there[PROJ] = fetch_weight(PROJ, 1)
    norm_two_forward(s, windows, s.live)
    saves.append(move(s.hidden, s.kept_hidden))
    saves.append(move(s.second, s.kept_second))
    there[FC1]()
    there[FC2]()
    feed_forward(s, windows)
    saves.append(move(s.active, s.kept_active))
    saves.append(move(s.slope, s.kept_slope))
    there[FC1] = fetch_weight(FC1, 1)
    there[FC2] = fetch_weight(FC2, 1)
    to_dense(s.work, s.plain, s.dense)
    upper_there = halo(2, s.dense.at[upper], s.upper, above)

    from_dense(s.dense, half, s.page, half, half)
    spread_columns(s, 1)
    spread_bias(s.table[1], s.spread, s.bias_rows, s.bias)
    region_masks(True, s.regions)
    live_there()
    shifted_live(s, windows)
    places_there[1]()
    for saved in saves:
        saved()
    upper_there()
    from_dense(s.upper, 0, s.page, 0, half)
    to_channels(s.page, s.moved, s.x)
    norm_one_forward(s, windows)
    there[QKV]()
    project_forward(s, windows)
    attend_forward(s, windows, s.live_two)
    there[PROJ]()
    s.work[...] = mm(s.w_proj[...], s.merged[...], 0, 0)
    norm_two_forward(s, windows, s.live_two)
    there[FC1]()
    there[FC2]()
    grad_lower_there = move(s.in_grad.at[lower], s.upper)
    feed_forward(s, windows)
    to_dense(s.work, s.moved, s.dense)
    out_there = halo(3, s.dense.at[upper], s.out_tokens.at[upper], below)
    out_kept = move(s.dense.at[lower], s.out_tokens.at[lower])

    spread_gains(s, 1)
    grad_there()
    grad_lower_there()
    from_dense(s.grad_upper, 0, s.page, 0, half)
    from_dense(s.upper, 0, s.page, half, half)
    to_channels(s.page, s.moved, s.grad)

    def backward(layer, live_ref, fetch):
        reducer.layer = layer
        phase = 1 - layer
        feed_backward(s, reducer, FEED_STEPS[phase])
        reducer.advance(AFTER_FEED[phase])
        fetch(0)
        norm_two_backward(s, windows, live_ref)
        reducer.advance(AFTER_NORM[phase])
        fetch(1)
        merge_backward(s, reducer)
        reducer.advance(AFTER_MERGE[phase])
        fetch(2)
        attend_backward(s, windows, reducer, ATTEND_STEPS[phase])
        fetch(3)
        project_backward(s, reducer)
        fetch(4)
        norm_one_backward(s, windows)
        fetch(5)
        reducer.settle(1)
        reducer.advance(AFTER_PROJECT[phase])

    back = {}

    def refill(point):
        if point == 0:
            back[0] = [move(s.kept_active, s.active), move(s.kept_slope, s.slope), move(s.kept_second, s.second)]
            back[0] += [fetch_weight(FC1, 0), fetch_weight(FC2, 0)]
        elif point == 1:
            back[1] = [move(s.kept_hidden, s.hidden)]
        elif point == 2:
            back[2] = [fetch_weight(PROJ, 0)]
        elif point == 3:
            back[2] += [move(s.kept_merged, s.merged)]
            back[3] = [move(s.kept_soft, s.soft)]
        elif point == 4:
            back[3] += [move(s.kept_qkv, s.qkv)]
            back[4] = [move(s.kept_normed, s.normed), fetch_weight(QKV, 0)]
        else:
            back[5] = [move(s.kept_x, s.x)]

    def needed(point):
        if point in back:
            for arrived in back.pop(point):
                arrived()

    backward(1, s.live_two, refill)
    out_there()
    out_kept()
    to_dense(s.grad, s.moved, s.dense)
    next_there = halo(4, s.dense.at[upper], s.next_upper, below)
    reducer.advance(10)

    from_dense(s.dense, half, s.page, half, half)
    small_gradients(s, s.small_own.at[1])
    spread_gains(s, 0)
    reducer.advance(11)
    next_there()
    from_dense(s.next_upper, 0, s.page, 0, half)
    to_channels(s.page, s.plain, s.grad)
    reducer.advance(12)
    needed(0)

    def wait_next(point):
        needed(point + 1)

    backward(0, s.live, wait_next)
    to_dense(s.grad, s.plain, s.dense)
    grad_kept = move(s.dense, s.grad_tokens)
    reducer.advance(27)
    small_gradients(s, s.small_own.at[0])
    steps = max(stages[-1] for stages in plan.times) + 1
    for time in range(28, steps):
        reducer.advance(time)
        if time - 29 < plan.halvings:
            reducer.small_step(time - 29)
    finish_small(s, plan, row)
    grad_kept()


def finish_small(s, plan, row):
    total = s.small_parts.at[plan.halvings - 1]
    outs = (
        (s.d_ln_gain, (G1, G2)),
        (s.d_ln_bias, (B1, B2)),
        (s.d_qv_bias, (QB, VB)),
        (s.d_proj_bias, (PB,)),
        (s.d_fc1_bias, tuple(range(F1B, F1B + FEEDS))),
        (s.d_fc2_bias, (F2B,)),
    )
    for layer in range(2):
        s.d_table[layer] = total[layer, VECTOR_ROWS:, :OFFSETS]
        for ref, indices in outs:
            whole = jnp.concatenate([total[layer, index : index + 1, :] for index in indices], axis=1)
            size = ref.shape[1]
            mine = jnp.zeros((1, size), F32)
            for share in range(plan.shares):
                mine = jnp.where(row == share, whole[:, share * size : (share + 1) * size], mine)
            ref[layer : layer + 1, :] = mine


def placements(cols):
    windows = cols // WIN
    patches = WIN * cols
    padded = -(-patches // LANES) * LANES
    plain = np.zeros((padded, windows * LANES), np.float32)
    moved = np.zeros((padded, windows * LANES), np.float32)
    for line in range(WIN):
        for col in range(cols):
            source = line * cols + col
            plain[source, (col // WIN) * LANES + line * WIN + col % WIN] = 1
            new_line, new_col = (line - SHIFT) % WIN, (col - SHIFT) % cols
            moved[source, (new_col // WIN) * LANES + new_line * WIN + new_col % WIN] = 1
    return plain.astype(BF), moved.astype(BF)


def table_spread():
    size = 2 * WIN - 1
    spread = np.zeros((WIN, 2 * LANES, TABLE), np.float32)
    for key_col in range(WIN):
        for offset in range(size):
            for col in range(WIN):
                spread[key_col, offset * WIN + col, offset * size + col - key_col + WIN - 1] = 1
    spread = spread.reshape(WIN // 2, 2, 2 * LANES, TABLE).swapaxes(1, 2)
    return spread.reshape(WIN * LANES, 2 * TABLE).astype(BF)


def per_device(
    page_tokens,
    blank_mask,
    cotangent,
    ln_gain,
    ln_bias,
    qv_bias,
    rel_table,
    w_qkv,
    w_proj,
    proj_bias,
    w_fc1,
    fc1_bias,
    w_fc2,
    fc2_bias,
):
    pages, shares = lax.axis_size(PAGE), lax.axis_size(ROW)
    plan = Plan(pages, shares)
    cols = page_tokens.shape[2]
    windows, lanes = cols // WIN, cols // WIN * LANES
    dense = ((WIN * cols * SPLITS, LANES), F32)
    half_dense = ((WIN * cols * SPLITS // 2, LANES), F32)
    plain, moved = (jnp.asarray(place) for place in placements(cols))
    live_rows = 8 * -(-windows // 8)
    live = jnp.pad(1.0 - blank_mask[0, 0].astype(F32), (0, live_rows - windows))
    small_inputs = dict(
        live=jnp.broadcast_to(live[:, None], (live_rows, LANES)),
        table=jnp.pad(rel_table, ((0, 0), (0, 0), (0, TABLE - OFFSETS))),
        ln_gain=ln_gain,
        ln_bias=ln_bias,
        qv_bias=qv_bias,
        proj_bias=proj_bias,
        fc1_bias=fc1_bias,
        fc2_bias=fc2_bias,
    )
    large_inputs = dict(
        in_tokens=page_tokens[0],
        in_grad=cotangent.reshape(dense[0]),
        in_plain=plain,
        in_moved=moved,
        in_spread=jnp.asarray(table_spread()),
        in_qkv=w_qkv,
        in_proj=w_proj,
        in_fc1=w_fc1,
        in_fc2=w_fc2,
    )
    saved = dict(
        x=((D, lanes), F32),
        normed=((D, lanes), BF),
        qkv=((3 * D, lanes), BF),
        soft=((windows * HEADS, LANES, LANES), BF),
        merged=((D, lanes), BF),
        hidden=((D, lanes), F32),
        second=((D, lanes), BF),
        active=((FF, lanes), BF),
        slope=((FF, lanes), BF),
    )
    units = ((UNITS, shares, CHUNK // shares, CHUNK), F32)
    large_outputs = dict(
        out_tokens=dense,
        grad_tokens=dense,
        sum_qkv=((2, D // shares, 3 * D), F32),
        sum_proj=((2, D // shares, D), F32),
        sum_fc1=((2, D // shares, FF), F32),
        sum_fc2=((2, FF // shares, D), F32),
        units_zero=units,
        units_one=units,
        kept_x=((D, lanes), F32),
        kept_normed=((D, lanes), BF),
        kept_qkv=((3 * D, lanes), BF),
        kept_soft=((windows * HEADS, LANES, LANES), BF),
        kept_merged=((D, lanes), BF),
        kept_hidden=((D, lanes), F32),
        kept_second=((D, lanes), BF),
        kept_active=((FF, lanes), BF),
        kept_slope=((FF, lanes), BF),
    )
    small_outputs = dict(
        d_ln_gain=((2, 2 * D // shares), F32),
        d_ln_bias=((2, 2 * D // shares), F32),
        d_qv_bias=((2, 2 * D // shares), F32),
        d_proj_bias=((2, D // shares), F32),
        d_fc1_bias=((2, FF // shares), F32),
        d_fc2_bias=((2, D // shares), F32),
        d_table=((2, HEADS, OFFSETS), F32),
    )
    small = (2, SMALL, D)
    vmem = dict(
        saved,
        tokens=((WIN, cols, D), BF),
        plain=(plain.shape, BF),
        moved=(moved.shape, BF),
        spread=((WIN * LANES, 2 * TABLE), BF),
        w_qkv=((D, 3 * D), BF),
        w_proj=((D, D), BF),
        w_fc1=((D, FF), BF),
        w_fc2=((FF, D), BF),
        page=((plain.shape[0], D), F32),
        dense=dense,
        upper=half_dense,
        grad_upper=half_dense,
        next_upper=half_dense,
        live_upper=((live_rows, LANES), F32),
        live_two=((live_rows, LANES), F32),
        work=((D, lanes), F32),
        grad=((D, lanes), F32),
        low=((D, lanes), BF),
        sums=((VECTORS, D, LANES), F32),
        gains=((2, D, LANES), F32),
        bias=((HEADS, LANES, LANES), F32),
        bias_rows=((HEADS * LANES, LANES), F32),
        regions=((2, LANES, LANES), F32),
        vector_rows=((VECTOR_ROWS, D), F32),
        staged=((2, CHUNK, CHUNK), F32),
        held=((HELD * CLASSES, shares, CHUNK // shares, CHUNK // 2), F32),
        small_own=(small, F32),
        small_parts=((plan.halvings,) + small, F32),
    )
    semaphores = dict(
        move_sems=pltpu.SemaphoreType.DMA((48,)),
        halo_sems=pltpu.SemaphoreType.DMA((2, 5)),
        send_sems=pltpu.SemaphoreType.DMA((2 * UNITS, plan.phases)),
        recv_sems=pltpu.SemaphoreType.DMA((2 * UNITS, plan.phases)),
        own_sems=pltpu.SemaphoreType.DMA((2 * UNITS, 2)),
        stage_sems=pltpu.SemaphoreType.DMA((2, shares)),
        small_sems=pltpu.SemaphoreType.DMA((2, plan.halvings)),
        free_sems=pltpu.SemaphoreType.REGULAR((CLASSES, plan.halvings)),
    )
    landing = [((RING,) + size, F32) for sizes in plan.sizes for size in sizes]
    layout = [*small_inputs, *large_inputs, *small_outputs, *large_outputs, *vmem, *semaphores]
    in_vmem, anywhere = pl.BlockSpec(memory_space=pltpu.VMEM), pl.BlockSpec(memory_space=pl.ANY)
    outputs = {**small_outputs, **large_outputs}
    results = pl.pallas_call(
        functools.partial(run, plan, layout),
        out_shape=[jax.ShapeDtypeStruct(*shape) for shape in outputs.values()],
        in_specs=[in_vmem] * len(small_inputs) + [anywhere] * len(large_inputs),
        out_specs=[in_vmem] * len(small_outputs) + [anywhere] * len(large_outputs),
        scratch_shapes=[pltpu.VMEM(*shape) for shape in vmem.values()]
        + list(semaphores.values())
        + [pltpu.VMEM(*shape) for shape in landing],
        compiler_params=pltpu.CompilerParams(
            vmem_limit_bytes=VMEM_LIMIT, collective_id=0, has_side_effects=True
        ),
        name="two_layers",
    )(*small_inputs.values(), *large_inputs.values())
    d_ln_gain, d_ln_bias, d_qv_bias, d_proj_bias, d_fc1_bias, d_fc2_bias, d_table = results[: len(small_outputs)]
    out_tokens, grad_tokens, sum_qkv, sum_proj, sum_fc1, sum_fc2 = results[len(small_outputs) :][:6]
    return (
        out_tokens.reshape(cotangent.shape),
        grad_tokens.reshape(cotangent.shape),
        d_ln_gain,
        d_ln_bias,
        d_qv_bias,
        d_table,
        sum_qkv,
        sum_proj,
        d_proj_bias,
        sum_fc1,
        d_fc1_bias,
        sum_fc2,
        d_fc2_bias,
    )


def solution(mesh):
    tokens, by_row, shares = P(PAGE, ROW, None, None), P(None, ROW), P(None, ROW, None)
    return jax.shard_map(
        per_device,
        mesh=mesh,
        in_specs=(tokens, P(PAGE, ROW, None), tokens) + (P(),) * 11,
        out_specs=(tokens, tokens)
        + (by_row, by_row, by_row, P(), shares, shares, by_row, shares, by_row, shares, by_row),
        check_vma=False,
    )
```

```python
import functools

import jax
import jax.numpy as jnp
import numpy as np
from jax import lax
from jax.experimental import pallas as pl
from jax.experimental.pallas import tpu as pltpu
from jax.sharding import PartitionSpec as P

WIN = 10
SHIFT = 5
AREA = WIN * WIN
LANES = 128
D = 512
HEADS = 16
HEAD_DIM = 32
FF = 2048
CHUNK = 512
FEEDS = FF // CHUNK
SPLITS = D // LANES
EPSILON = 1e-05
MASK_VALUE = -100.0
NEVER = -1e30
SCORE_SCALE = HEAD_DIM ** (-0.5)
VMEM_LIMIT = 63 * 1024 * 1024 + 512 * 1024
BF = jnp.bfloat16
F32 = jnp.float32
MESH = pl.DeviceIdType.MESH
PAGE, ROW = "page", "row"

G1, B1, G2, B2, QB, VB, PB, F2B, F1B, VECTORS = 0, 1, 2, 3, 4, 5, 6, 7, 8, 12
VECTOR_ROWS = 16
SMALL = VECTOR_ROWS + HEADS
OFFSETS = (2 * WIN - 1) ** 2
TABLE = 384

UNIT_FC1, UNIT_FC2, UNIT_PROJ, UNIT_QKV, UNITS = 0, 4, 8, 9, 12
CLASSES = 3
GROUPS = UNITS // CLASSES
TRIPLES = 2 * GROUPS
HELD = 4
RING = 3
QKV, PROJ, FC1, FC2 = range(4)
TARGETS = (
    ((FC1, 0, 0), (FC1, 0, 1), (FC1, 0, 2)),
    ((FC1, 0, 3), (FC2, 0, 0), (FC2, 1, 0)),
    ((FC2, 2, 0), (FC2, 3, 0), (PROJ, 0, 0)),
    ((QKV, 0, 0), (QKV, 0, 1), (QKV, 0, 2)),
)


def mm(left, right, left_dim, right_dim):
    return lax.dot_general(
        left, right, (((left_dim,), (right_dim,)), ((), ())), preferred_element_type=F32
    )


def split(values):
    high = values.astype(BF)
    return high, (values - high.astype(F32)).astype(BF)


def lane_tile(index):
    return pl.ds(pl.multiple_of(index * LANES, LANES), LANES)


def chunk_of(index):
    return pl.ds(pl.multiple_of(index * CHUNK, CHUNK), CHUNK)


def wide(column, count):
    return jnp.concatenate([column] * count, axis=1)


def fold(values):
    total = values[:, :LANES]
    for start in range(LANES, values.shape[1], LANES):
        total = total + values[:, start : start + LANES]
    return total


def norm_parts(values):
    center = values - jnp.sum(values, axis=0, keepdims=True) * (1.0 / D)
    spread = jnp.sum(center * center, axis=0, keepdims=True) * (1.0 / D)
    scale = lax.rsqrt(spread + EPSILON)
    return center * scale, scale


def norm_pull(grad, gain, hat, scale):
    scaled = grad * gain
    mean_one = jnp.sum(scaled, axis=0, keepdims=True) * (1.0 / D)
    mean_two = jnp.sum(scaled * hat, axis=0, keepdims=True) * (1.0 / D)
    return scale * (scaled - mean_one - hat * mean_two)


def gelu_parts(inner):
    step = 1.0 / (1.0 + (0.3275911 * 0.7071067811865476) * jnp.abs(inner))
    bell = jnp.exp(inner * inner * -0.5)
    poly = 0.5 * 1.061405429
    for factor in (-1.453152027, 1.421413741, -0.284496736, 0.254829592):
        poly = poly * step + 0.5 * factor
    tail = poly * step * bell
    below = jnp.where(inner >= 0, 1.0 - tail, tail)
    return inner * below, below + inner * bell * 0.3989422804014327


def to_channels(page_ref, place_ref, out_ref, exact=False):
    def step(index, carry):
        channels = pl.ds(pl.multiple_of(index * 256, 256), 256)
        values = page_ref[:, channels]
        if exact:
            out_ref[channels, :] = mm(values.astype(BF), place_ref[...], 0, 0)
        else:
            high, low = split(values)
            out_ref[channels, :] = mm(high, place_ref[...], 0, 0) + mm(low, place_ref[...], 0, 0)
        return carry

    lax.fori_loop(0, D // 256, step, 0)


def to_dense(values_ref, place_ref, dense_ref, padded):
    count = dense_ref.shape[0] // SPLITS
    for index in range(D // 256):
        high, low = split(values_ref[index * 256 : (index + 1) * 256, :])
        page = mm(place_ref[:padded, :], high, 1, 1) + mm(place_ref[:padded, :], low, 1, 1)
        for part in range(2):
            rows = pl.ds(2 * index + part, count, stride=SPLITS)
            dense_ref[rows, :] = page[:count, part * LANES : (part + 1) * LANES]


def from_dense(dense_ref, page_ref, row):
    count = dense_ref.shape[0] // SPLITS
    for part in range(SPLITS):
        rows = pl.ds(part, count, stride=SPLITS)
        page_ref[pl.ds(row, count), part * LANES : (part + 1) * LANES] = dense_ref[rows, :]


def add_halo(page_ref, place_ref, out_ref, count, padded):
    page_ref[pl.ds(count, padded - count), :] = jnp.zeros((padded - count, D), F32)

    def step(index, carry):
        channels = pl.ds(pl.multiple_of(index * 256, 256), 256)
        high, low = split(page_ref[:padded, channels])
        out_ref[channels, :] += mm(high, place_ref[:padded, :], 0, 0) + mm(low, place_ref[:padded, :], 0, 0)
        return carry

    lax.fori_loop(0, D // 256, step, 0)


def move_own(values_ref, swap_ref, out_ref, windows, first):
    for window in range(windows):
        sources = [(window + first + part) % windows * LANES for part in range(2)]
        values = jnp.concatenate([values_ref[:, start : start + LANES] for start in sources], axis=1)
        high, low = split(values)
        target = slice(window * LANES, (window + 1) * LANES)
        out_ref[:, target] = mm(high, swap_ref[...], 1, 0) + mm(low, swap_ref[...], 1, 0)


def vector_rows(s, layer):
    rows = s.vector_rows
    sources = ((G1, s.ln_gain, 0), (B1, s.ln_bias, 0), (G2, s.ln_gain, 1), (B2, s.ln_bias, 1))
    sources += ((QB, s.qv_bias, 0), (VB, s.qv_bias, 1), (PB, s.proj_bias, 0), (F2B, s.fc2_bias, 0))
    sources += tuple((F1B + part, s.fc1_bias, part) for part in range(FEEDS))
    for index, source, part in sources:
        rows[index : index + 1, :] = source[layer : layer + 1, part * D : (part + 1) * D]
    rows[VECTORS:, :] = jnp.zeros((VECTOR_ROWS - VECTORS, D), F32)
    return rows[...].T


def spread_columns(s, layer):
    columns = vector_rows(s, layer)
    for index in range(VECTORS):
        s.sums[index] = jnp.broadcast_to(columns[:, index : index + 1], (D, LANES))


def spread_gains(s, layer):
    columns = vector_rows(s, layer)
    for index, vector in enumerate((G1, G2)):
        s.gains[index] = jnp.broadcast_to(columns[:, vector : vector + 1], (D, LANES))


def spread_part(col):
    rows, lanes = (col // 2) * 2 * LANES, (col % 2) * TABLE
    return slice(rows, rows + 2 * LANES), slice(lanes, lanes + TABLE)


def spread_bias(s, layer):
    spread_ref, rows_ref, bias_ref = s.spread, s.bias_rows, s.bias
    s.padded_table[...] = jnp.zeros(s.padded_table.shape, F32)
    s.padded_table[:, :OFFSETS] = s.table[layer]
    high, low = split(s.padded_table[...])
    parts = []
    for col in range(WIN):
        chosen = spread_ref[spread_part(col)]
        parts.append(mm(high, chosen, 1, 1) + mm(low, chosen, 1, 1))
    source = jnp.concatenate(parts, axis=0)
    rows_ref[...] = jnp.zeros(rows_ref.shape, F32)
    for row in range(WIN):
        shift = (WIN - 1 - row) * WIN
        moved = source if shift == 0 else pltpu.roll(source, 2 * LANES - shift, axis=1)
        rows_ref[pl.ds(row * WIN * HEADS, WIN * HEADS), :] = moved[:, :LANES]
    for head in range(HEADS):
        bias_ref[head] = rows_ref[pl.ds(head, LANES, stride=HEADS), :]


def gather_bias(grad_ref, spread_ref, rows_ref):
    for head in range(HEADS):
        rows_ref[pl.ds(head, LANES, stride=HEADS), :] = grad_ref[head]
    total = jnp.zeros((WIN * HEADS, 2 * LANES), F32)
    for row in range(WIN):
        shift = (WIN - 1 - row) * WIN
        piece = rows_ref[pl.ds(row * WIN * HEADS, WIN * HEADS), :]
        piece = jnp.concatenate([piece, jnp.zeros_like(piece)], axis=1)
        total = total + (piece if shift == 0 else pltpu.roll(piece, shift, axis=1))
    table = jnp.zeros((HEADS, TABLE), F32)
    for col in range(WIN):
        for part in split(total[col * HEADS : (col + 1) * HEADS]):
            table = table + mm(part, spread_ref[spread_part(col)], 1, 0)
    return table


def region_masks(shifted_layer, out_ref):
    key = lax.broadcasted_iota(jnp.int32, (LANES, LANES), 0)
    query = lax.broadcasted_iota(jnp.int32, (LANES, LANES), 1)
    padding = jnp.where(key < AREA, 0.0, NEVER)
    out_ref[0] = padding
    out_ref[1] = padding
    if shifted_layer:
        last = lax.axis_index(ROW) == lax.axis_size(ROW) - 1
        rows_differ = ((key >= AREA // 2) != (query >= AREA // 2)) & last
        cols_differ = (key % WIN >= SHIFT) != (query % WIN >= SHIFT)
        out_ref[0] += jnp.where(rows_differ, MASK_VALUE, 0.0)
        out_ref[1] += jnp.where(rows_differ | cols_differ, MASK_VALUE, 0.0)


def shifted_live(s, windows):
    place = lax.broadcasted_iota(jnp.int32, (1, LANES), 1)
    for window in range(windows):
        here, after = slice(window, window + 1), slice((window + 1) % windows, (window + 1) % windows + 1)
        beyond = place % WIN >= SHIFT
        own = jnp.where(beyond, s.live[after, :], s.live[here, :])
        upper = jnp.where(beyond, s.live_upper[after, :], s.live_upper[here, :])
        s.live_two[here, :] = jnp.where(place >= AREA // 2, upper, own)


def head_rows(head, base=0):
    return pl.ds(base + head * HEAD_DIM, HEAD_DIM)


def norm_one_forward(s, windows):
    def step(index, carry):
        lanes = lane_tile(index)
        hat, _ = norm_parts(s.x[:, lanes])
        s.normed[:, lanes] = (hat * s.sums[G1] + s.sums[B1]).astype(BF)
        return carry

    lax.fori_loop(0, windows, step, 0)


def project_forward(s, windows):
    def step(index, carry):
        rows = chunk_of(index)
        bias = s.sums[jnp.where(index == 0, QB, VB)] * jnp.where(index == 1, 0.0, 1.0)
        out = mm(s.w_qkv[:, rows], s.normed[...], 0, 0)
        s.qkv[rows, :] = (out + wide(bias, windows)).astype(BF)
        return carry

    lax.fori_loop(0, 3, step, 0)


def attend_forward(s, windows, live_ref):
    def step(index, carry):
        lanes = lane_tile(index)
        live = jnp.broadcast_to(live_ref[pl.ds(index, 1), :], (LANES, LANES)).T
        masked = s.regions[jnp.where(index == windows - 1, 1, 0)] + MASK_VALUE * (1.0 - live)
        for head in range(HEADS):
            query = s.qkv[head_rows(head), lanes]
            key = s.qkv[head_rows(head, D), lanes]
            value = s.qkv[head_rows(head, 2 * D), lanes]
            scores = mm(key, query, 0, 0) * SCORE_SCALE + (s.bias[head] + masked)
            exponent = jnp.exp(scores - jnp.max(scores, axis=0, keepdims=True))
            total = jnp.sum(exponent, axis=0, keepdims=True)
            soft = (exponent * (1.0 / total)).astype(BF)
            s.soft[index * HEADS + head] = soft
            s.merged[head_rows(head), lanes] = mm(value, soft, 1, 0).astype(BF)
        return carry

    lax.fori_loop(0, windows, step, 0)


def norm_two_forward(s, windows, live_ref):
    def step(index, carry):
        lanes = lane_tile(index)
        hidden = s.x[:, lanes] + live_ref[pl.ds(index, 1), :] * (s.work[:, lanes] + s.sums[PB])
        s.hidden[:, lanes] = hidden
        s.work[:, lanes] = hidden + s.sums[F2B]
        hat, _ = norm_parts(hidden)
        s.second[:, lanes] = (hat * s.sums[G2] + s.sums[B2]).astype(BF)
        return carry

    lax.fori_loop(0, windows, step, 0)


def feed_forward(s, windows):
    def step(index, carry):
        rows = chunk_of(index)
        inner = mm(s.w_fc1[:, rows], s.second[...], 0, 0) + wide(s.sums[F1B + index], windows)
        active, slope = gelu_parts(inner)
        active = active.astype(BF)
        s.active[rows, :] = active
        s.slope[rows, :] = slope.astype(BF)
        s.work[...] += mm(s.w_fc2[rows, :], active, 0, 0)
        return carry

    lax.fori_loop(0, FEEDS, step, 0)


def feed_backward(s, sink, times):
    s.sums[...] = jnp.zeros(s.sums.shape, F32)
    s.bias[...] = jnp.zeros(s.bias.shape, F32)
    lowered = s.grad[...].astype(BF)
    s.low[...] = lowered
    s.sums[F2B] = fold(lowered.astype(F32))
    s.work[...] = jnp.zeros(s.work.shape, F32)

    def step(index, carry):
        rows = chunk_of(index)
        sink.put(0, mm(s.active[rows, :], s.low[...], 1, 1), feed_pieces(index, sink.shares), index == 0)
        grad_inner = mm(s.w_fc2[rows, :], s.low[...], 1, 0) * s.slope[rows, :].astype(F32)
        grad_inner = grad_inner.astype(BF)
        s.sums[F1B + index] = fold(grad_inner.astype(F32))
        sink.put(1, mm(s.second[...], grad_inner, 1, 1), row_pieces(UNIT_FC1 + index, sink.shares), index == 0)
        s.work[...] += mm(s.w_fc1[:, rows], grad_inner, 1, 0)
        sink.advance_at(index, times)
        return carry

    lax.fori_loop(0, FEEDS, step, 0)
    sink.settle(0)
    sink.settle(1)


def norm_two_backward(s, windows, live_ref):
    def step(index, carry):
        lanes = lane_tile(index)
        hat, scale = norm_parts(s.hidden[:, lanes])
        grad = s.work[:, lanes]
        s.sums[G2] += grad * hat
        s.sums[B2] += grad
        grad = s.grad[:, lanes] + norm_pull(grad, s.gains[1], hat, scale)
        s.grad[:, lanes] = grad
        grad_low = (grad * live_ref[pl.ds(index, 1), :]).astype(BF)
        s.low[:, lanes] = grad_low
        s.sums[PB] += grad_low.astype(F32)
        return carry

    lax.fori_loop(0, windows, step, 0)


def merge_backward(s, sink):
    sink.put(0, mm(s.merged[...], s.low[...], 1, 1), row_pieces(UNIT_PROJ, sink.shares), True)
    s.merged[...] = mm(s.w_proj[...], s.low[...], 1, 0).astype(BF)
    sink.settle(0)


def attend_backward(s, windows, sink, times):
    def step(index, carry):
        lanes = lane_tile(index)
        for head in range(HEADS):
            query = s.qkv[head_rows(head), lanes]
            key = s.qkv[head_rows(head, D), lanes]
            value = s.qkv[head_rows(head, 2 * D), lanes]
            grad_out = s.merged[head_rows(head), lanes]
            soft_low = s.soft[index * HEADS + head]
            soft = soft_low.astype(F32)
            grad_soft = mm(value, grad_out, 0, 0)
            inner = jnp.sum(soft * grad_soft, axis=0, keepdims=True)
            grad_scores = (soft * (grad_soft - inner)).astype(BF)
            s.bias[head] += grad_scores.astype(F32)
            grad_query = (mm(key, grad_scores, 1, 0) * SCORE_SCALE).astype(BF)
            grad_key = (mm(query, grad_scores, 1, 1) * SCORE_SCALE).astype(BF)
            grad_value = mm(grad_out, soft_low, 1, 1).astype(BF)
            s.qkv[head_rows(head), lanes] = grad_query
            s.qkv[head_rows(head, D), lanes] = grad_key
            s.qkv[head_rows(head, 2 * D), lanes] = grad_value
            s.sums[QB, head_rows(head), :] += grad_query.astype(F32)
            s.sums[VB, head_rows(head), :] += grad_value.astype(F32)
        sink.advance_at(index, times)
        return carry

    lax.fori_loop(0, windows, step, 0)


def project_backward(s, sink):
    def step(index, carry):
        rows = chunk_of(index)
        sink.put(1, mm(s.normed[...], s.qkv[rows, :], 1, 1), row_pieces(UNIT_QKV + index, sink.shares), index == 0)
        return carry

    lax.fori_loop(0, 3, step, 0)


def input_backward(s):
    s.work[...] = mm(s.w_qkv[...], s.qkv[...], 1, 0)


def norm_one_backward(s, windows):
    def step(index, carry):
        lanes = lane_tile(index)
        hat, scale = norm_parts(s.x[:, lanes])
        grad = s.work[:, lanes]
        s.sums[G1] += grad * hat
        s.sums[B1] += grad
        s.grad[:, lanes] += norm_pull(grad, s.gains[0], hat, scale)
        return carry

    lax.fori_loop(0, windows, step, 0)


def small_gradients(s, small_ref):
    places = lax.broadcasted_iota(jnp.int32, (D, LANES), 1)
    packed = jnp.zeros((D, LANES), F32)
    for index in range(VECTORS):
        packed = jnp.where(places == index, jnp.sum(s.sums[index], axis=1, keepdims=True), packed)
    small_ref[:VECTOR_ROWS, :] = packed.T[:VECTOR_ROWS]
    table = gather_bias(s.bias, s.spread, s.bias_rows)
    small_ref[VECTOR_ROWS:, :] = jnp.concatenate([table, jnp.zeros((HEADS, D - TABLE), F32)], axis=1)


def reversed_bits(value, count):
    turned = 0
    for bit in range(count):
        turned = turned * 2 + (value // 2**bit) % 2
    return turned


def row_pieces(unit, shares):
    rows, count = CHUNK // shares, shares.bit_length() - 1
    return [(share * rows, unit, reversed_bits(share, count)) for share in range(shares)]


def feed_pieces(index, shares):
    rows, count = CHUNK // shares, shares.bit_length() - 1
    pieces = []
    for share in range(shares // FEEDS):
        place = reversed_bits(index * (shares // FEEDS) + share, count)
        for part in range(FEEDS):
            pieces.append(((share * FEEDS + part) * rows, UNIT_FC2 + part, place))
    return pieces


class Plan:
    def __init__(self, pages, shares):
        self.shares, self.rows = shares, CHUNK // shares
        page_bits, row_bits = pages.bit_length() - 1, shares.bit_length() - 1
        others = page_bits - 1
        self.steps = []
        for kind in range(CLASSES):
            turn = kind % 2
            page = [(PAGE, 2 ** (1 + (bit + turn) % others)) for bit in range(others)]
            row = [(ROW, 2**bit) for bit in range(row_bits)]
            self.steps.append([(PAGE, 1)] + (row + page if kind == 2 else page + row))
        self.page_steps = [[0] + [at for at, step in enumerate(steps) if at and step[0] == PAGE] for steps in self.steps]
        self.halvings = page_bits + row_bits
        self.phases = self.halvings + page_bits
        self.sizes = []
        for kind in range(CLASSES):
            size = [shares, self.rows, CHUNK // 2]
            sizes = [tuple(size)]
            for level in range(1, self.halvings):
                size[self.split_axis(kind, level)] //= 2
                sizes.append(tuple(size))
            self.sizes.append(sizes)
        self.steps_at = self.schedule()

    def schedule(self):
        small = TRIPLES
        free, ready, stage_of, plan, now = {}, {}, {}, [], 0.0
        for triple in range(TRIPLES):
            for kind in range(CLASSES):
                stage_of[triple, kind] = 0
        stage_of[small, 0] = 0

        def link(key, phase):
            triple, kind = key
            if phase < self.halvings:
                axis, stride = self.steps[kind][phase]
                size = 2.0**-phase / 2 if triple != small else 0.125
            else:
                axis, stride = self.steps[kind][self.page_steps[kind][self.phases - 1 - phase]]
                size = 2.0 ** (phase - 2 * self.halvings)
            if axis == PAGE and stride == 1:
                return 0, size * PLAN_CORE
            return (axis, stride if axis == PAGE else 0), size * PLAN_LINK * (1.0 if stride == 1 or axis == PAGE else 1.5)

        def last_stage(key):
            return self.halvings if key[0] == small else self.phases

        def allowed(key, point):
            triple, kind = key
            stage = stage_of[key]
            if stage > last_stage(key):
                return False
            if triple == small:
                return point >= len(PLAN_POINTS) - 1
            if stage == 0 and point < PLAN_THERE[triple]:
                return False
            if triple > 0 and stage_of[triple - 1, kind] <= stage:
                return False
            if triple >= RING and stage < self.halvings and stage_of[triple - RING, kind] <= stage + 1:
                return False
            return not (stage == 0 and triple >= HELD and stage_of[triple - HELD, kind] <= self.halvings + 1)

        for point, work in enumerate(PLAN_POINTS):
            now += work
            if point == PLAN_HALO:
                free[ROW, 0] = max(now, free.get((ROW, 0), 0.0)) + PLAN_HALO_TIME
            steps, final = [], point == len(PLAN_POINTS) - 1
            while True:
                keys = [key for key in stage_of if allowed(key, point)]
                keys = [key for key in keys if final or ready.get(key, 0.0) <= now + PLAN_SLACK]
                if not keys:
                    break
                key = min(keys, key=lambda key: (max(ready.get(key, 0.0), now), -stage_of[key], key))
                stage = stage_of[key]
                now = max(now, ready.get(key, 0.0)) + (PLAN_ADD * 2.0**-stage if stage else 0.0)
                if stage < last_stage(key):
                    name, length = link(key, stage)
                    free[name] = max(now, free.get(name, 0.0)) + length
                    ready[key] = free[name] + PLAN_LATENCY
                steps.append((*key, stage))
                stage_of[key] += 1
            plan.append(steps)
        assert all(stage_of[key] > last_stage(key) for key in stage_of)
        return plan

    def split_axis(self, kind, level):
        if self.steps[kind][level][0] == ROW:
            return 0
        return 2 if self.page_steps[kind].index(level) < 2 else 1

    def partner(self, kind, level):
        axis, stride = self.steps[kind][level]
        page, row = lax.axis_index(PAGE), lax.axis_index(ROW)
        mine = page if axis == PAGE else row
        bit = (mine // stride) % 2
        other = mine + (1 - 2 * bit) * stride
        return bit, ((other, row) if axis == PAGE else (page, other))

    def part(self, kind, level, sent=False):
        starts, sizes = [0, 0, 0], [self.shares, self.rows, CHUNK // 2]
        for at in range(1, level + 1):
            axis = self.split_axis(kind, at)
            sizes[axis] //= 2
            bit, _ = self.partner(kind, at)
            which = 1 - bit if sent and at == level else bit
            starts[axis] = starts[axis] + which * sizes[axis]
        return (
            pl.ds(starts[0], sizes[0]),
            pl.ds(pl.multiple_of(starts[1], 8), sizes[1]),
            pl.ds(pl.multiple_of(starts[2], LANES), sizes[2]),
        )

    def place(self, kind, count):
        starts, sizes = [0, 0], [self.rows, CHUNK]
        for at in self.page_steps[kind][:count]:
            axis = self.split_axis(kind, at) - 1 if at else 1
            sizes[axis] //= 2
            bit, _ = self.partner(kind, at)
            starts[axis] = starts[axis] + bit * sizes[axis]
        return starts, sizes


class Reducer:
    def __init__(self, plan, s):
        self.plan, self.s = plan, s
        self.shares = plan.shares
        self.layer = 1

    def stage_copies(self, slot, pieces):
        return [
            pltpu.make_async_copy(
                self.s.staged.at[slot, pl.ds(start, self.plan.rows)],
                self.s.units[self.layer].at[unit, place],
                self.s.stage_sems.at[slot, number],
            )
            for number, (start, unit, place) in enumerate(pieces)
        ]

    def put(self, slot, grad, pieces, first):
        if first is not True:

            @pl.when(jnp.logical_not(first))
            def _():
                self.settle(slot)

        self.s.staged[slot] = grad
        for copy in self.stage_copies(slot, pieces):
            copy.start()

    def settle(self, slot):
        for copy in self.stage_copies(slot, row_pieces(0, self.shares)):
            copy.wait()

    def remote(self, source, target, unit, phase, device):
        return pltpu.make_async_remote_copy(
            src_ref=source,
            dst_ref=target,
            send_sem=self.s.send_sems.at[unit, phase],
            recv_sem=self.s.recv_sems.at[unit, phase],
            device_id=device,
            device_id_type=MESH,
        )

    def unit_half(self, triple, kind, which):
        layer, half = 1 - triple // GROUPS, CHUNK // 2
        unit = CLASSES * (triple % GROUPS) + kind
        return self.s.units[layer].at[unit, :, :, pl.ds(pl.multiple_of(which * half, half), half)]

    def held(self, triple, kind):
        return self.s.held.at[CLASSES * (triple % HELD) + kind]

    def halving(self, triple, kind, level):
        plan = self.plan
        bit, device = plan.partner(kind, level)
        target = self.s.landing[kind][level].at[triple % RING]
        if level == 0:
            source = self.unit_half(triple, kind, 1 - bit)
        else:
            source = self.held(triple, kind).at[plan.part(kind, level, True)]
        return self.remote(source, target, CLASSES * triple + kind, level, device)

    def own_half(self, triple, kind):
        bit, _ = self.plan.partner(kind, 0)
        sem = self.s.own_sems.at[CLASSES * triple + kind, 0]
        return pltpu.make_async_copy(self.unit_half(triple, kind, bit), self.held(triple, kind), sem)

    def result(self, triple, kind, count):
        which, row_block, col_block = TARGETS[triple % GROUPS][kind]
        starts, sizes = self.plan.place(kind, count)
        return self.s.results[which].at[
            1 - triple // GROUPS,
            pl.ds(pl.multiple_of(row_block * self.plan.rows + starts[0], 8), sizes[0]),
            pl.ds(pl.multiple_of(col_block * CHUNK + starts[1], LANES), sizes[1]),
        ]

    def finished(self, triple, kind):
        return self.held(triple, kind).at[self.plan.part(kind, self.plan.halvings - 1)].at[0]

    def keep(self, triple, kind):
        target = self.result(triple, kind, len(self.plan.page_steps[kind]))
        sem = self.s.own_sems.at[CLASSES * triple + kind, 1]
        return pltpu.make_async_copy(self.finished(triple, kind), target, sem)

    def gathering(self, triple, kind, phase):
        plan = self.plan
        count = len(plan.page_steps[kind]) - (phase - plan.halvings)
        target = self.result(triple, kind, count)
        source = self.finished(triple, kind) if phase == plan.halvings else target
        _, device = plan.partner(kind, plan.page_steps[kind][count - 1])
        return self.remote(source, target, CLASSES * triple + kind, phase, device)

    def start(self, triple, kind, phase):
        plan = self.plan
        if phase < plan.halvings:
            if triple >= RING:
                pl.semaphore_wait(self.s.free_sems.at[kind, phase], 1)
            self.halving(triple, kind, phase).start()
            if phase == 0:
                self.own_half(triple, kind).start()
        elif phase < plan.phases:
            if phase == plan.halvings:
                self.keep(triple, kind).start()
            self.gathering(triple, kind, phase).start()

    def finish(self, triple, kind, phase):
        plan, s = self.plan, self.s
        if phase < plan.halvings:
            self.halving(triple, kind, phase).wait()
            if phase == 0:
                self.own_half(triple, kind).wait()
            landed = s.landing[kind][phase].at[triple % RING]
            kept = self.held(triple, kind).at[plan.part(kind, phase)]
            for share in range(landed.shape[0]):
                kept[share] += landed[share]
            if triple < TRIPLES - RING:
                _, device = plan.partner(kind, phase)
                pl.semaphore_signal(s.free_sems.at[kind, phase], inc=1, device_id=device, device_id_type=MESH)
        else:
            if phase == plan.halvings:
                self.keep(triple, kind).wait()
            self.gathering(triple, kind, phase).wait()

    def advance(self, point):
        for triple, kind, stage in self.plan.steps_at[point]:
            if triple == TRIPLES:
                self.small_step(stage - 1)
                continue
            if stage > 0:
                self.finish(triple, kind, stage - 1)
            self.start(triple, kind, stage)

    def advance_at(self, index, points):
        for number, point in enumerate(points):
            if self.plan.steps_at[point]:

                @pl.when(index == number)
                def _(point=point):
                    self.advance(point)

    def small_copy(self, phase):
        s = self.s
        _, device = self.plan.partner(0, phase)
        return pltpu.make_async_remote_copy(
            src_ref=s.small_own if phase == 0 else s.small_parts.at[phase - 1],
            dst_ref=s.small_parts.at[phase],
            send_sem=s.small_sems.at[0, phase],
            recv_sem=s.small_sems.at[1, phase],
            device_id=device,
            device_id_type=MESH,
        )

    def small_step(self, phase):
        s = self.s
        if phase >= 0:
            self.small_copy(phase).wait()
            s.small_parts[phase] += s.small_own[...] if phase == 0 else s.small_parts[phase - 1]
        if phase + 1 < self.plan.halvings:
            self.small_copy(phase + 1).start()


PLAN_POINTS = (0, 2, 3) + (2.7,) * 6 + (5.2, 3, 3, 6) + (3.2,) * 4 + (0.3, 2, 3) + (2.7,) * 6 + (3, 3, 3, 3)
PLAN_THERE = (0, 0, 2, 10, 17, 17, 19, 26)
PLAN_HALO, PLAN_HALO_TIME = 9, 12.3
PLAN_CORE, PLAN_LINK, PLAN_LATENCY, PLAN_ADD, PLAN_SLACK = 1.7, 20.0, 2.0, 0.9, 0.0


class Moves:
    def __init__(self, sems):
        self.sems, self.used = sems, 0

    def __call__(self, source, target):
        number, self.used = self.used, self.used + 1
        make = functools.partial(pltpu.make_async_copy, source, target, self.sems.at[number])
        make().start()
        return lambda: make().wait()


class Refs:
    pass


def run(plan, layout, *refs):
    s = Refs()
    for name, ref in zip(layout, refs):
        setattr(s, name, ref)
    rest = list(refs[len(layout) :])
    s.landing = [[rest.pop(0) for _ in range(plan.halvings)] for _ in range(CLASSES)]
    s.results = (s.sum_qkv, s.sum_proj, s.sum_fc1, s.sum_fc2)
    s.units = (s.units_zero, s.units_one)
    windows = s.x.shape[1] // LANES
    patches = s.dense.shape[0] // SPLITS
    half, half_rows = patches // 2, s.dense.shape[0] // 2
    padded = 16 * -(-half // 16)
    upper, lower = pl.ds(0, half_rows), pl.ds(half_rows, half_rows)
    reducer = Reducer(plan, s)
    move = Moves(s.move_sems)
    page, row = lax.axis_index(PAGE), lax.axis_index(ROW)
    count = lax.axis_size(ROW)
    above, below = (page, (row + count - 1) % count), (page, (row + 1) % count)

    def halo(number, source, target, device):
        make = functools.partial(
            pltpu.make_async_remote_copy,
            src_ref=source,
            dst_ref=target,
            send_sem=s.halo_sems.at[0, number],
            recv_sem=s.halo_sems.at[1, number],
            device_id=device,
            device_id_type=MESH,
        )
        make().start()
        return lambda: make().wait()

    tokens_there = move(s.in_tokens, s.tokens)
    places_there = (move(s.in_plain, s.plain), move(s.in_moved, s.moved))
    swaps_there = (move(s.in_swap_on, s.swap_on), move(s.in_swap_back, s.swap_back))
    spread_there = move(s.in_spread, s.spread)
    weights = ((s.in_qkv, s.w_qkv), (s.in_proj, s.w_proj), (s.in_fc1, s.w_fc1), (s.in_fc2, s.w_fc2))

    def fetch_weight(which, layer):
        source, target = weights[which]
        return move(source.at[layer], target)

    there = [fetch_weight(which, 0) for which in range(4)]

    barrier = pltpu.get_barrier_semaphore()
    devices = [plan.partner(0, level)[1] for level in range(plan.halvings)] + [above, below]
    for device in devices:
        pl.semaphore_signal(barrier, inc=1, device_id=device, device_id_type=MESH)
    pl.semaphore_wait(barrier, len(devices))

    s.live[...] = jnp.zeros(s.live.shape, F32)
    for window in range(windows):
        s.live[window : window + 1, :] = jnp.full((1, LANES), 1.0 - s.blank[0, window].astype(F32))
    live_there = halo(0, s.live, s.live_upper, above)
    grad_there = halo(1, s.in_grad.at[upper], s.grad_upper, above)
    grad_lower_there = move(s.in_grad.at[lower], s.dense.at[lower])
    s.page[...] = jnp.zeros(s.page.shape, F32)
    tokens_there()
    cols = s.tokens.shape[1]
    for line in range(WIN):
        s.page[pl.ds(line * cols, cols), :] = s.tokens[line].astype(F32)
    places_there[0]()
    to_channels(s.page, s.plain, s.x, True)
    saves = [move(s.x, s.kept_x)]
    spread_columns(s, 0)
    spread_there()
    spread_bias(s, 0)
    region_masks(False, s.regions)
    norm_one_forward(s, windows)
    saves.append(move(s.normed, s.kept_normed))
    there[QKV]()
    project_forward(s, windows)
    saves.append(move(s.qkv, s.kept_qkv))
    there[QKV] = fetch_weight(QKV, 1)
    attend_forward(s, windows, s.live)
    saves.append(move(s.soft, s.kept_soft))
    saves.append(move(s.merged, s.kept_merged))
    there[PROJ]()
    s.work[...] = mm(s.w_proj[...], s.merged[...], 0, 0)
    there[PROJ] = fetch_weight(PROJ, 1)
    norm_two_forward(s, windows, s.live)
    saves.append(move(s.hidden, s.kept_hidden))
    saves.append(move(s.second, s.kept_second))
    there[FC1]()
    there[FC2]()
    feed_forward(s, windows)
    saves.append(move(s.active, s.kept_active))
    saves.append(move(s.slope, s.kept_slope))
    there[FC1] = fetch_weight(FC1, 1)
    there[FC2] = fetch_weight(FC2, 1)
    to_dense(s.work, s.plain, s.dense.at[upper], padded)
    upper_there = halo(2, s.dense.at[upper], s.upper, above)

    places_there[1]()
    swaps_there[0]()
    saves.pop(0)()
    move_own(s.work, s.swap_on, s.x, windows, 0)
    spread_columns(s, 1)
    spread_bias(s, 1)
    region_masks(True, s.regions)
    live_there()
    shifted_live(s, windows)
    grad_there()
    grad_lower_there()
    from_dense(s.grad_upper, s.page, 0)
    from_dense(s.dense.at[lower], s.page, half)
    to_channels(s.page, s.moved, s.grad)
    for saved in saves:
        saved()
    upper_there()
    from_dense(s.upper, s.page, 0)
    add_halo(s.page, s.moved, s.x, half, padded)
    norm_one_forward(s, windows)
    there[QKV]()
    project_forward(s, windows)
    attend_forward(s, windows, s.live_two)
    there[PROJ]()
    s.work[...] = mm(s.w_proj[...], s.merged[...], 0, 0)
    norm_two_forward(s, windows, s.live_two)
    there[FC1]()
    there[FC2]()
    feed_forward(s, windows)
    to_dense(s.work, s.moved, s.dense, s.moved.shape[0])
    out_there = halo(3, s.dense.at[upper], s.out_tokens.at[upper], below)
    out_kept = move(s.dense.at[lower], s.out_tokens.at[lower])

    spread_gains(s, 1)

    def backward(layer, live_ref, fetch, points):
        reducer.layer = layer
        first = 0 if layer else FEEDS
        feed_backward(s, reducer, points[:first])
        reducer.advance(points[first])
        fetch(0)
        norm_two_backward(s, windows, live_ref)
        reducer.advance(points[first + 1])
        fetch(1)
        merge_backward(s, reducer)
        reducer.advance(points[first + 2])
        fetch(2)
        attend_backward(s, windows, reducer, points[first + 3 :])
        fetch(3)

    back = {}

    def refill(point):
        if point == 0:
            back[0] = [move(s.kept_active, s.active), move(s.kept_slope, s.slope), move(s.kept_second, s.second)]
            back[0] += [fetch_weight(FC1, 0), fetch_weight(FC2, 0)]
        elif point == 1:
            back[1] = [move(s.kept_hidden, s.hidden)]
        elif point == 2:
            back[2] = [fetch_weight(PROJ, 0)]
        elif point == 3:
            back[2] += [move(s.kept_merged, s.merged)]
            back[3] = [move(s.kept_soft, s.soft)]
        elif point == 4:
            back[4] = [move(s.kept_x, s.x)]
        else:
            back[3] += [move(s.kept_qkv, s.qkv), move(s.kept_normed, s.normed), fetch_weight(QKV, 0)]

    def needed(point):
        if point in back:
            for arrived in back.pop(point):
                arrived()

    backward(1, s.live_two, refill, range(9))
    input_backward(s)
    norm_one_backward(s, windows)
    refill(4)
    out_there()
    to_dense(s.grad, s.moved, s.dense.at[upper], padded)
    next_there = halo(4, s.dense.at[upper], s.next_upper, below)
    reducer.advance(9)
    project_backward(s, reducer)
    refill(5)
    reducer.settle(1)
    reducer.advance(10)

    swaps_there[1]()
    move_own(s.grad, s.swap_back, s.work, windows, -1)
    small_gradients(s, s.small_own.at[1])
    spread_gains(s, 0)
    reducer.advance(11)
    next_there()
    from_dense(s.next_upper, s.page, 0)
    s.grad[...] = s.work[...]
    add_halo(s.page, s.plain, s.grad, half, padded)
    reducer.advance(12)
    needed(0)

    def wait_next(point):
        needed(point + 1)

    backward(0, s.live, wait_next, range(13, 26))
    project_backward(s, reducer)
    reducer.settle(1)
    reducer.advance(26)
    input_backward(s)
    reducer.advance(27)
    needed(4)
    norm_one_backward(s, windows)
    out_kept()
    to_dense(s.grad, s.plain, s.dense, s.plain.shape[0])
    grad_kept = move(s.dense, s.grad_tokens)
    reducer.advance(28)
    small_gradients(s, s.small_own.at[0])
    reducer.advance(29)
    finish_small(s, plan, row)
    grad_kept()


def finish_small(s, plan, row):
    total = s.small_parts.at[plan.halvings - 1]
    outs = (
        (s.d_ln_gain, (G1, G2)),
        (s.d_ln_bias, (B1, B2)),
        (s.d_qv_bias, (QB, VB)),
        (s.d_proj_bias, (PB,)),
        (s.d_fc1_bias, tuple(range(F1B, F1B + FEEDS))),
        (s.d_fc2_bias, (F2B,)),
    )
    for layer in range(2):
        s.d_table[layer] = total[layer, VECTOR_ROWS:, :OFFSETS]
        for ref, indices in outs:
            whole = jnp.concatenate([total[layer, index : index + 1, :] for index in indices], axis=1)
            size = ref.shape[1]
            mine = jnp.zeros((1, size), F32)
            for share in range(plan.shares):
                mine = jnp.where(row == share, whole[:, share * size : (share + 1) * size], mine)
            ref[layer : layer + 1, :] = mine


def placements(cols):
    windows = cols // WIN
    patches = WIN * cols
    padded = -(-patches // LANES) * LANES
    plain = np.zeros((padded, windows * LANES), np.float32)
    moved = np.zeros((padded, windows * LANES), np.float32)
    for line in range(WIN):
        for col in range(cols):
            source = line * cols + col
            plain[source, (col // WIN) * LANES + line * WIN + col % WIN] = 1
            new_line, new_col = (line - SHIFT) % WIN, (col - SHIFT) % cols
            moved[source, (new_col // WIN) * LANES + new_line * WIN + new_col % WIN] = 1
    return plain.astype(BF), moved.astype(BF)


def swaps():
    on = np.zeros((2 * LANES, LANES), np.float32)
    back = np.zeros((2 * LANES, LANES), np.float32)
    for line in range(SHIFT):
        for col in range(WIN):
            moved, plain = line * WIN + col, (line + SHIFT) * WIN + (col + SHIFT) % WIN
            on[plain + (LANES if col >= SHIFT else 0), moved] = 1
            back[moved + (LANES if col < SHIFT else 0), plain] = 1
    return on.astype(BF), back.astype(BF)


def table_spread():
    size = 2 * WIN - 1
    spread = np.zeros((WIN, 2 * LANES, TABLE), np.float32)
    for key_col in range(WIN):
        for offset in range(size):
            for col in range(WIN):
                spread[key_col, offset * WIN + col, offset * size + col - key_col + WIN - 1] = 1
    spread = spread.reshape(WIN // 2, 2, 2 * LANES, TABLE).swapaxes(1, 2)
    return spread.reshape(WIN * LANES, 2 * TABLE).astype(BF)


def copy_all(*refs):
    count = len(refs) // 2
    copies = [
        pltpu.make_async_copy(source, target, refs[-1].at[number])
        for number, (source, target) in enumerate(zip(refs[:count], refs[count:-1]))
    ]
    for copy in copies:
        copy.start()
    for copy in copies:
        copy.wait()


def hand_out(values):
    anywhere = pl.BlockSpec(memory_space=pl.ANY)
    return pl.pallas_call(
        copy_all,
        out_shape=[jax.ShapeDtypeStruct(value.shape, value.dtype) for value in values],
        in_specs=[anywhere] * len(values),
        out_specs=[anywhere] * len(values),
        scratch_shapes=[pltpu.SemaphoreType.DMA((len(values),))],
        name="results",
    )(*values)


def per_device(
    page_tokens,
    blank_mask,
    cotangent,
    ln_gain,
    ln_bias,
    qv_bias,
    rel_table,
    w_qkv,
    w_proj,
    proj_bias,
    w_fc1,
    fc1_bias,
    w_fc2,
    fc2_bias,
):
    pages, shares = lax.axis_size(PAGE), lax.axis_size(ROW)
    plan = Plan(pages, shares)
    cols = page_tokens.shape[2]
    windows, lanes = cols // WIN, cols // WIN * LANES
    dense = ((WIN * cols * SPLITS, LANES), F32)
    half_dense = ((WIN * cols * SPLITS // 2, LANES), F32)
    plain, moved = (jnp.asarray(place) for place in placements(cols))
    live_rows = 8 * -(-windows // 8)
    scalar_inputs = dict(blank=blank_mask[0])
    small_inputs = dict(
        table=rel_table,
        ln_gain=ln_gain,
        ln_bias=ln_bias,
        qv_bias=qv_bias,
        proj_bias=proj_bias,
        fc1_bias=fc1_bias,
        fc2_bias=fc2_bias,
    )
    large_inputs = dict(
        in_tokens=page_tokens[0],
        in_grad=cotangent.reshape(dense[0]),
        in_plain=plain,
        in_moved=moved,
        in_swap_on=jnp.asarray(swaps()[0]),
        in_swap_back=jnp.asarray(swaps()[1]),
        in_spread=jnp.asarray(table_spread()),
        in_qkv=w_qkv,
        in_proj=w_proj,
        in_fc1=w_fc1,
        in_fc2=w_fc2,
    )
    saved = dict(
        x=((D, lanes), F32),
        normed=((D, lanes), BF),
        qkv=((3 * D, lanes), BF),
        soft=((windows * HEADS, LANES, LANES), BF),
        merged=((D, lanes), BF),
        hidden=((D, lanes), F32),
        second=((D, lanes), BF),
        active=((FF, lanes), BF),
        slope=((FF, lanes), BF),
    )
    units = ((UNITS, shares, CHUNK // shares, CHUNK), F32)
    large_outputs = dict(
        out_tokens=dense,
        grad_tokens=dense,
        sum_qkv=((2, D // shares, 3 * D), F32),
        sum_proj=((2, D // shares, D), F32),
        sum_fc1=((2, D // shares, FF), F32),
        sum_fc2=((2, FF // shares, D), F32),
        units_zero=units,
        units_one=units,
        kept_x=((D, lanes), F32),
        kept_normed=((D, lanes), BF),
        kept_qkv=((3 * D, lanes), BF),
        kept_soft=((windows * HEADS, LANES, LANES), BF),
        kept_merged=((D, lanes), BF),
        kept_hidden=((D, lanes), F32),
        kept_second=((D, lanes), BF),
        kept_active=((FF, lanes), BF),
        kept_slope=((FF, lanes), BF),
    )
    small_outputs = dict(
        d_ln_gain=((2, 2 * D // shares), F32),
        d_ln_bias=((2, 2 * D // shares), F32),
        d_qv_bias=((2, 2 * D // shares), F32),
        d_proj_bias=((2, D // shares), F32),
        d_fc1_bias=((2, FF // shares), F32),
        d_fc2_bias=((2, D // shares), F32),
        d_table=((2, HEADS, OFFSETS), F32),
    )
    small = (2, SMALL, D)
    vmem = dict(
        saved,
        tokens=((WIN, cols, D), BF),
        plain=(plain.shape, BF),
        moved=(moved.shape, BF),
        spread=((WIN * LANES, 2 * TABLE), BF),
        w_qkv=((D, 3 * D), BF),
        w_proj=((D, D), BF),
        w_fc1=((D, FF), BF),
        w_fc2=((FF, D), BF),
        page=((plain.shape[0], D), F32),
        dense=dense,
        upper=half_dense,
        swap_on=((2 * LANES, LANES), BF),
        swap_back=((2 * LANES, LANES), BF),
        grad_upper=half_dense,
        next_upper=half_dense,
        live_upper=((live_rows, LANES), F32),
        live_two=((live_rows, LANES), F32),
        work=((D, lanes), F32),
        grad=((D, lanes), F32),
        low=((D, lanes), BF),
        sums=((VECTORS, D, LANES), F32),
        gains=((2, D, LANES), F32),
        bias=((HEADS, LANES, LANES), F32),
        bias_rows=((HEADS * LANES, LANES), F32),
        regions=((2, LANES, LANES), F32),
        padded_table=((HEADS, TABLE), F32),
        live=((live_rows, LANES), F32),
        vector_rows=((VECTOR_ROWS, D), F32),
        staged=((2, CHUNK, CHUNK), F32),
        held=((HELD * CLASSES, shares, CHUNK // shares, CHUNK // 2), F32),
        small_own=(small, F32),
        small_parts=((plan.halvings,) + small, F32),
    )
    semaphores = dict(
        move_sems=pltpu.SemaphoreType.DMA((48,)),
        halo_sems=pltpu.SemaphoreType.DMA((2, 5)),
        send_sems=pltpu.SemaphoreType.DMA((2 * UNITS, plan.phases)),
        recv_sems=pltpu.SemaphoreType.DMA((2 * UNITS, plan.phases)),
        own_sems=pltpu.SemaphoreType.DMA((2 * UNITS, 2)),
        stage_sems=pltpu.SemaphoreType.DMA((2, shares)),
        small_sems=pltpu.SemaphoreType.DMA((2, plan.halvings)),
        free_sems=pltpu.SemaphoreType.REGULAR((CLASSES, plan.halvings)),
    )
    landing = [((RING,) + size, F32) for sizes in plan.sizes for size in sizes]
    layout = [*scalar_inputs, *small_inputs, *large_inputs, *small_outputs, *large_outputs, *vmem, *semaphores]
    in_vmem, anywhere = pl.BlockSpec(memory_space=pltpu.VMEM), pl.BlockSpec(memory_space=pl.ANY)
    outputs = {**small_outputs, **large_outputs}
    results = pl.pallas_call(
        functools.partial(run, plan, layout),
        out_shape=[jax.ShapeDtypeStruct(*shape) for shape in outputs.values()],
        in_specs=[pl.BlockSpec(memory_space=pltpu.SMEM)] + [in_vmem] * len(small_inputs) + [anywhere] * len(large_inputs),
        out_specs=[in_vmem] * len(small_outputs) + [anywhere] * len(large_outputs),
        scratch_shapes=[pltpu.VMEM(*shape) for shape in vmem.values()]
        + list(semaphores.values())
        + [pltpu.VMEM(*shape) for shape in landing],
        compiler_params=pltpu.CompilerParams(
            vmem_limit_bytes=VMEM_LIMIT, collective_id=0, has_side_effects=True
        ),
        name="two_layers",
    )(*scalar_inputs.values(), *small_inputs.values(), *large_inputs.values())
    results = hand_out(results[: len(small_outputs) + 6])
    d_ln_gain, d_ln_bias, d_qv_bias, d_proj_bias, d_fc1_bias, d_fc2_bias, d_table = results[: len(small_outputs)]
    out_tokens, grad_tokens, sum_qkv, sum_proj, sum_fc1, sum_fc2 = results[len(small_outputs) :]
    return (
        out_tokens.reshape(cotangent.shape),
        grad_tokens.reshape(cotangent.shape),
        d_ln_gain,
        d_ln_bias,
        d_qv_bias,
        d_table,
        sum_qkv,
        sum_proj,
        d_proj_bias,
        sum_fc1,
        d_fc1_bias,
        sum_fc2,
        d_fc2_bias,
    )


def solution(mesh):
    tokens, by_row, shares = P(PAGE, ROW, None, None), P(None, ROW), P(None, ROW, None)
    return jax.shard_map(
        per_device,
        mesh=mesh,
        in_specs=(tokens, P(PAGE, ROW, None), tokens) + (P(),) * 11,
        out_specs=(tokens, tokens)
        + (by_row, by_row, by_row, P(), shares, shares, by_row, shares, by_row, shares, by_row),
        check_vma=False,
    )
```

```python
import functools

import jax
import jax.numpy as jnp
import numpy as np
from jax import lax
from jax.experimental import pallas as pl
from jax.experimental.pallas import tpu as pltpu
from jax.sharding import PartitionSpec as P

WIN = 10
SHIFT = 5
AREA = WIN * WIN
LANES = 128
D = 512
HEADS = 16
HEAD_DIM = 32
FF = 2048
CHUNK = 512
FEEDS = FF // CHUNK
SPLITS = D // LANES
EPSILON = 1e-05
MASK_VALUE = -100.0
NEVER = -1e30
SCORE_SCALE = HEAD_DIM ** (-0.5)
VMEM_LIMIT = 63 * 1024 * 1024 + 512 * 1024
BF = jnp.bfloat16
F32 = jnp.float32
MESH = pl.DeviceIdType.MESH
PAGE, ROW = "page", "row"

G1, B1, G2, B2, QB, VB, PB, F2B, F1B, VECTORS = 0, 1, 2, 3, 4, 5, 6, 7, 8, 12
VECTOR_ROWS = 16
SMALL = VECTOR_ROWS + HEADS
OFFSETS = (2 * WIN - 1) ** 2
TABLE = 384

UNIT_FC1, UNIT_FC2, UNIT_PROJ, UNIT_QKV, UNITS = 0, 4, 8, 9, 12
CLASSES = 3
GROUPS = UNITS // CLASSES
TRIPLES = 2 * GROUPS
HELD = 4
DONE = 5
RING = 3
QKV, PROJ, FC1, FC2 = range(4)
TARGETS = (
    ((FC1, 0, 0), (FC1, 0, 1), (FC1, 0, 2)),
    ((FC1, 0, 3), (FC2, 0, 0), (FC2, 1, 0)),
    ((FC2, 2, 0), (FC2, 3, 0), (PROJ, 0, 0)),
    ((QKV, 0, 0), (QKV, 0, 1), (QKV, 0, 2)),
)


def mm(left, right, left_dim, right_dim):
    return lax.dot_general(
        left, right, (((left_dim,), (right_dim,)), ((), ())), preferred_element_type=F32
    )


def split(values):
    high = values.astype(BF)
    return high, (values - high.astype(F32)).astype(BF)


def lane_tile(index):
    return pl.ds(pl.multiple_of(index * LANES, LANES), LANES)


def chunk_of(index):
    return pl.ds(pl.multiple_of(index * CHUNK, CHUNK), CHUNK)


def wide(column, count):
    return jnp.concatenate([column] * count, axis=1)


def fold(values):
    total = values[:, :LANES]
    for start in range(LANES, values.shape[1], LANES):
        total = total + values[:, start : start + LANES]
    return total


def norm_parts(values):
    center = values - jnp.sum(values, axis=0, keepdims=True) * (1.0 / D)
    spread = jnp.sum(center * center, axis=0, keepdims=True) * (1.0 / D)
    scale = lax.rsqrt(spread + EPSILON)
    return center * scale, scale


def norm_pull(grad, gain, hat, scale):
    scaled = grad * gain
    mean_one = jnp.sum(scaled, axis=0, keepdims=True) * (1.0 / D)
    mean_two = jnp.sum(scaled * hat, axis=0, keepdims=True) * (1.0 / D)
    return scale * (scaled - mean_one - hat * mean_two)


def gelu_parts(inner):
    step = 1.0 / (1.0 + (0.3275911 * 0.7071067811865476) * jnp.abs(inner))
    bell = jnp.exp(inner * inner * -0.5)
    poly = 0.5 * 1.061405429
    for factor in (-1.453152027, 1.421413741, -0.284496736, 0.254829592):
        poly = poly * step + 0.5 * factor
    tail = poly * step * bell
    below = jnp.where(inner >= 0, 1.0 - tail, tail)
    return inner * below, below + inner * bell * 0.3989422804014327


def to_channels(page_ref, place_ref, out_ref, exact=False):
    def step(index, carry):
        channels = pl.ds(pl.multiple_of(index * 256, 256), 256)
        values = page_ref[:, channels]
        if exact:
            out_ref[channels, :] = mm(values.astype(BF), place_ref[...], 0, 0)
        else:
            high, low = split(values)
            out_ref[channels, :] = mm(high, place_ref[...], 0, 0) + mm(low, place_ref[...], 0, 0)
        return carry

    lax.fori_loop(0, D // 256, step, 0)


def to_dense(values_ref, place_ref, dense_ref, padded):
    count = dense_ref.shape[0] // SPLITS
    for index in range(D // 256):
        high, low = split(values_ref[index * 256 : (index + 1) * 256, :])
        page = mm(place_ref[:padded, :], high, 1, 1) + mm(place_ref[:padded, :], low, 1, 1)
        for part in range(2):
            rows = pl.ds(2 * index + part, count, stride=SPLITS)
            dense_ref[rows, :] = page[:count, part * LANES : (part + 1) * LANES]


def from_dense(dense_ref, page_ref, row):
    count = dense_ref.shape[0] // SPLITS
    for part in range(SPLITS):
        rows = pl.ds(part, count, stride=SPLITS)
        page_ref[pl.ds(row, count), part * LANES : (part + 1) * LANES] = dense_ref[rows, :]


def add_halo(page_ref, place_ref, out_ref, count, padded):
    page_ref[pl.ds(count, padded - count), :] = jnp.zeros((padded - count, D), F32)

    def step(index, carry):
        channels = pl.ds(pl.multiple_of(index * 256, 256), 256)
        high, low = split(page_ref[:padded, channels])
        out_ref[channels, :] += mm(high, place_ref[:padded, :], 0, 0) + mm(low, place_ref[:padded, :], 0, 0)
        return carry

    lax.fori_loop(0, D // 256, step, 0)


def move_own(values_ref, swap_ref, out_ref, windows, first):
    for window in range(windows):
        sources = [(window + first + part) % windows * LANES for part in range(2)]
        values = jnp.concatenate([values_ref[:, start : start + LANES] for start in sources], axis=1)
        high, low = split(values)
        target = slice(window * LANES, (window + 1) * LANES)
        out_ref[:, target] = mm(high, swap_ref[...], 1, 0) + mm(low, swap_ref[...], 1, 0)


def vector_rows(s, layer):
    rows = s.vector_rows
    sources = ((G1, s.ln_gain, 0), (B1, s.ln_bias, 0), (G2, s.ln_gain, 1), (B2, s.ln_bias, 1))
    sources += ((QB, s.qv_bias, 0), (VB, s.qv_bias, 1), (PB, s.proj_bias, 0), (F2B, s.fc2_bias, 0))
    sources += tuple((F1B + part, s.fc1_bias, part) for part in range(FEEDS))
    for index, source, part in sources:
        rows[index : index + 1, :] = source[layer : layer + 1, part * D : (part + 1) * D]
    rows[VECTORS:, :] = jnp.zeros((VECTOR_ROWS - VECTORS, D), F32)
    return rows[...].T


def spread_columns(s, layer):
    columns = vector_rows(s, layer)
    for index in range(VECTORS):
        s.sums[index] = jnp.broadcast_to(columns[:, index : index + 1], (D, LANES))


def spread_gains(s, layer):
    columns = vector_rows(s, layer)
    for index, vector in enumerate((G1, G2)):
        s.gains[index] = jnp.broadcast_to(columns[:, vector : vector + 1], (D, LANES))


def spread_part(col):
    rows, lanes = (col // 2) * 2 * LANES, (col % 2) * TABLE
    return slice(rows, rows + 2 * LANES), slice(lanes, lanes + TABLE)


def spread_bias(s, layer):
    spread_ref, rows_ref, bias_ref = s.spread, s.bias_rows, s.bias
    s.padded_table[...] = jnp.zeros(s.padded_table.shape, F32)
    s.padded_table[:, :OFFSETS] = s.table[layer]
    high, low = split(s.padded_table[...])
    parts = []
    for col in range(WIN):
        chosen = spread_ref[spread_part(col)]
        parts.append(mm(high, chosen, 1, 1) + mm(low, chosen, 1, 1))
    source = jnp.concatenate(parts, axis=0)
    rows_ref[...] = jnp.zeros(rows_ref.shape, F32)
    for row in range(WIN):
        shift = (WIN - 1 - row) * WIN
        moved = source if shift == 0 else pltpu.roll(source, 2 * LANES - shift, axis=1)
        rows_ref[pl.ds(row * WIN * HEADS, WIN * HEADS), :] = moved[:, :LANES]
    for head in range(HEADS):
        bias_ref[head] = rows_ref[pl.ds(head, LANES, stride=HEADS), :]


def gather_bias(grad_ref, spread_ref, rows_ref):
    for head in range(HEADS):
        rows_ref[pl.ds(head, LANES, stride=HEADS), :] = grad_ref[head]
    total = jnp.zeros((WIN * HEADS, 2 * LANES), F32)
    for row in range(WIN):
        shift = (WIN - 1 - row) * WIN
        piece = rows_ref[pl.ds(row * WIN * HEADS, WIN * HEADS), :]
        piece = jnp.concatenate([piece, jnp.zeros_like(piece)], axis=1)
        total = total + (piece if shift == 0 else pltpu.roll(piece, shift, axis=1))
    table = jnp.zeros((HEADS, TABLE), F32)
    for col in range(WIN):
        for part in split(total[col * HEADS : (col + 1) * HEADS]):
            table = table + mm(part, spread_ref[spread_part(col)], 1, 0)
    return table


def region_masks(shifted_layer, out_ref):
    key = lax.broadcasted_iota(jnp.int32, (LANES, LANES), 0)
    query = lax.broadcasted_iota(jnp.int32, (LANES, LANES), 1)
    padding = jnp.where(key < AREA, 0.0, NEVER)
    out_ref[0] = padding
    out_ref[1] = padding
    if shifted_layer:
        last = lax.axis_index(ROW) == lax.axis_size(ROW) - 1
        rows_differ = ((key >= AREA // 2) != (query >= AREA // 2)) & last
        cols_differ = (key % WIN >= SHIFT) != (query % WIN >= SHIFT)
        out_ref[0] += jnp.where(rows_differ, MASK_VALUE, 0.0)
        out_ref[1] += jnp.where(rows_differ | cols_differ, MASK_VALUE, 0.0)


def shifted_live(s, windows):
    place = lax.broadcasted_iota(jnp.int32, (1, LANES), 1)
    for window in range(windows):
        here, after = slice(window, window + 1), slice((window + 1) % windows, (window + 1) % windows + 1)
        beyond = place % WIN >= SHIFT
        own = jnp.where(beyond, s.live[after, :], s.live[here, :])
        upper = jnp.where(beyond, s.live_upper[after, :], s.live_upper[here, :])
        s.live_two[here, :] = jnp.where(place >= AREA // 2, upper, own)


def head_rows(head, base=0):
    return pl.ds(base + head * HEAD_DIM, HEAD_DIM)


def norm_one_forward(s, windows):
    def step(index, carry):
        lanes = lane_tile(index)
        hat, _ = norm_parts(s.x[:, lanes])
        s.normed[:, lanes] = (hat * s.sums[G1] + s.sums[B1]).astype(BF)
        return carry

    lax.fori_loop(0, windows, step, 0)


def project_forward(s, windows):
    def step(index, carry):
        rows = chunk_of(index)
        bias = s.sums[jnp.where(index == 0, QB, VB)] * jnp.where(index == 1, 0.0, 1.0)
        out = mm(s.w_qkv[:, rows], s.normed[...], 0, 0)
        s.qkv[rows, :] = (out + wide(bias, windows)).astype(BF)
        return carry

    lax.fori_loop(0, 3, step, 0)


def attend_forward(s, windows, live_ref):
    def step(index, carry):
        lanes = lane_tile(index)
        live = jnp.broadcast_to(live_ref[pl.ds(index, 1), :], (LANES, LANES)).T
        masked = s.regions[jnp.where(index == windows - 1, 1, 0)] + MASK_VALUE * (1.0 - live)
        for head in range(HEADS):
            query = s.qkv[head_rows(head), lanes]
            key = s.qkv[head_rows(head, D), lanes]
            value = s.qkv[head_rows(head, 2 * D), lanes]
            scores = mm(key, query, 0, 0) * SCORE_SCALE + (s.bias[head] + masked)
            exponent = jnp.exp(scores - jnp.max(scores, axis=0, keepdims=True))
            total = jnp.sum(exponent, axis=0, keepdims=True)
            soft = (exponent * (1.0 / total)).astype(BF)
            s.soft[index * HEADS + head] = soft
            s.merged[head_rows(head), lanes] = mm(value, soft, 1, 0).astype(BF)
        return carry

    lax.fori_loop(0, windows, step, 0)


def norm_two_forward(s, windows, live_ref):
    def step(index, carry):
        lanes = lane_tile(index)
        hidden = s.x[:, lanes] + live_ref[pl.ds(index, 1), :] * (s.work[:, lanes] + s.sums[PB])
        s.hidden[:, lanes] = hidden
        s.work[:, lanes] = hidden + s.sums[F2B]
        hat, _ = norm_parts(hidden)
        s.second[:, lanes] = (hat * s.sums[G2] + s.sums[B2]).astype(BF)
        return carry

    lax.fori_loop(0, windows, step, 0)


def feed_forward(s, windows):
    def step(index, carry):
        rows = chunk_of(index)
        inner = mm(s.w_fc1[:, rows], s.second[...], 0, 0) + wide(s.sums[F1B + index], windows)
        active, slope = gelu_parts(inner)
        active = active.astype(BF)
        s.active[rows, :] = active
        s.slope[rows, :] = slope.astype(BF)
        s.work[...] += mm(s.w_fc2[rows, :], active, 0, 0)
        return carry

    lax.fori_loop(0, FEEDS, step, 0)


def feed_backward(s, sink, times):
    s.sums[...] = jnp.zeros(s.sums.shape, F32)
    s.bias[...] = jnp.zeros(s.bias.shape, F32)
    lowered = s.grad[...].astype(BF)
    s.low[...] = lowered
    s.sums[F2B] = fold(lowered.astype(F32))
    s.work[...] = jnp.zeros(s.work.shape, F32)

    def step(index, carry):
        rows = chunk_of(index)
        sink.put(0, mm(s.active[rows, :], s.low[...], 1, 1), feed_pieces(index, sink.shares), index == 0)
        grad_inner = mm(s.w_fc2[rows, :], s.low[...], 1, 0) * s.slope[rows, :].astype(F32)
        grad_inner = grad_inner.astype(BF)
        s.sums[F1B + index] = fold(grad_inner.astype(F32))
        sink.put(1, mm(s.second[...], grad_inner, 1, 1), row_pieces(UNIT_FC1 + index, sink.shares), index == 0)
        s.work[...] += mm(s.w_fc1[:, rows], grad_inner, 1, 0)
        sink.advance_at(index, times)
        return carry

    lax.fori_loop(0, FEEDS, step, 0)
    sink.settle(0)
    sink.settle(1)


def norm_two_backward(s, windows, live_ref):
    def step(index, carry):
        lanes = lane_tile(index)
        hat, scale = norm_parts(s.hidden[:, lanes])
        grad = s.work[:, lanes]
        s.sums[G2] += grad * hat
        s.sums[B2] += grad
        grad = s.grad[:, lanes] + norm_pull(grad, s.gains[1], hat, scale)
        s.grad[:, lanes] = grad
        grad_low = (grad * live_ref[pl.ds(index, 1), :]).astype(BF)
        s.low[:, lanes] = grad_low
        s.sums[PB] += grad_low.astype(F32)
        return carry

    lax.fori_loop(0, windows, step, 0)


def merge_backward(s, sink):
    sink.put(0, mm(s.merged[...], s.low[...], 1, 1), row_pieces(UNIT_PROJ, sink.shares), True)
    s.merged[...] = mm(s.w_proj[...], s.low[...], 1, 0).astype(BF)
    sink.settle(0)


def attend_backward(s, windows, sink, times):
    def step(index, carry):
        lanes = lane_tile(index)
        for head in range(HEADS):
            query = s.qkv[head_rows(head), lanes]
            key = s.qkv[head_rows(head, D), lanes]
            value = s.qkv[head_rows(head, 2 * D), lanes]
            grad_out = s.merged[head_rows(head), lanes]
            soft_low = s.soft[index * HEADS + head]
            soft = soft_low.astype(F32)
            grad_soft = mm(value, grad_out, 0, 0)
            inner = jnp.sum(soft * grad_soft, axis=0, keepdims=True)
            grad_scores = (soft * (grad_soft - inner)).astype(BF)
            s.bias[head] += grad_scores.astype(F32)
            grad_query = (mm(key, grad_scores, 1, 0) * SCORE_SCALE).astype(BF)
            grad_key = (mm(query, grad_scores, 1, 1) * SCORE_SCALE).astype(BF)
            grad_value = mm(grad_out, soft_low, 1, 1).astype(BF)
            s.qkv[head_rows(head), lanes] = grad_query
            s.qkv[head_rows(head, D), lanes] = grad_key
            s.qkv[head_rows(head, 2 * D), lanes] = grad_value
            s.sums[QB, head_rows(head), :] += grad_query.astype(F32)
            s.sums[VB, head_rows(head), :] += grad_value.astype(F32)
        sink.advance_at(index, times)
        return carry

    lax.fori_loop(0, windows, step, 0)


def project_backward(s, sink):
    def step(index, carry):
        rows = chunk_of(index)
        sink.put(1, mm(s.normed[...], s.qkv[rows, :], 1, 1), row_pieces(UNIT_QKV + index, sink.shares), index == 0)
        return carry

    lax.fori_loop(0, 3, step, 0)


def input_backward(s):
    s.work[...] = mm(s.w_qkv[...], s.qkv[...], 1, 0)


def norm_one_backward(s, windows):
    def step(index, carry):
        lanes = lane_tile(index)
        hat, scale = norm_parts(s.x[:, lanes])
        grad = s.work[:, lanes]
        s.sums[G1] += grad * hat
        s.sums[B1] += grad
        s.grad[:, lanes] += norm_pull(grad, s.gains[0], hat, scale)
        return carry

    lax.fori_loop(0, windows, step, 0)


def small_gradients(s, small_ref):
    places = lax.broadcasted_iota(jnp.int32, (D, LANES), 1)
    packed = jnp.zeros((D, LANES), F32)
    for index in range(VECTORS):
        packed = jnp.where(places == index, jnp.sum(s.sums[index], axis=1, keepdims=True), packed)
    small_ref[:VECTOR_ROWS, :] = packed.T[:VECTOR_ROWS]
    table = gather_bias(s.bias, s.spread, s.bias_rows)
    small_ref[VECTOR_ROWS:, :] = jnp.concatenate([table, jnp.zeros((HEADS, D - TABLE), F32)], axis=1)


def reversed_bits(value, count):
    turned = 0
    for bit in range(count):
        turned = turned * 2 + (value // 2**bit) % 2
    return turned


def row_pieces(unit, shares):
    rows, count = CHUNK // shares, shares.bit_length() - 1
    return [(share * rows, unit, reversed_bits(share, count)) for share in range(shares)]


def feed_pieces(index, shares):
    rows, count = CHUNK // shares, shares.bit_length() - 1
    pieces = []
    for share in range(shares // FEEDS):
        place = reversed_bits(index * (shares // FEEDS) + share, count)
        for part in range(FEEDS):
            pieces.append(((share * FEEDS + part) * rows, UNIT_FC2 + part, place))
    return pieces


class Plan:
    def __init__(self, pages, shares):
        self.shares, self.rows = shares, CHUNK // shares
        page_bits, row_bits = pages.bit_length() - 1, shares.bit_length() - 1
        others = page_bits - 1
        self.steps = []
        for kind in range(CLASSES):
            turn = kind % 2
            page = [(PAGE, 2 ** (1 + (bit + turn) % others)) for bit in range(others)]
            row = [(ROW, 2**bit) for bit in range(row_bits)]
            self.steps.append([(PAGE, 1)] + (row + page if kind == 2 else page + row))
        self.page_steps = [[0] + [at for at, step in enumerate(steps) if at and step[0] == PAGE] for steps in self.steps]
        self.halvings = page_bits + row_bits
        self.phases = self.halvings + page_bits
        self.sizes = []
        for kind in range(CLASSES):
            size = [shares, self.rows, CHUNK // 2]
            sizes = [tuple(size)]
            for level in range(1, self.halvings):
                size[self.split_axis(kind, level)] //= 2
                sizes.append(tuple(size))
            self.sizes.append(sizes)
        self.steps_at = self.schedule()

    def schedule(self):
        small = TRIPLES
        free, ready, stage_of, plan, now = {}, {}, {}, [], 0.0
        for triple in range(TRIPLES):
            for kind in range(CLASSES):
                stage_of[triple, kind] = 0
        stage_of[small, 0] = 0

        def link(key, phase):
            triple, kind = key
            if phase < self.halvings:
                axis, stride = self.steps[kind][phase]
                size = 2.0**-phase / 2 if triple != small else 0.125
            else:
                axis, stride = self.steps[kind][self.page_steps[kind][self.phases - 1 - phase]]
                size = 2.0 ** (phase - 2 * self.halvings)
            if axis == PAGE and stride == 1:
                return 0, size * PLAN_CORE
            return (axis, stride if axis == PAGE else 0), size * PLAN_LINK * (1.0 if stride == 1 or axis == PAGE else 1.5)

        def last_stage(key):
            return self.halvings if key[0] == small else self.phases + 1

        def allowed(key, point):
            triple, kind = key
            stage = stage_of[key]
            if stage > last_stage(key):
                return False
            if triple == small:
                return point >= len(PLAN_POINTS) - 1
            if stage == 0 and point < PLAN_THERE[triple]:
                return False
            if triple > 0 and stage_of[triple - 1, kind] <= stage:
                return False
            if triple >= RING and stage < self.halvings and stage_of[triple - RING, kind] <= stage + 1:
                return False
            if stage == 0 and triple >= DONE and stage_of[triple - DONE, kind] <= self.phases + 1:
                return False
            return not (stage == 0 and triple >= HELD and stage_of[triple - HELD, kind] <= self.halvings + 1)

        for point, work in enumerate(PLAN_POINTS):
            now += work
            if point == PLAN_HALO:
                free[ROW, 0] = max(now, free.get((ROW, 0), 0.0)) + PLAN_HALO_TIME
            steps, final = [], point == len(PLAN_POINTS) - 1
            while True:
                keys = [key for key in stage_of if allowed(key, point)]
                keys = [key for key in keys if final or ready.get(key, 0.0) <= now + PLAN_SLACK]
                if not keys:
                    break
                key = min(keys, key=lambda key: (max(ready.get(key, 0.0), now), -stage_of[key], key))
                stage = stage_of[key]
                now = max(now, ready.get(key, 0.0)) + (PLAN_ADD * 2.0**-stage if stage else 0.0)
                if stage == self.phases:
                    ready[key] = now + PLAN_LATENCY
                elif stage < last_stage(key):
                    name, length = link(key, stage)
                    free[name] = max(now, free.get(name, 0.0)) + length
                    ready[key] = free[name] + PLAN_LATENCY
                steps.append((*key, stage))
                stage_of[key] += 1
            plan.append(steps)
        assert all(stage_of[key] > last_stage(key) for key in stage_of)
        return plan

    def split_axis(self, kind, level):
        if self.steps[kind][level][0] == ROW:
            return 0
        return 2 if self.page_steps[kind].index(level) < 2 else 1

    def partner(self, kind, level):
        axis, stride = self.steps[kind][level]
        page, row = lax.axis_index(PAGE), lax.axis_index(ROW)
        mine = page if axis == PAGE else row
        bit = (mine // stride) % 2
        other = mine + (1 - 2 * bit) * stride
        return bit, ((other, row) if axis == PAGE else (page, other))

    def part(self, kind, level, sent=False):
        starts, sizes = [0, 0, 0], [self.shares, self.rows, CHUNK // 2]
        for at in range(1, level + 1):
            axis = self.split_axis(kind, at)
            sizes[axis] //= 2
            bit, _ = self.partner(kind, at)
            which = 1 - bit if sent and at == level else bit
            starts[axis] = starts[axis] + which * sizes[axis]
        return (
            pl.ds(starts[0], sizes[0]),
            pl.ds(pl.multiple_of(starts[1], 8), sizes[1]),
            pl.ds(pl.multiple_of(starts[2], LANES), sizes[2]),
        )

    def place(self, kind, count):
        starts, sizes = [0, 0], [self.rows, CHUNK]
        for at in self.page_steps[kind][:count]:
            axis = self.split_axis(kind, at) - 1 if at else 1
            sizes[axis] //= 2
            bit, _ = self.partner(kind, at)
            starts[axis] = starts[axis] + bit * sizes[axis]
        return starts, sizes


class Reducer:
    def __init__(self, plan, s):
        self.plan, self.s = plan, s
        self.shares = plan.shares
        self.layer = 1

    def stage_copies(self, slot, pieces):
        return [
            pltpu.make_async_copy(
                self.s.staged.at[pl.ds(slot * CHUNK + start, self.plan.rows)],
                self.s.units[self.layer].at[unit, place],
                self.s.stage_sems.at[slot, number],
            )
            for number, (start, unit, place) in enumerate(pieces)
        ]

    def put(self, slot, grad, pieces, first):
        if first is not True:

            @pl.when(jnp.logical_not(first))
            def _():
                self.settle(slot)

        self.s.staged[pl.ds(slot * CHUNK, CHUNK), :] = grad
        for copy in self.stage_copies(slot, pieces):
            copy.start()

    def settle(self, slot):
        for copy in self.stage_copies(slot, row_pieces(0, self.shares)):
            copy.wait()

    def remote(self, source, target, unit, phase, device):
        return pltpu.make_async_remote_copy(
            src_ref=source,
            dst_ref=target,
            send_sem=self.s.send_sems.at[unit, phase],
            recv_sem=self.s.recv_sems.at[unit, phase],
            device_id=device,
            device_id_type=MESH,
        )

    def unit_half(self, triple, kind, which):
        layer, half = 1 - triple // GROUPS, CHUNK // 2
        unit = CLASSES * (triple % GROUPS) + kind
        return self.s.units[layer].at[unit, :, :, pl.ds(pl.multiple_of(which * half, half), half)]

    def held(self, triple, kind):
        return self.s.held.at[CLASSES * (triple % HELD) + kind]

    def halving(self, triple, kind, level):
        plan = self.plan
        bit, device = plan.partner(kind, level)
        target = self.s.landing[kind][level].at[triple % RING]
        if level == 0:
            source = self.unit_half(triple, kind, 1 - bit)
        else:
            source = self.held(triple, kind).at[plan.part(kind, level, True)]
        return self.remote(source, target, CLASSES * triple + kind, level, device)

    def own_half(self, triple, kind):
        bit, _ = self.plan.partner(kind, 0)
        sem = self.s.own_sems.at[CLASSES * triple + kind, 0]
        return pltpu.make_async_copy(self.unit_half(triple, kind, bit), self.held(triple, kind), sem)

    def finished(self, triple, kind):
        return self.held(triple, kind).at[self.plan.part(kind, self.plan.halvings - 1)].at[0]

    def done(self, triple, kind, count):
        starts, sizes = self.plan.place(kind, count)
        return self.s.done.at[
            CLASSES * (triple % DONE) + kind,
            pl.ds(pl.multiple_of(starts[0], 8), sizes[0]),
            pl.ds(pl.multiple_of(starts[1], LANES), sizes[1]),
        ]

    def gathering(self, triple, kind, phase):
        plan = self.plan
        count = len(plan.page_steps[kind]) - (phase - plan.halvings)
        part = self.done(triple, kind, count)
        _, device = plan.partner(kind, plan.page_steps[kind][count - 1])
        return self.remote(part, part, CLASSES * triple + kind, phase, device)

    def result(self, triple, kind):
        which, row_block, col_block = TARGETS[triple % GROUPS][kind]
        rows = self.plan.rows
        target = self.s.results[which].at[
            1 - triple // GROUPS, pl.ds(row_block * rows, rows), pl.ds(col_block * CHUNK, CHUNK)
        ]
        sem = self.s.own_sems.at[CLASSES * triple + kind, 1]
        return pltpu.make_async_copy(self.done(triple, kind, 0), target, sem)

    def start(self, triple, kind, phase):
        plan = self.plan
        if phase < plan.halvings:
            if triple >= RING:
                pl.semaphore_wait(self.s.free_sems.at[kind, phase], 1)
            self.halving(triple, kind, phase).start()
            if phase == 0:
                self.own_half(triple, kind).start()
        elif phase < plan.phases:
            if phase == plan.halvings:
                self.done(triple, kind, len(plan.page_steps[kind]))[...] = self.finished(triple, kind)[...]
            self.gathering(triple, kind, phase).start()
        elif phase == plan.phases:
            self.result(triple, kind).start()

    def finish(self, triple, kind, phase):
        plan, s = self.plan, self.s
        if phase < plan.halvings:
            self.halving(triple, kind, phase).wait()
            if phase == 0:
                self.own_half(triple, kind).wait()
            landed = s.landing[kind][phase].at[triple % RING]
            kept = self.held(triple, kind).at[plan.part(kind, phase)]
            for share in range(landed.shape[0]):
                kept[share] += landed[share]
            if triple < TRIPLES - RING:
                _, device = plan.partner(kind, phase)
                pl.semaphore_signal(s.free_sems.at[kind, phase], inc=1, device_id=device, device_id_type=MESH)
        elif phase < plan.phases:
            self.gathering(triple, kind, phase).wait()
        else:
            self.result(triple, kind).wait()

    def advance(self, point):
        for triple, kind, stage in self.plan.steps_at[point]:
            if triple == TRIPLES:
                self.small_step(stage - 1)
                continue
            if stage > 0:
                self.finish(triple, kind, stage - 1)
            self.start(triple, kind, stage)

    def advance_at(self, index, points):
        for number, point in enumerate(points):
            if self.plan.steps_at[point]:

                @pl.when(index == number)
                def _(point=point):
                    self.advance(point)

    def small_copy(self, phase):
        s = self.s
        _, device = self.plan.partner(0, phase)
        return pltpu.make_async_remote_copy(
            src_ref=s.small_own if phase == 0 else s.small_parts.at[phase - 1],
            dst_ref=s.small_parts.at[phase],
            send_sem=s.small_sems.at[0, phase],
            recv_sem=s.small_sems.at[1, phase],
            device_id=device,
            device_id_type=MESH,
        )

    def small_step(self, phase):
        s = self.s
        if phase >= 0:
            self.small_copy(phase).wait()
            s.small_parts[phase] += s.small_own[...] if phase == 0 else s.small_parts[phase - 1]
        if phase + 1 < self.plan.halvings:
            self.small_copy(phase + 1).start()


PLAN_POINTS = (0, 2, 3) + (2.7,) * 6 + (5.2, 3, 3, 6) + (3.2,) * 4 + (0.3, 2, 3) + (2.7,) * 6 + (3, 3, 3, 3)
PLAN_THERE = (0, 0, 2, 10, 17, 17, 19, 26)
PLAN_HALO, PLAN_HALO_TIME = 9, 12.3
PLAN_CORE, PLAN_LINK, PLAN_LATENCY, PLAN_ADD, PLAN_SLACK = 1.7, 20.0, 2.0, 0.9, 0.0


class Moves:
    def __init__(self, sems):
        self.sems, self.used = sems, 0

    def __call__(self, source, target):
        number, self.used = self.used, self.used + 1
        make = functools.partial(pltpu.make_async_copy, source, target, self.sems.at[number])
        make().start()
        return lambda: make().wait()


class Refs:
    pass


def run(plan, layout, *refs):
    s = Refs()
    for name, ref in zip(layout, refs):
        setattr(s, name, ref)
    rest = list(refs[len(layout) :])
    s.landing = [[rest.pop(0) for _ in range(plan.halvings)] for _ in range(CLASSES)]
    s.results = (s.sum_qkv, s.sum_proj, s.sum_fc1, s.sum_fc2)
    s.units = (s.units_zero, s.units_one)
    s.page = s.staged.at[pl.ds(0, s.plain.shape[0])]
    s.spread = s.qkv.at[pl.ds(0, s.in_spread.shape[0])]
    windows = s.x.shape[1] // LANES
    patches = s.dense.shape[0] // SPLITS
    half, half_rows = patches // 2, s.dense.shape[0] // 2
    padded = 16 * -(-half // 16)
    upper, lower = pl.ds(0, half_rows), pl.ds(half_rows, half_rows)
    reducer = Reducer(plan, s)
    move = Moves(s.move_sems)
    page, row = lax.axis_index(PAGE), lax.axis_index(ROW)
    count = lax.axis_size(ROW)
    above, below = (page, (row + count - 1) % count), (page, (row + 1) % count)

    def halo(number, source, target, device):
        make = functools.partial(
            pltpu.make_async_remote_copy,
            src_ref=source,
            dst_ref=target,
            send_sem=s.halo_sems.at[0, number],
            recv_sem=s.halo_sems.at[1, number],
            device_id=device,
            device_id_type=MESH,
        )
        make().start()
        return lambda: make().wait()

    tokens_there = move(s.in_tokens, s.tokens)
    places_there = (move(s.in_plain, s.plain), move(s.in_moved, s.moved))
    swaps_there = (move(s.in_swap_on, s.swap_on), move(s.in_swap_back, s.swap_back))
    spread_there = move(s.in_spread, s.spread)
    weights = ((s.in_qkv, s.w_qkv), (s.in_proj, s.w_proj), (s.in_fc1, s.w_fc1), (s.in_fc2, s.w_fc2))

    def fetch_weight(which, layer):
        source, target = weights[which]
        return move(source.at[layer], target)

    there = [fetch_weight(which, 0) for which in range(4)]

    barrier = pltpu.get_barrier_semaphore()
    devices = [plan.partner(0, level)[1] for level in range(plan.halvings)] + [above, below]
    for device in devices:
        pl.semaphore_signal(barrier, inc=1, device_id=device, device_id_type=MESH)
    pl.semaphore_wait(barrier, len(devices))

    s.live[...] = jnp.zeros(s.live.shape, F32)
    for window in range(windows):
        s.live[window : window + 1, :] = jnp.full((1, LANES), 1.0 - s.blank[0, window].astype(F32))
    live_there = halo(0, s.live, s.live_upper, above)
    grad_there = halo(1, s.in_grad.at[upper], s.grad_upper, above)
    grad_lower_there = move(s.in_grad.at[lower], s.dense.at[lower])
    s.page[...] = jnp.zeros(s.page.shape, F32)
    tokens_there()
    cols = s.tokens.shape[1]
    for line in range(WIN):
        s.page[pl.ds(line * cols, cols), :] = s.tokens[line].astype(F32)
    places_there[0]()
    to_channels(s.page, s.plain, s.x, True)
    saves = [move(s.x, s.kept_x)]
    spread_columns(s, 0)
    spread_there()
    spread_bias(s, 0)
    region_masks(False, s.regions)
    norm_one_forward(s, windows)
    saves.append(move(s.normed, s.kept_normed))
    there[QKV]()
    project_forward(s, windows)
    qkv_saved = move(s.qkv, s.kept_qkv)
    there[QKV] = fetch_weight(QKV, 1)
    attend_forward(s, windows, s.live)
    saves.append(move(s.soft, s.kept_soft))
    saves.append(move(s.merged, s.kept_merged))
    there[PROJ]()
    s.work[...] = mm(s.w_proj[...], s.merged[...], 0, 0)
    there[PROJ] = fetch_weight(PROJ, 1)
    norm_two_forward(s, windows, s.live)
    saves.append(move(s.hidden, s.kept_hidden))
    saves.append(move(s.second, s.kept_second))
    there[FC1]()
    there[FC2]()
    feed_forward(s, windows)
    saves.append(move(s.active, s.kept_active))
    saves.append(move(s.slope, s.kept_slope))
    there[FC1] = fetch_weight(FC1, 1)
    there[FC2] = fetch_weight(FC2, 1)
    to_dense(s.work, s.plain, s.dense.at[upper], padded)
    upper_there = halo(2, s.dense.at[upper], s.upper, above)

    qkv_saved()
    spread_there = move(s.in_spread, s.spread)
    places_there[1]()
    swaps_there[0]()
    saves.pop(0)()
    move_own(s.work, s.swap_on, s.x, windows, 0)
    spread_columns(s, 1)
    spread_there()
    spread_bias(s, 1)
    region_masks(True, s.regions)
    live_there()
    shifted_live(s, windows)
    grad_there()
    grad_lower_there()
    from_dense(s.grad_upper, s.page, 0)
    from_dense(s.dense.at[lower], s.page, half)
    to_channels(s.page, s.moved, s.grad)
    for saved in saves:
        saved()
    upper_there()
    from_dense(s.upper, s.page, 0)
    add_halo(s.page, s.moved, s.x, half, padded)
    norm_one_forward(s, windows)
    there[QKV]()
    project_forward(s, windows)
    attend_forward(s, windows, s.live_two)
    there[PROJ]()
    s.work[...] = mm(s.w_proj[...], s.merged[...], 0, 0)
    norm_two_forward(s, windows, s.live_two)
    there[FC1]()
    there[FC2]()
    feed_forward(s, windows)
    to_dense(s.work, s.moved, s.dense, s.moved.shape[0])
    out_there = halo(3, s.dense.at[upper], s.out_tokens.at[upper], below)
    out_kept = move(s.dense.at[lower], s.out_tokens.at[lower])

    spread_gains(s, 1)

    def backward(layer, live_ref, fetch, points):
        reducer.layer = layer
        first = 0 if layer else FEEDS
        feed_backward(s, reducer, points[:first])
        reducer.advance(points[first])
        fetch(0)
        norm_two_backward(s, windows, live_ref)
        reducer.advance(points[first + 1])
        fetch(1)
        merge_backward(s, reducer)
        reducer.advance(points[first + 2])
        fetch(2)
        attend_backward(s, windows, reducer, points[first + 3 :])
        fetch(3)

    back = {}

    def refill(point):
        if point == 0:
            back[0] = [move(s.kept_active, s.active), move(s.kept_slope, s.slope), move(s.kept_second, s.second)]
            back[0] += [fetch_weight(FC1, 0), fetch_weight(FC2, 0)]
        elif point == 1:
            back[1] = [move(s.kept_hidden, s.hidden)]
        elif point == 2:
            back[2] = [fetch_weight(PROJ, 0)]
        elif point == 3:
            back[2] += [move(s.kept_merged, s.merged)]
            back[3] = [move(s.kept_soft, s.soft)]
        elif point == 4:
            back[4] = [move(s.kept_x, s.x)]
        else:
            back[3] += [move(s.kept_qkv, s.qkv), move(s.kept_normed, s.normed), fetch_weight(QKV, 0)]

    def needed(point):
        if point in back:
            for arrived in back.pop(point):
                arrived()

    backward(1, s.live_two, refill, range(9))
    input_backward(s)
    norm_one_backward(s, windows)
    refill(4)
    out_there()
    to_dense(s.grad, s.moved, s.dense.at[upper], padded)
    next_there = halo(4, s.dense.at[upper], s.next_upper, below)
    reducer.advance(9)
    project_backward(s, reducer)
    spread_there = move(s.in_spread, s.spread)
    reducer.settle(1)
    reducer.advance(10)

    swaps_there[1]()
    move_own(s.grad, s.swap_back, s.work, windows, -1)
    spread_there()
    small_gradients(s, s.small_own.at[1])
    refill(5)
    spread_gains(s, 0)
    reducer.advance(11)
    next_there()
    from_dense(s.next_upper, s.page, 0)
    s.grad[...] = s.work[...]
    add_halo(s.page, s.plain, s.grad, half, padded)
    reducer.advance(12)
    needed(0)

    def wait_next(point):
        needed(point + 1)

    backward(0, s.live, wait_next, range(13, 26))
    project_backward(s, reducer)
    reducer.settle(1)
    reducer.advance(26)
    input_backward(s)
    spread_there = move(s.in_spread, s.spread)
    reducer.advance(27)
    needed(4)
    norm_one_backward(s, windows)
    out_kept()
    to_dense(s.grad, s.plain, s.dense, s.plain.shape[0])
    grad_kept = move(s.dense, s.grad_tokens)
    reducer.advance(28)
    spread_there()
    small_gradients(s, s.small_own.at[0])
    reducer.advance(29)
    finish_small(s, plan, row)
    grad_kept()


def finish_small(s, plan, row):
    total = s.small_parts.at[plan.halvings - 1]
    outs = (
        (s.d_ln_gain, (G1, G2)),
        (s.d_ln_bias, (B1, B2)),
        (s.d_qv_bias, (QB, VB)),
        (s.d_proj_bias, (PB,)),
        (s.d_fc1_bias, tuple(range(F1B, F1B + FEEDS))),
        (s.d_fc2_bias, (F2B,)),
    )
    for layer in range(2):
        s.d_table[layer] = total[layer, VECTOR_ROWS:, :OFFSETS]
        for ref, indices in outs:
            whole = jnp.concatenate([total[layer, index : index + 1, :] for index in indices], axis=1)
            size = ref.shape[1]
            mine = jnp.zeros((1, size), F32)
            for share in range(plan.shares):
                mine = jnp.where(row == share, whole[:, share * size : (share + 1) * size], mine)
            ref[layer : layer + 1, :] = mine


def placements(cols):
    windows = cols // WIN
    patches = WIN * cols
    padded = -(-patches // LANES) * LANES
    plain = np.zeros((padded, windows * LANES), np.float32)
    moved = np.zeros((padded, windows * LANES), np.float32)
    for line in range(WIN):
        for col in range(cols):
            source = line * cols + col
            plain[source, (col // WIN) * LANES + line * WIN + col % WIN] = 1
            new_line, new_col = (line - SHIFT) % WIN, (col - SHIFT) % cols
            moved[source, (new_col // WIN) * LANES + new_line * WIN + new_col % WIN] = 1
    return plain.astype(BF), moved.astype(BF)


def swaps():
    on = np.zeros((2 * LANES, LANES), np.float32)
    back = np.zeros((2 * LANES, LANES), np.float32)
    for line in range(SHIFT):
        for col in range(WIN):
            moved, plain = line * WIN + col, (line + SHIFT) * WIN + (col + SHIFT) % WIN
            on[plain + (LANES if col >= SHIFT else 0), moved] = 1
            back[moved + (LANES if col < SHIFT else 0), plain] = 1
    return on.astype(BF), back.astype(BF)


def table_spread():
    size = 2 * WIN - 1
    spread = np.zeros((WIN, 2 * LANES, TABLE), np.float32)
    for key_col in range(WIN):
        for offset in range(size):
            for col in range(WIN):
                spread[key_col, offset * WIN + col, offset * size + col - key_col + WIN - 1] = 1
    spread = spread.reshape(WIN // 2, 2, 2 * LANES, TABLE).swapaxes(1, 2)
    return spread.reshape(WIN * LANES, 2 * TABLE).astype(BF)


def copy_all(*refs):
    *refs, sems = refs
    count = len(refs) // 3
    sources, targets, held = refs[:count], refs[count : 2 * count], refs[2 * count :]
    ways = [*zip(sources, held), *zip(held, targets)]
    copies = [pltpu.make_async_copy(*way, sems.at[number]) for number, way in enumerate(ways)]
    for copy in copies[:count]:
        copy.start()
    for incoming, outgoing in zip(copies[:count], copies[count:]):
        incoming.wait()
        outgoing.start()
    for copy in copies[count:]:
        copy.wait()


def hand_out(values):
    anywhere = pl.BlockSpec(memory_space=pl.ANY)
    return pl.pallas_call(
        copy_all,
        out_shape=[jax.ShapeDtypeStruct(value.shape, value.dtype) for value in values],
        in_specs=[anywhere] * len(values),
        out_specs=[anywhere] * len(values),
        scratch_shapes=[pltpu.VMEM(value.shape, value.dtype) for value in values]
        + [pltpu.SemaphoreType.DMA((2 * len(values),))],
        compiler_params=pltpu.CompilerParams(vmem_limit_bytes=VMEM_LIMIT),
        name="results",
    )(*values)


def per_device(
    page_tokens,
    blank_mask,
    cotangent,
    ln_gain,
    ln_bias,
    qv_bias,
    rel_table,
    w_qkv,
    w_proj,
    proj_bias,
    w_fc1,
    fc1_bias,
    w_fc2,
    fc2_bias,
):
    pages, shares = lax.axis_size(PAGE), lax.axis_size(ROW)
    plan = Plan(pages, shares)
    cols = page_tokens.shape[2]
    windows, lanes = cols // WIN, cols // WIN * LANES
    dense = ((WIN * cols * SPLITS, LANES), F32)
    half_dense = ((WIN * cols * SPLITS // 2, LANES), F32)
    plain, moved = (jnp.asarray(place) for place in placements(cols))
    live_rows = 8 * -(-windows // 8)
    scalar_inputs = dict(blank=blank_mask[0])
    small_inputs = dict(
        table=rel_table,
        ln_gain=ln_gain,
        ln_bias=ln_bias,
        qv_bias=qv_bias,
        proj_bias=proj_bias,
        fc1_bias=fc1_bias,
        fc2_bias=fc2_bias,
    )
    large_inputs = dict(
        in_tokens=page_tokens[0],
        in_grad=cotangent.reshape(dense[0]),
        in_plain=plain,
        in_moved=moved,
        in_swap_on=jnp.asarray(swaps()[0]),
        in_swap_back=jnp.asarray(swaps()[1]),
        in_spread=jnp.asarray(table_spread()),
        in_qkv=w_qkv,
        in_proj=w_proj,
        in_fc1=w_fc1,
        in_fc2=w_fc2,
    )
    saved = dict(
        x=((D, lanes), F32),
        normed=((D, lanes), BF),
        qkv=((3 * D, lanes), BF),
        soft=((windows * HEADS, LANES, LANES), BF),
        merged=((D, lanes), BF),
        hidden=((D, lanes), F32),
        second=((D, lanes), BF),
        active=((FF, lanes), BF),
        slope=((FF, lanes), BF),
    )
    units = ((UNITS, shares, CHUNK // shares, CHUNK), F32)
    large_outputs = dict(
        out_tokens=dense,
        grad_tokens=dense,
        sum_qkv=((2, D // shares, 3 * D), F32),
        sum_proj=((2, D // shares, D), F32),
        sum_fc1=((2, D // shares, FF), F32),
        sum_fc2=((2, FF // shares, D), F32),
        units_zero=units,
        units_one=units,
        kept_x=((D, lanes), F32),
        kept_normed=((D, lanes), BF),
        kept_qkv=((3 * D, lanes), BF),
        kept_soft=((windows * HEADS, LANES, LANES), BF),
        kept_merged=((D, lanes), BF),
        kept_hidden=((D, lanes), F32),
        kept_second=((D, lanes), BF),
        kept_active=((FF, lanes), BF),
        kept_slope=((FF, lanes), BF),
    )
    small_outputs = dict(
        d_ln_gain=((2, 2 * D // shares), F32),
        d_ln_bias=((2, 2 * D // shares), F32),
        d_qv_bias=((2, 2 * D // shares), F32),
        d_proj_bias=((2, D // shares), F32),
        d_fc1_bias=((2, FF // shares), F32),
        d_fc2_bias=((2, D // shares), F32),
        d_table=((2, HEADS, OFFSETS), F32),
    )
    small = (2, SMALL, D)
    vmem = dict(
        saved,
        tokens=((WIN, cols, D), BF),
        plain=(plain.shape, BF),
        moved=(moved.shape, BF),
        w_qkv=((D, 3 * D), BF),
        w_proj=((D, D), BF),
        w_fc1=((D, FF), BF),
        w_fc2=((FF, D), BF),
        dense=dense,
        upper=half_dense,
        swap_on=((2 * LANES, LANES), BF),
        swap_back=((2 * LANES, LANES), BF),
        grad_upper=half_dense,
        next_upper=half_dense,
        live_upper=((live_rows, LANES), F32),
        live_two=((live_rows, LANES), F32),
        work=((D, lanes), F32),
        grad=((D, lanes), F32),
        low=((D, lanes), BF),
        sums=((VECTORS, D, LANES), F32),
        gains=((2, D, LANES), F32),
        bias=((HEADS, LANES, LANES), F32),
        bias_rows=((HEADS * LANES, LANES), F32),
        regions=((2, LANES, LANES), F32),
        padded_table=((HEADS, TABLE), F32),
        live=((live_rows, LANES), F32),
        vector_rows=((VECTOR_ROWS, D), F32),
        staged=((2 * CHUNK, CHUNK), F32),
        done=((DONE * CLASSES, CHUNK // shares, CHUNK), F32),
        held=((HELD * CLASSES, shares, CHUNK // shares, CHUNK // 2), F32),
        small_own=(small, F32),
        small_parts=((plan.halvings,) + small, F32),
    )
    semaphores = dict(
        move_sems=pltpu.SemaphoreType.DMA((48,)),
        halo_sems=pltpu.SemaphoreType.DMA((2, 5)),
        send_sems=pltpu.SemaphoreType.DMA((2 * UNITS, plan.phases)),
        recv_sems=pltpu.SemaphoreType.DMA((2 * UNITS, plan.phases)),
        own_sems=pltpu.SemaphoreType.DMA((2 * UNITS, 2)),
        stage_sems=pltpu.SemaphoreType.DMA((2, shares)),
        small_sems=pltpu.SemaphoreType.DMA((2, plan.halvings)),
        free_sems=pltpu.SemaphoreType.REGULAR((CLASSES, plan.halvings)),
    )
    landing = [((RING,) + size, F32) for sizes in plan.sizes for size in sizes]
    layout = [*scalar_inputs, *small_inputs, *large_inputs, *small_outputs, *large_outputs, *vmem, *semaphores]
    in_vmem, anywhere = pl.BlockSpec(memory_space=pltpu.VMEM), pl.BlockSpec(memory_space=pl.ANY)
    outputs = {**small_outputs, **large_outputs}
    results = pl.pallas_call(
        functools.partial(run, plan, layout),
        out_shape=[jax.ShapeDtypeStruct(*shape) for shape in outputs.values()],
        in_specs=[pl.BlockSpec(memory_space=pltpu.SMEM)] + [in_vmem] * len(small_inputs) + [anywhere] * len(large_inputs),
        out_specs=[in_vmem] * len(small_outputs) + [anywhere] * len(large_outputs),
        scratch_shapes=[pltpu.VMEM(*shape) for shape in vmem.values()]
        + list(semaphores.values())
        + [pltpu.VMEM(*shape) for shape in landing],
        compiler_params=pltpu.CompilerParams(
            vmem_limit_bytes=VMEM_LIMIT, collective_id=0, has_side_effects=True
        ),
        name="two_layers",
    )(*scalar_inputs.values(), *small_inputs.values(), *large_inputs.values())
    results = hand_out(results[: len(small_outputs) + 6])
    d_ln_gain, d_ln_bias, d_qv_bias, d_proj_bias, d_fc1_bias, d_fc2_bias, d_table = results[: len(small_outputs)]
    out_tokens, grad_tokens, sum_qkv, sum_proj, sum_fc1, sum_fc2 = results[len(small_outputs) :]
    return (
        out_tokens.reshape(cotangent.shape),
        grad_tokens.reshape(cotangent.shape),
        d_ln_gain,
        d_ln_bias,
        d_qv_bias,
        d_table,
        sum_qkv,
        sum_proj,
        d_proj_bias,
        sum_fc1,
        d_fc1_bias,
        sum_fc2,
        d_fc2_bias,
    )


def solution(mesh):
    tokens, by_row, shares = P(PAGE, ROW, None, None), P(None, ROW), P(None, ROW, None)
    return jax.shard_map(
        per_device,
        mesh=mesh,
        in_specs=(tokens, P(PAGE, ROW, None), tokens) + (P(),) * 11,
        out_specs=(tokens, tokens)
        + (by_row, by_row, by_row, P(), shares, shares, by_row, shares, by_row, shares, by_row),
        check_vma=False,
    )
```

```python
import functools

import jax
import jax.numpy as jnp
import numpy as np
from jax import lax
from jax.experimental import pallas as pl
from jax.experimental.pallas import tpu as pltpu
from jax.sharding import PartitionSpec as P

WIN = 10
SHIFT = 5
AREA = WIN * WIN
LANES = 128
D = 512
HEADS = 16
HEAD_DIM = 32
FF = 2048
CHUNK = 512
FEEDS = FF // CHUNK
STRIP = 16
SPLITS = D // LANES
EPSILON = 1e-05
MASK_VALUE = -100.0
NEVER = -1e30
SCORE_SCALE = HEAD_DIM ** (-0.5)
VMEM_LIMIT = 63 * 1024 * 1024 + 512 * 1024
BF = jnp.bfloat16
F32 = jnp.float32
MESH = pl.DeviceIdType.MESH
PAGE, ROW = "page", "row"

G1, B1, G2, B2, QB, VB, PB, F2B, F1B, VECTORS = 0, 1, 2, 3, 4, 5, 6, 7, 8, 12
VECTOR_ROWS = 16
SMALL = VECTOR_ROWS + HEADS
OFFSETS = (2 * WIN - 1) ** 2
TABLE = 384

UNIT_FC1, UNIT_FC2, UNIT_PROJ, UNIT_QKV, UNITS = 0, 4, 8, 9, 12
CLASSES = 3
GROUPS = UNITS // CLASSES
TRIPLES = 2 * GROUPS
HELD = 4
DONE = 5
RING = 3
QKV, PROJ, FC1, FC2 = range(4)
TARGETS = (
    ((FC1, 0, 0), (FC1, 0, 1), (FC1, 0, 2)),
    ((FC1, 0, 3), (FC2, 0, 0), (FC2, 1, 0)),
    ((FC2, 2, 0), (FC2, 3, 0), (PROJ, 0, 0)),
    ((QKV, 0, 0), (QKV, 0, 1), (QKV, 0, 2)),
)


def mm(left, right, left_dim, right_dim):
    return lax.dot_general(
        left, right, (((left_dim,), (right_dim,)), ((), ())), preferred_element_type=F32
    )


def split(values):
    high = values.astype(BF)
    return high, (values - high.astype(F32)).astype(BF)


def lane_tile(index):
    return pl.ds(pl.multiple_of(index * LANES, LANES), LANES)


def chunk_of(index):
    return pl.ds(pl.multiple_of(index * CHUNK, CHUNK), CHUNK)


def wide(column, count):
    return jnp.concatenate([column] * count, axis=1)


def fold(values):
    total = values[:, :LANES]
    for start in range(LANES, values.shape[1], LANES):
        total = total + values[:, start : start + LANES]
    return total


def norm_parts(values):
    center = values - jnp.sum(values, axis=0, keepdims=True) * (1.0 / D)
    spread = jnp.sum(center * center, axis=0, keepdims=True) * (1.0 / D)
    scale = lax.rsqrt(spread + EPSILON)
    return center * scale, scale


def norm_pull(grad, gain, hat, scale):
    scaled = grad * gain
    mean_one = jnp.sum(scaled, axis=0, keepdims=True) * (1.0 / D)
    mean_two = jnp.sum(scaled * hat, axis=0, keepdims=True) * (1.0 / D)
    return scale * (scaled - mean_one - hat * mean_two)


def gelu_parts(inner):
    step = 1.0 / (1.0 + (0.3275911 * 0.7071067811865476) * jnp.abs(inner))
    bell = jnp.exp(inner * inner * -0.5)
    poly = 0.5 * 1.061405429
    for factor in (-1.453152027, 1.421413741, -0.284496736, 0.254829592):
        poly = poly * step + 0.5 * factor
    tail = poly * step * bell
    below = jnp.where(inner >= 0, 1.0 - tail, tail)
    return inner * below, below + inner * bell * 0.3989422804014327


def to_channels(page_ref, place_ref, out_ref, exact=False):
    def step(index, carry):
        channels = pl.ds(pl.multiple_of(index * 256, 256), 256)
        values = page_ref[:, channels]
        if exact:
            out_ref[channels, :] = mm(values.astype(BF), place_ref[...], 0, 0)
        else:
            high, low = split(values)
            out_ref[channels, :] = mm(high, place_ref[...], 0, 0) + mm(low, place_ref[...], 0, 0)
        return carry

    lax.fori_loop(0, D // 256, step, 0)


def to_dense(values_ref, place_ref, dense_ref, padded):
    count = dense_ref.shape[0] // SPLITS
    for index in range(D // 256):
        high, low = split(values_ref[index * 256 : (index + 1) * 256, :])
        page = mm(place_ref[:padded, :], high, 1, 1) + mm(place_ref[:padded, :], low, 1, 1)
        for part in range(2):
            rows = pl.ds(2 * index + part, count, stride=SPLITS)
            dense_ref[rows, :] = page[:count, part * LANES : (part + 1) * LANES]


def from_dense(dense_ref, page_ref, row):
    count = dense_ref.shape[0] // SPLITS
    for part in range(SPLITS):
        rows = pl.ds(part, count, stride=SPLITS)
        page_ref[pl.ds(row, count), part * LANES : (part + 1) * LANES] = dense_ref[rows, :]


def add_halo(page_ref, place_ref, out_ref, count, padded):
    page_ref[pl.ds(count, padded - count), :] = jnp.zeros((padded - count, D), F32)

    def step(index, carry):
        channels = pl.ds(pl.multiple_of(index * 256, 256), 256)
        high, low = split(page_ref[:padded, channels])
        out_ref[channels, :] += mm(high, place_ref[:padded, :], 0, 0) + mm(low, place_ref[:padded, :], 0, 0)
        return carry

    lax.fori_loop(0, D // 256, step, 0)


def move_own(values_ref, swap_ref, out_ref, windows, first):
    for window in range(windows):
        sources = [(window + first + part) % windows * LANES for part in range(2)]
        values = jnp.concatenate([values_ref[:, start : start + LANES] for start in sources], axis=1)
        high, low = split(values)
        target = slice(window * LANES, (window + 1) * LANES)
        out_ref[:, target] = mm(high, swap_ref[...], 1, 0) + mm(low, swap_ref[...], 1, 0)


def vector_rows(s, layer):
    rows = s.vector_rows
    sources = ((G1, s.ln_gain, 0), (B1, s.ln_bias, 0), (G2, s.ln_gain, 1), (B2, s.ln_bias, 1))
    sources += ((QB, s.qv_bias, 0), (VB, s.qv_bias, 1), (PB, s.proj_bias, 0), (F2B, s.fc2_bias, 0))
    sources += tuple((F1B + part, s.fc1_bias, part) for part in range(FEEDS))
    for index, source, part in sources:
        rows[index : index + 1, :] = source[layer : layer + 1, part * D : (part + 1) * D]
    rows[VECTORS:, :] = jnp.zeros((VECTOR_ROWS - VECTORS, D), F32)
    return rows[...].T


def spread_columns(s, layer):
    columns = vector_rows(s, layer)
    for index in range(VECTORS):
        s.sums[index] = jnp.broadcast_to(columns[:, index : index + 1], (D, LANES))


def spread_gains(s, layer):
    columns = vector_rows(s, layer)
    for index, vector in enumerate((G1, G2)):
        s.gains[index] = jnp.broadcast_to(columns[:, vector : vector + 1], (D, LANES))


def spread_part(col):
    rows, lanes = (col // 2) * 2 * LANES, (col % 2) * TABLE
    return slice(rows, rows + 2 * LANES), slice(lanes, lanes + TABLE)


def spread_bias(s, layer):
    spread_ref, rows_ref, bias_ref = s.spread, s.bias_rows, s.bias
    s.padded_table[...] = jnp.zeros(s.padded_table.shape, F32)
    s.padded_table[:, :OFFSETS] = s.table[layer]
    high, low = split(s.padded_table[...])
    parts = []
    for col in range(WIN):
        chosen = spread_ref[spread_part(col)]
        parts.append(mm(high, chosen, 1, 1) + mm(low, chosen, 1, 1))
    source = jnp.concatenate(parts, axis=0)
    rows_ref[...] = jnp.zeros(rows_ref.shape, F32)
    for row in range(WIN):
        shift = (WIN - 1 - row) * WIN
        moved = source if shift == 0 else pltpu.roll(source, 2 * LANES - shift, axis=1)
        rows_ref[pl.ds(row * WIN * HEADS, WIN * HEADS), :] = moved[:, :LANES]
    for head in range(HEADS):
        bias_ref[head] = rows_ref[pl.ds(head, LANES, stride=HEADS), :]


def gather_bias(grad_ref, spread_ref, rows_ref):
    for head in range(HEADS):
        rows_ref[pl.ds(head, LANES, stride=HEADS), :] = grad_ref[head]
    total = jnp.zeros((WIN * HEADS, 2 * LANES), F32)
    for row in range(WIN):
        shift = (WIN - 1 - row) * WIN
        piece = rows_ref[pl.ds(row * WIN * HEADS, WIN * HEADS), :]
        piece = jnp.concatenate([piece, jnp.zeros_like(piece)], axis=1)
        total = total + (piece if shift == 0 else pltpu.roll(piece, shift, axis=1))
    table = jnp.zeros((HEADS, TABLE), F32)
    for col in range(WIN):
        for part in split(total[col * HEADS : (col + 1) * HEADS]):
            table = table + mm(part, spread_ref[spread_part(col)], 1, 0)
    return table


def region_masks(shifted_layer, out_ref):
    key = lax.broadcasted_iota(jnp.int32, (LANES, LANES), 0)
    query = lax.broadcasted_iota(jnp.int32, (LANES, LANES), 1)
    padding = jnp.where(key < AREA, 0.0, NEVER)
    out_ref[0] = padding
    out_ref[1] = padding
    if shifted_layer:
        last = lax.axis_index(ROW) == lax.axis_size(ROW) - 1
        rows_differ = ((key >= AREA // 2) != (query >= AREA // 2)) & last
        cols_differ = (key % WIN >= SHIFT) != (query % WIN >= SHIFT)
        out_ref[0] += jnp.where(rows_differ, MASK_VALUE, 0.0)
        out_ref[1] += jnp.where(rows_differ | cols_differ, MASK_VALUE, 0.0)


def shifted_live(s, windows):
    place = lax.broadcasted_iota(jnp.int32, (1, LANES), 1)
    for window in range(windows):
        here, after = slice(window, window + 1), slice((window + 1) % windows, (window + 1) % windows + 1)
        beyond = place % WIN >= SHIFT
        own = jnp.where(beyond, s.live[after, :], s.live[here, :])
        upper = jnp.where(beyond, s.live_upper[after, :], s.live_upper[here, :])
        s.live_two[here, :] = jnp.where(place >= AREA // 2, upper, own)


def head_rows(head, base=0):
    return pl.ds(base + head * HEAD_DIM, HEAD_DIM)


def norm_one_forward(s, windows):
    def step(index, carry):
        lanes = lane_tile(index)
        hat, _ = norm_parts(s.x[:, lanes])
        s.normed[:, lanes] = (hat * s.sums[G1] + s.sums[B1]).astype(BF)
        return carry

    lax.fori_loop(0, windows, step, 0)


def project_forward(s, windows):
    def step(index, carry):
        rows = chunk_of(index)
        bias = s.sums[jnp.where(index == 0, QB, VB)] * jnp.where(index == 1, 0.0, 1.0)
        out = mm(s.w_qkv[:, rows], s.normed[...], 0, 0)
        s.qkv[rows, :] = (out + wide(bias, windows)).astype(BF)
        return carry

    lax.fori_loop(0, 3, step, 0)


def attend_forward(s, windows, live_ref):
    def step(index, carry):
        lanes = lane_tile(index)
        live = jnp.broadcast_to(live_ref[pl.ds(index, 1), :], (LANES, LANES)).T
        masked = s.regions[jnp.where(index == windows - 1, 1, 0)] + MASK_VALUE * (1.0 - live)
        for head in range(HEADS):
            query = s.qkv[head_rows(head), lanes]
            key = s.qkv[head_rows(head, D), lanes]
            value = s.qkv[head_rows(head, 2 * D), lanes]
            scores = mm(key, query, 0, 0) * SCORE_SCALE + (s.bias[head] + masked)
            exponent = jnp.exp(scores - jnp.max(scores, axis=0, keepdims=True))
            total = jnp.sum(exponent, axis=0, keepdims=True)
            soft = (exponent * (1.0 / total)).astype(BF)
            s.soft[index * HEADS + head] = soft
            s.merged[head_rows(head), lanes] = mm(value, soft, 1, 0).astype(BF)
        return carry

    lax.fori_loop(0, windows, step, 0)


def norm_two_forward(s, windows, live_ref):
    def step(index, carry):
        lanes = lane_tile(index)
        hidden = s.x[:, lanes] + live_ref[pl.ds(index, 1), :] * (s.work[:, lanes] + s.sums[PB])
        s.hidden[:, lanes] = hidden
        s.work[:, lanes] = hidden + s.sums[F2B]
        hat, _ = norm_parts(hidden)
        s.second[:, lanes] = (hat * s.sums[G2] + s.sums[B2]).astype(BF)
        return carry

    lax.fori_loop(0, windows, step, 0)


def feed_forward(s, windows):
    shares, rows = s.held.shape[1:3]
    parts = windows * LANES // 256
    per_share = rows // STRIP

    def step(index, carry):
        inner = mm(s.w_fc1[:, chunk_of(index)], s.second[...], 0, 0)
        for part in range(parts):
            s.held[part] = inner[:, part * 256 : (part + 1) * 256].reshape(shares, rows, 256)

        def strip(number, carry):
            inside = pl.ds(pl.multiple_of(number % per_share * STRIP, STRIP), STRIP)
            target = pl.ds(pl.multiple_of(index * CHUNK + number * STRIP, STRIP), STRIP)
            bias = wide(s.sums[F1B + index, pl.ds(pl.multiple_of(number * STRIP, STRIP), STRIP), :], 2)
            for part in range(parts):
                active, slope = gelu_parts(s.held[part, number // per_share, inside, :] + bias)
                s.active[target, part * 256 : (part + 1) * 256] = active.astype(BF)
                s.slope[target, part * 256 : (part + 1) * 256] = slope.astype(BF)
            return carry

        lax.fori_loop(0, CHUNK // STRIP, strip, 0, unroll=2)
        return carry

    lax.fori_loop(0, FEEDS, step, 0)
    s.work[...] += mm(s.w_fc2[...], s.active[...], 0, 0)


def feed_backward(s, sink, times):
    s.sums[...] = jnp.zeros(s.sums.shape, F32)
    s.bias[...] = jnp.zeros(s.bias.shape, F32)
    lowered = s.grad[...].astype(BF)
    s.low[...] = lowered
    s.sums[F2B] = fold(lowered.astype(F32))
    s.work[...] = jnp.zeros(s.work.shape, F32)

    def step(index, carry):
        rows = chunk_of(index)
        sink.put(0, mm(s.active[rows, :], s.low[...], 1, 1), feed_pieces(index, sink.shares), index == 0)
        grad_inner = mm(s.w_fc2[rows, :], s.low[...], 1, 0) * s.slope[rows, :].astype(F32)
        grad_inner = grad_inner.astype(BF)
        s.sums[F1B + index] = fold(grad_inner.astype(F32))
        sink.put(1, mm(s.second[...], grad_inner, 1, 1), row_pieces(UNIT_FC1 + index, sink.shares), index == 0)
        s.work[...] += mm(s.w_fc1[:, rows], grad_inner, 1, 0)
        sink.advance_at(index, times)
        return carry

    lax.fori_loop(0, FEEDS, step, 0)
    sink.settle(0)
    sink.settle(1)


def norm_two_backward(s, windows, live_ref):
    def step(index, carry):
        lanes = lane_tile(index)
        hat, scale = norm_parts(s.hidden[:, lanes])
        grad = s.work[:, lanes]
        s.sums[G2] += grad * hat
        s.sums[B2] += grad
        grad = s.grad[:, lanes] + norm_pull(grad, s.gains[1], hat, scale)
        s.grad[:, lanes] = grad
        grad_low = (grad * live_ref[pl.ds(index, 1), :]).astype(BF)
        s.low[:, lanes] = grad_low
        s.sums[PB] += grad_low.astype(F32)
        return carry

    lax.fori_loop(0, windows, step, 0)


def merge_backward(s, sink):
    sink.put(0, mm(s.merged[...], s.low[...], 1, 1), row_pieces(UNIT_PROJ, sink.shares), True)
    s.merged[...] = mm(s.w_proj[...], s.low[...], 1, 0).astype(BF)
    sink.settle(0)


def attend_backward(s, windows, sink, times):
    def step(index, carry):
        lanes = lane_tile(index)
        for head in range(HEADS):
            query = s.qkv[head_rows(head), lanes]
            key = s.qkv[head_rows(head, D), lanes]
            value = s.qkv[head_rows(head, 2 * D), lanes]
            grad_out = s.merged[head_rows(head), lanes]
            soft_low = s.soft[index * HEADS + head]
            soft = soft_low.astype(F32)
            grad_soft = mm(value, grad_out, 0, 0)
            inner = jnp.sum(soft * grad_soft, axis=0, keepdims=True)
            grad_scores = (soft * (grad_soft - inner)).astype(BF)
            s.bias[head] += grad_scores.astype(F32)
            grad_query = (mm(key, grad_scores, 1, 0) * SCORE_SCALE).astype(BF)
            grad_key = (mm(query, grad_scores, 1, 1) * SCORE_SCALE).astype(BF)
            grad_value = mm(grad_out, soft_low, 1, 1).astype(BF)
            s.qkv[head_rows(head), lanes] = grad_query
            s.qkv[head_rows(head, D), lanes] = grad_key
            s.qkv[head_rows(head, 2 * D), lanes] = grad_value
            s.sums[QB, head_rows(head), :] += grad_query.astype(F32)
            s.sums[VB, head_rows(head), :] += grad_value.astype(F32)
        sink.advance_at(index, times)
        return carry

    lax.fori_loop(0, windows, step, 0)


def project_backward(s, sink):
    def step(index, carry):
        rows = chunk_of(index)
        sink.put(1, mm(s.normed[...], s.qkv[rows, :], 1, 1), row_pieces(UNIT_QKV + index, sink.shares), index == 0)
        return carry

    lax.fori_loop(0, 3, step, 0)


def input_backward(s):
    s.work[...] = mm(s.w_qkv[...], s.qkv[...], 1, 0)


def norm_one_backward(s, windows):
    def step(index, carry):
        lanes = lane_tile(index)
        hat, scale = norm_parts(s.x[:, lanes])
        grad = s.work[:, lanes]
        s.sums[G1] += grad * hat
        s.sums[B1] += grad
        s.grad[:, lanes] += norm_pull(grad, s.gains[0], hat, scale)
        return carry

    lax.fori_loop(0, windows, step, 0)


def small_gradients(s, small_ref):
    places = lax.broadcasted_iota(jnp.int32, (D, LANES), 1)
    packed = jnp.zeros((D, LANES), F32)
    for index in range(VECTORS):
        packed = jnp.where(places == index, jnp.sum(s.sums[index], axis=1, keepdims=True), packed)
    small_ref[:VECTOR_ROWS, :] = packed.T[:VECTOR_ROWS]
    table = gather_bias(s.bias, s.spread, s.bias_rows)
    small_ref[VECTOR_ROWS:, :] = jnp.concatenate([table, jnp.zeros((HEADS, D - TABLE), F32)], axis=1)


def reversed_bits(value, count):
    turned = 0
    for bit in range(count):
        turned = turned * 2 + (value // 2**bit) % 2
    return turned


def row_pieces(unit, shares):
    rows, count = CHUNK // shares, shares.bit_length() - 1
    return [(share * rows, unit, reversed_bits(share, count)) for share in range(shares)]


def feed_pieces(index, shares):
    rows, count = CHUNK // shares, shares.bit_length() - 1
    pieces = []
    for share in range(shares // FEEDS):
        place = reversed_bits(index * (shares // FEEDS) + share, count)
        for part in range(FEEDS):
            pieces.append(((share * FEEDS + part) * rows, UNIT_FC2 + part, place))
    return pieces


class Plan:
    def __init__(self, pages, shares):
        self.shares, self.rows = shares, CHUNK // shares
        page_bits, row_bits = pages.bit_length() - 1, shares.bit_length() - 1
        others = page_bits - 1
        self.steps = []
        for kind in range(CLASSES):
            turn = kind % 2
            page = [(PAGE, 2 ** (1 + (bit + turn) % others)) for bit in range(others)]
            row = [(ROW, 2**bit) for bit in range(row_bits)]
            self.steps.append([(PAGE, 1)] + (row + page if kind == 2 else page + row))
        self.page_steps = [[0] + [at for at, step in enumerate(steps) if at and step[0] == PAGE] for steps in self.steps]
        self.halvings = page_bits + row_bits
        self.phases = self.halvings + page_bits
        self.sizes = []
        for kind in range(CLASSES):
            size = [shares, self.rows, CHUNK // 2]
            sizes = [tuple(size)]
            for level in range(1, self.halvings):
                size[self.split_axis(kind, level)] //= 2
                sizes.append(tuple(size))
            self.sizes.append(sizes)
        self.steps_at = self.schedule()

    def schedule(self):
        small = TRIPLES
        free, ready, stage_of, plan, now = {}, {}, {}, [], 0.0
        for triple in range(TRIPLES):
            for kind in range(CLASSES):
                stage_of[triple, kind] = 0
        stage_of[small, 0] = 0

        def link(key, phase):
            triple, kind = key
            if phase < self.halvings:
                axis, stride = self.steps[kind][phase]
                size = 2.0**-phase / 2 if triple != small else 0.125
            else:
                axis, stride = self.steps[kind][self.page_steps[kind][self.phases - 1 - phase]]
                size = 2.0 ** (phase - 2 * self.halvings)
            if axis == PAGE and stride == 1:
                return 0, size * PLAN_CORE
            return (axis, stride if axis == PAGE else 0), size * PLAN_LINK * (1.0 if stride == 1 or axis == PAGE else 1.5)

        def last_stage(key):
            return self.halvings if key[0] == small else self.phases + 1

        def allowed(key, point):
            triple, kind = key
            stage = stage_of[key]
            if stage > last_stage(key):
                return False
            if triple == small:
                return point >= len(PLAN_POINTS) - 1
            if stage == 0 and point < PLAN_THERE[triple]:
                return False
            if triple > 0 and stage_of[triple - 1, kind] <= stage:
                return False
            if triple >= RING and stage < self.halvings and stage_of[triple - RING, kind] <= stage + 1:
                return False
            if stage == 0 and triple >= DONE and stage_of[triple - DONE, kind] <= self.phases + 1:
                return False
            return not (stage == 0 and triple >= HELD and stage_of[triple - HELD, kind] <= self.halvings + 1)

        for point, work in enumerate(PLAN_POINTS):
            now += work
            if point == PLAN_HALO:
                free[ROW, 0] = max(now, free.get((ROW, 0), 0.0)) + PLAN_HALO_TIME
            steps, final = [], point == len(PLAN_POINTS) - 1
            while True:
                keys = [key for key in stage_of if allowed(key, point)]
                keys = [key for key in keys if final or ready.get(key, 0.0) <= now + PLAN_SLACK]
                if not keys:
                    break
                key = min(keys, key=lambda key: (max(ready.get(key, 0.0), now), -stage_of[key], key))
                stage = stage_of[key]
                now = max(now, ready.get(key, 0.0)) + (PLAN_ADD * 2.0**-stage if stage else 0.0)
                if stage == self.phases:
                    ready[key] = now + PLAN_LATENCY
                elif stage < last_stage(key):
                    name, length = link(key, stage)
                    free[name] = max(now, free.get(name, 0.0)) + length
                    ready[key] = free[name] + PLAN_LATENCY
                steps.append((*key, stage))
                stage_of[key] += 1
            plan.append(steps)
        assert all(stage_of[key] > last_stage(key) for key in stage_of)
        return plan

    def split_axis(self, kind, level):
        if self.steps[kind][level][0] == ROW:
            return 0
        return 2 if self.page_steps[kind].index(level) < 2 else 1

    def partner(self, kind, level):
        axis, stride = self.steps[kind][level]
        page, row = lax.axis_index(PAGE), lax.axis_index(ROW)
        mine = page if axis == PAGE else row
        bit = (mine // stride) % 2
        other = mine + (1 - 2 * bit) * stride
        return bit, ((other, row) if axis == PAGE else (page, other))

    def part(self, kind, level, sent=False):
        starts, sizes = [0, 0, 0], [self.shares, self.rows, CHUNK // 2]
        for at in range(1, level + 1):
            axis = self.split_axis(kind, at)
            sizes[axis] //= 2
            bit, _ = self.partner(kind, at)
            which = 1 - bit if sent and at == level else bit
            starts[axis] = starts[axis] + which * sizes[axis]
        return (
            pl.ds(starts[0], sizes[0]),
            pl.ds(pl.multiple_of(starts[1], 8), sizes[1]),
            pl.ds(pl.multiple_of(starts[2], LANES), sizes[2]),
        )

    def place(self, kind, count):
        starts, sizes = [0, 0], [self.rows, CHUNK]
        for at in self.page_steps[kind][:count]:
            axis = self.split_axis(kind, at) - 1 if at else 1
            sizes[axis] //= 2
            bit, _ = self.partner(kind, at)
            starts[axis] = starts[axis] + bit * sizes[axis]
        return starts, sizes


class Reducer:
    def __init__(self, plan, s):
        self.plan, self.s = plan, s
        self.shares = plan.shares
        self.layer = 1

    def stage_copies(self, slot, pieces):
        return [
            pltpu.make_async_copy(
                self.s.staged.at[pl.ds(slot * CHUNK + start, self.plan.rows)],
                self.s.units[self.layer].at[unit, place],
                self.s.stage_sems.at[slot, number],
            )
            for number, (start, unit, place) in enumerate(pieces)
        ]

    def put(self, slot, grad, pieces, first):
        if first is not True:

            @pl.when(jnp.logical_not(first))
            def _():
                self.settle(slot)

        self.s.staged[pl.ds(slot * CHUNK, CHUNK), :] = grad
        for copy in self.stage_copies(slot, pieces):
            copy.start()

    def settle(self, slot):
        for copy in self.stage_copies(slot, row_pieces(0, self.shares)):
            copy.wait()

    def remote(self, source, target, unit, phase, device):
        return pltpu.make_async_remote_copy(
            src_ref=source,
            dst_ref=target,
            send_sem=self.s.send_sems.at[unit, phase],
            recv_sem=self.s.recv_sems.at[unit, phase],
            device_id=device,
            device_id_type=MESH,
        )

    def unit_half(self, triple, kind, which):
        layer, half = 1 - triple // GROUPS, CHUNK // 2
        unit = CLASSES * (triple % GROUPS) + kind
        return self.s.units[layer].at[unit, :, :, pl.ds(pl.multiple_of(which * half, half), half)]

    def held(self, triple, kind):
        return self.s.held.at[CLASSES * (triple % HELD) + kind]

    def halving(self, triple, kind, level):
        plan = self.plan
        bit, device = plan.partner(kind, level)
        target = self.s.landing[kind][level].at[triple % RING]
        if level == 0:
            source = self.unit_half(triple, kind, 1 - bit)
        else:
            source = self.held(triple, kind).at[plan.part(kind, level, True)]
        return self.remote(source, target, CLASSES * triple + kind, level, device)

    def own_half(self, triple, kind):
        bit, _ = self.plan.partner(kind, 0)
        sem = self.s.own_sems.at[CLASSES * triple + kind, 0]
        return pltpu.make_async_copy(self.unit_half(triple, kind, bit), self.held(triple, kind), sem)

    def finished(self, triple, kind):
        return self.held(triple, kind).at[self.plan.part(kind, self.plan.halvings - 1)].at[0]

    def done(self, triple, kind, count):
        starts, sizes = self.plan.place(kind, count)
        return self.s.done.at[
            CLASSES * (triple % DONE) + kind,
            pl.ds(pl.multiple_of(starts[0], 8), sizes[0]),
            pl.ds(pl.multiple_of(starts[1], LANES), sizes[1]),
        ]

    def gathering(self, triple, kind, phase):
        plan = self.plan
        count = len(plan.page_steps[kind]) - (phase - plan.halvings)
        part = self.done(triple, kind, count)
        _, device = plan.partner(kind, plan.page_steps[kind][count - 1])
        return self.remote(part, part, CLASSES * triple + kind, phase, device)

    def result(self, triple, kind):
        which, row_block, col_block = TARGETS[triple % GROUPS][kind]
        rows = self.plan.rows
        target = self.s.results[which].at[
            1 - triple // GROUPS, pl.ds(row_block * rows, rows), pl.ds(col_block * CHUNK, CHUNK)
        ]
        sem = self.s.own_sems.at[CLASSES * triple + kind, 1]
        return pltpu.make_async_copy(self.done(triple, kind, 0), target, sem)

    def start(self, triple, kind, phase):
        plan = self.plan
        if phase < plan.halvings:
            if triple >= RING:
                pl.semaphore_wait(self.s.free_sems.at[kind, phase], 1)
            self.halving(triple, kind, phase).start()
            if phase == 0:
                self.own_half(triple, kind).start()
        elif phase < plan.phases:
            if phase == plan.halvings:
                self.done(triple, kind, len(plan.page_steps[kind]))[...] = self.finished(triple, kind)[...]
            self.gathering(triple, kind, phase).start()
        elif phase == plan.phases:
            self.result(triple, kind).start()

    def finish(self, triple, kind, phase):
        plan, s = self.plan, self.s
        if phase < plan.halvings:
            self.halving(triple, kind, phase).wait()
            if phase == 0:
                self.own_half(triple, kind).wait()
            landed = s.landing[kind][phase].at[triple % RING]
            kept = self.held(triple, kind).at[plan.part(kind, phase)]

            def add(share, carry):
                kept[share] += landed[share]
                return carry

            lax.fori_loop(0, landed.shape[0], add, 0)
            if triple < TRIPLES - RING:
                _, device = plan.partner(kind, phase)
                pl.semaphore_signal(s.free_sems.at[kind, phase], inc=1, device_id=device, device_id_type=MESH)
        elif phase < plan.phases:
            self.gathering(triple, kind, phase).wait()
        else:
            self.result(triple, kind).wait()

    def advance(self, point):
        for triple, kind, stage in self.plan.steps_at[point]:
            if triple == TRIPLES:
                self.small_step(stage - 1)
                continue
            if stage > 0:
                self.finish(triple, kind, stage - 1)
            self.start(triple, kind, stage)

    def advance_at(self, index, points):
        for number, point in enumerate(points):
            if self.plan.steps_at[point]:

                @pl.when(index == number)
                def _(point=point):
                    self.advance(point)

    def small_copy(self, phase):
        s = self.s
        _, device = self.plan.partner(0, phase)
        return pltpu.make_async_remote_copy(
            src_ref=s.small_own if phase == 0 else s.small_parts.at[phase - 1],
            dst_ref=s.small_parts.at[phase],
            send_sem=s.small_sems.at[0, phase],
            recv_sem=s.small_sems.at[1, phase],
            device_id=device,
            device_id_type=MESH,
        )

    def small_step(self, phase):
        s = self.s
        if phase >= 0:
            self.small_copy(phase).wait()
            s.small_parts[phase] += s.small_own[...] if phase == 0 else s.small_parts[phase - 1]
        if phase + 1 < self.plan.halvings:
            self.small_copy(phase + 1).start()


PLAN_POINTS = (0, 2, 3) + (2.7,) * 6 + (5.2, 3, 3, 6) + (3.2,) * 4 + (0.3, 2, 3) + (2.7,) * 6 + (3, 3, 3, 3)
PLAN_THERE = (0, 0, 2, 10, 17, 17, 19, 26)
PLAN_HALO, PLAN_HALO_TIME = 9, 12.3
PLAN_CORE, PLAN_LINK, PLAN_LATENCY, PLAN_ADD, PLAN_SLACK = 1.7, 20.0, 2.0, 0.9, 0.0


class Moves:
    def __init__(self, sems):
        self.sems, self.used = sems, 0

    def __call__(self, source, target):
        number, self.used = self.used, self.used + 1
        make = functools.partial(pltpu.make_async_copy, source, target, self.sems.at[number])
        make().start()
        return lambda: make().wait()


class Refs:
    pass


def run(plan, layout, *refs):
    s = Refs()
    for name, ref in zip(layout, refs):
        setattr(s, name, ref)
    rest = list(refs[len(layout) :])
    s.landing = [[rest.pop(0) for _ in range(plan.halvings)] for _ in range(CLASSES)]
    s.results = (s.sum_qkv, s.sum_proj, s.sum_fc1, s.sum_fc2)
    s.units = (s.units_zero, s.units_one)
    s.page = s.staged.at[pl.ds(0, s.plain.shape[0])]
    s.spread = s.qkv.at[pl.ds(0, s.in_spread.shape[0])]
    windows = s.x.shape[1] // LANES
    patches = s.dense.shape[0] // SPLITS
    half, half_rows = patches // 2, s.dense.shape[0] // 2
    padded = 16 * -(-half // 16)
    upper, lower = pl.ds(0, half_rows), pl.ds(half_rows, half_rows)
    reducer = Reducer(plan, s)
    move = Moves(s.move_sems)
    page, row = lax.axis_index(PAGE), lax.axis_index(ROW)
    count = lax.axis_size(ROW)
    above, below = (page, (row + count - 1) % count), (page, (row + 1) % count)

    def halo(number, source, target, device):
        make = functools.partial(
            pltpu.make_async_remote_copy,
            src_ref=source,
            dst_ref=target,
            send_sem=s.halo_sems.at[0, number],
            recv_sem=s.halo_sems.at[1, number],
            device_id=device,
            device_id_type=MESH,
        )
        make().start()
        return lambda: make().wait()

    tokens_there = move(s.in_tokens, s.tokens)
    places_there = (move(s.in_plain, s.plain), move(s.in_moved, s.moved))
    swaps_there = (move(s.in_swap_on, s.swap_on), move(s.in_swap_back, s.swap_back))
    spread_there = move(s.in_spread, s.spread)
    weights = ((s.in_qkv, s.w_qkv), (s.in_proj, s.w_proj), (s.in_fc1, s.w_fc1), (s.in_fc2, s.w_fc2))

    def fetch_weight(which, layer):
        source, target = weights[which]
        return move(source.at[layer], target)

    there = [fetch_weight(which, 0) for which in range(4)]

    barrier = pltpu.get_barrier_semaphore()
    devices = [plan.partner(0, level)[1] for level in range(plan.halvings)] + [above, below]
    for device in devices:
        pl.semaphore_signal(barrier, inc=1, device_id=device, device_id_type=MESH)
    pl.semaphore_wait(barrier, len(devices))

    s.live[...] = jnp.zeros(s.live.shape, F32)
    for window in range(windows):
        s.live[window : window + 1, :] = jnp.full((1, LANES), 1.0 - s.blank[0, window].astype(F32))
    live_there = halo(0, s.live, s.live_upper, above)
    grad_there = halo(1, s.in_grad.at[upper], s.grad_upper, above)
    grad_lower_there = move(s.in_grad.at[lower], s.dense.at[lower])
    s.page[...] = jnp.zeros(s.page.shape, F32)
    tokens_there()
    cols = s.tokens.shape[1]
    for line in range(WIN):
        s.page[pl.ds(line * cols, cols), :] = s.tokens[line].astype(F32)
    places_there[0]()
    to_channels(s.page, s.plain, s.x, True)
    saves = [move(s.x, s.kept_x)]
    spread_columns(s, 0)
    spread_there()
    spread_bias(s, 0)
    region_masks(False, s.regions)
    norm_one_forward(s, windows)
    saves.append(move(s.normed, s.kept_normed))
    there[QKV]()
    project_forward(s, windows)
    qkv_saved = move(s.qkv, s.kept_qkv)
    there[QKV] = fetch_weight(QKV, 1)
    attend_forward(s, windows, s.live)
    saves.append(move(s.soft, s.kept_soft))
    saves.append(move(s.merged, s.kept_merged))
    there[PROJ]()
    s.work[...] = mm(s.w_proj[...], s.merged[...], 0, 0)
    there[PROJ] = fetch_weight(PROJ, 1)
    norm_two_forward(s, windows, s.live)
    saves.append(move(s.hidden, s.kept_hidden))
    saves.append(move(s.second, s.kept_second))
    there[FC1]()
    there[FC2]()
    feed_forward(s, windows)
    saves.append(move(s.active, s.kept_active))
    saves.append(move(s.slope, s.kept_slope))
    there[FC1] = fetch_weight(FC1, 1)
    there[FC2] = fetch_weight(FC2, 1)
    to_dense(s.work, s.plain, s.dense.at[upper], padded)
    upper_there = halo(2, s.dense.at[upper], s.upper, above)

    qkv_saved()
    spread_there = move(s.in_spread, s.spread)
    places_there[1]()
    swaps_there[0]()
    saves.pop(0)()
    move_own(s.work, s.swap_on, s.x, windows, 0)
    spread_columns(s, 1)
    spread_there()
    spread_bias(s, 1)
    region_masks(True, s.regions)
    live_there()
    shifted_live(s, windows)
    grad_there()
    grad_lower_there()
    from_dense(s.grad_upper, s.page, 0)
    from_dense(s.dense.at[lower], s.page, half)
    to_channels(s.page, s.moved, s.grad)
    for saved in saves:
        saved()
    upper_there()
    from_dense(s.upper, s.page, 0)
    add_halo(s.page, s.moved, s.x, half, padded)
    norm_one_forward(s, windows)
    there[QKV]()
    project_forward(s, windows)
    attend_forward(s, windows, s.live_two)
    there[PROJ]()
    s.work[...] = mm(s.w_proj[...], s.merged[...], 0, 0)
    norm_two_forward(s, windows, s.live_two)
    there[FC1]()
    there[FC2]()
    feed_forward(s, windows)
    to_dense(s.work, s.moved, s.dense, s.moved.shape[0])
    out_there = halo(3, s.dense.at[upper], s.out_tokens.at[upper], below)
    out_kept = move(s.dense.at[lower], s.out_tokens.at[lower])

    spread_gains(s, 1)

    def backward(layer, live_ref, fetch, points):
        reducer.layer = layer
        first = 0 if layer else FEEDS
        feed_backward(s, reducer, points[:first])
        reducer.advance(points[first])
        fetch(0)
        norm_two_backward(s, windows, live_ref)
        reducer.advance(points[first + 1])
        fetch(1)
        merge_backward(s, reducer)
        reducer.advance(points[first + 2])
        fetch(2)
        attend_backward(s, windows, reducer, points[first + 3 :])
        fetch(3)

    back = {}

    def refill(point):
        if point == 0:
            back[0] = [move(s.kept_active, s.active), move(s.kept_slope, s.slope), move(s.kept_second, s.second)]
            back[0] += [fetch_weight(FC1, 0), fetch_weight(FC2, 0)]
        elif point == 1:
            back[1] = [move(s.kept_hidden, s.hidden)]
        elif point == 2:
            back[2] = [fetch_weight(PROJ, 0)]
        elif point == 3:
            back[2] += [move(s.kept_merged, s.merged)]
            back[3] = [move(s.kept_soft, s.soft)]
        elif point == 4:
            back[4] = [move(s.kept_x, s.x)]
        else:
            back[3] += [move(s.kept_qkv, s.qkv), move(s.kept_normed, s.normed), fetch_weight(QKV, 0)]

    def needed(point):
        if point in back:
            for arrived in back.pop(point):
                arrived()

    backward(1, s.live_two, refill, range(9))
    input_backward(s)
    norm_one_backward(s, windows)
    refill(4)
    out_there()
    to_dense(s.grad, s.moved, s.dense.at[upper], padded)
    next_there = halo(4, s.dense.at[upper], s.next_upper, below)
    reducer.advance(9)
    project_backward(s, reducer)
    spread_there = move(s.in_spread, s.spread)
    reducer.settle(1)
    reducer.advance(10)

    swaps_there[1]()
    move_own(s.grad, s.swap_back, s.work, windows, -1)
    spread_there()
    small_gradients(s, s.small_own.at[1])
    refill(5)
    spread_gains(s, 0)
    reducer.advance(11)
    next_there()
    from_dense(s.next_upper, s.page, 0)
    s.grad[...] = s.work[...]
    add_halo(s.page, s.plain, s.grad, half, padded)
    reducer.advance(12)
    needed(0)

    def wait_next(point):
        needed(point + 1)

    backward(0, s.live, wait_next, range(13, 26))
    project_backward(s, reducer)
    reducer.settle(1)
    reducer.advance(26)
    input_backward(s)
    spread_there = move(s.in_spread, s.spread)
    reducer.advance(27)
    needed(4)
    norm_one_backward(s, windows)
    out_kept()
    to_dense(s.grad, s.plain, s.dense, s.plain.shape[0])
    grad_kept = move(s.dense, s.grad_tokens)
    reducer.advance(28)
    spread_there()
    small_gradients(s, s.small_own.at[0])
    reducer.advance(29)
    finish_small(s, plan, row)
    grad_kept()


def finish_small(s, plan, row):
    total = s.small_parts.at[plan.halvings - 1]
    outs = (
        (s.d_ln_gain, (G1, G2)),
        (s.d_ln_bias, (B1, B2)),
        (s.d_qv_bias, (QB, VB)),
        (s.d_proj_bias, (PB,)),
        (s.d_fc1_bias, tuple(range(F1B, F1B + FEEDS))),
        (s.d_fc2_bias, (F2B,)),
    )
    for layer in range(2):
        s.d_table[layer] = total[layer, VECTOR_ROWS:, :OFFSETS]
        for ref, indices in outs:
            whole = jnp.concatenate([total[layer, index : index + 1, :] for index in indices], axis=1)
            size = ref.shape[1]
            mine = jnp.zeros((1, size), F32)
            for share in range(plan.shares):
                mine = jnp.where(row == share, whole[:, share * size : (share + 1) * size], mine)
            ref[layer : layer + 1, :] = mine


def placements(cols):
    windows = cols // WIN
    patches = WIN * cols
    padded = -(-patches // LANES) * LANES
    plain = np.zeros((padded, windows * LANES), np.float32)
    moved = np.zeros((padded, windows * LANES), np.float32)
    for line in range(WIN):
        for col in range(cols):
            source = line * cols + col
            plain[source, (col // WIN) * LANES + line * WIN + col % WIN] = 1
            new_line, new_col = (line - SHIFT) % WIN, (col - SHIFT) % cols
            moved[source, (new_col // WIN) * LANES + new_line * WIN + new_col % WIN] = 1
    return plain.astype(BF), moved.astype(BF)


def swaps():
    on = np.zeros((2 * LANES, LANES), np.float32)
    back = np.zeros((2 * LANES, LANES), np.float32)
    for line in range(SHIFT):
        for col in range(WIN):
            moved, plain = line * WIN + col, (line + SHIFT) * WIN + (col + SHIFT) % WIN
            on[plain + (LANES if col >= SHIFT else 0), moved] = 1
            back[moved + (LANES if col < SHIFT else 0), plain] = 1
    return on.astype(BF), back.astype(BF)


def table_spread():
    size = 2 * WIN - 1
    spread = np.zeros((WIN, 2 * LANES, TABLE), np.float32)
    for key_col in range(WIN):
        for offset in range(size):
            for col in range(WIN):
                spread[key_col, offset * WIN + col, offset * size + col - key_col + WIN - 1] = 1
    spread = spread.reshape(WIN // 2, 2, 2 * LANES, TABLE).swapaxes(1, 2)
    return spread.reshape(WIN * LANES, 2 * TABLE).astype(BF)


def copy_all(*refs):
    *refs, sems = refs
    count = len(refs) // 3
    sources, targets, held = refs[:count], refs[count : 2 * count], refs[2 * count :]
    ways = [*zip(sources, held), *zip(held, targets)]
    copies = [pltpu.make_async_copy(*way, sems.at[number]) for number, way in enumerate(ways)]
    for copy in copies[:count]:
        copy.start()
    for incoming, outgoing in zip(copies[:count], copies[count:]):
        incoming.wait()
        outgoing.start()
    for copy in copies[count:]:
        copy.wait()


def hand_out(values):
    anywhere = pl.BlockSpec(memory_space=pl.ANY)
    return pl.pallas_call(
        copy_all,
        out_shape=[jax.ShapeDtypeStruct(value.shape, value.dtype) for value in values],
        in_specs=[anywhere] * len(values),
        out_specs=[anywhere] * len(values),
        scratch_shapes=[pltpu.VMEM(value.shape, value.dtype) for value in values]
        + [pltpu.SemaphoreType.DMA((2 * len(values),))],
        compiler_params=pltpu.CompilerParams(vmem_limit_bytes=VMEM_LIMIT),
        name="results",
    )(*values)


def per_device(
    page_tokens,
    blank_mask,
    cotangent,
    ln_gain,
    ln_bias,
    qv_bias,
    rel_table,
    w_qkv,
    w_proj,
    proj_bias,
    w_fc1,
    fc1_bias,
    w_fc2,
    fc2_bias,
):
    pages, shares = lax.axis_size(PAGE), lax.axis_size(ROW)
    plan = Plan(pages, shares)
    cols = page_tokens.shape[2]
    windows, lanes = cols // WIN, cols // WIN * LANES
    dense = ((WIN * cols * SPLITS, LANES), F32)
    half_dense = ((WIN * cols * SPLITS // 2, LANES), F32)
    plain, moved = (jnp.asarray(place) for place in placements(cols))
    live_rows = 8 * -(-windows // 8)
    scalar_inputs = dict(blank=blank_mask[0])
    small_inputs = dict(
        table=rel_table,
        ln_gain=ln_gain,
        ln_bias=ln_bias,
        qv_bias=qv_bias,
        proj_bias=proj_bias,
        fc1_bias=fc1_bias,
        fc2_bias=fc2_bias,
    )
    large_inputs = dict(
        in_tokens=page_tokens[0],
        in_grad=cotangent.reshape(dense[0]),
        in_plain=plain,
        in_moved=moved,
        in_swap_on=jnp.asarray(swaps()[0]),
        in_swap_back=jnp.asarray(swaps()[1]),
        in_spread=jnp.asarray(table_spread()),
        in_qkv=w_qkv,
        in_proj=w_proj,
        in_fc1=w_fc1,
        in_fc2=w_fc2,
    )
    saved = dict(
        x=((D, lanes), F32),
        normed=((D, lanes), BF),
        qkv=((3 * D, lanes), BF),
        soft=((windows * HEADS, LANES, LANES), BF),
        merged=((D, lanes), BF),
        hidden=((D, lanes), F32),
        second=((D, lanes), BF),
        active=((FF, lanes), BF),
        slope=((FF, lanes), BF),
    )
    units = ((UNITS, shares, CHUNK // shares, CHUNK), F32)
    large_outputs = dict(
        out_tokens=dense,
        grad_tokens=dense,
        sum_qkv=((2, D // shares, 3 * D), F32),
        sum_proj=((2, D // shares, D), F32),
        sum_fc1=((2, D // shares, FF), F32),
        sum_fc2=((2, FF // shares, D), F32),
        units_zero=units,
        units_one=units,
        kept_x=((D, lanes), F32),
        kept_normed=((D, lanes), BF),
        kept_qkv=((3 * D, lanes), BF),
        kept_soft=((windows * HEADS, LANES, LANES), BF),
        kept_merged=((D, lanes), BF),
        kept_hidden=((D, lanes), F32),
        kept_second=((D, lanes), BF),
        kept_active=((FF, lanes), BF),
        kept_slope=((FF, lanes), BF),
    )
    small_outputs = dict(
        d_ln_gain=((2, 2 * D // shares), F32),
        d_ln_bias=((2, 2 * D // shares), F32),
        d_qv_bias=((2, 2 * D // shares), F32),
        d_proj_bias=((2, D // shares), F32),
        d_fc1_bias=((2, FF // shares), F32),
        d_fc2_bias=((2, D // shares), F32),
        d_table=((2, HEADS, OFFSETS), F32),
    )
    small = (2, SMALL, D)
    vmem = dict(
        saved,
        tokens=((WIN, cols, D), BF),
        plain=(plain.shape, BF),
        moved=(moved.shape, BF),
        w_qkv=((D, 3 * D), BF),
        w_proj=((D, D), BF),
        w_fc1=((D, FF), BF),
        w_fc2=((FF, D), BF),
        dense=dense,
        upper=half_dense,
        swap_on=((2 * LANES, LANES), BF),
        swap_back=((2 * LANES, LANES), BF),
        grad_upper=half_dense,
        next_upper=half_dense,
        live_upper=((live_rows, LANES), F32),
        live_two=((live_rows, LANES), F32),
        work=((D, lanes), F32),
        grad=((D, lanes), F32),
        low=((D, lanes), BF),
        sums=((VECTORS, D, LANES), F32),
        gains=((2, D, LANES), F32),
        bias=((HEADS, LANES, LANES), F32),
        bias_rows=((HEADS * LANES, LANES), F32),
        regions=((2, LANES, LANES), F32),
        padded_table=((HEADS, TABLE), F32),
        live=((live_rows, LANES), F32),
        vector_rows=((VECTOR_ROWS, D), F32),
        staged=((2 * CHUNK, CHUNK), F32),
        done=((DONE * CLASSES, CHUNK // shares, CHUNK), F32),
        held=((HELD * CLASSES, shares, CHUNK // shares, CHUNK // 2), F32),
        small_own=(small, F32),
        small_parts=((plan.halvings,) + small, F32),
    )
    semaphores = dict(
        move_sems=pltpu.SemaphoreType.DMA((48,)),
        halo_sems=pltpu.SemaphoreType.DMA((2, 5)),
        send_sems=pltpu.SemaphoreType.DMA((2 * UNITS, plan.phases)),
        recv_sems=pltpu.SemaphoreType.DMA((2 * UNITS, plan.phases)),
        own_sems=pltpu.SemaphoreType.DMA((2 * UNITS, 2)),
        stage_sems=pltpu.SemaphoreType.DMA((2, shares)),
        small_sems=pltpu.SemaphoreType.DMA((2, plan.halvings)),
        free_sems=pltpu.SemaphoreType.REGULAR((CLASSES, plan.halvings)),
    )
    landing = [((RING,) + size, F32) for sizes in plan.sizes for size in sizes]
    layout = [*scalar_inputs, *small_inputs, *large_inputs, *small_outputs, *large_outputs, *vmem, *semaphores]
    in_vmem, anywhere = pl.BlockSpec(memory_space=pltpu.VMEM), pl.BlockSpec(memory_space=pl.ANY)
    outputs = {**small_outputs, **large_outputs}
    results = pl.pallas_call(
        functools.partial(run, plan, layout),
        out_shape=[jax.ShapeDtypeStruct(*shape) for shape in outputs.values()],
        in_specs=[pl.BlockSpec(memory_space=pltpu.SMEM)] + [in_vmem] * len(small_inputs) + [anywhere] * len(large_inputs),
        out_specs=[in_vmem] * len(small_outputs) + [anywhere] * len(large_outputs),
        scratch_shapes=[pltpu.VMEM(*shape) for shape in vmem.values()]
        + list(semaphores.values())
        + [pltpu.VMEM(*shape) for shape in landing],
        compiler_params=pltpu.CompilerParams(
            vmem_limit_bytes=VMEM_LIMIT, collective_id=0, has_side_effects=True
        ),
        name="two_layers",
    )(*scalar_inputs.values(), *small_inputs.values(), *large_inputs.values())
    results = hand_out(results[: len(small_outputs) + 6])
    d_ln_gain, d_ln_bias, d_qv_bias, d_proj_bias, d_fc1_bias, d_fc2_bias, d_table = results[: len(small_outputs)]
    out_tokens, grad_tokens, sum_qkv, sum_proj, sum_fc1, sum_fc2 = results[len(small_outputs) :]
    return (
        out_tokens.reshape(cotangent.shape),
        grad_tokens.reshape(cotangent.shape),
        d_ln_gain,
        d_ln_bias,
        d_qv_bias,
        d_table,
        sum_qkv,
        sum_proj,
        d_proj_bias,
        sum_fc1,
        d_fc1_bias,
        sum_fc2,
        d_fc2_bias,
    )


def solution(mesh):
    tokens, by_row, shares = P(PAGE, ROW, None, None), P(None, ROW), P(None, ROW, None)
    return jax.shard_map(
        per_device,
        mesh=mesh,
        in_specs=(tokens, P(PAGE, ROW, None), tokens) + (P(),) * 11,
        out_specs=(tokens, tokens)
        + (by_row, by_row, by_row, P(), shares, shares, by_row, shares, by_row, shares, by_row),
        check_vma=False,
    )
```

```python
import functools

import jax
import jax.numpy as jnp
import numpy as np
from jax import lax
from jax.experimental import pallas as pl
from jax.experimental.pallas import tpu as pltpu
from jax.sharding import PartitionSpec as P

WIN = 10
SHIFT = 5
AREA = WIN * WIN
LANES = 128
D = 512
HEADS = 16
HEAD_DIM = 32
FF = 2048
CHUNK = 512
FEEDS = FF // CHUNK
ABREAST = 2
SPLITS = D // LANES
EPSILON = 1e-05
MASK_VALUE = -100.0
NEVER = -1e30
SCORE_SCALE = HEAD_DIM ** (-0.5)
VMEM_LIMIT = 63 * 1024 * 1024 + 512 * 1024
BF = jnp.bfloat16
F32 = jnp.float32
MESH = pl.DeviceIdType.MESH
PAGE, ROW = "page", "row"

G1, B1, G2, B2, QB, VB, PB, F2B, F1B, VECTORS = 0, 1, 2, 3, 4, 5, 6, 7, 8, 12
VECTOR_ROWS = 16
SMALL = VECTOR_ROWS + HEADS
OFFSETS = (2 * WIN - 1) ** 2
TABLE = 384

UNIT_FC1, UNIT_FC2, UNIT_PROJ, UNIT_QKV, UNITS = 0, 4, 8, 9, 12
CLASSES = 3
GROUPS = UNITS // CLASSES
TRIPLES = 2 * GROUPS
HELD = 4
DONE = 5
RING = 3
QKV, PROJ, FC1, FC2 = range(4)
TARGETS = (
    ((FC1, 0, 0), (FC1, 0, 1), (FC1, 0, 2)),
    ((FC1, 0, 3), (FC2, 0, 0), (FC2, 1, 0)),
    ((FC2, 2, 0), (FC2, 3, 0), (PROJ, 0, 0)),
    ((QKV, 0, 0), (QKV, 0, 1), (QKV, 0, 2)),
)


def mm(left, right, left_dim, right_dim):
    return lax.dot_general(
        left, right, (((left_dim,), (right_dim,)), ((), ())), preferred_element_type=F32
    )


def split(values):
    high = values.astype(BF)
    return high, (values - high.astype(F32)).astype(BF)


def lane_tile(index):
    return pl.ds(pl.multiple_of(index * LANES, LANES), LANES)


def chunk_of(index):
    return pl.ds(pl.multiple_of(index * CHUNK, CHUNK), CHUNK)


def wide(column, count):
    return jnp.concatenate([column] * count, axis=1)


def fold(values):
    total = values[:, :LANES]
    for start in range(LANES, values.shape[1], LANES):
        total = total + values[:, start : start + LANES]
    return total


def norm_parts(values):
    center = values - jnp.sum(values, axis=0, keepdims=True) * (1.0 / D)
    spread = jnp.sum(center * center, axis=0, keepdims=True) * (1.0 / D)
    scale = lax.rsqrt(spread + EPSILON)
    return center * scale, scale


def norm_pull(grad, gain, hat, scale):
    scaled = grad * gain
    mean_one = jnp.sum(scaled, axis=0, keepdims=True) * (1.0 / D)
    mean_two = jnp.sum(scaled * hat, axis=0, keepdims=True) * (1.0 / D)
    return scale * (scaled - mean_one - hat * mean_two)


def gelu_parts(inner):
    step = 1.0 / (1.0 + (0.3275911 * 0.7071067811865476) * jnp.abs(inner))
    bell = jnp.exp(inner * inner * -0.5)
    poly = 0.5 * 1.061405429
    for factor in (-1.453152027, 1.421413741, -0.284496736, 0.254829592):
        poly = poly * step + 0.5 * factor
    tail = poly * step * bell
    below = jnp.where(inner >= 0, 1.0 - tail, tail)
    return inner * below, below + inner * bell * 0.3989422804014327


def to_channels(page_ref, place_ref, out_ref, exact=False):
    def step(index, carry):
        channels = pl.ds(pl.multiple_of(index * 256, 256), 256)
        values = page_ref[:, channels]
        if exact:
            out_ref[channels, :] = mm(values.astype(BF), place_ref[...], 0, 0)
        else:
            high, low = split(values)
            out_ref[channels, :] = mm(high, place_ref[...], 0, 0) + mm(low, place_ref[...], 0, 0)
        return carry

    lax.fori_loop(0, D // 256, step, 0)


def to_dense(values_ref, place_ref, dense_ref, padded):
    count = dense_ref.shape[0] // SPLITS
    for index in range(D // 256):
        high, low = split(values_ref[index * 256 : (index + 1) * 256, :])
        page = mm(place_ref[:padded, :], high, 1, 1) + mm(place_ref[:padded, :], low, 1, 1)
        for part in range(2):
            rows = pl.ds(2 * index + part, count, stride=SPLITS)
            dense_ref[rows, :] = page[:count, part * LANES : (part + 1) * LANES]


def from_dense(dense_ref, page_ref, row):
    count = dense_ref.shape[0] // SPLITS
    for part in range(SPLITS):
        rows = pl.ds(part, count, stride=SPLITS)
        page_ref[pl.ds(row, count), part * LANES : (part + 1) * LANES] = dense_ref[rows, :]


def add_halo(page_ref, place_ref, out_ref, count, padded):
    page_ref[pl.ds(count, padded - count), :] = jnp.zeros((padded - count, D), F32)

    def step(index, carry):
        channels = pl.ds(pl.multiple_of(index * 256, 256), 256)
        high, low = split(page_ref[:padded, channels])
        out_ref[channels, :] += mm(high, place_ref[:padded, :], 0, 0) + mm(low, place_ref[:padded, :], 0, 0)
        return carry

    lax.fori_loop(0, D // 256, step, 0)


def move_own(values_ref, swap_ref, out_ref, windows, first):
    for window in range(windows):
        sources = [(window + first + part) % windows * LANES for part in range(2)]
        values = jnp.concatenate([values_ref[:, start : start + LANES] for start in sources], axis=1)
        high, low = split(values)
        target = slice(window * LANES, (window + 1) * LANES)
        out_ref[:, target] = mm(high, swap_ref[...], 1, 0) + mm(low, swap_ref[...], 1, 0)


def vector_rows(s, layer):
    rows = s.vector_rows
    sources = ((G1, s.ln_gain, 0), (B1, s.ln_bias, 0), (G2, s.ln_gain, 1), (B2, s.ln_bias, 1))
    sources += ((QB, s.qv_bias, 0), (VB, s.qv_bias, 1), (PB, s.proj_bias, 0), (F2B, s.fc2_bias, 0))
    sources += tuple((F1B + part, s.fc1_bias, part) for part in range(FEEDS))
    for index, source, part in sources:
        rows[index : index + 1, :] = source[layer : layer + 1, part * D : (part + 1) * D]
    rows[VECTORS:, :] = jnp.zeros((VECTOR_ROWS - VECTORS, D), F32)
    return rows[...].T


def spread_columns(s, layer):
    columns = vector_rows(s, layer)
    for index in range(VECTORS):
        s.sums[index] = jnp.broadcast_to(columns[:, index : index + 1], (D, LANES))


def spread_gains(s, layer):
    columns = vector_rows(s, layer)
    for index, vector in enumerate((G1, G2)):
        s.gains[index] = jnp.broadcast_to(columns[:, vector : vector + 1], (D, LANES))


def spread_part(col):
    rows, lanes = (col // 2) * 2 * LANES, (col % 2) * TABLE
    return slice(rows, rows + 2 * LANES), slice(lanes, lanes + TABLE)


def spread_bias(s, layer):
    spread_ref, rows_ref, bias_ref = s.spread, s.bias_rows, s.bias
    s.padded_table[...] = jnp.zeros(s.padded_table.shape, F32)
    s.padded_table[:, :OFFSETS] = s.table[layer]
    high, low = split(s.padded_table[...])
    parts = []
    for col in range(WIN):
        chosen = spread_ref[spread_part(col)]
        parts.append(mm(high, chosen, 1, 1) + mm(low, chosen, 1, 1))
    source = jnp.concatenate(parts, axis=0)
    rows_ref[...] = jnp.zeros(rows_ref.shape, F32)
    for row in range(WIN):
        shift = (WIN - 1 - row) * WIN
        moved = source if shift == 0 else pltpu.roll(source, 2 * LANES - shift, axis=1)
        rows_ref[pl.ds(row * WIN * HEADS, WIN * HEADS), :] = moved[:, :LANES]
    for head in range(HEADS):
        bias_ref[head] = rows_ref[pl.ds(head, LANES, stride=HEADS), :]


def gather_bias(grad_ref, spread_ref, rows_ref):
    for head in range(HEADS):
        rows_ref[pl.ds(head, LANES, stride=HEADS), :] = grad_ref[head]
    total = jnp.zeros((WIN * HEADS, 2 * LANES), F32)
    for row in range(WIN):
        shift = (WIN - 1 - row) * WIN
        piece = rows_ref[pl.ds(row * WIN * HEADS, WIN * HEADS), :]
        piece = jnp.concatenate([piece, jnp.zeros_like(piece)], axis=1)
        total = total + (piece if shift == 0 else pltpu.roll(piece, shift, axis=1))
    table = jnp.zeros((HEADS, TABLE), F32)
    for col in range(WIN):
        for part in split(total[col * HEADS : (col + 1) * HEADS]):
            table = table + mm(part, spread_ref[spread_part(col)], 1, 0)
    return table


def region_masks(shifted_layer, out_ref):
    key = lax.broadcasted_iota(jnp.int32, (LANES, LANES), 0)
    query = lax.broadcasted_iota(jnp.int32, (LANES, LANES), 1)
    padding = jnp.where(key < AREA, 0.0, NEVER)
    out_ref[0] = padding
    out_ref[1] = padding
    if shifted_layer:
        last = lax.axis_index(ROW) == lax.axis_size(ROW) - 1
        rows_differ = ((key >= AREA // 2) != (query >= AREA // 2)) & last
        cols_differ = (key % WIN >= SHIFT) != (query % WIN >= SHIFT)
        out_ref[0] += jnp.where(rows_differ, MASK_VALUE, 0.0)
        out_ref[1] += jnp.where(rows_differ | cols_differ, MASK_VALUE, 0.0)


def shifted_live(s, windows):
    place = lax.broadcasted_iota(jnp.int32, (1, LANES), 1)
    for window in range(windows):
        here, after = slice(window, window + 1), slice((window + 1) % windows, (window + 1) % windows + 1)
        beyond = place % WIN >= SHIFT
        own = jnp.where(beyond, s.live[after, :], s.live[here, :])
        upper = jnp.where(beyond, s.live_upper[after, :], s.live_upper[here, :])
        s.live_two[here, :] = jnp.where(place >= AREA // 2, upper, own)


def head_rows(head, base=0):
    return pl.ds(base + head * HEAD_DIM, HEAD_DIM)


def norm_one_forward(s, windows):
    def step(index, carry):
        lanes = lane_tile(index)
        hat, _ = norm_parts(s.x[:, lanes])
        s.normed[:, lanes] = (hat * s.sums[G1] + s.sums[B1]).astype(BF)
        return carry

    lax.fori_loop(0, windows, step, 0, unroll=2)


def project_forward(s, windows):
    def step(index, carry):
        rows = chunk_of(index)
        bias = s.sums[jnp.where(index == 0, QB, VB)] * jnp.where(index == 1, 0.0, 1.0)
        out = mm(s.w_qkv[:, rows], s.normed[...], 0, 0)
        s.qkv[rows, :] = (out + wide(bias, windows)).astype(BF)
        return carry

    lax.fori_loop(0, 3, step, 0)


def attend_forward(s, windows, live_ref):
    def step(index, carry):
        lanes = lane_tile(index)
        live = jnp.broadcast_to(live_ref[pl.ds(index, 1), :], (LANES, LANES)).T
        masked = s.regions[jnp.where(index == windows - 1, 1, 0)] + MASK_VALUE * (1.0 - live)
        for head in range(HEADS):
            query = s.qkv[head_rows(head), lanes]
            key = s.qkv[head_rows(head, D), lanes]
            value = s.qkv[head_rows(head, 2 * D), lanes]
            scores = mm(key, query, 0, 0) * SCORE_SCALE + (s.bias[head] + masked)
            exponent = jnp.exp(scores - jnp.max(scores, axis=0, keepdims=True))
            total = jnp.sum(exponent, axis=0, keepdims=True)
            soft = (exponent * (1.0 / total)).astype(BF)
            s.soft[index * HEADS + head] = soft
            s.merged[head_rows(head), lanes] = mm(value, soft, 1, 0).astype(BF)
        return carry

    lax.fori_loop(0, windows, step, 0, unroll=2)


def norm_two_forward(s, windows, live_ref):
    def step(index, carry):
        lanes = lane_tile(index)
        hidden = s.x[:, lanes] + live_ref[pl.ds(index, 1), :] * (s.work[:, lanes] + s.sums[PB])
        s.hidden[:, lanes] = hidden
        s.work[:, lanes] = hidden + s.sums[F2B]
        hat, _ = norm_parts(hidden)
        s.second[:, lanes] = (hat * s.sums[G2] + s.sums[B2]).astype(BF)
        return carry

    lax.fori_loop(0, windows, step, 0, unroll=2)


def feed_forward(s, windows):
    def step(index, carry):
        rows = chunk_of(index)
        inner = mm(s.w_fc1[:, rows], s.second[...], 0, 0) + wide(s.sums[F1B + index], windows)
        active, slope = gelu_parts(inner)
        active = active.astype(BF)
        s.active[rows, :] = active
        s.slope[rows, :] = slope.astype(BF)
        s.work[...] += mm(s.w_fc2[rows, :], active, 0, 0)
        return carry

    lax.fori_loop(0, FEEDS, step, 0)


def feed_backward(s, sink, times):
    s.sums[...] = jnp.zeros(s.sums.shape, F32)
    s.bias[...] = jnp.zeros(s.bias.shape, F32)
    lowered = s.grad[...].astype(BF)
    s.low[...] = lowered
    s.sums[F2B] = fold(lowered.astype(F32))
    s.work[...] = jnp.zeros(s.work.shape, F32)

    def step(index, carry):
        rows = chunk_of(index)
        sink.put(0, mm(s.active[rows, :], s.low[...], 1, 1), feed_pieces(index, sink.shares), index == 0)
        grad_inner = mm(s.w_fc2[rows, :], s.low[...], 1, 0) * s.slope[rows, :].astype(F32)
        grad_inner = grad_inner.astype(BF)
        s.sums[F1B + index] = fold(grad_inner.astype(F32))
        sink.put(1, mm(s.second[...], grad_inner, 1, 1), row_pieces(UNIT_FC1 + index, sink.shares), index == 0)
        s.work[...] += mm(s.w_fc1[:, rows], grad_inner, 1, 0)
        sink.advance_at(index, times)
        return carry

    lax.fori_loop(0, FEEDS, step, 0)
    sink.settle(0)
    sink.settle(1)


def norm_two_backward(s, windows, live_ref):
    def step(index, carry):
        lanes = lane_tile(index)
        hat, scale = norm_parts(s.hidden[:, lanes])
        grad = s.work[:, lanes]
        s.sums[G2] += grad * hat
        s.sums[B2] += grad
        grad = s.grad[:, lanes] + norm_pull(grad, s.gains[1], hat, scale)
        s.grad[:, lanes] = grad
        grad_low = (grad * live_ref[pl.ds(index, 1), :]).astype(BF)
        s.low[:, lanes] = grad_low
        s.sums[PB] += grad_low.astype(F32)
        return carry

    lax.fori_loop(0, windows, step, 0, unroll=2)


def merge_backward(s, sink):
    sink.put(0, mm(s.merged[...], s.low[...], 1, 1), row_pieces(UNIT_PROJ, sink.shares), True)
    s.merged[...] = mm(s.w_proj[...], s.low[...], 1, 0).astype(BF)
    sink.settle(0)


def attend_backward(s, windows, sink, times):
    def window(index):
        lanes = lane_tile(index)
        for head in range(HEADS):
            query = s.qkv[head_rows(head), lanes]
            key = s.qkv[head_rows(head, D), lanes]
            value = s.qkv[head_rows(head, 2 * D), lanes]
            grad_out = s.merged[head_rows(head), lanes]
            soft_low = s.soft[index * HEADS + head]
            soft = soft_low.astype(F32)
            grad_soft = mm(value, grad_out, 0, 0)
            inner = jnp.sum(soft * grad_soft, axis=0, keepdims=True)
            grad_scores = (soft * (grad_soft - inner)).astype(BF)
            s.bias[head] += grad_scores.astype(F32)
            grad_query = (mm(key, grad_scores, 1, 0) * SCORE_SCALE).astype(BF)
            grad_key = (mm(query, grad_scores, 1, 1) * SCORE_SCALE).astype(BF)
            grad_value = mm(grad_out, soft_low, 1, 1).astype(BF)
            s.qkv[head_rows(head), lanes] = grad_query
            s.qkv[head_rows(head, D), lanes] = grad_key
            s.qkv[head_rows(head, 2 * D), lanes] = grad_value
            s.sums[QB, head_rows(head), :] += grad_query.astype(F32)
            s.sums[VB, head_rows(head), :] += grad_value.astype(F32)

    def step(index, carry):
        for part in range(ABREAST):
            window(ABREAST * index + part)
        sink.advance_at(index, times)
        return carry

    lax.fori_loop(0, windows // ABREAST, step, 0)


def project_backward(s, sink):
    def step(index, carry):
        rows = chunk_of(index)
        sink.put(1, mm(s.normed[...], s.qkv[rows, :], 1, 1), row_pieces(UNIT_QKV + index, sink.shares), index == 0)
        return carry

    lax.fori_loop(0, 3, step, 0)


def input_backward(s):
    s.work[...] = mm(s.w_qkv[...], s.qkv[...], 1, 0)


def norm_one_backward(s, windows):
    def step(index, carry):
        lanes = lane_tile(index)
        hat, scale = norm_parts(s.x[:, lanes])
        grad = s.work[:, lanes]
        s.sums[G1] += grad * hat
        s.sums[B1] += grad
        s.grad[:, lanes] += norm_pull(grad, s.gains[0], hat, scale)
        return carry

    lax.fori_loop(0, windows, step, 0, unroll=2)


def small_gradients(s, small_ref):
    places = lax.broadcasted_iota(jnp.int32, (D, LANES), 1)
    packed = jnp.zeros((D, LANES), F32)
    for index in range(VECTORS):
        packed = jnp.where(places == index, jnp.sum(s.sums[index], axis=1, keepdims=True), packed)
    small_ref[:VECTOR_ROWS, :] = packed.T[:VECTOR_ROWS]
    table = gather_bias(s.bias, s.spread, s.bias_rows)
    small_ref[VECTOR_ROWS:, :] = jnp.concatenate([table, jnp.zeros((HEADS, D - TABLE), F32)], axis=1)


def reversed_bits(value, count):
    turned = 0
    for bit in range(count):
        turned = turned * 2 + (value // 2**bit) % 2
    return turned


def row_pieces(unit, shares):
    rows, count = CHUNK // shares, shares.bit_length() - 1
    return [(share * rows, unit, reversed_bits(share, count)) for share in range(shares)]


def feed_pieces(index, shares):
    rows, count = CHUNK // shares, shares.bit_length() - 1
    pieces = []
    for share in range(shares // FEEDS):
        place = reversed_bits(index * (shares // FEEDS) + share, count)
        for part in range(FEEDS):
            pieces.append(((share * FEEDS + part) * rows, UNIT_FC2 + part, place))
    return pieces


class Plan:
    def __init__(self, pages, shares):
        self.shares, self.rows = shares, CHUNK // shares
        page_bits, row_bits = pages.bit_length() - 1, shares.bit_length() - 1
        others = page_bits - 1
        self.steps = []
        for kind in range(CLASSES):
            turn = kind % 2
            page = [(PAGE, 2 ** (1 + (bit + turn) % others)) for bit in range(others)]
            row = [(ROW, 2**bit) for bit in range(row_bits)]
            self.steps.append([(PAGE, 1)] + (row + page if kind == 2 else page + row))
        self.page_steps = [[0] + [at for at, step in enumerate(steps) if at and step[0] == PAGE] for steps in self.steps]
        self.halvings = page_bits + row_bits
        self.phases = self.halvings + page_bits
        self.sizes = []
        for kind in range(CLASSES):
            size = [shares, self.rows, CHUNK // 2]
            sizes = [tuple(size)]
            for level in range(1, self.halvings):
                size[self.split_axis(kind, level)] //= 2
                sizes.append(tuple(size))
            self.sizes.append(sizes)
        self.steps_at = self.schedule()

    def schedule(self):
        small = TRIPLES
        free, ready, stage_of, plan, now = {}, {}, {}, [], 0.0
        for triple in range(TRIPLES):
            for kind in range(CLASSES):
                stage_of[triple, kind] = 0
        stage_of[small, 0] = 0

        def link(key, phase):
            triple, kind = key
            if phase < self.halvings:
                axis, stride = self.steps[kind][phase]
                size = 2.0**-phase / 2 if triple != small else 0.125
            else:
                axis, stride = self.steps[kind][self.page_steps[kind][self.phases - 1 - phase]]
                size = 2.0 ** (phase - 2 * self.halvings)
            if axis == PAGE and stride == 1:
                return 0, size * PLAN_CORE
            return (axis, stride if axis == PAGE else 0), size * PLAN_LINK * (1.0 if stride == 1 or axis == PAGE else 1.5)

        def last_stage(key):
            return self.halvings if key[0] == small else self.phases + 1

        def allowed(key, point):
            triple, kind = key
            stage = stage_of[key]
            if stage > last_stage(key):
                return False
            if triple == small:
                return point >= len(PLAN_POINTS) - 1
            if stage == 0 and point < PLAN_THERE[triple]:
                return False
            if triple > 0 and stage_of[triple - 1, kind] <= stage:
                return False
            if triple >= RING and stage < self.halvings and stage_of[triple - RING, kind] <= stage + 1:
                return False
            if stage == 0 and triple >= DONE and stage_of[triple - DONE, kind] <= self.phases + 1:
                return False
            return not (stage == 0 and triple >= HELD and stage_of[triple - HELD, kind] <= self.halvings + 1)

        for point, work in enumerate(PLAN_POINTS):
            now += work
            if point == PLAN_HALO:
                free[ROW, 0] = max(now, free.get((ROW, 0), 0.0)) + PLAN_HALO_TIME
            steps, final = [], point == len(PLAN_POINTS) - 1
            while True:
                keys = [key for key in stage_of if allowed(key, point)]
                keys = [key for key in keys if final or ready.get(key, 0.0) <= now + PLAN_SLACK]
                if not keys:
                    break
                key = min(keys, key=lambda key: (max(ready.get(key, 0.0), now), -stage_of[key], key))
                stage = stage_of[key]
                now = max(now, ready.get(key, 0.0)) + (PLAN_ADD * 2.0**-stage if stage else 0.0)
                if stage == self.phases:
                    ready[key] = now + PLAN_LATENCY
                elif stage < last_stage(key):
                    name, length = link(key, stage)
                    free[name] = max(now, free.get(name, 0.0)) + length
                    ready[key] = free[name] + PLAN_LATENCY
                steps.append((*key, stage))
                stage_of[key] += 1
            plan.append(steps)
        assert all(stage_of[key] > last_stage(key) for key in stage_of)
        return plan

    def split_axis(self, kind, level):
        if self.steps[kind][level][0] == ROW:
            return 0
        return 2 if self.page_steps[kind].index(level) < 2 else 1

    def partner(self, kind, level):
        axis, stride = self.steps[kind][level]
        page, row = lax.axis_index(PAGE), lax.axis_index(ROW)
        mine = page if axis == PAGE else row
        bit = (mine // stride) % 2
        other = mine + (1 - 2 * bit) * stride
        return bit, ((other, row) if axis == PAGE else (page, other))

    def part(self, kind, level, sent=False):
        starts, sizes = [0, 0, 0], [self.shares, self.rows, CHUNK // 2]
        for at in range(1, level + 1):
            axis = self.split_axis(kind, at)
            sizes[axis] //= 2
            bit, _ = self.partner(kind, at)
            which = 1 - bit if sent and at == level else bit
            starts[axis] = starts[axis] + which * sizes[axis]
        return (
            pl.ds(starts[0], sizes[0]),
            pl.ds(pl.multiple_of(starts[1], 8), sizes[1]),
            pl.ds(pl.multiple_of(starts[2], LANES), sizes[2]),
        )

    def place(self, kind, count):
        starts, sizes = [0, 0], [self.rows, CHUNK]
        for at in self.page_steps[kind][:count]:
            axis = self.split_axis(kind, at) - 1 if at else 1
            sizes[axis] //= 2
            bit, _ = self.partner(kind, at)
            starts[axis] = starts[axis] + bit * sizes[axis]
        return starts, sizes


class Reducer:
    def __init__(self, plan, s):
        self.plan, self.s = plan, s
        self.shares = plan.shares
        self.layer = 1

    def stage_copies(self, slot, pieces):
        return [
            pltpu.make_async_copy(
                self.s.staged.at[pl.ds(slot * CHUNK + start, self.plan.rows)],
                self.s.units[self.layer].at[unit, place],
                self.s.stage_sems.at[slot, number],
            )
            for number, (start, unit, place) in enumerate(pieces)
        ]

    def put(self, slot, grad, pieces, first):
        if first is not True:

            @pl.when(jnp.logical_not(first))
            def _():
                self.settle(slot)

        self.s.staged[pl.ds(slot * CHUNK, CHUNK), :] = grad
        for copy in self.stage_copies(slot, pieces):
            copy.start()

    def settle(self, slot):
        for copy in self.stage_copies(slot, row_pieces(0, self.shares)):
            copy.wait()

    def remote(self, source, target, unit, phase, device):
        return pltpu.make_async_remote_copy(
            src_ref=source,
            dst_ref=target,
            send_sem=self.s.send_sems.at[unit, phase],
            recv_sem=self.s.recv_sems.at[unit, phase],
            device_id=device,
            device_id_type=MESH,
        )

    def unit_half(self, triple, kind, which):
        layer, half = 1 - triple // GROUPS, CHUNK // 2
        unit = CLASSES * (triple % GROUPS) + kind
        return self.s.units[layer].at[unit, :, :, pl.ds(pl.multiple_of(which * half, half), half)]

    def held(self, triple, kind):
        return self.s.held.at[CLASSES * (triple % HELD) + kind]

    def halving(self, triple, kind, level):
        plan = self.plan
        bit, device = plan.partner(kind, level)
        target = self.s.landing[kind][level].at[triple % RING]
        if level == 0:
            source = self.unit_half(triple, kind, 1 - bit)
        else:
            source = self.held(triple, kind).at[plan.part(kind, level, True)]
        return self.remote(source, target, CLASSES * triple + kind, level, device)

    def own_half(self, triple, kind):
        bit, _ = self.plan.partner(kind, 0)
        sem = self.s.own_sems.at[CLASSES * triple + kind, 0]
        return pltpu.make_async_copy(self.unit_half(triple, kind, bit), self.held(triple, kind), sem)

    def finished(self, triple, kind):
        return self.held(triple, kind).at[self.plan.part(kind, self.plan.halvings - 1)].at[0]

    def done(self, triple, kind, count):
        starts, sizes = self.plan.place(kind, count)
        return self.s.done.at[
            CLASSES * (triple % DONE) + kind,
            pl.ds(pl.multiple_of(starts[0], 8), sizes[0]),
            pl.ds(pl.multiple_of(starts[1], LANES), sizes[1]),
        ]

    def gathering(self, triple, kind, phase):
        plan = self.plan
        count = len(plan.page_steps[kind]) - (phase - plan.halvings)
        part = self.done(triple, kind, count)
        _, device = plan.partner(kind, plan.page_steps[kind][count - 1])
        return self.remote(part, part, CLASSES * triple + kind, phase, device)

    def result(self, triple, kind):
        which, row_block, col_block = TARGETS[triple % GROUPS][kind]
        rows = self.plan.rows
        target = self.s.results[which].at[
            1 - triple // GROUPS, pl.ds(row_block * rows, rows), pl.ds(col_block * CHUNK, CHUNK)
        ]
        sem = self.s.own_sems.at[CLASSES * triple + kind, 1]
        return pltpu.make_async_copy(self.done(triple, kind, 0), target, sem)

    def start(self, triple, kind, phase):
        plan = self.plan
        if phase < plan.halvings:
            if triple >= RING:
                pl.semaphore_wait(self.s.free_sems.at[kind, phase], 1)
            self.halving(triple, kind, phase).start()
            if phase == 0:
                self.own_half(triple, kind).start()
        elif phase < plan.phases:
            if phase == plan.halvings:
                self.done(triple, kind, len(plan.page_steps[kind]))[...] = self.finished(triple, kind)[...]
            self.gathering(triple, kind, phase).start()
        elif phase == plan.phases:
            self.result(triple, kind).start()

    def finish(self, triple, kind, phase):
        plan, s = self.plan, self.s
        if phase < plan.halvings:
            self.halving(triple, kind, phase).wait()
            if phase == 0:
                self.own_half(triple, kind).wait()
            landed = s.landing[kind][phase].at[triple % RING]
            kept = self.held(triple, kind).at[plan.part(kind, phase)]
            for share in range(landed.shape[0]):
                kept[share] += landed[share]
            if triple < TRIPLES - RING:
                _, device = plan.partner(kind, phase)
                pl.semaphore_signal(s.free_sems.at[kind, phase], inc=1, device_id=device, device_id_type=MESH)
        elif phase < plan.phases:
            self.gathering(triple, kind, phase).wait()
        else:
            self.result(triple, kind).wait()

    def advance(self, point):
        for triple, kind, stage in self.plan.steps_at[point]:
            if triple == TRIPLES:
                self.small_step(stage - 1)
                continue
            if stage > 0:
                self.finish(triple, kind, stage - 1)
            self.start(triple, kind, stage)

    def advance_at(self, index, points):
        for number, point in enumerate(points):
            if self.plan.steps_at[point]:

                @pl.when(index == number)
                def _(point=point):
                    self.advance(point)

    def small_copy(self, phase):
        s = self.s
        _, device = self.plan.partner(0, phase)
        return pltpu.make_async_remote_copy(
            src_ref=s.small_own if phase == 0 else s.small_parts.at[phase - 1],
            dst_ref=s.small_parts.at[phase],
            send_sem=s.small_sems.at[0, phase],
            recv_sem=s.small_sems.at[1, phase],
            device_id=device,
            device_id_type=MESH,
        )

    def small_step(self, phase):
        s = self.s
        if phase >= 0:
            self.small_copy(phase).wait()
            s.small_parts[phase] += s.small_own[...] if phase == 0 else s.small_parts[phase - 1]
        if phase + 1 < self.plan.halvings:
            self.small_copy(phase + 1).start()


PLAN_POINTS = (0, 2, 3) + (5.4,) * 3 + (5.2, 3, 3, 6) + (3.2,) * 4 + (0.3, 2, 3) + (5.4,) * 3 + (3, 3, 3, 3)
PLAN_THERE = (0, 0, 2, 7, 14, 14, 16, 20)
PLAN_HALO, PLAN_HALO_TIME = 6, 14.0
PLAN_CORE, PLAN_LINK, PLAN_LATENCY, PLAN_ADD, PLAN_SLACK = 1.7, 22.7, 2.0, 0.9, 0.0


class Moves:
    def __init__(self, sems):
        self.sems, self.used = sems, 0

    def __call__(self, source, target):
        number, self.used = self.used, self.used + 1
        make = functools.partial(pltpu.make_async_copy, source, target, self.sems.at[number])
        make().start()
        return lambda: make().wait()


class Refs:
    pass


def run(plan, layout, *refs):
    s = Refs()
    for name, ref in zip(layout, refs):
        setattr(s, name, ref)
    rest = list(refs[len(layout) :])
    s.landing = [[rest.pop(0) for _ in range(plan.halvings)] for _ in range(CLASSES)]
    s.results = (s.sum_qkv, s.sum_proj, s.sum_fc1, s.sum_fc2)
    s.units = (s.units_zero, s.units_one)
    s.page = s.staged.at[pl.ds(0, s.plain.shape[0])]
    s.spread = s.qkv.at[pl.ds(0, s.in_spread.shape[0])]
    windows = s.x.shape[1] // LANES
    patches = s.dense.shape[0] // SPLITS
    half, half_rows = patches // 2, s.dense.shape[0] // 2
    padded = 16 * -(-half // 16)
    upper, lower = pl.ds(0, half_rows), pl.ds(half_rows, half_rows)
    reducer = Reducer(plan, s)
    move = Moves(s.move_sems)
    page, row = lax.axis_index(PAGE), lax.axis_index(ROW)
    count = lax.axis_size(ROW)
    above, below = (page, (row + count - 1) % count), (page, (row + 1) % count)

    def halo(number, source, target, device):
        make = functools.partial(
            pltpu.make_async_remote_copy,
            src_ref=source,
            dst_ref=target,
            send_sem=s.halo_sems.at[0, number],
            recv_sem=s.halo_sems.at[1, number],
            device_id=device,
            device_id_type=MESH,
        )
        make().start()
        return lambda: make().wait()

    tokens_there = move(s.in_tokens, s.tokens)
    places_there = (move(s.in_plain, s.plain), move(s.in_moved, s.moved))
    swaps_there = (move(s.in_swap_on, s.swap_on), move(s.in_swap_back, s.swap_back))
    spread_there = move(s.in_spread, s.spread)
    weights = ((s.in_qkv, s.w_qkv), (s.in_proj, s.w_proj), (s.in_fc1, s.w_fc1), (s.in_fc2, s.w_fc2))

    def fetch_weight(which, layer):
        source, target = weights[which]
        return move(source.at[layer], target)

    there = [fetch_weight(which, 0) for which in range(4)]

    barrier = pltpu.get_barrier_semaphore()
    devices = [plan.partner(0, level)[1] for level in range(plan.halvings)] + [above, below]
    for device in devices:
        pl.semaphore_signal(barrier, inc=1, device_id=device, device_id_type=MESH)
    pl.semaphore_wait(barrier, len(devices))

    s.live[...] = jnp.zeros(s.live.shape, F32)
    for window in range(windows):
        s.live[window : window + 1, :] = jnp.full((1, LANES), 1.0 - s.blank[0, window].astype(F32))
    live_there = halo(0, s.live, s.live_upper, above)
    grad_there = halo(1, s.in_grad.at[upper], s.grad_upper, above)
    grad_lower_there = move(s.in_grad.at[lower], s.dense.at[lower])
    s.page[...] = jnp.zeros(s.page.shape, F32)
    tokens_there()
    cols = s.tokens.shape[1]
    for line in range(WIN):
        s.page[pl.ds(line * cols, cols), :] = s.tokens[line].astype(F32)
    places_there[0]()
    to_channels(s.page, s.plain, s.x, True)
    saves = [move(s.x, s.kept_x)]
    spread_columns(s, 0)
    spread_there()
    spread_bias(s, 0)
    region_masks(False, s.regions)
    norm_one_forward(s, windows)
    saves.append(move(s.normed, s.kept_normed))
    there[QKV]()
    project_forward(s, windows)
    qkv_saved = move(s.qkv, s.kept_qkv)
    there[QKV] = fetch_weight(QKV, 1)
    attend_forward(s, windows, s.live)
    saves.append(move(s.soft, s.kept_soft))
    saves.append(move(s.merged, s.kept_merged))
    there[PROJ]()
    s.work[...] = mm(s.w_proj[...], s.merged[...], 0, 0)
    there[PROJ] = fetch_weight(PROJ, 1)
    norm_two_forward(s, windows, s.live)
    saves.append(move(s.hidden, s.kept_hidden))
    saves.append(move(s.second, s.kept_second))
    there[FC1]()
    there[FC2]()
    feed_forward(s, windows)
    saves.append(move(s.active, s.kept_active))
    saves.append(move(s.slope, s.kept_slope))
    there[FC1] = fetch_weight(FC1, 1)
    there[FC2] = fetch_weight(FC2, 1)
    to_dense(s.work, s.plain, s.dense.at[upper], padded)
    upper_there = halo(2, s.dense.at[upper], s.upper, above)

    qkv_saved()
    spread_there = move(s.in_spread, s.spread)
    places_there[1]()
    swaps_there[0]()
    saves.pop(0)()
    move_own(s.work, s.swap_on, s.x, windows, 0)
    spread_columns(s, 1)
    spread_there()
    spread_bias(s, 1)
    region_masks(True, s.regions)
    live_there()
    shifted_live(s, windows)
    grad_there()
    grad_lower_there()
    from_dense(s.grad_upper, s.page, 0)
    from_dense(s.dense.at[lower], s.page, half)
    to_channels(s.page, s.moved, s.grad)
    for saved in saves:
        saved()
    upper_there()
    from_dense(s.upper, s.page, 0)
    add_halo(s.page, s.moved, s.x, half, padded)
    norm_one_forward(s, windows)
    there[QKV]()
    project_forward(s, windows)
    attend_forward(s, windows, s.live_two)
    there[PROJ]()
    s.work[...] = mm(s.w_proj[...], s.merged[...], 0, 0)
    norm_two_forward(s, windows, s.live_two)
    there[FC1]()
    there[FC2]()
    feed_forward(s, windows)
    to_dense(s.work, s.moved, s.dense, s.moved.shape[0])
    out_there = halo(3, s.dense.at[upper], s.out_tokens.at[upper], below)
    out_kept = move(s.dense.at[lower], s.out_tokens.at[lower])

    spread_gains(s, 1)

    def backward(layer, live_ref, fetch, points):
        reducer.layer = layer
        first = 0 if layer else FEEDS
        feed_backward(s, reducer, points[:first])
        reducer.advance(points[first])
        fetch(0)
        norm_two_backward(s, windows, live_ref)
        reducer.advance(points[first + 1])
        fetch(1)
        merge_backward(s, reducer)
        reducer.advance(points[first + 2])
        fetch(2)
        attend_backward(s, windows, reducer, points[first + 3 :])
        fetch(3)

    back = {}

    def refill(point):
        if point == 0:
            back[0] = [move(s.kept_active, s.active), move(s.kept_slope, s.slope), move(s.kept_second, s.second)]
            back[0] += [fetch_weight(FC1, 0), fetch_weight(FC2, 0)]
        elif point == 1:
            back[1] = [move(s.kept_hidden, s.hidden)]
        elif point == 2:
            back[2] = [fetch_weight(PROJ, 0)]
        elif point == 3:
            back[2] += [move(s.kept_merged, s.merged)]
            back[3] = [move(s.kept_soft, s.soft)]
        elif point == 4:
            back[4] = [move(s.kept_x, s.x)]
        else:
            back[3] += [move(s.kept_qkv, s.qkv), move(s.kept_normed, s.normed), fetch_weight(QKV, 0)]

    def needed(point):
        if point in back:
            for arrived in back.pop(point):
                arrived()

    backward(1, s.live_two, refill, range(6))
    input_backward(s)
    norm_one_backward(s, windows)
    refill(4)
    out_there()
    to_dense(s.grad, s.moved, s.dense.at[upper], padded)
    next_there = halo(4, s.dense.at[upper], s.next_upper, below)
    reducer.advance(6)
    project_backward(s, reducer)
    spread_there = move(s.in_spread, s.spread)
    reducer.settle(1)
    reducer.advance(7)

    swaps_there[1]()
    move_own(s.grad, s.swap_back, s.work, windows, -1)
    spread_there()
    small_gradients(s, s.small_own.at[1])
    refill(5)
    spread_gains(s, 0)
    reducer.advance(8)
    next_there()
    from_dense(s.next_upper, s.page, 0)
    s.grad[...] = s.work[...]
    add_halo(s.page, s.plain, s.grad, half, padded)
    reducer.advance(9)
    needed(0)

    def wait_next(point):
        needed(point + 1)

    backward(0, s.live, wait_next, range(10, 20))
    project_backward(s, reducer)
    reducer.settle(1)
    reducer.advance(20)
    input_backward(s)
    spread_there = move(s.in_spread, s.spread)
    reducer.advance(21)
    needed(4)
    norm_one_backward(s, windows)
    out_kept()
    to_dense(s.grad, s.plain, s.dense, s.plain.shape[0])
    grad_kept = move(s.dense, s.grad_tokens)
    reducer.advance(22)
    spread_there()
    small_gradients(s, s.small_own.at[0])
    reducer.advance(23)
    finish_small(s, plan, row)
    grad_kept()


def finish_small(s, plan, row):
    total = s.small_parts.at[plan.halvings - 1]
    outs = (
        (s.d_ln_gain, (G1, G2)),
        (s.d_ln_bias, (B1, B2)),
        (s.d_qv_bias, (QB, VB)),
        (s.d_proj_bias, (PB,)),
        (s.d_fc1_bias, tuple(range(F1B, F1B + FEEDS))),
        (s.d_fc2_bias, (F2B,)),
    )
    for layer in range(2):
        s.d_table[layer] = total[layer, VECTOR_ROWS:, :OFFSETS]
        for ref, indices in outs:
            whole = jnp.concatenate([total[layer, index : index + 1, :] for index in indices], axis=1)
            size = ref.shape[1]
            mine = jnp.zeros((1, size), F32)
            for share in range(plan.shares):
                mine = jnp.where(row == share, whole[:, share * size : (share + 1) * size], mine)
            ref[layer : layer + 1, :] = mine


def placements(cols):
    windows = cols // WIN
    patches = WIN * cols
    padded = -(-patches // LANES) * LANES
    plain = np.zeros((padded, windows * LANES), np.float32)
    moved = np.zeros((padded, windows * LANES), np.float32)
    for line in range(WIN):
        for col in range(cols):
            source = line * cols + col
            plain[source, (col // WIN) * LANES + line * WIN + col % WIN] = 1
            new_line, new_col = (line - SHIFT) % WIN, (col - SHIFT) % cols
            moved[source, (new_col // WIN) * LANES + new_line * WIN + new_col % WIN] = 1
    return plain.astype(BF), moved.astype(BF)


def swaps():
    on = np.zeros((2 * LANES, LANES), np.float32)
    back = np.zeros((2 * LANES, LANES), np.float32)
    for line in range(SHIFT):
        for col in range(WIN):
            moved, plain = line * WIN + col, (line + SHIFT) * WIN + (col + SHIFT) % WIN
            on[plain + (LANES if col >= SHIFT else 0), moved] = 1
            back[moved + (LANES if col < SHIFT else 0), plain] = 1
    return on.astype(BF), back.astype(BF)


def table_spread():
    size = 2 * WIN - 1
    spread = np.zeros((WIN, 2 * LANES, TABLE), np.float32)
    for key_col in range(WIN):
        for offset in range(size):
            for col in range(WIN):
                spread[key_col, offset * WIN + col, offset * size + col - key_col + WIN - 1] = 1
    spread = spread.reshape(WIN // 2, 2, 2 * LANES, TABLE).swapaxes(1, 2)
    return spread.reshape(WIN * LANES, 2 * TABLE).astype(BF)


def copy_all(*refs):
    *refs, sems = refs
    count = len(refs) // 3
    sources, targets, held = refs[:count], refs[count : 2 * count], refs[2 * count :]
    ways = [*zip(sources, held), *zip(held, targets)]
    copies = [pltpu.make_async_copy(*way, sems.at[number]) for number, way in enumerate(ways)]
    for copy in copies[:count]:
        copy.start()
    for incoming, outgoing in zip(copies[:count], copies[count:]):
        incoming.wait()
        outgoing.start()
    for copy in copies[count:]:
        copy.wait()


def hand_out(values):
    anywhere = pl.BlockSpec(memory_space=pl.ANY)
    return pl.pallas_call(
        copy_all,
        out_shape=[jax.ShapeDtypeStruct(value.shape, value.dtype) for value in values],
        in_specs=[anywhere] * len(values),
        out_specs=[anywhere] * len(values),
        scratch_shapes=[pltpu.VMEM(value.shape, value.dtype) for value in values]
        + [pltpu.SemaphoreType.DMA((2 * len(values),))],
        compiler_params=pltpu.CompilerParams(vmem_limit_bytes=VMEM_LIMIT),
        name="results",
    )(*values)


def per_device(
    page_tokens,
    blank_mask,
    cotangent,
    ln_gain,
    ln_bias,
    qv_bias,
    rel_table,
    w_qkv,
    w_proj,
    proj_bias,
    w_fc1,
    fc1_bias,
    w_fc2,
    fc2_bias,
):
    pages, shares = lax.axis_size(PAGE), lax.axis_size(ROW)
    plan = Plan(pages, shares)
    cols = page_tokens.shape[2]
    windows, lanes = cols // WIN, cols // WIN * LANES
    dense = ((WIN * cols * SPLITS, LANES), F32)
    half_dense = ((WIN * cols * SPLITS // 2, LANES), F32)
    plain, moved = (jnp.asarray(place) for place in placements(cols))
    live_rows = 8 * -(-windows // 8)
    scalar_inputs = dict(blank=blank_mask[0])
    small_inputs = dict(
        table=rel_table,
        ln_gain=ln_gain,
        ln_bias=ln_bias,
        qv_bias=qv_bias,
        proj_bias=proj_bias,
        fc1_bias=fc1_bias,
        fc2_bias=fc2_bias,
    )
    large_inputs = dict(
        in_tokens=page_tokens[0],
        in_grad=cotangent.reshape(dense[0]),
        in_plain=plain,
        in_moved=moved,
        in_swap_on=jnp.asarray(swaps()[0]),
        in_swap_back=jnp.asarray(swaps()[1]),
        in_spread=jnp.asarray(table_spread()),
        in_qkv=w_qkv,
        in_proj=w_proj,
        in_fc1=w_fc1,
        in_fc2=w_fc2,
    )
    saved = dict(
        x=((D, lanes), F32),
        normed=((D, lanes), BF),
        qkv=((3 * D, lanes), BF),
        soft=((windows * HEADS, LANES, LANES), BF),
        merged=((D, lanes), BF),
        hidden=((D, lanes), F32),
        second=((D, lanes), BF),
        active=((FF, lanes), BF),
        slope=((FF, lanes), BF),
    )
    units = ((UNITS, shares, CHUNK // shares, CHUNK), F32)
    large_outputs = dict(
        out_tokens=dense,
        grad_tokens=dense,
        sum_qkv=((2, D // shares, 3 * D), F32),
        sum_proj=((2, D // shares, D), F32),
        sum_fc1=((2, D // shares, FF), F32),
        sum_fc2=((2, FF // shares, D), F32),
        units_zero=units,
        units_one=units,
        kept_x=((D, lanes), F32),
        kept_normed=((D, lanes), BF),
        kept_qkv=((3 * D, lanes), BF),
        kept_soft=((windows * HEADS, LANES, LANES), BF),
        kept_merged=((D, lanes), BF),
        kept_hidden=((D, lanes), F32),
        kept_second=((D, lanes), BF),
        kept_active=((FF, lanes), BF),
        kept_slope=((FF, lanes), BF),
    )
    small_outputs = dict(
        d_ln_gain=((2, 2 * D // shares), F32),
        d_ln_bias=((2, 2 * D // shares), F32),
        d_qv_bias=((2, 2 * D // shares), F32),
        d_proj_bias=((2, D // shares), F32),
        d_fc1_bias=((2, FF // shares), F32),
        d_fc2_bias=((2, D // shares), F32),
        d_table=((2, HEADS, OFFSETS), F32),
    )
    small = (2, SMALL, D)
    vmem = dict(
        saved,
        tokens=((WIN, cols, D), BF),
        plain=(plain.shape, BF),
        moved=(moved.shape, BF),
        w_qkv=((D, 3 * D), BF),
        w_proj=((D, D), BF),
        w_fc1=((D, FF), BF),
        w_fc2=((FF, D), BF),
        dense=dense,
        upper=half_dense,
        swap_on=((2 * LANES, LANES), BF),
        swap_back=((2 * LANES, LANES), BF),
        grad_upper=half_dense,
        next_upper=half_dense,
        live_upper=((live_rows, LANES), F32),
        live_two=((live_rows, LANES), F32),
        work=((D, lanes), F32),
        grad=((D, lanes), F32),
        low=((D, lanes), BF),
        sums=((VECTORS, D, LANES), F32),
        gains=((2, D, LANES), F32),
        bias=((HEADS, LANES, LANES), F32),
        bias_rows=((HEADS * LANES, LANES), F32),
        regions=((2, LANES, LANES), F32),
        padded_table=((HEADS, TABLE), F32),
        live=((live_rows, LANES), F32),
        vector_rows=((VECTOR_ROWS, D), F32),
        staged=((2 * CHUNK, CHUNK), F32),
        done=((DONE * CLASSES, CHUNK // shares, CHUNK), F32),
        held=((HELD * CLASSES, shares, CHUNK // shares, CHUNK // 2), F32),
        small_own=(small, F32),
        small_parts=((plan.halvings,) + small, F32),
    )
    semaphores = dict(
        move_sems=pltpu.SemaphoreType.DMA((48,)),
        halo_sems=pltpu.SemaphoreType.DMA((2, 5)),
        send_sems=pltpu.SemaphoreType.DMA((2 * UNITS, plan.phases)),
        recv_sems=pltpu.SemaphoreType.DMA((2 * UNITS, plan.phases)),
        own_sems=pltpu.SemaphoreType.DMA((2 * UNITS, 2)),
        stage_sems=pltpu.SemaphoreType.DMA((2, shares)),
        small_sems=pltpu.SemaphoreType.DMA((2, plan.halvings)),
        free_sems=pltpu.SemaphoreType.REGULAR((CLASSES, plan.halvings)),
    )
    landing = [((RING,) + size, F32) for sizes in plan.sizes for size in sizes]
    layout = [*scalar_inputs, *small_inputs, *large_inputs, *small_outputs, *large_outputs, *vmem, *semaphores]
    in_vmem, anywhere = pl.BlockSpec(memory_space=pltpu.VMEM), pl.BlockSpec(memory_space=pl.ANY)
    outputs = {**small_outputs, **large_outputs}
    results = pl.pallas_call(
        functools.partial(run, plan, layout),
        out_shape=[jax.ShapeDtypeStruct(*shape) for shape in outputs.values()],
        in_specs=[pl.BlockSpec(memory_space=pltpu.SMEM)] + [in_vmem] * len(small_inputs) + [anywhere] * len(large_inputs),
        out_specs=[in_vmem] * len(small_outputs) + [anywhere] * len(large_outputs),
        scratch_shapes=[pltpu.VMEM(*shape) for shape in vmem.values()]
        + list(semaphores.values())
        + [pltpu.VMEM(*shape) for shape in landing],
        compiler_params=pltpu.CompilerParams(
            vmem_limit_bytes=VMEM_LIMIT, collective_id=0, has_side_effects=True
        ),
        name="two_layers",
    )(*scalar_inputs.values(), *small_inputs.values(), *large_inputs.values())
    results = hand_out(results[: len(small_outputs) + 6])
    d_ln_gain, d_ln_bias, d_qv_bias, d_proj_bias, d_fc1_bias, d_fc2_bias, d_table = results[: len(small_outputs)]
    out_tokens, grad_tokens, sum_qkv, sum_proj, sum_fc1, sum_fc2 = results[len(small_outputs) :]
    return (
        out_tokens.reshape(cotangent.shape),
        grad_tokens.reshape(cotangent.shape),
        d_ln_gain,
        d_ln_bias,
        d_qv_bias,
        d_table,
        sum_qkv,
        sum_proj,
        d_proj_bias,
        sum_fc1,
        d_fc1_bias,
        sum_fc2,
        d_fc2_bias,
    )


def solution(mesh):
    tokens, by_row, shares = P(PAGE, ROW, None, None), P(None, ROW), P(None, ROW, None)
    return jax.shard_map(
        per_device,
        mesh=mesh,
        in_specs=(tokens, P(PAGE, ROW, None), tokens) + (P(),) * 11,
        out_specs=(tokens, tokens)
        + (by_row, by_row, by_row, P(), shares, shares, by_row, shares, by_row, shares, by_row),
        check_vma=False,
    )
```

```python
import functools

import jax
import jax.numpy as jnp
import numpy as np
from jax import lax
from jax.experimental import pallas as pl
from jax.experimental.pallas import tpu as pltpu
from jax.sharding import PartitionSpec as P

WIN = 10
SHIFT = 5
AREA = WIN * WIN
LANES = 128
D = 512
HEADS = 16
HEAD_DIM = 32
FF = 2048
CHUNK = 512
FEEDS = FF // CHUNK
SPLITS = D // LANES
EPSILON = 1e-05
MASK_VALUE = -100.0
NEVER = -1e30
SCORE_SCALE = HEAD_DIM ** (-0.5)
VMEM_LIMIT = 63 * 1024 * 1024 + 512 * 1024
BF = jnp.bfloat16
F32 = jnp.float32
MESH = pl.DeviceIdType.MESH
PAGE, ROW = "page", "row"

G1, B1, G2, B2, QB, VB, PB, F2B, F1B, VECTORS = 0, 1, 2, 3, 4, 5, 6, 7, 8, 12
VECTOR_ROWS = 16
SMALL = VECTOR_ROWS + HEADS
OFFSETS = (2 * WIN - 1) ** 2
TABLE = 384

UNIT_FC1, UNIT_FC2, UNIT_PROJ, UNIT_QKV, UNITS = 0, 4, 8, 9, 12
CLASSES = 3
GROUPS = UNITS // CLASSES
TRIPLES = 2 * GROUPS
HELD = 4
DONE = 5
RING = 3
QKV, PROJ, FC1, FC2 = range(4)
TARGETS = (
    ((FC1, 0, 0), (FC1, 0, 1), (FC1, 0, 2)),
    ((FC1, 0, 3), (FC2, 0, 0), (FC2, 1, 0)),
    ((FC2, 2, 0), (FC2, 3, 0), (PROJ, 0, 0)),
    ((QKV, 0, 0), (QKV, 0, 1), (QKV, 0, 2)),
)


def mm(left, right, left_dim, right_dim):
    return lax.dot_general(
        left, right, (((left_dim,), (right_dim,)), ((), ())), preferred_element_type=F32
    )


def split(values):
    high = values.astype(BF)
    return high, (values - high.astype(F32)).astype(BF)


def lane_tile(index):
    return pl.ds(pl.multiple_of(index * LANES, LANES), LANES)


def chunk_of(index):
    return pl.ds(pl.multiple_of(index * CHUNK, CHUNK), CHUNK)


def wide(column, count):
    return jnp.concatenate([column] * count, axis=1)


def fold(values):
    total = values[:, :LANES]
    for start in range(LANES, values.shape[1], LANES):
        total = total + values[:, start : start + LANES]
    return total


def norm_parts(values):
    center = values - jnp.sum(values, axis=0, keepdims=True) * (1.0 / D)
    spread = jnp.sum(center * center, axis=0, keepdims=True) * (1.0 / D)
    scale = lax.rsqrt(spread + EPSILON)
    return center * scale, scale


def norm_pull(grad, gain, hat, scale):
    scaled = grad * gain
    mean_one = jnp.sum(scaled, axis=0, keepdims=True) * (1.0 / D)
    mean_two = jnp.sum(scaled * hat, axis=0, keepdims=True) * (1.0 / D)
    return scale * (scaled - mean_one - hat * mean_two)


def gelu_parts(inner):
    step = 1.0 / (1.0 + (0.3275911 * 0.7071067811865476) * jnp.abs(inner))
    bell = jnp.exp(inner * inner * -0.5)
    poly = 0.5 * 1.061405429
    for factor in (-1.453152027, 1.421413741, -0.284496736, 0.254829592):
        poly = poly * step + 0.5 * factor
    tail = poly * step * bell
    below = jnp.where(inner >= 0, 1.0 - tail, tail)
    return inner * below, below + inner * bell * 0.3989422804014327


def to_channels(page_ref, place_ref, out_ref, exact=False):
    def step(index, carry):
        channels = pl.ds(pl.multiple_of(index * 256, 256), 256)
        values = page_ref[:, channels]
        if exact:
            out_ref[channels, :] = mm(values.astype(BF), place_ref[...], 0, 0)
        else:
            high, low = split(values)
            out_ref[channels, :] = mm(high, place_ref[...], 0, 0) + mm(low, place_ref[...], 0, 0)
        return carry

    lax.fori_loop(0, D // 256, step, 0)


def to_dense(values_ref, place_ref, dense_ref, padded):
    count = dense_ref.shape[0] // SPLITS
    for index in range(D // 256):
        high, low = split(values_ref[index * 256 : (index + 1) * 256, :])
        page = mm(place_ref[:padded, :], high, 1, 1) + mm(place_ref[:padded, :], low, 1, 1)
        for part in range(2):
            rows = pl.ds(2 * index + part, count, stride=SPLITS)
            dense_ref[rows, :] = page[:count, part * LANES : (part + 1) * LANES]


def from_dense(dense_ref, page_ref, row):
    count = dense_ref.shape[0] // SPLITS
    for part in range(SPLITS):
        rows = pl.ds(part, count, stride=SPLITS)
        page_ref[pl.ds(row, count), part * LANES : (part + 1) * LANES] = dense_ref[rows, :]


def add_halo(page_ref, place_ref, out_ref, count, padded):
    page_ref[pl.ds(count, padded - count), :] = jnp.zeros((padded - count, D), F32)

    def step(index, carry):
        channels = pl.ds(pl.multiple_of(index * 256, 256), 256)
        high, low = split(page_ref[:padded, channels])
        out_ref[channels, :] += mm(high, place_ref[:padded, :], 0, 0) + mm(low, place_ref[:padded, :], 0, 0)
        return carry

    lax.fori_loop(0, D // 256, step, 0)


def move_own(values_ref, swap_ref, out_ref, windows, first):
    for window in range(windows):
        sources = [(window + first + part) % windows * LANES for part in range(2)]
        values = jnp.concatenate([values_ref[:, start : start + LANES] for start in sources], axis=1)
        high, low = split(values)
        target = slice(window * LANES, (window + 1) * LANES)
        out_ref[:, target] = mm(high, swap_ref[...], 1, 0) + mm(low, swap_ref[...], 1, 0)


def vector_rows(s, layer):
    rows = s.vector_rows
    sources = ((G1, s.ln_gain, 0), (B1, s.ln_bias, 0), (G2, s.ln_gain, 1), (B2, s.ln_bias, 1))
    sources += ((QB, s.qv_bias, 0), (VB, s.qv_bias, 1), (PB, s.proj_bias, 0), (F2B, s.fc2_bias, 0))
    sources += tuple((F1B + part, s.fc1_bias, part) for part in range(FEEDS))
    for index, source, part in sources:
        rows[index : index + 1, :] = source[layer : layer + 1, part * D : (part + 1) * D]
    rows[VECTORS:, :] = jnp.zeros((VECTOR_ROWS - VECTORS, D), F32)
    return rows[...].T


def spread_columns(s, layer):
    columns = vector_rows(s, layer)
    for index in range(VECTORS):
        s.sums[index] = jnp.broadcast_to(columns[:, index : index + 1], (D, LANES))


def spread_gains(s, layer):
    columns = vector_rows(s, layer)
    for index, vector in enumerate((G1, G2)):
        s.gains[index] = jnp.broadcast_to(columns[:, vector : vector + 1], (D, LANES))


def spread_part(col):
    rows, lanes = (col // 2) * 2 * LANES, (col % 2) * TABLE
    return slice(rows, rows + 2 * LANES), slice(lanes, lanes + TABLE)


def spread_bias(s, layer):
    spread_ref, rows_ref, bias_ref = s.spread, s.bias_rows, s.bias
    s.padded_table[...] = jnp.zeros(s.padded_table.shape, F32)
    s.padded_table[:, :OFFSETS] = s.table[layer]
    high, low = split(s.padded_table[...])
    parts = []
    for col in range(WIN):
        chosen = spread_ref[spread_part(col)]
        parts.append(mm(high, chosen, 1, 1) + mm(low, chosen, 1, 1))
    source = jnp.concatenate(parts, axis=0)
    rows_ref[...] = jnp.zeros(rows_ref.shape, F32)
    for row in range(WIN):
        shift = (WIN - 1 - row) * WIN
        moved = source if shift == 0 else pltpu.roll(source, 2 * LANES - shift, axis=1)
        rows_ref[pl.ds(row * WIN * HEADS, WIN * HEADS), :] = moved[:, :LANES]
    for head in range(HEADS):
        bias_ref[head] = rows_ref[pl.ds(head, LANES, stride=HEADS), :]


def gather_bias(grad_ref, spread_ref, rows_ref):
    for head in range(HEADS):
        rows_ref[pl.ds(head, LANES, stride=HEADS), :] = grad_ref[head]
    total = jnp.zeros((WIN * HEADS, 2 * LANES), F32)
    for row in range(WIN):
        shift = (WIN - 1 - row) * WIN
        piece = rows_ref[pl.ds(row * WIN * HEADS, WIN * HEADS), :]
        piece = jnp.concatenate([piece, jnp.zeros_like(piece)], axis=1)
        total = total + (piece if shift == 0 else pltpu.roll(piece, shift, axis=1))
    table = jnp.zeros((HEADS, TABLE), F32)
    for col in range(WIN):
        for part in split(total[col * HEADS : (col + 1) * HEADS]):
            table = table + mm(part, spread_ref[spread_part(col)], 1, 0)
    return table


def region_masks(shifted_layer, out_ref):
    key = lax.broadcasted_iota(jnp.int32, (LANES, LANES), 0)
    query = lax.broadcasted_iota(jnp.int32, (LANES, LANES), 1)
    padding = jnp.where(key < AREA, 0.0, NEVER)
    out_ref[0] = padding
    out_ref[1] = padding
    if shifted_layer:
        last = lax.axis_index(ROW) == lax.axis_size(ROW) - 1
        rows_differ = ((key >= AREA // 2) != (query >= AREA // 2)) & last
        cols_differ = (key % WIN >= SHIFT) != (query % WIN >= SHIFT)
        out_ref[0] += jnp.where(rows_differ, MASK_VALUE, 0.0)
        out_ref[1] += jnp.where(rows_differ | cols_differ, MASK_VALUE, 0.0)


def shifted_live(s, windows):
    place = lax.broadcasted_iota(jnp.int32, (1, LANES), 1)
    for window in range(windows):
        here, after = slice(window, window + 1), slice((window + 1) % windows, (window + 1) % windows + 1)
        beyond = place % WIN >= SHIFT
        own = jnp.where(beyond, s.live[after, :], s.live[here, :])
        upper = jnp.where(beyond, s.live_upper[after, :], s.live_upper[here, :])
        s.live_two[here, :] = jnp.where(place >= AREA // 2, upper, own)


def head_rows(head, base=0):
    return pl.ds(base + head * HEAD_DIM, HEAD_DIM)


def norm_one_forward(s, windows):
    def step(index, carry):
        lanes = lane_tile(index)
        hat, _ = norm_parts(s.x[:, lanes])
        s.normed[:, lanes] = (hat * s.sums[G1] + s.sums[B1]).astype(BF)
        return carry

    lax.fori_loop(0, windows, step, 0)


def project_forward(s, windows):
    def step(index, carry):
        rows = chunk_of(index)
        bias = s.sums[jnp.where(index == 0, QB, VB)] * jnp.where(index == 1, 0.0, 1.0)
        out = mm(s.w_qkv[:, rows], s.normed[...], 0, 0)
        s.qkv[rows, :] = (out + wide(bias, windows)).astype(BF)
        return carry

    lax.fori_loop(0, 3, step, 0)


def attend_forward(s, windows, live_ref):
    def step(index, carry):
        lanes = lane_tile(index)
        live = jnp.broadcast_to(live_ref[pl.ds(index, 1), :], (LANES, LANES)).T
        masked = s.regions[jnp.where(index == windows - 1, 1, 0)] + MASK_VALUE * (1.0 - live)
        for head in range(HEADS):
            query = s.qkv[head_rows(head), lanes]
            key = s.qkv[head_rows(head, D), lanes]
            value = s.qkv[head_rows(head, 2 * D), lanes]
            scores = mm(key, query, 0, 0) * SCORE_SCALE + (s.bias[head] + masked)
            exponent = jnp.exp(scores - jnp.max(scores, axis=0, keepdims=True))
            total = jnp.sum(exponent, axis=0, keepdims=True)
            soft = (exponent * (1.0 / total)).astype(BF)
            s.soft[index * HEADS + head] = soft
            s.merged[head_rows(head), lanes] = mm(value, soft, 1, 0).astype(BF)
        return carry

    lax.fori_loop(0, windows, step, 0)


def norm_two_forward(s, windows, live_ref):
    def step(index, carry):
        lanes = lane_tile(index)
        hidden = s.x[:, lanes] + live_ref[pl.ds(index, 1), :] * (s.work[:, lanes] + s.sums[PB])
        s.hidden[:, lanes] = hidden
        s.work[:, lanes] = hidden + s.sums[F2B]
        hat, _ = norm_parts(hidden)
        s.second[:, lanes] = (hat * s.sums[G2] + s.sums[B2]).astype(BF)
        return carry

    lax.fori_loop(0, windows, step, 0)


def feed_forward(s, windows):
    def step(index, carry):
        rows = chunk_of(index)
        inner = mm(s.w_fc1[:, rows], s.second[...], 0, 0) + wide(s.sums[F1B + index], windows)
        active, slope = gelu_parts(inner)
        active = active.astype(BF)
        s.active[rows, :] = active
        s.slope[rows, :] = slope.astype(BF)
        s.work[...] += mm(s.w_fc2[rows, :], active, 0, 0)
        return carry

    lax.fori_loop(0, FEEDS, step, 0)


def feed_backward(s, sink, times):
    s.sums[...] = jnp.zeros(s.sums.shape, F32)
    s.bias[...] = jnp.zeros(s.bias.shape, F32)
    lowered = s.grad[...].astype(BF)
    s.low[...] = lowered
    s.sums[F2B] = fold(lowered.astype(F32))
    s.work[...] = jnp.zeros(s.work.shape, F32)

    def step(index, carry):
        rows = chunk_of(index)
        sink.put(0, mm(s.active[rows, :], s.low[...], 1, 1), feed_pieces(index, sink.shares), index == 0)
        grad_inner = mm(s.w_fc2[rows, :], s.low[...], 1, 0) * s.slope[rows, :].astype(F32)
        grad_inner = grad_inner.astype(BF)
        s.sums[F1B + index] = fold(grad_inner.astype(F32))
        sink.put(1, mm(s.second[...], grad_inner, 1, 1), row_pieces(UNIT_FC1 + index, sink.shares), index == 0)
        s.work[...] += mm(s.w_fc1[:, rows], grad_inner, 1, 0)
        sink.advance_at(index, times)
        return carry

    lax.fori_loop(0, FEEDS, step, 0)
    sink.settle(0)
    sink.settle(1)


def norm_two_backward(s, windows, live_ref):
    def step(index, carry):
        lanes = lane_tile(index)
        hat, scale = norm_parts(s.hidden[:, lanes])
        grad = s.work[:, lanes]
        s.sums[G2] += grad * hat
        s.sums[B2] += grad
        grad = s.grad[:, lanes] + norm_pull(grad, s.gains[1], hat, scale)
        s.grad[:, lanes] = grad
        grad_low = (grad * live_ref[pl.ds(index, 1), :]).astype(BF)
        s.low[:, lanes] = grad_low
        s.sums[PB] += grad_low.astype(F32)
        return carry

    lax.fori_loop(0, windows, step, 0)


def merge_backward(s, sink):
    sink.put(0, mm(s.merged[...], s.low[...], 1, 1), row_pieces(UNIT_PROJ, sink.shares), True)
    s.merged[...] = mm(s.w_proj[...], s.low[...], 1, 0).astype(BF)
    sink.settle(0)


def attend_backward(s, windows, sink, times):
    def step(index, carry):
        lanes = lane_tile(index)
        for head in range(HEADS):
            query = s.qkv[head_rows(head), lanes]
            key = s.qkv[head_rows(head, D), lanes]
            value = s.qkv[head_rows(head, 2 * D), lanes]
            grad_out = s.merged[head_rows(head), lanes]
            soft_low = s.soft[index * HEADS + head]
            soft = soft_low.astype(F32)
            grad_soft = mm(value, grad_out, 0, 0)
            inner = jnp.sum(soft * grad_soft, axis=0, keepdims=True)
            grad_scores = (soft * (grad_soft - inner)).astype(BF)
            s.bias[head] += grad_scores.astype(F32)
            grad_query = (mm(key, grad_scores, 1, 0) * SCORE_SCALE).astype(BF)
            grad_key = (mm(query, grad_scores, 1, 1) * SCORE_SCALE).astype(BF)
            grad_value = mm(grad_out, soft_low, 1, 1).astype(BF)
            s.qkv[head_rows(head), lanes] = grad_query
            s.qkv[head_rows(head, D), lanes] = grad_key
            s.qkv[head_rows(head, 2 * D), lanes] = grad_value
            s.sums[QB, head_rows(head), :] += grad_query.astype(F32)
            s.sums[VB, head_rows(head), :] += grad_value.astype(F32)
        sink.advance_at(index, times)
        return carry

    lax.fori_loop(0, windows, step, 0)


def project_backward(s, sink):
    def step(index, carry):
        rows = chunk_of(index)
        sink.put(1, mm(s.normed[...], s.qkv[rows, :], 1, 1), row_pieces(UNIT_QKV + index, sink.shares), index == 0)
        return carry

    lax.fori_loop(0, 3, step, 0)


def input_backward(s):
    s.work[...] = mm(s.w_qkv[...], s.qkv[...], 1, 0)


def norm_one_backward(s, windows):
    def step(index, carry):
        lanes = lane_tile(index)
        hat, scale = norm_parts(s.x[:, lanes])
        grad = s.work[:, lanes]
        s.sums[G1] += grad * hat
        s.sums[B1] += grad
        s.grad[:, lanes] += norm_pull(grad, s.gains[0], hat, scale)
        return carry

    lax.fori_loop(0, windows, step, 0)


def small_gradients(s, small_ref):
    places = lax.broadcasted_iota(jnp.int32, (D, LANES), 1)
    packed = jnp.zeros((D, LANES), F32)
    for index in range(VECTORS):
        packed = jnp.where(places == index, jnp.sum(s.sums[index], axis=1, keepdims=True), packed)
    small_ref[:VECTOR_ROWS, :] = packed.T[:VECTOR_ROWS]
    table = gather_bias(s.bias, s.spread, s.bias_rows)
    small_ref[VECTOR_ROWS:, :] = jnp.concatenate([table, jnp.zeros((HEADS, D - TABLE), F32)], axis=1)


def reversed_bits(value, count):
    turned = 0
    for bit in range(count):
        turned = turned * 2 + (value // 2**bit) % 2
    return turned


def row_pieces(unit, shares):
    rows, count = CHUNK // shares, shares.bit_length() - 1
    return [(share * rows, unit, reversed_bits(share, count)) for share in range(shares)]


def feed_pieces(index, shares):
    rows, count = CHUNK // shares, shares.bit_length() - 1
    pieces = []
    for share in range(shares // FEEDS):
        place = reversed_bits(index * (shares // FEEDS) + share, count)
        for part in range(FEEDS):
            pieces.append(((share * FEEDS + part) * rows, UNIT_FC2 + part, place))
    return pieces


class Plan:
    def __init__(self, pages, shares):
        self.shares, self.rows = shares, CHUNK // shares
        page_bits, row_bits = pages.bit_length() - 1, shares.bit_length() - 1
        others = page_bits - 1
        self.steps = []
        for kind in range(CLASSES):
            turn = kind % 2
            page = [(PAGE, 2 ** (1 + (bit + turn) % others)) for bit in range(others)]
            row = [(ROW, 2**bit) for bit in range(row_bits)]
            self.steps.append([(PAGE, 1)] + (row + page if kind == 2 else page + row))
        self.page_steps = [[0] + [at for at, step in enumerate(steps) if at and step[0] == PAGE] for steps in self.steps]
        self.halvings = page_bits + row_bits
        self.phases = self.halvings + page_bits
        self.sizes, self.axes = [], []
        for steps in self.steps:
            size, sizes, axes = [shares, self.rows, CHUNK], [], []
            for axis, _ in steps:
                axes.append(0 if axis == ROW else 1 if size[1] >= 16 else 2)
                size[axes[-1]] //= 2
                sizes.append(tuple(size))
            self.sizes.append(sizes)
            self.axes.append(axes)
        self.steps_at = self.schedule()

    def schedule(self):
        small = TRIPLES
        free, ready, stage_of, plan, now = {}, {}, {}, [], 0.0
        for triple in range(TRIPLES):
            for kind in range(CLASSES):
                stage_of[triple, kind] = 0
        stage_of[small, 0] = 0

        def link(key, phase):
            triple, kind = key
            if phase < self.halvings:
                axis, stride = self.steps[kind][phase]
                size = 2.0**-phase / 2 if triple != small else 0.125
            else:
                axis, stride = self.steps[kind][self.page_steps[kind][self.phases - 1 - phase]]
                size = 2.0 ** (phase - 2 * self.halvings)
            if axis == PAGE and stride == 1:
                return 0, size * PLAN_CORE
            return (axis, stride if axis == PAGE else 0), size * PLAN_LINK * (1.0 if stride == 1 or axis == PAGE else 1.5)

        def last_stage(key):
            return self.halvings if key[0] == small else self.phases + 1

        def allowed(key, point):
            triple, kind = key
            stage = stage_of[key]
            if stage > last_stage(key):
                return False
            if triple == small:
                return point >= len(PLAN_POINTS) - 1
            if stage == 0 and point < PLAN_THERE[triple]:
                return False
            if triple > 0 and stage_of[triple - 1, kind] <= stage:
                return False
            if triple >= RING and stage < self.halvings and stage_of[triple - RING, kind] <= stage + 1:
                return False
            if stage == 0 and triple >= DONE and stage_of[triple - DONE, kind] <= self.phases + 1:
                return False
            return not (stage == 0 and triple >= HELD and stage_of[triple - HELD, kind] <= self.halvings + 1)

        for point, work in enumerate(PLAN_POINTS):
            now += work
            if point == PLAN_HALO:
                free[ROW, 0] = max(now, free.get((ROW, 0), 0.0)) + PLAN_HALO_TIME
            steps, final = [], point == len(PLAN_POINTS) - 1
            while True:
                keys = [key for key in stage_of if allowed(key, point)]
                keys = [key for key in keys if final or ready.get(key, 0.0) <= now + PLAN_SLACK]
                if not keys:
                    break
                key = min(keys, key=lambda key: (max(ready.get(key, 0.0), now), -stage_of[key], key))
                stage = stage_of[key]
                now = max(now, ready.get(key, 0.0)) + (PLAN_ADD * 2.0**-stage if stage else 0.0)
                if stage == self.phases:
                    ready[key] = now + PLAN_LATENCY
                elif stage < last_stage(key):
                    name, length = link(key, stage)
                    free[name] = max(now, free.get(name, 0.0)) + length
                    ready[key] = free[name] + PLAN_LATENCY
                steps.append((*key, stage))
                stage_of[key] += 1
            plan.append(steps)
        assert all(stage_of[key] > last_stage(key) for key in stage_of)
        return plan

    def partner(self, kind, level):
        axis, stride = self.steps[kind][level]
        page, row = lax.axis_index(PAGE), lax.axis_index(ROW)
        mine = page if axis == PAGE else row
        bit = (mine // stride) % 2
        other = mine + (1 - 2 * bit) * stride
        return bit, ((other, row) if axis == PAGE else (page, other))

    def half(self, kind, which):
        slices = [slice(None)] * 3
        axis, size = self.axes[kind][0], self.sizes[kind][0]
        slices[axis] = pl.ds(pl.multiple_of(which * size[axis], 8), size[axis])
        return tuple(slices)

    def part(self, kind, level, sent=False):
        starts, sizes = [0, 0, 0], list(self.sizes[kind][0])
        for at in range(1, level + 1):
            axis = self.axes[kind][at]
            sizes[axis] //= 2
            bit, _ = self.partner(kind, at)
            which = 1 - bit if sent and at == level else bit
            starts[axis] = starts[axis] + which * sizes[axis]
        return (
            pl.ds(starts[0], sizes[0]),
            pl.ds(pl.multiple_of(starts[1], 8), sizes[1]),
            pl.ds(pl.multiple_of(starts[2], LANES), sizes[2]),
        )

    def place(self, kind, count):
        starts, sizes = [0, 0], [self.rows, CHUNK]
        for at in self.page_steps[kind][:count]:
            axis = self.axes[kind][at] - 1
            sizes[axis] //= 2
            bit, _ = self.partner(kind, at)
            starts[axis] = starts[axis] + bit * sizes[axis]
        return starts, sizes


class Reducer:
    def __init__(self, plan, s):
        self.plan, self.s = plan, s
        self.shares = plan.shares
        self.layer = 1

    def stage_copies(self, slot, pieces):
        return [
            pltpu.make_async_copy(
                self.s.staged.at[pl.ds(slot * CHUNK + start, self.plan.rows)],
                self.s.units[self.layer].at[unit, place],
                self.s.stage_sems.at[slot, number],
            )
            for number, (start, unit, place) in enumerate(pieces)
        ]

    def put(self, slot, grad, pieces, first):
        if first is not True:

            @pl.when(jnp.logical_not(first))
            def _():
                self.settle(slot)

        self.s.staged[pl.ds(slot * CHUNK, CHUNK), :] = grad
        for copy in self.stage_copies(slot, pieces):
            copy.start()

    def settle(self, slot):
        for copy in self.stage_copies(slot, row_pieces(0, self.shares)):
            copy.wait()

    def remote(self, source, target, unit, phase, device):
        return pltpu.make_async_remote_copy(
            src_ref=source,
            dst_ref=target,
            send_sem=self.s.send_sems.at[unit, phase],
            recv_sem=self.s.recv_sems.at[unit, phase],
            device_id=device,
            device_id_type=MESH,
        )

    def unit_half(self, triple, kind, which):
        unit = CLASSES * (triple % GROUPS) + kind
        return self.s.units[1 - triple // GROUPS].at[unit].at[self.plan.half(kind, which)]

    def held(self, triple, kind):
        return self.s.held.at[CLASSES * (triple % HELD) + kind]

    def halving(self, triple, kind, level):
        plan = self.plan
        bit, device = plan.partner(kind, level)
        target = self.s.landing[kind][level].at[triple % RING]
        if level == 0:
            source = self.unit_half(triple, kind, 1 - bit)
        else:
            source = self.held(triple, kind).at[plan.part(kind, level, True)]
        return self.remote(source, target, CLASSES * triple + kind, level, device)

    def own_half(self, triple, kind):
        bit, _ = self.plan.partner(kind, 0)
        sem = self.s.own_sems.at[CLASSES * triple + kind, 0]
        return pltpu.make_async_copy(self.unit_half(triple, kind, bit), self.held(triple, kind), sem)

    def finished(self, triple, kind):
        return self.held(triple, kind).at[self.plan.part(kind, self.plan.halvings - 1)].at[0]

    def done(self, triple, kind, count):
        starts, sizes = self.plan.place(kind, count)
        return self.s.done.at[
            CLASSES * (triple % DONE) + kind,
            pl.ds(pl.multiple_of(starts[0], 8), sizes[0]),
            pl.ds(pl.multiple_of(starts[1], LANES), sizes[1]),
        ]

    def gathering(self, triple, kind, phase):
        plan = self.plan
        count = len(plan.page_steps[kind]) - (phase - plan.halvings)
        part = self.done(triple, kind, count)
        _, device = plan.partner(kind, plan.page_steps[kind][count - 1])
        return self.remote(part, part, CLASSES * triple + kind, phase, device)

    def result(self, triple, kind):
        which, row_block, col_block = TARGETS[triple % GROUPS][kind]
        rows = self.plan.rows
        target = self.s.results[which].at[
            1 - triple // GROUPS, pl.ds(row_block * rows, rows), pl.ds(col_block * CHUNK, CHUNK)
        ]
        sem = self.s.own_sems.at[CLASSES * triple + kind, 1]
        return pltpu.make_async_copy(self.done(triple, kind, 0), target, sem)

    def start(self, triple, kind, phase):
        plan = self.plan
        if phase < plan.halvings:
            if triple >= RING:
                pl.semaphore_wait(self.s.free_sems.at[kind, phase], 1)
            self.halving(triple, kind, phase).start()
            if phase == 0:
                self.own_half(triple, kind).start()
        elif phase < plan.phases:
            if phase == plan.halvings:
                self.done(triple, kind, len(plan.page_steps[kind]))[...] = self.finished(triple, kind)[...]
            self.gathering(triple, kind, phase).start()
        elif phase == plan.phases:
            self.result(triple, kind).start()

    def finish(self, triple, kind, phase):
        plan, s = self.plan, self.s
        if phase < plan.halvings:
            self.halving(triple, kind, phase).wait()
            if phase == 0:
                self.own_half(triple, kind).wait()
            landed = s.landing[kind][phase].at[triple % RING]
            kept = self.held(triple, kind).at[plan.part(kind, phase)]
            for share in range(landed.shape[0]):
                kept[share] += landed[share]
            if triple < TRIPLES - RING:
                _, device = plan.partner(kind, phase)
                pl.semaphore_signal(s.free_sems.at[kind, phase], inc=1, device_id=device, device_id_type=MESH)
        elif phase < plan.phases:
            self.gathering(triple, kind, phase).wait()
        else:
            self.result(triple, kind).wait()

    def advance(self, point):
        for triple, kind, stage in self.plan.steps_at[point]:
            if triple == TRIPLES:
                self.small_step(stage - 1)
                continue
            if stage > 0:
                self.finish(triple, kind, stage - 1)
            self.start(triple, kind, stage)

    def advance_at(self, index, points):
        for number, point in enumerate(points):
            if self.plan.steps_at[point]:

                @pl.when(index == number)
                def _(point=point):
                    self.advance(point)

    def small_copy(self, phase):
        s = self.s
        _, device = self.plan.partner(0, phase)
        return pltpu.make_async_remote_copy(
            src_ref=s.small_own if phase == 0 else s.small_parts.at[phase - 1],
            dst_ref=s.small_parts.at[phase],
            send_sem=s.small_sems.at[0, phase],
            recv_sem=s.small_sems.at[1, phase],
            device_id=device,
            device_id_type=MESH,
        )

    def small_step(self, phase):
        s = self.s
        if phase >= 0:
            self.small_copy(phase).wait()
            s.small_parts[phase] += s.small_own[...] if phase == 0 else s.small_parts[phase - 1]
        if phase + 1 < self.plan.halvings:
            self.small_copy(phase + 1).start()


PLAN_POINTS = (0, 2, 3) + (2.7,) * 6 + (5.2, 3, 3, 6) + (3.2,) * 4 + (0.3, 2, 3) + (2.7,) * 6 + (3, 3, 3, 3)
PLAN_THERE = (0, 0, 2, 10, 17, 17, 19, 26)
PLAN_HALO, PLAN_HALO_TIME = 9, 12.3
PLAN_CORE, PLAN_LINK, PLAN_LATENCY, PLAN_ADD, PLAN_SLACK = 5.0, 20.0, 3.0, 0.9, 0.0


class Moves:
    def __init__(self, sems):
        self.sems, self.used = sems, 0

    def __call__(self, source, target):
        number, self.used = self.used, self.used + 1
        make = functools.partial(pltpu.make_async_copy, source, target, self.sems.at[number])
        make().start()
        return lambda: make().wait()


class Refs:
    pass


def run(plan, layout, *refs):
    s = Refs()
    for name, ref in zip(layout, refs):
        setattr(s, name, ref)
    rest = list(refs[len(layout) :])
    s.landing = [[rest.pop(0) for _ in range(plan.halvings)] for _ in range(CLASSES)]
    s.results = (s.sum_qkv, s.sum_proj, s.sum_fc1, s.sum_fc2)
    s.units = (s.units_zero, s.units_one)
    s.page = s.staged.at[pl.ds(0, s.plain.shape[0])]
    s.spread = s.qkv.at[pl.ds(0, s.in_spread.shape[0])]
    windows = s.x.shape[1] // LANES
    patches = s.dense.shape[0] // SPLITS
    half, half_rows = patches // 2, s.dense.shape[0] // 2
    padded = 16 * -(-half // 16)
    upper, lower = pl.ds(0, half_rows), pl.ds(half_rows, half_rows)
    reducer = Reducer(plan, s)
    move = Moves(s.move_sems)
    page, row = lax.axis_index(PAGE), lax.axis_index(ROW)
    count = lax.axis_size(ROW)
    above, below = (page, (row + count - 1) % count), (page, (row + 1) % count)

    def halo(number, source, target, device):
        make = functools.partial(
            pltpu.make_async_remote_copy,
            src_ref=source,
            dst_ref=target,
            send_sem=s.halo_sems.at[0, number],
            recv_sem=s.halo_sems.at[1, number],
            device_id=device,
            device_id_type=MESH,
        )
        make().start()
        return lambda: make().wait()

    tokens_there = move(s.in_tokens, s.tokens)
    places_there = (move(s.in_plain, s.plain), move(s.in_moved, s.moved))
    swaps_there = (move(s.in_swap_on, s.swap_on), move(s.in_swap_back, s.swap_back))
    spread_there = move(s.in_spread, s.spread)
    weights = ((s.in_qkv, s.w_qkv), (s.in_proj, s.w_proj), (s.in_fc1, s.w_fc1), (s.in_fc2, s.w_fc2))

    def fetch_weight(which, layer):
        source, target = weights[which]
        return move(source.at[layer], target)

    there = [fetch_weight(which, 0) for which in range(4)]

    barrier = pltpu.get_barrier_semaphore()
    devices = [plan.partner(0, level)[1] for level in range(plan.halvings)] + [above, below]
    for device in devices:
        pl.semaphore_signal(barrier, inc=1, device_id=device, device_id_type=MESH)
    pl.semaphore_wait(barrier, len(devices))

    s.live[...] = jnp.zeros(s.live.shape, F32)
    for window in range(windows):
        s.live[window : window + 1, :] = jnp.full((1, LANES), 1.0 - s.blank[0, window].astype(F32))
    live_there = halo(0, s.live, s.live_upper, above)
    grad_there = halo(1, s.in_grad.at[upper], s.grad_upper, above)
    grad_lower_there = move(s.in_grad.at[lower], s.dense.at[lower])
    s.page[...] = jnp.zeros(s.page.shape, F32)
    tokens_there()
    cols = s.tokens.shape[1]
    for line in range(WIN):
        s.page[pl.ds(line * cols, cols), :] = s.tokens[line].astype(F32)
    places_there[0]()
    to_channels(s.page, s.plain, s.x, True)
    saves = [move(s.x, s.kept_x)]
    spread_columns(s, 0)
    spread_there()
    spread_bias(s, 0)
    region_masks(False, s.regions)
    norm_one_forward(s, windows)
    saves.append(move(s.normed, s.kept_normed))
    there[QKV]()
    project_forward(s, windows)
    qkv_saved = move(s.qkv, s.kept_qkv)
    there[QKV] = fetch_weight(QKV, 1)
    attend_forward(s, windows, s.live)
    saves.append(move(s.soft, s.kept_soft))
    saves.append(move(s.merged, s.kept_merged))
    there[PROJ]()
    s.work[...] = mm(s.w_proj[...], s.merged[...], 0, 0)
    there[PROJ] = fetch_weight(PROJ, 1)
    norm_two_forward(s, windows, s.live)
    saves.append(move(s.hidden, s.kept_hidden))
    saves.append(move(s.second, s.kept_second))
    there[FC1]()
    there[FC2]()
    feed_forward(s, windows)
    saves.append(move(s.active, s.kept_active))
    saves.append(move(s.slope, s.kept_slope))
    there[FC1] = fetch_weight(FC1, 1)
    there[FC2] = fetch_weight(FC2, 1)
    to_dense(s.work, s.plain, s.dense.at[upper], padded)
    upper_there = halo(2, s.dense.at[upper], s.upper, above)

    qkv_saved()
    spread_there = move(s.in_spread, s.spread)
    places_there[1]()
    swaps_there[0]()
    saves.pop(0)()
    move_own(s.work, s.swap_on, s.x, windows, 0)
    spread_columns(s, 1)
    spread_there()
    spread_bias(s, 1)
    region_masks(True, s.regions)
    live_there()
    shifted_live(s, windows)
    grad_there()
    grad_lower_there()
    from_dense(s.grad_upper, s.page, 0)
    from_dense(s.dense.at[lower], s.page, half)
    to_channels(s.page, s.moved, s.grad)
    for saved in saves:
        saved()
    upper_there()
    from_dense(s.upper, s.page, 0)
    add_halo(s.page, s.moved, s.x, half, padded)
    norm_one_forward(s, windows)
    there[QKV]()
    project_forward(s, windows)
    attend_forward(s, windows, s.live_two)
    there[PROJ]()
    s.work[...] = mm(s.w_proj[...], s.merged[...], 0, 0)
    norm_two_forward(s, windows, s.live_two)
    there[FC1]()
    there[FC2]()
    feed_forward(s, windows)
    to_dense(s.work, s.moved, s.dense, s.moved.shape[0])
    out_there = halo(3, s.dense.at[upper], s.out_tokens.at[upper], below)
    out_kept = move(s.dense.at[lower], s.out_tokens.at[lower])

    spread_gains(s, 1)

    def backward(layer, live_ref, fetch, points):
        reducer.layer = layer
        first = 0 if layer else FEEDS
        feed_backward(s, reducer, points[:first])
        reducer.advance(points[first])
        fetch(0)
        norm_two_backward(s, windows, live_ref)
        reducer.advance(points[first + 1])
        fetch(1)
        merge_backward(s, reducer)
        reducer.advance(points[first + 2])
        fetch(2)
        attend_backward(s, windows, reducer, points[first + 3 :])
        fetch(3)

    back = {}

    def refill(point):
        if point == 0:
            back[0] = [move(s.kept_active, s.active), move(s.kept_slope, s.slope), move(s.kept_second, s.second)]
            back[0] += [fetch_weight(FC1, 0), fetch_weight(FC2, 0)]
        elif point == 1:
            back[1] = [move(s.kept_hidden, s.hidden)]
        elif point == 2:
            back[2] = [fetch_weight(PROJ, 0)]
        elif point == 3:
            back[2] += [move(s.kept_merged, s.merged)]
            back[3] = [move(s.kept_soft, s.soft)]
        elif point == 4:
            back[4] = [move(s.kept_x, s.x)]
        else:
            back[3] += [move(s.kept_qkv, s.qkv), move(s.kept_normed, s.normed), fetch_weight(QKV, 0)]

    def needed(point):
        if point in back:
            for arrived in back.pop(point):
                arrived()

    backward(1, s.live_two, refill, range(9))
    input_backward(s)
    norm_one_backward(s, windows)
    refill(4)
    out_there()
    to_dense(s.grad, s.moved, s.dense.at[upper], padded)
    next_there = halo(4, s.dense.at[upper], s.next_upper, below)
    reducer.advance(9)
    project_backward(s, reducer)
    spread_there = move(s.in_spread, s.spread)
    reducer.settle(1)
    reducer.advance(10)

    swaps_there[1]()
    move_own(s.grad, s.swap_back, s.work, windows, -1)
    spread_there()
    small_gradients(s, s.small_own.at[1])
    refill(5)
    spread_gains(s, 0)
    reducer.advance(11)
    next_there()
    from_dense(s.next_upper, s.page, 0)
    s.grad[...] = s.work[...]
    add_halo(s.page, s.plain, s.grad, half, padded)
    reducer.advance(12)
    needed(0)

    def wait_next(point):
        needed(point + 1)

    backward(0, s.live, wait_next, range(13, 26))
    project_backward(s, reducer)
    reducer.settle(1)
    reducer.advance(26)
    input_backward(s)
    spread_there = move(s.in_spread, s.spread)
    reducer.advance(27)
    needed(4)
    norm_one_backward(s, windows)
    out_kept()
    to_dense(s.grad, s.plain, s.dense, s.plain.shape[0])
    grad_kept = move(s.dense, s.grad_tokens)
    reducer.advance(28)
    spread_there()
    small_gradients(s, s.small_own.at[0])
    reducer.advance(29)
    finish_small(s, plan, row)
    grad_kept()


def finish_small(s, plan, row):
    total = s.small_parts.at[plan.halvings - 1]
    outs = (
        (s.d_ln_gain, (G1, G2)),
        (s.d_ln_bias, (B1, B2)),
        (s.d_qv_bias, (QB, VB)),
        (s.d_proj_bias, (PB,)),
        (s.d_fc1_bias, tuple(range(F1B, F1B + FEEDS))),
        (s.d_fc2_bias, (F2B,)),
    )
    for layer in range(2):
        s.d_table[layer] = total[layer, VECTOR_ROWS:, :OFFSETS]
        for ref, indices in outs:
            whole = jnp.concatenate([total[layer, index : index + 1, :] for index in indices], axis=1)
            size = ref.shape[1]
            mine = jnp.zeros((1, size), F32)
            for share in range(plan.shares):
                mine = jnp.where(row == share, whole[:, share * size : (share + 1) * size], mine)
            ref[layer : layer + 1, :] = mine


def placements(cols):
    windows = cols // WIN
    patches = WIN * cols
    padded = -(-patches // LANES) * LANES
    plain = np.zeros((padded, windows * LANES), np.float32)
    moved = np.zeros((padded, windows * LANES), np.float32)
    for line in range(WIN):
        for col in range(cols):
            source = line * cols + col
            plain[source, (col // WIN) * LANES + line * WIN + col % WIN] = 1
            new_line, new_col = (line - SHIFT) % WIN, (col - SHIFT) % cols
            moved[source, (new_col // WIN) * LANES + new_line * WIN + new_col % WIN] = 1
    return plain.astype(BF), moved.astype(BF)


def swaps():
    on = np.zeros((2 * LANES, LANES), np.float32)
    back = np.zeros((2 * LANES, LANES), np.float32)
    for line in range(SHIFT):
        for col in range(WIN):
            moved, plain = line * WIN + col, (line + SHIFT) * WIN + (col + SHIFT) % WIN
            on[plain + (LANES if col >= SHIFT else 0), moved] = 1
            back[moved + (LANES if col < SHIFT else 0), plain] = 1
    return on.astype(BF), back.astype(BF)


def table_spread():
    size = 2 * WIN - 1
    spread = np.zeros((WIN, 2 * LANES, TABLE), np.float32)
    for key_col in range(WIN):
        for offset in range(size):
            for col in range(WIN):
                spread[key_col, offset * WIN + col, offset * size + col - key_col + WIN - 1] = 1
    spread = spread.reshape(WIN // 2, 2, 2 * LANES, TABLE).swapaxes(1, 2)
    return spread.reshape(WIN * LANES, 2 * TABLE).astype(BF)


def copy_all(*refs):
    *refs, sems = refs
    count = len(refs) // 3
    sources, targets, held = refs[:count], refs[count : 2 * count], refs[2 * count :]
    ways = [*zip(sources, held), *zip(held, targets)]
    copies = [pltpu.make_async_copy(*way, sems.at[number]) for number, way in enumerate(ways)]
    for copy in copies[:count]:
        copy.start()
    for incoming, outgoing in zip(copies[:count], copies[count:]):
        incoming.wait()
        outgoing.start()
    for copy in copies[count:]:
        copy.wait()


def hand_out(values):
    anywhere = pl.BlockSpec(memory_space=pl.ANY)
    return pl.pallas_call(
        copy_all,
        out_shape=[jax.ShapeDtypeStruct(value.shape, value.dtype) for value in values],
        in_specs=[anywhere] * len(values),
        out_specs=[anywhere] * len(values),
        scratch_shapes=[pltpu.VMEM(value.shape, value.dtype) for value in values]
        + [pltpu.SemaphoreType.DMA((2 * len(values),))],
        compiler_params=pltpu.CompilerParams(vmem_limit_bytes=VMEM_LIMIT),
        name="results",
    )(*values)


def per_device(
    page_tokens,
    blank_mask,
    cotangent,
    ln_gain,
    ln_bias,
    qv_bias,
    rel_table,
    w_qkv,
    w_proj,
    proj_bias,
    w_fc1,
    fc1_bias,
    w_fc2,
    fc2_bias,
):
    pages, shares = lax.axis_size(PAGE), lax.axis_size(ROW)
    plan = Plan(pages, shares)
    cols = page_tokens.shape[2]
    windows, lanes = cols // WIN, cols // WIN * LANES
    dense = ((WIN * cols * SPLITS, LANES), F32)
    half_dense = ((WIN * cols * SPLITS // 2, LANES), F32)
    plain, moved = (jnp.asarray(place) for place in placements(cols))
    live_rows = 8 * -(-windows // 8)
    scalar_inputs = dict(blank=blank_mask[0])
    small_inputs = dict(
        table=rel_table,
        ln_gain=ln_gain,
        ln_bias=ln_bias,
        qv_bias=qv_bias,
        proj_bias=proj_bias,
        fc1_bias=fc1_bias,
        fc2_bias=fc2_bias,
    )
    large_inputs = dict(
        in_tokens=page_tokens[0],
        in_grad=cotangent.reshape(dense[0]),
        in_plain=plain,
        in_moved=moved,
        in_swap_on=jnp.asarray(swaps()[0]),
        in_swap_back=jnp.asarray(swaps()[1]),
        in_spread=jnp.asarray(table_spread()),
        in_qkv=w_qkv,
        in_proj=w_proj,
        in_fc1=w_fc1,
        in_fc2=w_fc2,
    )
    saved = dict(
        x=((D, lanes), F32),
        normed=((D, lanes), BF),
        qkv=((3 * D, lanes), BF),
        soft=((windows * HEADS, LANES, LANES), BF),
        merged=((D, lanes), BF),
        hidden=((D, lanes), F32),
        second=((D, lanes), BF),
        active=((FF, lanes), BF),
        slope=((FF, lanes), BF),
    )
    units = ((UNITS, shares, CHUNK // shares, CHUNK), F32)
    large_outputs = dict(
        out_tokens=dense,
        grad_tokens=dense,
        sum_qkv=((2, D // shares, 3 * D), F32),
        sum_proj=((2, D // shares, D), F32),
        sum_fc1=((2, D // shares, FF), F32),
        sum_fc2=((2, FF // shares, D), F32),
        units_zero=units,
        units_one=units,
        kept_x=((D, lanes), F32),
        kept_normed=((D, lanes), BF),
        kept_qkv=((3 * D, lanes), BF),
        kept_soft=((windows * HEADS, LANES, LANES), BF),
        kept_merged=((D, lanes), BF),
        kept_hidden=((D, lanes), F32),
        kept_second=((D, lanes), BF),
        kept_active=((FF, lanes), BF),
        kept_slope=((FF, lanes), BF),
    )
    small_outputs = dict(
        d_ln_gain=((2, 2 * D // shares), F32),
        d_ln_bias=((2, 2 * D // shares), F32),
        d_qv_bias=((2, 2 * D // shares), F32),
        d_proj_bias=((2, D // shares), F32),
        d_fc1_bias=((2, FF // shares), F32),
        d_fc2_bias=((2, D // shares), F32),
        d_table=((2, HEADS, OFFSETS), F32),
    )
    small = (2, SMALL, D)
    vmem = dict(
        saved,
        tokens=((WIN, cols, D), BF),
        plain=(plain.shape, BF),
        moved=(moved.shape, BF),
        w_qkv=((D, 3 * D), BF),
        w_proj=((D, D), BF),
        w_fc1=((D, FF), BF),
        w_fc2=((FF, D), BF),
        dense=dense,
        upper=half_dense,
        swap_on=((2 * LANES, LANES), BF),
        swap_back=((2 * LANES, LANES), BF),
        grad_upper=half_dense,
        next_upper=half_dense,
        live_upper=((live_rows, LANES), F32),
        live_two=((live_rows, LANES), F32),
        work=((D, lanes), F32),
        grad=((D, lanes), F32),
        low=((D, lanes), BF),
        sums=((VECTORS, D, LANES), F32),
        gains=((2, D, LANES), F32),
        bias=((HEADS, LANES, LANES), F32),
        bias_rows=((HEADS * LANES, LANES), F32),
        regions=((2, LANES, LANES), F32),
        padded_table=((HEADS, TABLE), F32),
        live=((live_rows, LANES), F32),
        vector_rows=((VECTOR_ROWS, D), F32),
        staged=((2 * CHUNK, CHUNK), F32),
        done=((DONE * CLASSES, CHUNK // shares, CHUNK), F32),
        held=((HELD * CLASSES,) + plan.sizes[0][0], F32),
        small_own=(small, F32),
        small_parts=((plan.halvings,) + small, F32),
    )
    semaphores = dict(
        move_sems=pltpu.SemaphoreType.DMA((48,)),
        halo_sems=pltpu.SemaphoreType.DMA((2, 5)),
        send_sems=pltpu.SemaphoreType.DMA((2 * UNITS, plan.phases)),
        recv_sems=pltpu.SemaphoreType.DMA((2 * UNITS, plan.phases)),
        own_sems=pltpu.SemaphoreType.DMA((2 * UNITS, 2)),
        stage_sems=pltpu.SemaphoreType.DMA((2, shares)),
        small_sems=pltpu.SemaphoreType.DMA((2, plan.halvings)),
        free_sems=pltpu.SemaphoreType.REGULAR((CLASSES, plan.halvings)),
    )
    landing = [((RING,) + size, F32) for sizes in plan.sizes for size in sizes]
    layout = [*scalar_inputs, *small_inputs, *large_inputs, *small_outputs, *large_outputs, *vmem, *semaphores]
    in_vmem, anywhere = pl.BlockSpec(memory_space=pltpu.VMEM), pl.BlockSpec(memory_space=pl.ANY)
    outputs = {**small_outputs, **large_outputs}
    results = pl.pallas_call(
        functools.partial(run, plan, layout),
        out_shape=[jax.ShapeDtypeStruct(*shape) for shape in outputs.values()],
        in_specs=[pl.BlockSpec(memory_space=pltpu.SMEM)] + [in_vmem] * len(small_inputs) + [anywhere] * len(large_inputs),
        out_specs=[in_vmem] * len(small_outputs) + [anywhere] * len(large_outputs),
        scratch_shapes=[pltpu.VMEM(*shape) for shape in vmem.values()]
        + list(semaphores.values())
        + [pltpu.VMEM(*shape) for shape in landing],
        compiler_params=pltpu.CompilerParams(
            vmem_limit_bytes=VMEM_LIMIT, collective_id=0, has_side_effects=True
        ),
        name="two_layers",
    )(*scalar_inputs.values(), *small_inputs.values(), *large_inputs.values())
    results = hand_out(results[: len(small_outputs) + 6])
    d_ln_gain, d_ln_bias, d_qv_bias, d_proj_bias, d_fc1_bias, d_fc2_bias, d_table = results[: len(small_outputs)]
    out_tokens, grad_tokens, sum_qkv, sum_proj, sum_fc1, sum_fc2 = results[len(small_outputs) :]
    return (
        out_tokens.reshape(cotangent.shape),
        grad_tokens.reshape(cotangent.shape),
        d_ln_gain,
        d_ln_bias,
        d_qv_bias,
        d_table,
        sum_qkv,
        sum_proj,
        d_proj_bias,
        sum_fc1,
        d_fc1_bias,
        sum_fc2,
        d_fc2_bias,
    )


def solution(mesh):
    tokens, by_row, shares = P(PAGE, ROW, None, None), P(None, ROW), P(None, ROW, None)
    return jax.shard_map(
        per_device,
        mesh=mesh,
        in_specs=(tokens, P(PAGE, ROW, None), tokens) + (P(),) * 11,
        out_specs=(tokens, tokens)
        + (by_row, by_row, by_row, P(), shares, shares, by_row, shares, by_row, shares, by_row),
        check_vma=False,
    )
```

```python
import functools

import jax
import jax.numpy as jnp
import numpy as np
from jax import lax
from jax.experimental import pallas as pl
from jax.experimental.pallas import tpu as pltpu
from jax.sharding import PartitionSpec as P

WIN = 10
SHIFT = 5
AREA = WIN * WIN
LANES = 128
D = 512
HEADS = 16
QUAD = 4
HEAD_DIM = 32
FF = 2048
CHUNK = 512
FEEDS = FF // CHUNK
SPLITS = D // LANES
EPSILON = 1e-05
MASK_VALUE = -100.0
NEVER = -1e30
SCORE_SCALE = HEAD_DIM ** (-0.5)
VMEM_LIMIT = 63 * 1024 * 1024 + 512 * 1024
BF = jnp.bfloat16
F32 = jnp.float32
MESH = pl.DeviceIdType.MESH
PAGE, ROW = "page", "row"

G1, B1, G2, B2, QB, VB, PB, F2B, F1B, VECTORS = 0, 1, 2, 3, 4, 5, 6, 7, 8, 12
VECTOR_ROWS = 16
SMALL = VECTOR_ROWS + HEADS
OFFSETS = (2 * WIN - 1) ** 2
TABLE = 384

UNIT_FC1, UNIT_FC2, UNIT_PROJ, UNIT_QKV, UNITS = 0, 4, 8, 9, 12
CLASSES = 3
GROUPS = UNITS // CLASSES
TRIPLES = 2 * GROUPS
HELD = 4
DONE = 5
RING = 3
QKV, PROJ, FC1, FC2 = range(4)
TARGETS = (
    ((FC1, 0, 0), (FC1, 0, 1), (FC1, 0, 2)),
    ((FC1, 0, 3), (FC2, 0, 0), (FC2, 1, 0)),
    ((FC2, 2, 0), (FC2, 3, 0), (PROJ, 0, 0)),
    ((QKV, 0, 0), (QKV, 0, 1), (QKV, 0, 2)),
)


def mm(left, right, left_dim, right_dim):
    return lax.dot_general(
        left, right, (((left_dim,), (right_dim,)), ((), ())), preferred_element_type=F32
    )


def split(values):
    high = values.astype(BF)
    return high, (values - high.astype(F32)).astype(BF)


def lane_tile(index):
    return pl.ds(pl.multiple_of(index * LANES, LANES), LANES)


def chunk_of(index):
    return pl.ds(pl.multiple_of(index * CHUNK, CHUNK), CHUNK)


def wide(column, count):
    return jnp.concatenate([column] * count, axis=1)


def fold(values):
    total = values[:, :LANES]
    for start in range(LANES, values.shape[1], LANES):
        total = total + values[:, start : start + LANES]
    return total


def norm_parts(values):
    center = values - jnp.sum(values, axis=0, keepdims=True) * (1.0 / D)
    spread = jnp.sum(center * center, axis=0, keepdims=True) * (1.0 / D)
    scale = lax.rsqrt(spread + EPSILON)
    return center * scale, scale


def norm_pull(grad, gain, hat, scale):
    scaled = grad * gain
    mean_one = jnp.sum(scaled, axis=0, keepdims=True) * (1.0 / D)
    mean_two = jnp.sum(scaled * hat, axis=0, keepdims=True) * (1.0 / D)
    return scale * (scaled - mean_one - hat * mean_two)


def gelu_parts(inner):
    step = 1.0 / (1.0 + (0.3275911 * 0.7071067811865476) * jnp.abs(inner))
    bell = jnp.exp(inner * inner * -0.5)
    poly = 0.5 * 1.061405429
    for factor in (-1.453152027, 1.421413741, -0.284496736, 0.254829592):
        poly = poly * step + 0.5 * factor
    tail = poly * step * bell
    below = jnp.where(inner >= 0, 1.0 - tail, tail)
    return inner * below, below + inner * bell * 0.3989422804014327


def to_channels(page_ref, place_ref, out_ref, exact=False):
    def step(index, carry):
        channels = pl.ds(pl.multiple_of(index * 256, 256), 256)
        values = page_ref[:, channels]
        if exact:
            out_ref[channels, :] = mm(values.astype(BF), place_ref[...], 0, 0)
        else:
            high, low = split(values)
            out_ref[channels, :] = mm(high, place_ref[...], 0, 0) + mm(low, place_ref[...], 0, 0)
        return carry

    lax.fori_loop(0, D // 256, step, 0)


def to_dense(values_ref, place_ref, dense_ref, padded):
    count = dense_ref.shape[0] // SPLITS
    for index in range(D // 256):
        high, low = split(values_ref[index * 256 : (index + 1) * 256, :])
        page = mm(place_ref[:padded, :], high, 1, 1) + mm(place_ref[:padded, :], low, 1, 1)
        for part in range(2):
            rows = pl.ds(2 * index + part, count, stride=SPLITS)
            dense_ref[rows, :] = page[:count, part * LANES : (part + 1) * LANES]


def from_dense(dense_ref, page_ref, row):
    count = dense_ref.shape[0] // SPLITS
    for part in range(SPLITS):
        rows = pl.ds(part, count, stride=SPLITS)
        page_ref[pl.ds(row, count), part * LANES : (part + 1) * LANES] = dense_ref[rows, :]


def add_halo(page_ref, place_ref, out_ref, count, padded):
    page_ref[pl.ds(count, padded - count), :] = jnp.zeros((padded - count, D), F32)

    def step(index, carry):
        channels = pl.ds(pl.multiple_of(index * 256, 256), 256)
        high, low = split(page_ref[:padded, channels])
        out_ref[channels, :] += mm(high, place_ref[:padded, :], 0, 0) + mm(low, place_ref[:padded, :], 0, 0)
        return carry

    lax.fori_loop(0, D // 256, step, 0)


def move_own(values_ref, swap_ref, out_ref, windows, first):
    for window in range(windows):
        sources = [(window + first + part) % windows * LANES for part in range(2)]
        values = jnp.concatenate([values_ref[:, start : start + LANES] for start in sources], axis=1)
        high, low = split(values)
        target = slice(window * LANES, (window + 1) * LANES)
        out_ref[:, target] = mm(high, swap_ref[...], 1, 0) + mm(low, swap_ref[...], 1, 0)


def vector_rows(s, layer):
    rows = s.vector_rows
    sources = ((G1, s.ln_gain, 0), (B1, s.ln_bias, 0), (G2, s.ln_gain, 1), (B2, s.ln_bias, 1))
    sources += ((QB, s.qv_bias, 0), (VB, s.qv_bias, 1), (PB, s.proj_bias, 0), (F2B, s.fc2_bias, 0))
    sources += tuple((F1B + part, s.fc1_bias, part) for part in range(FEEDS))
    for index, source, part in sources:
        rows[index : index + 1, :] = source[layer : layer + 1, part * D : (part + 1) * D]
    rows[VECTORS:, :] = jnp.zeros((VECTOR_ROWS - VECTORS, D), F32)
    return rows[...].T


def spread_columns(s, layer):
    columns = vector_rows(s, layer)
    for index in range(VECTORS):
        s.sums[index] = jnp.broadcast_to(columns[:, index : index + 1], (D, LANES))


def spread_gains(s, layer):
    columns = vector_rows(s, layer)
    for index, vector in enumerate((G1, G2)):
        s.gains[index] = jnp.broadcast_to(columns[:, vector : vector + 1], (D, LANES))


def spread_part(col):
    rows, lanes = (col // 2) * 2 * LANES, (col % 2) * TABLE
    return slice(rows, rows + 2 * LANES), slice(lanes, lanes + TABLE)


def spread_bias(s, layer):
    spread_ref, rows_ref, bias_ref = s.spread, s.bias_rows, s.bias
    s.padded_table[...] = jnp.zeros(s.padded_table.shape, F32)
    s.padded_table[:, :OFFSETS] = s.table[layer]
    high, low = split(s.padded_table[...])
    parts = []
    for col in range(WIN):
        chosen = spread_ref[spread_part(col)]
        parts.append(mm(high, chosen, 1, 1) + mm(low, chosen, 1, 1))
    source = jnp.concatenate(parts, axis=0)
    rows_ref[...] = jnp.zeros(rows_ref.shape, F32)
    for row in range(WIN):
        shift = (WIN - 1 - row) * WIN
        moved = source if shift == 0 else pltpu.roll(source, 2 * LANES - shift, axis=1)
        rows_ref[pl.ds(row * WIN * HEADS, WIN * HEADS), :] = moved[:, :LANES]
    for head in range(HEADS):
        bias_ref[head] = rows_ref[pl.ds(head, LANES, stride=HEADS), :]


def gather_bias(grad_ref, spread_ref, rows_ref):
    for head in range(HEADS):
        rows_ref[pl.ds(head, LANES, stride=HEADS), :] = grad_ref[head]
    total = jnp.zeros((WIN * HEADS, 2 * LANES), F32)
    for row in range(WIN):
        shift = (WIN - 1 - row) * WIN
        piece = rows_ref[pl.ds(row * WIN * HEADS, WIN * HEADS), :]
        piece = jnp.concatenate([piece, jnp.zeros_like(piece)], axis=1)
        total = total + (piece if shift == 0 else pltpu.roll(piece, shift, axis=1))
    table = jnp.zeros((HEADS, TABLE), F32)
    for col in range(WIN):
        for part in split(total[col * HEADS : (col + 1) * HEADS]):
            table = table + mm(part, spread_ref[spread_part(col)], 1, 0)
    return table


def region_masks(shifted_layer, out_ref):
    key = lax.broadcasted_iota(jnp.int32, (LANES, LANES), 0)
    query = lax.broadcasted_iota(jnp.int32, (LANES, LANES), 1)
    padding = jnp.where(key < AREA, 0.0, NEVER)
    out_ref[0] = padding
    out_ref[1] = padding
    if shifted_layer:
        last = lax.axis_index(ROW) == lax.axis_size(ROW) - 1
        rows_differ = ((key >= AREA // 2) != (query >= AREA // 2)) & last
        cols_differ = (key % WIN >= SHIFT) != (query % WIN >= SHIFT)
        out_ref[0] += jnp.where(rows_differ, MASK_VALUE, 0.0)
        out_ref[1] += jnp.where(rows_differ | cols_differ, MASK_VALUE, 0.0)


def shifted_live(s, windows):
    place = lax.broadcasted_iota(jnp.int32, (1, LANES), 1)
    for window in range(windows):
        here, after = slice(window, window + 1), slice((window + 1) % windows, (window + 1) % windows + 1)
        beyond = place % WIN >= SHIFT
        own = jnp.where(beyond, s.live[after, :], s.live[here, :])
        upper = jnp.where(beyond, s.live_upper[after, :], s.live_upper[here, :])
        s.live_two[here, :] = jnp.where(place >= AREA // 2, upper, own)


def quad_rows(quad, base=0):
    return pl.ds(base + quad * LANES, LANES)


def heads_of(rows):
    return [rows[head * HEAD_DIM : (head + 1) * HEAD_DIM] for head in range(QUAD)]


def diagonal(rows):
    blank = jnp.zeros((HEAD_DIM, LANES), BF)
    lines = []
    for head, value in enumerate(heads_of(rows)):
        lines.append(jnp.concatenate([value if at == head else blank for at in range(QUAD)], axis=1))
    return jnp.concatenate(lines, axis=0)


def spread_rows(rows):
    blank = jnp.zeros((HEAD_DIM, LANES), BF)
    first, second, third, fourth = heads_of(rows)
    lines = ((first, blank), (blank, third), (second, blank), (blank, fourth))
    return jnp.concatenate([jnp.concatenate(line, axis=1) for line in lines], axis=0)


def by_head(rows, squares, transposed=False):
    first, second, third, fourth = squares
    top, bottom = ((first, third), (second, fourth)) if transposed else ((first, second), (third, fourth))
    tile = jnp.concatenate([jnp.concatenate(top, axis=1), jnp.concatenate(bottom, axis=1)], axis=0)
    out = mm(spread_rows(rows), tile, 1, 1 if transposed else 0)
    left, right = out[:, :LANES], out[:, LANES:]
    parts = (left[:HEAD_DIM], right[2 * HEAD_DIM : 3 * HEAD_DIM], left[HEAD_DIM : 2 * HEAD_DIM], right[3 * HEAD_DIM :])
    return jnp.concatenate(parts, axis=0)


def norm_one_forward(s, windows):
    def step(index, carry):
        lanes = lane_tile(index)
        hat, _ = norm_parts(s.x[:, lanes])
        s.normed[:, lanes] = (hat * s.sums[G1] + s.sums[B1]).astype(BF)
        return carry

    lax.fori_loop(0, windows, step, 0)


def project_forward(s, windows):
    def step(index, carry):
        rows = chunk_of(index)
        bias = s.sums[jnp.where(index == 0, QB, VB)] * jnp.where(index == 1, 0.0, 1.0)
        out = mm(s.w_qkv[:, rows], s.normed[...], 0, 0)
        s.qkv[rows, :] = (out + wide(bias, windows)).astype(BF)
        return carry

    lax.fori_loop(0, 3, step, 0)


def attend_forward(s, windows, live_ref):
    def step(index, carry):
        lanes = lane_tile(index)
        live = jnp.broadcast_to(live_ref[pl.ds(index, 1), :], (LANES, LANES)).T
        masked = s.regions[jnp.where(index == windows - 1, 1, 0)] + MASK_VALUE * (1.0 - live)
        for quad in range(HEADS // QUAD):
            query = s.qkv[quad_rows(quad), lanes]
            key = s.qkv[quad_rows(quad, D), lanes]
            value = s.qkv[quad_rows(quad, 2 * D), lanes]
            products = mm(key, diagonal(query), 0, 0)
            squares = []
            for part in range(QUAD):
                head = quad * QUAD + part
                scores = products[:, part * LANES : (part + 1) * LANES] * SCORE_SCALE + (s.bias[head] + masked)
                exponent = jnp.exp(scores - jnp.max(scores, axis=0, keepdims=True))
                total = jnp.sum(exponent, axis=0, keepdims=True)
                soft = (exponent * (1.0 / total)).astype(BF)
                s.soft[index * HEADS + head] = soft
                squares.append(soft)
            s.merged[quad_rows(quad), lanes] = by_head(value, squares).astype(BF)
        return carry

    lax.fori_loop(0, windows, step, 0)


def norm_two_forward(s, windows, live_ref):
    def step(index, carry):
        lanes = lane_tile(index)
        hidden = s.x[:, lanes] + live_ref[pl.ds(index, 1), :] * (s.work[:, lanes] + s.sums[PB])
        s.hidden[:, lanes] = hidden
        s.work[:, lanes] = hidden + s.sums[F2B]
        hat, _ = norm_parts(hidden)
        s.second[:, lanes] = (hat * s.sums[G2] + s.sums[B2]).astype(BF)
        return carry

    lax.fori_loop(0, windows, step, 0)


def feed_forward(s, windows):
    def step(index, carry):
        rows = chunk_of(index)
        inner = mm(s.w_fc1[:, rows], s.second[...], 0, 0) + wide(s.sums[F1B + index], windows)
        active, slope = gelu_parts(inner)
        active = active.astype(BF)
        s.active[rows, :] = active
        s.slope[rows, :] = slope.astype(BF)
        s.work[...] += mm(s.w_fc2[rows, :], active, 0, 0)
        return carry

    lax.fori_loop(0, FEEDS, step, 0)


def feed_backward(s, sink, times):
    s.sums[...] = jnp.zeros(s.sums.shape, F32)
    s.bias[...] = jnp.zeros(s.bias.shape, F32)
    lowered = s.grad[...].astype(BF)
    s.low[...] = lowered
    s.sums[F2B] = fold(lowered.astype(F32))
    s.work[...] = jnp.zeros(s.work.shape, F32)

    def step(index, carry):
        rows = chunk_of(index)
        sink.put(0, mm(s.active[rows, :], s.low[...], 1, 1), feed_pieces(index, sink.shares), index == 0)
        grad_inner = mm(s.w_fc2[rows, :], s.low[...], 1, 0) * s.slope[rows, :].astype(F32)
        grad_inner = grad_inner.astype(BF)
        s.sums[F1B + index] = fold(grad_inner.astype(F32))
        sink.put(1, mm(s.second[...], grad_inner, 1, 1), row_pieces(UNIT_FC1 + index, sink.shares), index == 0)
        s.work[...] += mm(s.w_fc1[:, rows], grad_inner, 1, 0)
        sink.advance_at(index, times)
        return carry

    lax.fori_loop(0, FEEDS, step, 0)
    sink.settle(0)
    sink.settle(1)


def norm_two_backward(s, windows, live_ref):
    def step(index, carry):
        lanes = lane_tile(index)
        hat, scale = norm_parts(s.hidden[:, lanes])
        grad = s.work[:, lanes]
        s.sums[G2] += grad * hat
        s.sums[B2] += grad
        grad = s.grad[:, lanes] + norm_pull(grad, s.gains[1], hat, scale)
        s.grad[:, lanes] = grad
        grad_low = (grad * live_ref[pl.ds(index, 1), :]).astype(BF)
        s.low[:, lanes] = grad_low
        s.sums[PB] += grad_low.astype(F32)
        return carry

    lax.fori_loop(0, windows, step, 0)


def merge_backward(s, sink):
    sink.put(0, mm(s.merged[...], s.low[...], 1, 1), row_pieces(UNIT_PROJ, sink.shares), True)
    s.merged[...] = mm(s.w_proj[...], s.low[...], 1, 0).astype(BF)
    sink.settle(0)


def attend_backward(s, windows, sink, times):
    def step(index, carry):
        lanes = lane_tile(index)
        for quad in range(HEADS // QUAD):
            query = s.qkv[quad_rows(quad), lanes]
            key = s.qkv[quad_rows(quad, D), lanes]
            value = s.qkv[quad_rows(quad, 2 * D), lanes]
            grad_out = s.merged[quad_rows(quad), lanes]
            products = mm(value, diagonal(grad_out), 0, 0)
            softs, grads = [], []
            for part in range(QUAD):
                head = quad * QUAD + part
                soft_low = s.soft[index * HEADS + head]
                soft = soft_low.astype(F32)
                grad_soft = products[:, part * LANES : (part + 1) * LANES]
                inner = jnp.sum(soft * grad_soft, axis=0, keepdims=True)
                grad_scores = (soft * (grad_soft - inner)).astype(BF)
                s.bias[head] += grad_scores.astype(F32)
                softs.append(soft_low)
                grads.append(grad_scores)
            grad_query = (by_head(key, grads) * SCORE_SCALE).astype(BF)
            grad_key = (by_head(query, grads, True) * SCORE_SCALE).astype(BF)
            grad_value = by_head(grad_out, softs, True).astype(BF)
            s.qkv[quad_rows(quad), lanes] = grad_query
            s.qkv[quad_rows(quad, D), lanes] = grad_key
            s.qkv[quad_rows(quad, 2 * D), lanes] = grad_value
            s.sums[QB, quad_rows(quad), :] += grad_query.astype(F32)
            s.sums[VB, quad_rows(quad), :] += grad_value.astype(F32)
        sink.advance_at(index, times)
        return carry

    lax.fori_loop(0, windows, step, 0)


def project_backward(s, sink):
    def step(index, carry):
        rows = chunk_of(index)
        sink.put(1, mm(s.normed[...], s.qkv[rows, :], 1, 1), row_pieces(UNIT_QKV + index, sink.shares), index == 0)
        return carry

    lax.fori_loop(0, 3, step, 0)


def input_backward(s):
    s.work[...] = mm(s.w_qkv[...], s.qkv[...], 1, 0)


def norm_one_backward(s, windows):
    def step(index, carry):
        lanes = lane_tile(index)
        hat, scale = norm_parts(s.x[:, lanes])
        grad = s.work[:, lanes]
        s.sums[G1] += grad * hat
        s.sums[B1] += grad
        s.grad[:, lanes] += norm_pull(grad, s.gains[0], hat, scale)
        return carry

    lax.fori_loop(0, windows, step, 0)


def small_gradients(s, small_ref):
    places = lax.broadcasted_iota(jnp.int32, (D, LANES), 1)
    packed = jnp.zeros((D, LANES), F32)
    for index in range(VECTORS):
        packed = jnp.where(places == index, jnp.sum(s.sums[index], axis=1, keepdims=True), packed)
    small_ref[:VECTOR_ROWS, :] = packed.T[:VECTOR_ROWS]
    table = gather_bias(s.bias, s.spread, s.bias_rows)
    small_ref[VECTOR_ROWS:, :] = jnp.concatenate([table, jnp.zeros((HEADS, D - TABLE), F32)], axis=1)


def reversed_bits(value, count):
    turned = 0
    for bit in range(count):
        turned = turned * 2 + (value // 2**bit) % 2
    return turned


def row_pieces(unit, shares):
    rows, count = CHUNK // shares, shares.bit_length() - 1
    return [(share * rows, unit, reversed_bits(share, count)) for share in range(shares)]


def feed_pieces(index, shares):
    rows, count = CHUNK // shares, shares.bit_length() - 1
    pieces = []
    for share in range(shares // FEEDS):
        place = reversed_bits(index * (shares // FEEDS) + share, count)
        for part in range(FEEDS):
            pieces.append(((share * FEEDS + part) * rows, UNIT_FC2 + part, place))
    return pieces


class Plan:
    def __init__(self, pages, shares):
        self.shares, self.rows = shares, CHUNK // shares
        page_bits, row_bits = pages.bit_length() - 1, shares.bit_length() - 1
        others = page_bits - 1
        self.steps = []
        for kind in range(CLASSES):
            turn = kind % 2
            page = [(PAGE, 2 ** (1 + (bit + turn) % others)) for bit in range(others)]
            row = [(ROW, 2**bit) for bit in range(row_bits)]
            self.steps.append([(PAGE, 1)] + (row + page if kind == 2 else page + row))
        self.page_steps = [[0] + [at for at, step in enumerate(steps) if at and step[0] == PAGE] for steps in self.steps]
        self.halvings = page_bits + row_bits
        self.phases = self.halvings + page_bits
        self.sizes, self.axes = [], []
        for steps in self.steps:
            size, sizes, axes = [shares, self.rows, CHUNK], [], []
            for axis, _ in steps:
                axes.append(0 if axis == ROW else 1 if size[1] >= 16 else 2)
                size[axes[-1]] //= 2
                sizes.append(tuple(size))
            self.sizes.append(sizes)
            self.axes.append(axes)
        self.steps_at = self.schedule()

    def schedule(self):
        small = TRIPLES
        free, ready, stage_of, plan, now = {}, {}, {}, [], 0.0
        for triple in range(TRIPLES):
            for kind in range(CLASSES):
                stage_of[triple, kind] = 0
        stage_of[small, 0] = 0

        def link(key, phase):
            triple, kind = key
            if phase < self.halvings:
                axis, stride = self.steps[kind][phase]
                size = 2.0**-phase / 2 if triple != small else 0.125
            else:
                axis, stride = self.steps[kind][self.page_steps[kind][self.phases - 1 - phase]]
                size = 2.0 ** (phase - 2 * self.halvings)
            if axis == PAGE and stride == 1:
                return 0, size * PLAN_CORE
            return (axis, stride if axis == PAGE else 0), size * PLAN_LINK * (1.0 if stride == 1 or axis == PAGE else 1.5)

        def last_stage(key):
            return self.halvings if key[0] == small else self.phases + 1

        def allowed(key, point):
            triple, kind = key
            stage = stage_of[key]
            if stage > last_stage(key):
                return False
            if triple == small:
                return point >= len(PLAN_POINTS) - 1
            if stage == 0 and point < PLAN_THERE[triple]:
                return False
            if triple > 0 and stage_of[triple - 1, kind] <= stage:
                return False
            if triple >= RING and stage < self.halvings and stage_of[triple - RING, kind] <= stage + 1:
                return False
            if stage == 0 and triple >= DONE and stage_of[triple - DONE, kind] <= self.phases + 1:
                return False
            return not (stage == 0 and triple >= HELD and stage_of[triple - HELD, kind] <= self.halvings + 1)

        for point, work in enumerate(PLAN_POINTS):
            now += work
            if point == PLAN_HALO:
                free[ROW, 0] = max(now, free.get((ROW, 0), 0.0)) + PLAN_HALO_TIME
            steps, final = [], point == len(PLAN_POINTS) - 1
            while True:
                keys = [key for key in stage_of if allowed(key, point)]
                keys = [key for key in keys if final or ready.get(key, 0.0) <= now + PLAN_SLACK]
                if not keys:
                    break
                key = min(keys, key=lambda key: (max(ready.get(key, 0.0), now), -stage_of[key], key))
                stage = stage_of[key]
                now = max(now, ready.get(key, 0.0)) + (PLAN_ADD * 2.0**-stage if stage else 0.0)
                if stage == self.phases:
                    ready[key] = now + PLAN_LATENCY
                elif stage < last_stage(key):
                    name, length = link(key, stage)
                    free[name] = max(now, free.get(name, 0.0)) + length
                    ready[key] = free[name] + PLAN_LATENCY
                steps.append((*key, stage))
                stage_of[key] += 1
            plan.append(steps)
        assert all(stage_of[key] > last_stage(key) for key in stage_of)
        return plan

    def partner(self, kind, level):
        axis, stride = self.steps[kind][level]
        page, row = lax.axis_index(PAGE), lax.axis_index(ROW)
        mine = page if axis == PAGE else row
        bit = (mine // stride) % 2
        other = mine + (1 - 2 * bit) * stride
        return bit, ((other, row) if axis == PAGE else (page, other))

    def half(self, kind, which):
        slices = [slice(None)] * 3
        axis, size = self.axes[kind][0], self.sizes[kind][0]
        slices[axis] = pl.ds(pl.multiple_of(which * size[axis], 8), size[axis])
        return tuple(slices)

    def part(self, kind, level, sent=False):
        starts, sizes = [0, 0, 0], list(self.sizes[kind][0])
        for at in range(1, level + 1):
            axis = self.axes[kind][at]
            sizes[axis] //= 2
            bit, _ = self.partner(kind, at)
            which = 1 - bit if sent and at == level else bit
            starts[axis] = starts[axis] + which * sizes[axis]
        return (
            pl.ds(starts[0], sizes[0]),
            pl.ds(pl.multiple_of(starts[1], 8), sizes[1]),
            pl.ds(pl.multiple_of(starts[2], LANES), sizes[2]),
        )

    def place(self, kind, count):
        starts, sizes = [0, 0], [self.rows, CHUNK]
        for at in self.page_steps[kind][:count]:
            axis = self.axes[kind][at] - 1
            sizes[axis] //= 2
            bit, _ = self.partner(kind, at)
            starts[axis] = starts[axis] + bit * sizes[axis]
        return starts, sizes


class Reducer:
    def __init__(self, plan, s):
        self.plan, self.s = plan, s
        self.shares = plan.shares
        self.layer = 1

    def stage_copies(self, slot, pieces):
        return [
            pltpu.make_async_copy(
                self.s.staged.at[pl.ds(slot * CHUNK + start, self.plan.rows)],
                self.s.units[self.layer].at[unit, place],
                self.s.stage_sems.at[slot, number],
            )
            for number, (start, unit, place) in enumerate(pieces)
        ]

    def put(self, slot, grad, pieces, first):
        if first is not True:

            @pl.when(jnp.logical_not(first))
            def _():
                self.settle(slot)

        self.s.staged[pl.ds(slot * CHUNK, CHUNK), :] = grad
        for copy in self.stage_copies(slot, pieces):
            copy.start()

    def settle(self, slot):
        for copy in self.stage_copies(slot, row_pieces(0, self.shares)):
            copy.wait()

    def remote(self, source, target, unit, phase, device):
        return pltpu.make_async_remote_copy(
            src_ref=source,
            dst_ref=target,
            send_sem=self.s.send_sems.at[unit, phase],
            recv_sem=self.s.recv_sems.at[unit, phase],
            device_id=device,
            device_id_type=MESH,
        )

    def unit_half(self, triple, kind, which):
        unit = CLASSES * (triple % GROUPS) + kind
        return self.s.units[1 - triple // GROUPS].at[unit].at[self.plan.half(kind, which)]

    def held(self, triple, kind):
        return self.s.held.at[CLASSES * (triple % HELD) + kind]

    def halving(self, triple, kind, level):
        plan = self.plan
        bit, device = plan.partner(kind, level)
        target = self.s.landing[kind][level].at[triple % RING]
        if level == 0:
            source = self.unit_half(triple, kind, 1 - bit)
        else:
            source = self.held(triple, kind).at[plan.part(kind, level, True)]
        return self.remote(source, target, CLASSES * triple + kind, level, device)

    def own_half(self, triple, kind):
        bit, _ = self.plan.partner(kind, 0)
        sem = self.s.own_sems.at[CLASSES * triple + kind, 0]
        return pltpu.make_async_copy(self.unit_half(triple, kind, bit), self.held(triple, kind), sem)

    def finished(self, triple, kind):
        return self.held(triple, kind).at[self.plan.part(kind, self.plan.halvings - 1)].at[0]

    def done(self, triple, kind, count):
        starts, sizes = self.plan.place(kind, count)
        return self.s.done.at[
            CLASSES * (triple % DONE) + kind,
            pl.ds(pl.multiple_of(starts[0], 8), sizes[0]),
            pl.ds(pl.multiple_of(starts[1], LANES), sizes[1]),
        ]

    def gathering(self, triple, kind, phase):
        plan = self.plan
        count = len(plan.page_steps[kind]) - (phase - plan.halvings)
        part = self.done(triple, kind, count)
        _, device = plan.partner(kind, plan.page_steps[kind][count - 1])
        return self.remote(part, part, CLASSES * triple + kind, phase, device)

    def result(self, triple, kind):
        which, row_block, col_block = TARGETS[triple % GROUPS][kind]
        rows = self.plan.rows
        target = self.s.results[which].at[
            1 - triple // GROUPS, pl.ds(row_block * rows, rows), pl.ds(col_block * CHUNK, CHUNK)
        ]
        sem = self.s.own_sems.at[CLASSES * triple + kind, 1]
        return pltpu.make_async_copy(self.done(triple, kind, 0), target, sem)

    def start(self, triple, kind, phase):
        plan = self.plan
        if phase < plan.halvings:
            if triple >= RING:
                pl.semaphore_wait(self.s.free_sems.at[kind, phase], 1)
            self.halving(triple, kind, phase).start()
            if phase == 0:
                self.own_half(triple, kind).start()
        elif phase < plan.phases:
            if phase == plan.halvings:
                self.done(triple, kind, len(plan.page_steps[kind]))[...] = self.finished(triple, kind)[...]
            self.gathering(triple, kind, phase).start()
        elif phase == plan.phases:
            self.result(triple, kind).start()

    def finish(self, triple, kind, phase):
        plan, s = self.plan, self.s
        if phase < plan.halvings:
            self.halving(triple, kind, phase).wait()
            if phase == 0:
                self.own_half(triple, kind).wait()
            landed = s.landing[kind][phase].at[triple % RING]
            kept = self.held(triple, kind).at[plan.part(kind, phase)]
            for share in range(landed.shape[0]):
                kept[share] += landed[share]
            if triple < TRIPLES - RING:
                _, device = plan.partner(kind, phase)
                pl.semaphore_signal(s.free_sems.at[kind, phase], inc=1, device_id=device, device_id_type=MESH)
        elif phase < plan.phases:
            self.gathering(triple, kind, phase).wait()
        else:
            self.result(triple, kind).wait()

    def advance(self, point):
        for triple, kind, stage in self.plan.steps_at[point]:
            if triple == TRIPLES:
                self.small_step(stage - 1)
                continue
            if stage > 0:
                self.finish(triple, kind, stage - 1)
            self.start(triple, kind, stage)

    def advance_at(self, index, points):
        for number, point in enumerate(points):
            if self.plan.steps_at[point]:

                @pl.when(index == number)
                def _(point=point):
                    self.advance(point)

    def small_copy(self, phase):
        s = self.s
        _, device = self.plan.partner(0, phase)
        return pltpu.make_async_remote_copy(
            src_ref=s.small_own if phase == 0 else s.small_parts.at[phase - 1],
            dst_ref=s.small_parts.at[phase],
            send_sem=s.small_sems.at[0, phase],
            recv_sem=s.small_sems.at[1, phase],
            device_id=device,
            device_id_type=MESH,
        )

    def small_step(self, phase):
        s = self.s
        if phase >= 0:
            self.small_copy(phase).wait()
            s.small_parts[phase] += s.small_own[...] if phase == 0 else s.small_parts[phase - 1]
        if phase + 1 < self.plan.halvings:
            self.small_copy(phase + 1).start()


PLAN_POINTS = (0, 2, 3) + (2.7,) * 6 + (5.2, 3, 3, 6) + (3.2,) * 4 + (0.3, 2, 3) + (2.7,) * 6 + (3, 3, 3, 3)
PLAN_THERE = (0, 0, 2, 10, 17, 17, 19, 26)
PLAN_HALO, PLAN_HALO_TIME = 9, 12.3
PLAN_CORE, PLAN_LINK, PLAN_LATENCY, PLAN_ADD, PLAN_SLACK = 1.7, 20.0, 2.0, 0.9, 0.0


class Moves:
    def __init__(self, sems):
        self.sems, self.used = sems, 0

    def __call__(self, source, target):
        number, self.used = self.used, self.used + 1
        make = functools.partial(pltpu.make_async_copy, source, target, self.sems.at[number])
        make().start()
        return lambda: make().wait()


class Refs:
    pass


def run(plan, layout, *refs):
    s = Refs()
    for name, ref in zip(layout, refs):
        setattr(s, name, ref)
    rest = list(refs[len(layout) :])
    s.landing = [[rest.pop(0) for _ in range(plan.halvings)] for _ in range(CLASSES)]
    s.results = (s.sum_qkv, s.sum_proj, s.sum_fc1, s.sum_fc2)
    s.units = (s.units_zero, s.units_one)
    s.page = s.staged.at[pl.ds(0, s.plain.shape[0])]
    s.spread = s.qkv.at[pl.ds(0, s.in_spread.shape[0])]
    windows = s.x.shape[1] // LANES
    patches = s.dense.shape[0] // SPLITS
    half, half_rows = patches // 2, s.dense.shape[0] // 2
    padded = 16 * -(-half // 16)
    upper, lower = pl.ds(0, half_rows), pl.ds(half_rows, half_rows)
    reducer = Reducer(plan, s)
    move = Moves(s.move_sems)
    page, row = lax.axis_index(PAGE), lax.axis_index(ROW)
    count = lax.axis_size(ROW)
    above, below = (page, (row + count - 1) % count), (page, (row + 1) % count)

    def halo(number, source, target, device):
        make = functools.partial(
            pltpu.make_async_remote_copy,
            src_ref=source,
            dst_ref=target,
            send_sem=s.halo_sems.at[0, number],
            recv_sem=s.halo_sems.at[1, number],
            device_id=device,
            device_id_type=MESH,
        )
        make().start()
        return lambda: make().wait()

    tokens_there = move(s.in_tokens, s.tokens)
    places_there = (move(s.in_plain, s.plain), move(s.in_moved, s.moved))
    swaps_there = (move(s.in_swap_on, s.swap_on), move(s.in_swap_back, s.swap_back))
    spread_there = move(s.in_spread, s.spread)
    weights = ((s.in_qkv, s.w_qkv), (s.in_proj, s.w_proj), (s.in_fc1, s.w_fc1), (s.in_fc2, s.w_fc2))

    def fetch_weight(which, layer):
        source, target = weights[which]
        return move(source.at[layer], target)

    there = [fetch_weight(which, 0) for which in range(4)]

    barrier = pltpu.get_barrier_semaphore()
    devices = [plan.partner(0, level)[1] for level in range(plan.halvings)] + [above, below]
    for device in devices:
        pl.semaphore_signal(barrier, inc=1, device_id=device, device_id_type=MESH)
    pl.semaphore_wait(barrier, len(devices))

    s.live[...] = jnp.zeros(s.live.shape, F32)
    for window in range(windows):
        s.live[window : window + 1, :] = jnp.full((1, LANES), 1.0 - s.blank[0, window].astype(F32))
    live_there = halo(0, s.live, s.live_upper, above)
    grad_there = halo(1, s.in_grad.at[upper], s.grad_upper, above)
    grad_lower_there = move(s.in_grad.at[lower], s.dense.at[lower])
    s.page[...] = jnp.zeros(s.page.shape, F32)
    tokens_there()
    cols = s.tokens.shape[1]
    for line in range(WIN):
        s.page[pl.ds(line * cols, cols), :] = s.tokens[line].astype(F32)
    places_there[0]()
    to_channels(s.page, s.plain, s.x, True)
    saves = [move(s.x, s.kept_x)]
    spread_columns(s, 0)
    spread_there()
    spread_bias(s, 0)
    region_masks(False, s.regions)
    norm_one_forward(s, windows)
    saves.append(move(s.normed, s.kept_normed))
    there[QKV]()
    project_forward(s, windows)
    qkv_saved = move(s.qkv, s.kept_qkv)
    there[QKV] = fetch_weight(QKV, 1)
    attend_forward(s, windows, s.live)
    saves.append(move(s.soft, s.kept_soft))
    saves.append(move(s.merged, s.kept_merged))
    there[PROJ]()
    s.work[...] = mm(s.w_proj[...], s.merged[...], 0, 0)
    there[PROJ] = fetch_weight(PROJ, 1)
    norm_two_forward(s, windows, s.live)
    saves.append(move(s.hidden, s.kept_hidden))
    saves.append(move(s.second, s.kept_second))
    there[FC1]()
    there[FC2]()
    feed_forward(s, windows)
    saves.append(move(s.active, s.kept_active))
    saves.append(move(s.slope, s.kept_slope))
    there[FC1] = fetch_weight(FC1, 1)
    there[FC2] = fetch_weight(FC2, 1)
    to_dense(s.work, s.plain, s.dense.at[upper], padded)
    upper_there = halo(2, s.dense.at[upper], s.upper, above)

    qkv_saved()
    spread_there = move(s.in_spread, s.spread)
    places_there[1]()
    swaps_there[0]()
    saves.pop(0)()
    move_own(s.work, s.swap_on, s.x, windows, 0)
    spread_columns(s, 1)
    spread_there()
    spread_bias(s, 1)
    region_masks(True, s.regions)
    live_there()
    shifted_live(s, windows)
    grad_there()
    grad_lower_there()
    from_dense(s.grad_upper, s.page, 0)
    from_dense(s.dense.at[lower], s.page, half)
    to_channels(s.page, s.moved, s.grad)
    for saved in saves:
        saved()
    upper_there()
    from_dense(s.upper, s.page, 0)
    add_halo(s.page, s.moved, s.x, half, padded)
    norm_one_forward(s, windows)
    there[QKV]()
    project_forward(s, windows)
    attend_forward(s, windows, s.live_two)
    there[PROJ]()
    s.work[...] = mm(s.w_proj[...], s.merged[...], 0, 0)
    norm_two_forward(s, windows, s.live_two)
    there[FC1]()
    there[FC2]()
    feed_forward(s, windows)
    to_dense(s.work, s.moved, s.dense, s.moved.shape[0])
    out_there = halo(3, s.dense.at[upper], s.out_tokens.at[upper], below)
    out_kept = move(s.dense.at[lower], s.out_tokens.at[lower])

    spread_gains(s, 1)

    def backward(layer, live_ref, fetch, points):
        reducer.layer = layer
        first = 0 if layer else FEEDS
        feed_backward(s, reducer, points[:first])
        reducer.advance(points[first])
        fetch(0)
        norm_two_backward(s, windows, live_ref)
        reducer.advance(points[first + 1])
        fetch(1)
        merge_backward(s, reducer)
        reducer.advance(points[first + 2])
        fetch(2)
        attend_backward(s, windows, reducer, points[first + 3 :])
        fetch(3)

    back = {}

    def refill(point):
        if point == 0:
            back[0] = [move(s.kept_active, s.active), move(s.kept_slope, s.slope), move(s.kept_second, s.second)]
            back[0] += [fetch_weight(FC1, 0), fetch_weight(FC2, 0)]
        elif point == 1:
            back[1] = [move(s.kept_hidden, s.hidden)]
        elif point == 2:
            back[2] = [fetch_weight(PROJ, 0)]
        elif point == 3:
            back[2] += [move(s.kept_merged, s.merged)]
            back[3] = [move(s.kept_soft, s.soft)]
        elif point == 4:
            back[4] = [move(s.kept_x, s.x)]
        else:
            back[3] += [move(s.kept_qkv, s.qkv), move(s.kept_normed, s.normed), fetch_weight(QKV, 0)]

    def needed(point):
        if point in back:
            for arrived in back.pop(point):
                arrived()

    backward(1, s.live_two, refill, range(9))
    input_backward(s)
    norm_one_backward(s, windows)
    refill(4)
    out_there()
    to_dense(s.grad, s.moved, s.dense.at[upper], padded)
    next_there = halo(4, s.dense.at[upper], s.next_upper, below)
    reducer.advance(9)
    project_backward(s, reducer)
    spread_there = move(s.in_spread, s.spread)
    reducer.settle(1)
    reducer.advance(10)

    swaps_there[1]()
    move_own(s.grad, s.swap_back, s.work, windows, -1)
    spread_there()
    small_gradients(s, s.small_own.at[1])
    refill(5)
    spread_gains(s, 0)
    reducer.advance(11)
    next_there()
    from_dense(s.next_upper, s.page, 0)
    s.grad[...] = s.work[...]
    add_halo(s.page, s.plain, s.grad, half, padded)
    reducer.advance(12)
    needed(0)

    def wait_next(point):
        needed(point + 1)

    backward(0, s.live, wait_next, range(13, 26))
    project_backward(s, reducer)
    reducer.settle(1)
    reducer.advance(26)
    input_backward(s)
    spread_there = move(s.in_spread, s.spread)
    reducer.advance(27)
    needed(4)
    norm_one_backward(s, windows)
    out_kept()
    to_dense(s.grad, s.plain, s.dense, s.plain.shape[0])
    grad_kept = move(s.dense, s.grad_tokens)
    reducer.advance(28)
    spread_there()
    small_gradients(s, s.small_own.at[0])
    reducer.advance(29)
    finish_small(s, plan, row)
    grad_kept()


def finish_small(s, plan, row):
    total = s.small_parts.at[plan.halvings - 1]
    outs = (
        (s.d_ln_gain, (G1, G2)),
        (s.d_ln_bias, (B1, B2)),
        (s.d_qv_bias, (QB, VB)),
        (s.d_proj_bias, (PB,)),
        (s.d_fc1_bias, tuple(range(F1B, F1B + FEEDS))),
        (s.d_fc2_bias, (F2B,)),
    )
    for layer in range(2):
        s.d_table[layer] = total[layer, VECTOR_ROWS:, :OFFSETS]
        for ref, indices in outs:
            whole = jnp.concatenate([total[layer, index : index + 1, :] for index in indices], axis=1)
            size = ref.shape[1]
            mine = jnp.zeros((1, size), F32)
            for share in range(plan.shares):
                mine = jnp.where(row == share, whole[:, share * size : (share + 1) * size], mine)
            ref[layer : layer + 1, :] = mine


def placements(cols):
    windows = cols // WIN
    patches = WIN * cols
    padded = -(-patches // LANES) * LANES
    plain = np.zeros((padded, windows * LANES), np.float32)
    moved = np.zeros((padded, windows * LANES), np.float32)
    for line in range(WIN):
        for col in range(cols):
            source = line * cols + col
            plain[source, (col // WIN) * LANES + line * WIN + col % WIN] = 1
            new_line, new_col = (line - SHIFT) % WIN, (col - SHIFT) % cols
            moved[source, (new_col // WIN) * LANES + new_line * WIN + new_col % WIN] = 1
    return plain.astype(BF), moved.astype(BF)


def swaps():
    on = np.zeros((2 * LANES, LANES), np.float32)
    back = np.zeros((2 * LANES, LANES), np.float32)
    for line in range(SHIFT):
        for col in range(WIN):
            moved, plain = line * WIN + col, (line + SHIFT) * WIN + (col + SHIFT) % WIN
            on[plain + (LANES if col >= SHIFT else 0), moved] = 1
            back[moved + (LANES if col < SHIFT else 0), plain] = 1
    return on.astype(BF), back.astype(BF)


def table_spread():
    size = 2 * WIN - 1
    spread = np.zeros((WIN, 2 * LANES, TABLE), np.float32)
    for key_col in range(WIN):
        for offset in range(size):
            for col in range(WIN):
                spread[key_col, offset * WIN + col, offset * size + col - key_col + WIN - 1] = 1
    spread = spread.reshape(WIN // 2, 2, 2 * LANES, TABLE).swapaxes(1, 2)
    return spread.reshape(WIN * LANES, 2 * TABLE).astype(BF)


def copy_all(*refs):
    *refs, sems = refs
    count = len(refs) // 3
    sources, targets, held = refs[:count], refs[count : 2 * count], refs[2 * count :]
    ways = [*zip(sources, held), *zip(held, targets)]
    copies = [pltpu.make_async_copy(*way, sems.at[number]) for number, way in enumerate(ways)]
    for copy in copies[:count]:
        copy.start()
    for incoming, outgoing in zip(copies[:count], copies[count:]):
        incoming.wait()
        outgoing.start()
    for copy in copies[count:]:
        copy.wait()


def hand_out(values):
    anywhere = pl.BlockSpec(memory_space=pl.ANY)
    return pl.pallas_call(
        copy_all,
        out_shape=[jax.ShapeDtypeStruct(value.shape, value.dtype) for value in values],
        in_specs=[anywhere] * len(values),
        out_specs=[anywhere] * len(values),
        scratch_shapes=[pltpu.VMEM(value.shape, value.dtype) for value in values]
        + [pltpu.SemaphoreType.DMA((2 * len(values),))],
        compiler_params=pltpu.CompilerParams(vmem_limit_bytes=VMEM_LIMIT),
        name="results",
    )(*values)


def per_device(
    page_tokens,
    blank_mask,
    cotangent,
    ln_gain,
    ln_bias,
    qv_bias,
    rel_table,
    w_qkv,
    w_proj,
    proj_bias,
    w_fc1,
    fc1_bias,
    w_fc2,
    fc2_bias,
):
    pages, shares = lax.axis_size(PAGE), lax.axis_size(ROW)
    plan = Plan(pages, shares)
    cols = page_tokens.shape[2]
    windows, lanes = cols // WIN, cols // WIN * LANES
    dense = ((WIN * cols * SPLITS, LANES), F32)
    half_dense = ((WIN * cols * SPLITS // 2, LANES), F32)
    plain, moved = (jnp.asarray(place) for place in placements(cols))
    live_rows = 8 * -(-windows // 8)
    scalar_inputs = dict(blank=blank_mask[0])
    small_inputs = dict(
        table=rel_table,
        ln_gain=ln_gain,
        ln_bias=ln_bias,
        qv_bias=qv_bias,
        proj_bias=proj_bias,
        fc1_bias=fc1_bias,
        fc2_bias=fc2_bias,
    )
    large_inputs = dict(
        in_tokens=page_tokens[0],
        in_grad=cotangent.reshape(dense[0]),
        in_plain=plain,
        in_moved=moved,
        in_swap_on=jnp.asarray(swaps()[0]),
        in_swap_back=jnp.asarray(swaps()[1]),
        in_spread=jnp.asarray(table_spread()),
        in_qkv=w_qkv,
        in_proj=w_proj,
        in_fc1=w_fc1,
        in_fc2=w_fc2,
    )
    saved = dict(
        x=((D, lanes), F32),
        normed=((D, lanes), BF),
        qkv=((3 * D, lanes), BF),
        soft=((windows * HEADS, LANES, LANES), BF),
        merged=((D, lanes), BF),
        hidden=((D, lanes), F32),
        second=((D, lanes), BF),
        active=((FF, lanes), BF),
        slope=((FF, lanes), BF),
    )
    units = ((UNITS, shares, CHUNK // shares, CHUNK), F32)
    large_outputs = dict(
        out_tokens=dense,
        grad_tokens=dense,
        sum_qkv=((2, D // shares, 3 * D), F32),
        sum_proj=((2, D // shares, D), F32),
        sum_fc1=((2, D // shares, FF), F32),
        sum_fc2=((2, FF // shares, D), F32),
        units_zero=units,
        units_one=units,
        kept_x=((D, lanes), F32),
        kept_normed=((D, lanes), BF),
        kept_qkv=((3 * D, lanes), BF),
        kept_soft=((windows * HEADS, LANES, LANES), BF),
        kept_merged=((D, lanes), BF),
        kept_hidden=((D, lanes), F32),
        kept_second=((D, lanes), BF),
        kept_active=((FF, lanes), BF),
        kept_slope=((FF, lanes), BF),
    )
    small_outputs = dict(
        d_ln_gain=((2, 2 * D // shares), F32),
        d_ln_bias=((2, 2 * D // shares), F32),
        d_qv_bias=((2, 2 * D // shares), F32),
        d_proj_bias=((2, D // shares), F32),
        d_fc1_bias=((2, FF // shares), F32),
        d_fc2_bias=((2, D // shares), F32),
        d_table=((2, HEADS, OFFSETS), F32),
    )
    small = (2, SMALL, D)
    vmem = dict(
        saved,
        tokens=((WIN, cols, D), BF),
        plain=(plain.shape, BF),
        moved=(moved.shape, BF),
        w_qkv=((D, 3 * D), BF),
        w_proj=((D, D), BF),
        w_fc1=((D, FF), BF),
        w_fc2=((FF, D), BF),
        dense=dense,
        upper=half_dense,
        swap_on=((2 * LANES, LANES), BF),
        swap_back=((2 * LANES, LANES), BF),
        grad_upper=half_dense,
        next_upper=half_dense,
        live_upper=((live_rows, LANES), F32),
        live_two=((live_rows, LANES), F32),
        work=((D, lanes), F32),
        grad=((D, lanes), F32),
        low=((D, lanes), BF),
        sums=((VECTORS, D, LANES), F32),
        gains=((2, D, LANES), F32),
        bias=((HEADS, LANES, LANES), F32),
        bias_rows=((HEADS * LANES, LANES), F32),
        regions=((2, LANES, LANES), F32),
        padded_table=((HEADS, TABLE), F32),
        live=((live_rows, LANES), F32),
        vector_rows=((VECTOR_ROWS, D), F32),
        staged=((2 * CHUNK, CHUNK), F32),
        done=((DONE * CLASSES, CHUNK // shares, CHUNK), F32),
        held=((HELD * CLASSES,) + plan.sizes[0][0], F32),
        small_own=(small, F32),
        small_parts=((plan.halvings,) + small, F32),
    )
    semaphores = dict(
        move_sems=pltpu.SemaphoreType.DMA((48,)),
        halo_sems=pltpu.SemaphoreType.DMA((2, 5)),
        send_sems=pltpu.SemaphoreType.DMA((2 * UNITS, plan.phases)),
        recv_sems=pltpu.SemaphoreType.DMA((2 * UNITS, plan.phases)),
        own_sems=pltpu.SemaphoreType.DMA((2 * UNITS, 2)),
        stage_sems=pltpu.SemaphoreType.DMA((2, shares)),
        small_sems=pltpu.SemaphoreType.DMA((2, plan.halvings)),
        free_sems=pltpu.SemaphoreType.REGULAR((CLASSES, plan.halvings)),
    )
    landing = [((RING,) + size, F32) for sizes in plan.sizes for size in sizes]
    layout = [*scalar_inputs, *small_inputs, *large_inputs, *small_outputs, *large_outputs, *vmem, *semaphores]
    in_vmem, anywhere = pl.BlockSpec(memory_space=pltpu.VMEM), pl.BlockSpec(memory_space=pl.ANY)
    outputs = {**small_outputs, **large_outputs}
    results = pl.pallas_call(
        functools.partial(run, plan, layout),
        out_shape=[jax.ShapeDtypeStruct(*shape) for shape in outputs.values()],
        in_specs=[pl.BlockSpec(memory_space=pltpu.SMEM)] + [in_vmem] * len(small_inputs) + [anywhere] * len(large_inputs),
        out_specs=[in_vmem] * len(small_outputs) + [anywhere] * len(large_outputs),
        scratch_shapes=[pltpu.VMEM(*shape) for shape in vmem.values()]
        + list(semaphores.values())
        + [pltpu.VMEM(*shape) for shape in landing],
        compiler_params=pltpu.CompilerParams(
            vmem_limit_bytes=VMEM_LIMIT, collective_id=0, has_side_effects=True
        ),
        name="two_layers",
    )(*scalar_inputs.values(), *small_inputs.values(), *large_inputs.values())
    results = hand_out(results[: len(small_outputs) + 6])
    d_ln_gain, d_ln_bias, d_qv_bias, d_proj_bias, d_fc1_bias, d_fc2_bias, d_table = results[: len(small_outputs)]
    out_tokens, grad_tokens, sum_qkv, sum_proj, sum_fc1, sum_fc2 = results[len(small_outputs) :]
    return (
        out_tokens.reshape(cotangent.shape),
        grad_tokens.reshape(cotangent.shape),
        d_ln_gain,
        d_ln_bias,
        d_qv_bias,
        d_table,
        sum_qkv,
        sum_proj,
        d_proj_bias,
        sum_fc1,
        d_fc1_bias,
        sum_fc2,
        d_fc2_bias,
    )


def solution(mesh):
    tokens, by_row, shares = P(PAGE, ROW, None, None), P(None, ROW), P(None, ROW, None)
    return jax.shard_map(
        per_device,
        mesh=mesh,
        in_specs=(tokens, P(PAGE, ROW, None), tokens) + (P(),) * 11,
        out_specs=(tokens, tokens)
        + (by_row, by_row, by_row, P(), shares, shares, by_row, shares, by_row, shares, by_row),
        check_vma=False,
    )
```

```python
import functools

import jax
import jax.numpy as jnp
import numpy as np
from jax import lax
from jax.experimental import pallas as pl
from jax.experimental.pallas import tpu as pltpu
from jax.sharding import PartitionSpec as P

WIN = 10
SHIFT = 5
AREA = WIN * WIN
LANES = 128
D = 512
HEADS = 16
HEAD_DIM = 32
FF = 2048
CHUNK = 512
FEEDS = FF // CHUNK
SPLITS = D // LANES
EPSILON = 1e-05
MASK_VALUE = -100.0
NEVER = -1e30
SCORE_SCALE = HEAD_DIM ** (-0.5)
VMEM_LIMIT = 63 * 1024 * 1024 + 512 * 1024
BF = jnp.bfloat16
F32 = jnp.float32
MESH = pl.DeviceIdType.MESH
PAGE, ROW = "page", "row"

G1, B1, G2, B2, QB, VB, PB, F2B, F1B, VECTORS = 0, 1, 2, 3, 4, 5, 6, 7, 8, 12
VECTOR_ROWS = 16
SMALL = VECTOR_ROWS + HEADS
OFFSETS = (2 * WIN - 1) ** 2
TABLE = 384

UNIT_FC1, UNIT_FC2, UNIT_PROJ, UNIT_QKV, UNITS = 0, 4, 8, 9, 12
CLASSES = 3
GROUPS = UNITS // CLASSES
TRIPLES = 2 * GROUPS
HELD = 4
DONE = 5
RING = 3
QKV, PROJ, FC1, FC2 = range(4)
TARGETS = (
    ((FC1, 0, 0), (FC1, 0, 1), (FC1, 0, 2)),
    ((FC1, 0, 3), (FC2, 0, 0), (FC2, 1, 0)),
    ((FC2, 2, 0), (FC2, 3, 0), (PROJ, 0, 0)),
    ((QKV, 0, 0), (QKV, 0, 1), (QKV, 0, 2)),
)


def mm(left, right, left_dim, right_dim):
    return lax.dot_general(
        left, right, (((left_dim,), (right_dim,)), ((), ())), preferred_element_type=F32
    )


def split(values):
    high = values.astype(BF)
    return high, (values - high.astype(F32)).astype(BF)


def lane_tile(index):
    return pl.ds(pl.multiple_of(index * LANES, LANES), LANES)


def chunk_of(index):
    return pl.ds(pl.multiple_of(index * CHUNK, CHUNK), CHUNK)


def wide(column, count):
    return jnp.concatenate([column] * count, axis=1)


def fold(values):
    total = values[:, :LANES]
    for start in range(LANES, values.shape[1], LANES):
        total = total + values[:, start : start + LANES]
    return total


def norm_parts(values):
    center = values - jnp.sum(values, axis=0, keepdims=True) * (1.0 / D)
    spread = jnp.sum(center * center, axis=0, keepdims=True) * (1.0 / D)
    scale = lax.rsqrt(spread + EPSILON)
    return center * scale, scale


def norm_pull(grad, gain, hat, scale):
    scaled = grad * gain
    mean_one = jnp.sum(scaled, axis=0, keepdims=True) * (1.0 / D)
    mean_two = jnp.sum(scaled * hat, axis=0, keepdims=True) * (1.0 / D)
    return scale * (scaled - mean_one - hat * mean_two)


def gelu_parts(inner):
    step = 1.0 / (1.0 + (0.3275911 * 0.7071067811865476) * jnp.abs(inner))
    bell = jnp.exp(inner * inner * -0.5)
    poly = 0.5 * 1.061405429
    for factor in (-1.453152027, 1.421413741, -0.284496736, 0.254829592):
        poly = poly * step + 0.5 * factor
    tail = poly * step * bell
    below = jnp.where(inner >= 0, 1.0 - tail, tail)
    return inner * below, below + inner * bell * 0.3989422804014327


def to_channels(page_ref, place_ref, out_ref, exact=False):
    def step(index, carry):
        channels = pl.ds(pl.multiple_of(index * 256, 256), 256)
        values = page_ref[:, channels]
        if exact:
            out_ref[channels, :] = mm(values.astype(BF), place_ref[...], 0, 0)
        else:
            high, low = split(values)
            out_ref[channels, :] = mm(high, place_ref[...], 0, 0) + mm(low, place_ref[...], 0, 0)
        return carry

    lax.fori_loop(0, D // 256, step, 0)


def to_dense(values_ref, place_ref, dense_ref, padded):
    count = dense_ref.shape[0] // SPLITS
    for index in range(D // 256):
        high, low = split(values_ref[index * 256 : (index + 1) * 256, :])
        page = mm(place_ref[:padded, :], high, 1, 1) + mm(place_ref[:padded, :], low, 1, 1)
        for part in range(2):
            rows = pl.ds(2 * index + part, count, stride=SPLITS)
            dense_ref[rows, :] = page[:count, part * LANES : (part + 1) * LANES]


def from_dense(dense_ref, page_ref, row):
    count = dense_ref.shape[0] // SPLITS
    for part in range(SPLITS):
        rows = pl.ds(part, count, stride=SPLITS)
        page_ref[pl.ds(row, count), part * LANES : (part + 1) * LANES] = dense_ref[rows, :]


def add_halo(page_ref, place_ref, out_ref, count, padded):
    page_ref[pl.ds(count, padded - count), :] = jnp.zeros((padded - count, D), F32)

    def step(index, carry):
        channels = pl.ds(pl.multiple_of(index * 256, 256), 256)
        high, low = split(page_ref[:padded, channels])
        out_ref[channels, :] += mm(high, place_ref[:padded, :], 0, 0) + mm(low, place_ref[:padded, :], 0, 0)
        return carry

    lax.fori_loop(0, D // 256, step, 0)


def move_own(values_ref, swap_ref, out_ref, windows, first):
    for window in range(windows):
        sources = [(window + first + part) % windows * LANES for part in range(2)]
        values = jnp.concatenate([values_ref[:, start : start + LANES] for start in sources], axis=1)
        high, low = split(values)
        target = slice(window * LANES, (window + 1) * LANES)
        out_ref[:, target] = mm(high, swap_ref[...], 1, 0) + mm(low, swap_ref[...], 1, 0)


def vector_rows(s, layer):
    rows = s.vector_rows
    sources = ((G1, s.ln_gain, 0), (B1, s.ln_bias, 0), (G2, s.ln_gain, 1), (B2, s.ln_bias, 1))
    sources += ((QB, s.qv_bias, 0), (VB, s.qv_bias, 1), (PB, s.proj_bias, 0), (F2B, s.fc2_bias, 0))
    sources += tuple((F1B + part, s.fc1_bias, part) for part in range(FEEDS))
    for index, source, part in sources:
        rows[index : index + 1, :] = source[layer : layer + 1, part * D : (part + 1) * D]
    rows[VECTORS:, :] = jnp.zeros((VECTOR_ROWS - VECTORS, D), F32)
    return rows[...].T


def spread_columns(s, layer):
    columns = vector_rows(s, layer)
    for index in range(VECTORS):
        s.sums[index] = jnp.broadcast_to(columns[:, index : index + 1], (D, LANES))


def spread_gains(s, layer):
    columns = vector_rows(s, layer)
    for index, vector in enumerate((G1, G2)):
        s.gains[index] = jnp.broadcast_to(columns[:, vector : vector + 1], (D, LANES))


def spread_part(col):
    rows, lanes = (col // 2) * 2 * LANES, (col % 2) * TABLE
    return slice(rows, rows + 2 * LANES), slice(lanes, lanes + TABLE)


def spread_bias(s, layer):
    spread_ref, rows_ref, bias_ref = s.spread, s.bias_rows, s.bias
    s.padded_table[...] = jnp.zeros(s.padded_table.shape, F32)
    s.padded_table[:, :OFFSETS] = s.table[layer]
    high, low = split(s.padded_table[...])
    parts = []
    for col in range(WIN):
        chosen = spread_ref[spread_part(col)]
        parts.append(mm(high, chosen, 1, 1) + mm(low, chosen, 1, 1))
    source = jnp.concatenate(parts, axis=0)
    rows_ref[...] = jnp.zeros(rows_ref.shape, F32)
    for row in range(WIN):
        shift = (WIN - 1 - row) * WIN
        moved = source if shift == 0 else pltpu.roll(source, 2 * LANES - shift, axis=1)
        rows_ref[pl.ds(row * WIN * HEADS, WIN * HEADS), :] = moved[:, :LANES]
    for head in range(HEADS):
        bias_ref[head] = rows_ref[pl.ds(head, LANES, stride=HEADS), :]


def gather_bias(grad_ref, spread_ref, rows_ref):
    for head in range(HEADS):
        rows_ref[pl.ds(head, LANES, stride=HEADS), :] = grad_ref[head]
    total = jnp.zeros((WIN * HEADS, 2 * LANES), F32)
    for row in range(WIN):
        shift = (WIN - 1 - row) * WIN
        piece = rows_ref[pl.ds(row * WIN * HEADS, WIN * HEADS), :]
        piece = jnp.concatenate([piece, jnp.zeros_like(piece)], axis=1)
        total = total + (piece if shift == 0 else pltpu.roll(piece, shift, axis=1))
    table = jnp.zeros((HEADS, TABLE), F32)
    for col in range(WIN):
        for part in split(total[col * HEADS : (col + 1) * HEADS]):
            table = table + mm(part, spread_ref[spread_part(col)], 1, 0)
    return table


def region_masks(shifted_layer, out_ref):
    key = lax.broadcasted_iota(jnp.int32, (LANES, LANES), 0)
    query = lax.broadcasted_iota(jnp.int32, (LANES, LANES), 1)
    padding = jnp.where(key < AREA, 0.0, NEVER)
    out_ref[0] = padding
    out_ref[1] = padding
    if shifted_layer:
        last = lax.axis_index(ROW) == lax.axis_size(ROW) - 1
        rows_differ = ((key >= AREA // 2) != (query >= AREA // 2)) & last
        cols_differ = (key % WIN >= SHIFT) != (query % WIN >= SHIFT)
        out_ref[0] += jnp.where(rows_differ, MASK_VALUE, 0.0)
        out_ref[1] += jnp.where(rows_differ | cols_differ, MASK_VALUE, 0.0)


def shifted_live(s, windows):
    place = lax.broadcasted_iota(jnp.int32, (1, LANES), 1)
    for window in range(windows):
        here, after = slice(window, window + 1), slice((window + 1) % windows, (window + 1) % windows + 1)
        beyond = place % WIN >= SHIFT
        own = jnp.where(beyond, s.live[after, :], s.live[here, :])
        upper = jnp.where(beyond, s.live_upper[after, :], s.live_upper[here, :])
        s.live_two[here, :] = jnp.where(place >= AREA // 2, upper, own)


def head_rows(head, base=0):
    return pl.ds(base + head * HEAD_DIM, HEAD_DIM)


def norm_one_forward(s, windows):
    def step(index, carry):
        lanes = lane_tile(index)
        hat, _ = norm_parts(s.x[:, lanes])
        s.normed[:, lanes] = (hat * s.sums[G1] + s.sums[B1]).astype(BF)
        return carry

    lax.fori_loop(0, windows, step, 0)


def project_forward(s, windows):
    def step(index, carry):
        rows = chunk_of(index)
        bias = s.sums[jnp.where(index == 0, QB, VB)] * jnp.where(index == 1, 0.0, 1.0)
        out = mm(s.w_qkv[:, rows], s.normed[...], 0, 0)
        s.qkv[rows, :] = (out + wide(bias, windows)).astype(BF)
        return carry

    lax.fori_loop(0, 3, step, 0)


def attend_forward(s, windows, live_ref):
    def step(index, carry):
        lanes = lane_tile(index)
        live = jnp.broadcast_to(live_ref[pl.ds(index, 1), :], (LANES, LANES)).T
        masked = s.regions[jnp.where(index == windows - 1, 1, 0)] + MASK_VALUE * (1.0 - live)
        for head in range(HEADS):
            query = s.qkv[head_rows(head), lanes]
            key = s.qkv[head_rows(head, D), lanes]
            value = s.qkv[head_rows(head, 2 * D), lanes]
            scores = mm(key, query, 0, 0) * SCORE_SCALE + (s.bias[head] + masked)
            exponent = jnp.exp(scores - jnp.max(scores, axis=0, keepdims=True))
            total = jnp.sum(exponent, axis=0, keepdims=True)
            soft = (exponent * (1.0 / total)).astype(BF)
            s.soft[index * HEADS + head] = soft
            s.merged[head_rows(head), lanes] = mm(value, soft, 1, 0).astype(BF)
        return carry

    lax.fori_loop(0, windows, step, 0)


def norm_two_forward(s, windows, live_ref):
    def step(index, carry):
        lanes = lane_tile(index)
        hidden = s.x[:, lanes] + live_ref[pl.ds(index, 1), :] * (s.work[:, lanes] + s.sums[PB])
        s.hidden[:, lanes] = hidden
        s.work[:, lanes] = hidden + s.sums[F2B]
        hat, _ = norm_parts(hidden)
        s.second[:, lanes] = (hat * s.sums[G2] + s.sums[B2]).astype(BF)
        return carry

    lax.fori_loop(0, windows, step, 0)


def feed_forward(s, windows):
    def step(index, carry):
        rows = chunk_of(index)
        inner = mm(s.w_fc1[:, rows], s.second[...], 0, 0) + wide(s.sums[F1B + index], windows)
        active, slope = gelu_parts(inner)
        active = active.astype(BF)
        s.active[rows, :] = active
        s.slope[rows, :] = slope.astype(BF)
        s.work[...] += mm(s.w_fc2[rows, :], active, 0, 0)
        return carry

    lax.fori_loop(0, FEEDS, step, 0)


def feed_backward(s, sink, times):
    s.sums[...] = jnp.zeros(s.sums.shape, F32)
    s.bias[...] = jnp.zeros(s.bias.shape, F32)
    lowered = s.grad[...].astype(BF)
    s.low[...] = lowered
    s.sums[F2B] = fold(lowered.astype(F32))
    s.work[...] = jnp.zeros(s.work.shape, F32)

    claims = sink.layer == 0
    if claims:
        for unit in range(UNIT_FC2, UNIT_FC2 + FEEDS):
            sink.claim(unit)

    def step(index, carry):
        rows = chunk_of(index)
        if claims:
            sink.claim(UNIT_FC1 + index)
        sink.put(0, mm(s.active[rows, :], s.low[...], 1, 1), feed_pieces(index, sink.shares), index == 0)
        grad_inner = mm(s.w_fc2[rows, :], s.low[...], 1, 0) * s.slope[rows, :].astype(F32)
        grad_inner = grad_inner.astype(BF)
        s.sums[F1B + index] = fold(grad_inner.astype(F32))
        sink.put(1, mm(s.second[...], grad_inner, 1, 1), row_pieces(UNIT_FC1 + index, sink.shares), index == 0)
        s.work[...] += mm(s.w_fc1[:, rows], grad_inner, 1, 0)
        sink.advance_at(index, times)
        return carry

    lax.fori_loop(0, FEEDS, step, 0)
    sink.settle(0)
    sink.settle(1)


def norm_two_backward(s, windows, live_ref):
    def step(index, carry):
        lanes = lane_tile(index)
        hat, scale = norm_parts(s.hidden[:, lanes])
        grad = s.work[:, lanes]
        s.sums[G2] += grad * hat
        s.sums[B2] += grad
        grad = s.grad[:, lanes] + norm_pull(grad, s.gains[1], hat, scale)
        s.grad[:, lanes] = grad
        grad_low = (grad * live_ref[pl.ds(index, 1), :]).astype(BF)
        s.low[:, lanes] = grad_low
        s.sums[PB] += grad_low.astype(F32)
        return carry

    lax.fori_loop(0, windows, step, 0)


def merge_backward(s, sink):
    if sink.layer == 0:
        sink.claim(UNIT_PROJ)
    sink.put(0, mm(s.merged[...], s.low[...], 1, 1), row_pieces(UNIT_PROJ, sink.shares), True)
    s.merged[...] = mm(s.w_proj[...], s.low[...], 1, 0).astype(BF)
    sink.settle(0)


def attend_backward(s, windows, sink, times):
    def step(index, carry):
        lanes = lane_tile(index)
        for head in range(HEADS):
            query = s.qkv[head_rows(head), lanes]
            key = s.qkv[head_rows(head, D), lanes]
            value = s.qkv[head_rows(head, 2 * D), lanes]
            grad_out = s.merged[head_rows(head), lanes]
            soft_low = s.soft[index * HEADS + head]
            soft = soft_low.astype(F32)
            grad_soft = mm(value, grad_out, 0, 0)
            inner = jnp.sum(soft * grad_soft, axis=0, keepdims=True)
            grad_scores = (soft * (grad_soft - inner)).astype(BF)
            s.bias[head] += grad_scores.astype(F32)
            grad_query = (mm(key, grad_scores, 1, 0) * SCORE_SCALE).astype(BF)
            grad_key = (mm(query, grad_scores, 1, 1) * SCORE_SCALE).astype(BF)
            grad_value = mm(grad_out, soft_low, 1, 1).astype(BF)
            s.qkv[head_rows(head), lanes] = grad_query
            s.qkv[head_rows(head, D), lanes] = grad_key
            s.qkv[head_rows(head, 2 * D), lanes] = grad_value
            s.sums[QB, head_rows(head), :] += grad_query.astype(F32)
            s.sums[VB, head_rows(head), :] += grad_value.astype(F32)
        sink.advance_at(index, times)
        return carry

    lax.fori_loop(0, windows, step, 0)


def project_backward(s, sink):
    def step(index, carry):
        rows = chunk_of(index)
        sink.claim(UNIT_QKV + index)
        sink.put(1, mm(s.normed[...], s.qkv[rows, :], 1, 1), row_pieces(UNIT_QKV + index, sink.shares), index == 0)
        return carry

    lax.fori_loop(0, 3, step, 0)


def input_backward(s):
    s.work[...] = mm(s.w_qkv[...], s.qkv[...], 1, 0)


def norm_one_backward(s, windows):
    def step(index, carry):
        lanes = lane_tile(index)
        hat, scale = norm_parts(s.x[:, lanes])
        grad = s.work[:, lanes]
        s.sums[G1] += grad * hat
        s.sums[B1] += grad
        s.grad[:, lanes] += norm_pull(grad, s.gains[0], hat, scale)
        return carry

    lax.fori_loop(0, windows, step, 0)


def small_gradients(s, small_ref):
    places = lax.broadcasted_iota(jnp.int32, (D, LANES), 1)
    packed = jnp.zeros((D, LANES), F32)
    for index in range(VECTORS):
        packed = jnp.where(places == index, jnp.sum(s.sums[index], axis=1, keepdims=True), packed)
    small_ref[:VECTOR_ROWS, :] = packed.T[:VECTOR_ROWS]
    table = gather_bias(s.bias, s.spread, s.bias_rows)
    small_ref[VECTOR_ROWS:, :] = jnp.concatenate([table, jnp.zeros((HEADS, D - TABLE), F32)], axis=1)


def reversed_bits(value, count):
    turned = 0
    for bit in range(count):
        turned = turned * 2 + (value // 2**bit) % 2
    return turned


def row_pieces(unit, shares):
    rows, count = CHUNK // shares, shares.bit_length() - 1
    return [(share * rows, unit, reversed_bits(share, count)) for share in range(shares)]


def feed_pieces(index, shares):
    rows, count = CHUNK // shares, shares.bit_length() - 1
    pieces = []
    for share in range(shares // FEEDS):
        place = reversed_bits(index * (shares // FEEDS) + share, count)
        for part in range(FEEDS):
            pieces.append(((share * FEEDS + part) * rows, UNIT_FC2 + part, place))
    return pieces


class Plan:
    def __init__(self, pages, shares):
        self.shares, self.rows = shares, CHUNK // shares
        page_bits, row_bits = pages.bit_length() - 1, shares.bit_length() - 1
        others = page_bits - 1
        self.steps = []
        for kind in range(CLASSES):
            turn = kind % 2
            page = [(PAGE, 2 ** (1 + (bit + turn) % others)) for bit in range(others)]
            row = [(ROW, 2**bit) for bit in range(row_bits)]
            self.steps.append([(PAGE, 1)] + (row + page if kind == 2 else page + row))
        self.page_steps = [[0] + [at for at, step in enumerate(steps) if at and step[0] == PAGE] for steps in self.steps]
        self.halvings = page_bits + row_bits
        self.phases = self.halvings + page_bits
        self.sizes, self.axes = [], []
        for steps in self.steps:
            size, sizes, axes = [shares, self.rows, CHUNK], [], []
            for axis, _ in steps:
                axes.append(0 if axis == ROW else 1 if size[1] >= 16 else 2)
                size[axes[-1]] //= 2
                sizes.append(tuple(size))
            self.sizes.append(sizes)
            self.axes.append(axes)
        self.steps_at = self.schedule()

    def schedule(self):
        small = TRIPLES
        free, ready, stage_of, plan, now = {}, {}, {}, [], 0.0
        for triple in range(TRIPLES):
            for kind in range(CLASSES):
                stage_of[triple, kind] = 0
        stage_of[small, 0] = 0

        def link(key, phase):
            triple, kind = key
            if phase < self.halvings:
                axis, stride = self.steps[kind][phase]
                size = 2.0**-phase / 2 if triple != small else 0.125
            else:
                axis, stride = self.steps[kind][self.page_steps[kind][self.phases - 1 - phase]]
                size = 2.0 ** (phase - 2 * self.halvings)
            if axis == PAGE and stride == 1:
                return 0, size * PLAN_CORE
            return (axis, stride if axis == PAGE else 0), size * PLAN_LINK * (1.0 if stride == 1 or axis == PAGE else 1.5)

        def last_stage(key):
            return self.halvings if key[0] == small else self.phases + 1

        def allowed(key, point):
            triple, kind = key
            stage = stage_of[key]
            if stage > last_stage(key):
                return False
            if triple == small:
                return point >= len(PLAN_POINTS) - 1
            if stage == 0 and point < PLAN_THERE[triple]:
                return False
            if triple > 0 and stage_of[triple - 1, kind] <= stage:
                return False
            if triple >= RING and stage < self.halvings and stage_of[triple - RING, kind] <= stage + 1:
                return False
            if stage == 0 and triple >= DONE and stage_of[triple - DONE, kind] <= self.phases + 1:
                return False
            return not (stage == 0 and triple >= HELD and stage_of[triple - HELD, kind] <= self.halvings + 1)

        for point, work in enumerate(PLAN_POINTS):
            now += work
            if point == PLAN_HALO:
                free[ROW, 0] = max(now, free.get((ROW, 0), 0.0)) + PLAN_HALO_TIME
            steps, final = [], point == len(PLAN_POINTS) - 1
            while True:
                keys = [key for key in stage_of if allowed(key, point)]
                needed = PLAN_FORCE.get(point, -1)
                keys = [
                    key
                    for key in keys
                    if final or ready.get(key, 0.0) <= now + PLAN_SLACK or (key[0] <= needed and stage_of[key] <= 1)
                ]
                if not keys:
                    break
                key = min(keys, key=lambda key: (max(ready.get(key, 0.0), now), -stage_of[key], key))
                stage = stage_of[key]
                now = max(now, ready.get(key, 0.0)) + (PLAN_ADD * 2.0**-stage if stage else 0.0)
                if stage == self.phases:
                    ready[key] = now + PLAN_LATENCY
                elif stage < last_stage(key):
                    name, length = link(key, stage)
                    free[name] = max(now, free.get(name, 0.0)) + length
                    ready[key] = free[name] + PLAN_LATENCY
                steps.append((*key, stage))
                stage_of[key] += 1
            plan.append(steps)
        assert all(stage_of[key] > last_stage(key) for key in stage_of)
        return plan

    def partner(self, kind, level):
        axis, stride = self.steps[kind][level]
        page, row = lax.axis_index(PAGE), lax.axis_index(ROW)
        mine = page if axis == PAGE else row
        bit = (mine // stride) % 2
        other = mine + (1 - 2 * bit) * stride
        return bit, ((other, row) if axis == PAGE else (page, other))

    def part(self, kind, level, sent=False):
        starts, sizes = [0, 0, 0], list(self.sizes[kind][0])
        for at in range(1, level + 1):
            axis = self.axes[kind][at]
            sizes[axis] //= 2
            bit, _ = self.partner(kind, at)
            which = 1 - bit if sent and at == level else bit
            starts[axis] = starts[axis] + which * sizes[axis]
        return (
            pl.ds(starts[0], sizes[0]),
            pl.ds(pl.multiple_of(starts[1], 8), sizes[1]),
            pl.ds(pl.multiple_of(starts[2], LANES), sizes[2]),
        )

    def place(self, kind, count):
        starts, sizes = [0, 0], [self.rows, CHUNK]
        for at in self.page_steps[kind][:count]:
            axis = self.axes[kind][at] - 1
            sizes[axis] //= 2
            bit, _ = self.partner(kind, at)
            starts[axis] = starts[axis] + bit * sizes[axis]
        return starts, sizes


class Reducer:
    def __init__(self, plan, s):
        self.plan, self.s = plan, s
        self.shares = plan.shares
        self.layer = 1

    def stage_copies(self, slot, pieces):
        s, plan = self.s, self.plan
        bit, device = plan.partner(0, 0)
        rows = plan.rows // 2
        copies = []
        for number, (start, unit, place) in enumerate(pieces):
            start = slot * CHUNK + start
            number_sems = s.stage_sems.at[slot, number]
            overall = self.first_unit() + unit
            sent = pltpu.make_async_remote_copy(
                src_ref=s.staged.at[pl.ds(pl.multiple_of(start + (1 - bit) * rows, 8), rows)],
                dst_ref=s.first_landing.at[overall % (RING * CLASSES), place],
                send_sem=number_sems.at[0],
                recv_sem=s.first_sems.at[overall, place],
                device_id=device,
                device_id_type=MESH,
            )
            kept = pltpu.make_async_copy(
                s.staged.at[pl.ds(pl.multiple_of(start + bit * rows, 8), rows)],
                s.units[self.layer].at[unit, place],
                number_sems.at[1],
            )
            copies.append((sent, kept))
        return copies

    def first_unit(self):
        return UNITS * (1 - self.layer)

    def claim(self, unit):
        pl.semaphore_wait(self.s.first_free.at[self.first_unit() + unit], 1)

    def put(self, slot, grad, pieces, first):
        if first is not True:

            @pl.when(jnp.logical_not(first))
            def _():
                self.settle(slot)

        self.s.staged[pl.ds(slot * CHUNK, CHUNK), :] = grad
        for sent, kept in self.stage_copies(slot, pieces):
            sent.start()
            kept.start()

    def settle(self, slot):
        for sent, kept in self.stage_copies(slot, row_pieces(0, self.shares)):
            sent.wait_send()
            kept.wait()

    def first_arrived(self, triple, kind):
        s, unit = self.s, CLASSES * triple + kind
        landed = s.first_landing.at[unit % (RING * CLASSES)]
        _, device = self.plan.partner(0, 0)
        for place in range(self.shares):
            pltpu.make_async_remote_copy(
                src_ref=landed.at[place],
                dst_ref=landed.at[place],
                send_sem=s.first_sems.at[unit, place],
                recv_sem=s.first_sems.at[unit, place],
                device_id=device,
                device_id_type=MESH,
            ).wait_recv()

    def remote(self, source, target, unit, phase, device):
        return pltpu.make_async_remote_copy(
            src_ref=source,
            dst_ref=target,
            send_sem=self.s.send_sems.at[unit, phase],
            recv_sem=self.s.recv_sems.at[unit, phase],
            device_id=device,
            device_id_type=MESH,
        )

    def held(self, triple, kind):
        return self.s.held.at[CLASSES * (triple % HELD) + kind]

    def landed(self, triple, kind, level):
        if level == 0:
            return self.s.first_landing.at[(CLASSES * triple + kind) % (RING * CLASSES)]
        return self.s.landing[kind][level - 1].at[triple % RING]

    def halving(self, triple, kind, level):
        _, device = self.plan.partner(kind, level)
        source = self.held(triple, kind).at[self.plan.part(kind, level, True)]
        return self.remote(source, self.landed(triple, kind, level), CLASSES * triple + kind, level, device)

    def own_half(self, triple, kind):
        source = self.s.units[1 - triple // GROUPS].at[CLASSES * (triple % GROUPS) + kind]
        sem = self.s.own_sems.at[CLASSES * triple + kind, 0]
        return pltpu.make_async_copy(source, self.held(triple, kind), sem)

    def finished(self, triple, kind):
        return self.held(triple, kind).at[self.plan.part(kind, self.plan.halvings - 1)].at[0]

    def done(self, triple, kind, count):
        starts, sizes = self.plan.place(kind, count)
        return self.s.done.at[
            CLASSES * (triple % DONE) + kind,
            pl.ds(pl.multiple_of(starts[0], 8), sizes[0]),
            pl.ds(pl.multiple_of(starts[1], LANES), sizes[1]),
        ]

    def gathering(self, triple, kind, phase):
        plan = self.plan
        count = len(plan.page_steps[kind]) - (phase - plan.halvings)
        part = self.done(triple, kind, count)
        _, device = plan.partner(kind, plan.page_steps[kind][count - 1])
        return self.remote(part, part, CLASSES * triple + kind, phase, device)

    def result(self, triple, kind):
        which, row_block, col_block = TARGETS[triple % GROUPS][kind]
        rows = self.plan.rows
        target = self.s.results[which].at[
            1 - triple // GROUPS, pl.ds(row_block * rows, rows), pl.ds(col_block * CHUNK, CHUNK)
        ]
        sem = self.s.own_sems.at[CLASSES * triple + kind, 1]
        return pltpu.make_async_copy(self.done(triple, kind, 0), target, sem)

    def start(self, triple, kind, phase):
        plan = self.plan
        if phase == 0:
            self.own_half(triple, kind).start()
        elif phase < plan.halvings:
            if triple >= RING:
                pl.semaphore_wait(self.s.free_sems.at[kind, phase], 1)
            self.halving(triple, kind, phase).start()
        elif phase < plan.phases:
            if phase == plan.halvings:
                self.done(triple, kind, len(plan.page_steps[kind]))[...] = self.finished(triple, kind)[...]
            self.gathering(triple, kind, phase).start()
        elif phase == plan.phases:
            self.result(triple, kind).start()

    def finish(self, triple, kind, phase):
        plan, s = self.plan, self.s
        if phase < plan.halvings:
            if phase == 0:
                self.first_arrived(triple, kind)
                self.own_half(triple, kind).wait()
            else:
                self.halving(triple, kind, phase).wait()
            landed = self.landed(triple, kind, phase)
            kept = self.held(triple, kind).at[plan.part(kind, phase)]
            for share in range(landed.shape[0]):
                kept[share] += landed[share]
            if triple < TRIPLES - RING:
                _, device = plan.partner(kind, phase)
                free = s.free_sems.at[kind, phase]
                if phase == 0:
                    free = s.first_free.at[CLASSES * (triple + RING) + kind]
                pl.semaphore_signal(free, inc=1, device_id=device, device_id_type=MESH)
        elif phase < plan.phases:
            self.gathering(triple, kind, phase).wait()
        else:
            self.result(triple, kind).wait()

    def advance(self, point):
        for triple, kind, stage in self.plan.steps_at[point]:
            if triple == TRIPLES:
                self.small_step(stage - 1)
                continue
            if stage > 0:
                self.finish(triple, kind, stage - 1)
            self.start(triple, kind, stage)

    def advance_at(self, index, points):
        for number, point in enumerate(points):
            if self.plan.steps_at[point]:

                @pl.when(index == number)
                def _(point=point):
                    self.advance(point)

    def small_copy(self, phase):
        s = self.s
        _, device = self.plan.partner(0, phase)
        return pltpu.make_async_remote_copy(
            src_ref=s.small_own if phase == 0 else s.small_parts.at[phase - 1],
            dst_ref=s.small_parts.at[phase],
            send_sem=s.small_sems.at[0, phase],
            recv_sem=s.small_sems.at[1, phase],
            device_id=device,
            device_id_type=MESH,
        )

    def small_step(self, phase):
        s = self.s
        if phase >= 0:
            self.small_copy(phase).wait()
            s.small_parts[phase] += s.small_own[...] if phase == 0 else s.small_parts[phase - 1]
        if phase + 1 < self.plan.halvings:
            self.small_copy(phase + 1).start()


PLAN_POINTS = (0, 2, 3) + (2.7,) * 6 + (5.2, 3, 3, 6) + (3.2,) * 4 + (0.3, 2, 3) + (2.7,) * 6 + (3, 3, 3, 3)
PLAN_THERE = (0, 0, 2, 10, 17, 17, 19, 26)
PLAN_FORCE = {9: 0, 12: 3, 25: 4}
PLAN_HALO, PLAN_HALO_TIME = 9, 12.3
PLAN_CORE, PLAN_LINK, PLAN_LATENCY, PLAN_ADD, PLAN_SLACK = 1.7, 20.0, 2.0, 0.9, 0.0


class Moves:
    def __init__(self, sems):
        self.sems, self.used = sems, 0

    def __call__(self, source, target):
        number, self.used = self.used, self.used + 1
        make = functools.partial(pltpu.make_async_copy, source, target, self.sems.at[number])
        make().start()
        return lambda: make().wait()


class Refs:
    pass


def run(plan, layout, *refs):
    s = Refs()
    for name, ref in zip(layout, refs):
        setattr(s, name, ref)
    rest = list(refs[len(layout) :])
    s.landing = [[rest.pop(0) for _ in range(1, plan.halvings)] for _ in range(CLASSES)]
    s.results = (s.sum_qkv, s.sum_proj, s.sum_fc1, s.sum_fc2)
    s.units = (s.units_zero, s.units_one)
    s.page = s.staged.at[pl.ds(0, s.plain.shape[0])]
    s.spread = s.qkv.at[pl.ds(0, s.in_spread.shape[0])]
    windows = s.x.shape[1] // LANES
    patches = s.dense.shape[0] // SPLITS
    half, half_rows = patches // 2, s.dense.shape[0] // 2
    padded = 16 * -(-half // 16)
    upper, lower = pl.ds(0, half_rows), pl.ds(half_rows, half_rows)
    reducer = Reducer(plan, s)
    move = Moves(s.move_sems)
    page, row = lax.axis_index(PAGE), lax.axis_index(ROW)
    count = lax.axis_size(ROW)
    above, below = (page, (row + count - 1) % count), (page, (row + 1) % count)

    def halo(number, source, target, device):
        make = functools.partial(
            pltpu.make_async_remote_copy,
            src_ref=source,
            dst_ref=target,
            send_sem=s.halo_sems.at[0, number],
            recv_sem=s.halo_sems.at[1, number],
            device_id=device,
            device_id_type=MESH,
        )
        make().start()
        return lambda: make().wait()

    tokens_there = move(s.in_tokens, s.tokens)
    places_there = (move(s.in_plain, s.plain), move(s.in_moved, s.moved))
    swaps_there = (move(s.in_swap_on, s.swap_on), move(s.in_swap_back, s.swap_back))
    spread_there = move(s.in_spread, s.spread)
    weights = ((s.in_qkv, s.w_qkv), (s.in_proj, s.w_proj), (s.in_fc1, s.w_fc1), (s.in_fc2, s.w_fc2))

    def fetch_weight(which, layer):
        source, target = weights[which]
        return move(source.at[layer], target)

    there = [fetch_weight(which, 0) for which in range(4)]

    barrier = pltpu.get_barrier_semaphore()
    devices = [plan.partner(0, level)[1] for level in range(plan.halvings)] + [above, below]
    for device in devices:
        pl.semaphore_signal(barrier, inc=1, device_id=device, device_id_type=MESH)
    pl.semaphore_wait(barrier, len(devices))

    s.live[...] = jnp.zeros(s.live.shape, F32)
    for window in range(windows):
        s.live[window : window + 1, :] = jnp.full((1, LANES), 1.0 - s.blank[0, window].astype(F32))
    live_there = halo(0, s.live, s.live_upper, above)
    grad_there = halo(1, s.in_grad.at[upper], s.grad_upper, above)
    grad_lower_there = move(s.in_grad.at[lower], s.dense.at[lower])
    s.page[...] = jnp.zeros(s.page.shape, F32)
    tokens_there()
    cols = s.tokens.shape[1]
    for line in range(WIN):
        s.page[pl.ds(line * cols, cols), :] = s.tokens[line].astype(F32)
    places_there[0]()
    to_channels(s.page, s.plain, s.x, True)
    saves = [move(s.x, s.kept_x)]
    spread_columns(s, 0)
    spread_there()
    spread_bias(s, 0)
    region_masks(False, s.regions)
    norm_one_forward(s, windows)
    saves.append(move(s.normed, s.kept_normed))
    there[QKV]()
    project_forward(s, windows)
    qkv_saved = move(s.qkv, s.kept_qkv)
    there[QKV] = fetch_weight(QKV, 1)
    attend_forward(s, windows, s.live)
    saves.append(move(s.soft, s.kept_soft))
    saves.append(move(s.merged, s.kept_merged))
    there[PROJ]()
    s.work[...] = mm(s.w_proj[...], s.merged[...], 0, 0)
    there[PROJ] = fetch_weight(PROJ, 1)
    norm_two_forward(s, windows, s.live)
    saves.append(move(s.hidden, s.kept_hidden))
    saves.append(move(s.second, s.kept_second))
    there[FC1]()
    there[FC2]()
    feed_forward(s, windows)
    saves.append(move(s.active, s.kept_active))
    saves.append(move(s.slope, s.kept_slope))
    there[FC1] = fetch_weight(FC1, 1)
    there[FC2] = fetch_weight(FC2, 1)
    to_dense(s.work, s.plain, s.dense.at[upper], padded)
    upper_there = halo(2, s.dense.at[upper], s.upper, above)

    qkv_saved()
    spread_there = move(s.in_spread, s.spread)
    places_there[1]()
    swaps_there[0]()
    saves.pop(0)()
    move_own(s.work, s.swap_on, s.x, windows, 0)
    spread_columns(s, 1)
    spread_there()
    spread_bias(s, 1)
    region_masks(True, s.regions)
    live_there()
    shifted_live(s, windows)
    grad_there()
    grad_lower_there()
    from_dense(s.grad_upper, s.page, 0)
    from_dense(s.dense.at[lower], s.page, half)
    to_channels(s.page, s.moved, s.grad)
    for saved in saves:
        saved()
    upper_there()
    from_dense(s.upper, s.page, 0)
    add_halo(s.page, s.moved, s.x, half, padded)
    norm_one_forward(s, windows)
    there[QKV]()
    project_forward(s, windows)
    attend_forward(s, windows, s.live_two)
    there[PROJ]()
    s.work[...] = mm(s.w_proj[...], s.merged[...], 0, 0)
    norm_two_forward(s, windows, s.live_two)
    there[FC1]()
    there[FC2]()
    feed_forward(s, windows)
    to_dense(s.work, s.moved, s.dense, s.moved.shape[0])
    out_there = halo(3, s.dense.at[upper], s.out_tokens.at[upper], below)
    out_kept = move(s.dense.at[lower], s.out_tokens.at[lower])

    spread_gains(s, 1)

    def backward(layer, live_ref, fetch, points):
        reducer.layer = layer
        first = 0 if layer else FEEDS
        feed_backward(s, reducer, points[:first])
        reducer.advance(points[first])
        fetch(0)
        norm_two_backward(s, windows, live_ref)
        reducer.advance(points[first + 1])
        fetch(1)
        merge_backward(s, reducer)
        reducer.advance(points[first + 2])
        fetch(2)
        attend_backward(s, windows, reducer, points[first + 3 :])
        fetch(3)

    back = {}

    def refill(point):
        if point == 0:
            back[0] = [move(s.kept_active, s.active), move(s.kept_slope, s.slope), move(s.kept_second, s.second)]
            back[0] += [fetch_weight(FC1, 0), fetch_weight(FC2, 0)]
        elif point == 1:
            back[1] = [move(s.kept_hidden, s.hidden)]
        elif point == 2:
            back[2] = [fetch_weight(PROJ, 0)]
        elif point == 3:
            back[2] += [move(s.kept_merged, s.merged)]
            back[3] = [move(s.kept_soft, s.soft)]
        elif point == 4:
            back[4] = [move(s.kept_x, s.x)]
        else:
            back[3] += [move(s.kept_qkv, s.qkv), move(s.kept_normed, s.normed), fetch_weight(QKV, 0)]

    def needed(point):
        if point in back:
            for arrived in back.pop(point):
                arrived()

    backward(1, s.live_two, refill, range(9))
    input_backward(s)
    norm_one_backward(s, windows)
    refill(4)
    out_there()
    to_dense(s.grad, s.moved, s.dense.at[upper], padded)
    next_there = halo(4, s.dense.at[upper], s.next_upper, below)
    reducer.advance(9)
    project_backward(s, reducer)
    spread_there = move(s.in_spread, s.spread)
    reducer.settle(1)
    reducer.advance(10)

    swaps_there[1]()
    move_own(s.grad, s.swap_back, s.work, windows, -1)
    spread_there()
    small_gradients(s, s.small_own.at[1])
    refill(5)
    spread_gains(s, 0)
    reducer.advance(11)
    next_there()
    from_dense(s.next_upper, s.page, 0)
    s.grad[...] = s.work[...]
    add_halo(s.page, s.plain, s.grad, half, padded)
    reducer.advance(12)
    needed(0)

    def wait_next(point):
        needed(point + 1)

    backward(0, s.live, wait_next, range(13, 26))
    project_backward(s, reducer)
    reducer.settle(1)
    reducer.advance(26)
    input_backward(s)
    spread_there = move(s.in_spread, s.spread)
    reducer.advance(27)
    needed(4)
    norm_one_backward(s, windows)
    out_kept()
    to_dense(s.grad, s.plain, s.dense, s.plain.shape[0])
    grad_kept = move(s.dense, s.grad_tokens)
    reducer.advance(28)
    spread_there()
    small_gradients(s, s.small_own.at[0])
    reducer.advance(29)
    finish_small(s, plan, row)
    grad_kept()


def finish_small(s, plan, row):
    total = s.small_parts.at[plan.halvings - 1]
    outs = (
        (s.d_ln_gain, (G1, G2)),
        (s.d_ln_bias, (B1, B2)),
        (s.d_qv_bias, (QB, VB)),
        (s.d_proj_bias, (PB,)),
        (s.d_fc1_bias, tuple(range(F1B, F1B + FEEDS))),
        (s.d_fc2_bias, (F2B,)),
    )
    for layer in range(2):
        s.d_table[layer] = total[layer, VECTOR_ROWS:, :OFFSETS]
        for ref, indices in outs:
            whole = jnp.concatenate([total[layer, index : index + 1, :] for index in indices], axis=1)
            size = ref.shape[1]
            mine = jnp.zeros((1, size), F32)
            for share in range(plan.shares):
                mine = jnp.where(row == share, whole[:, share * size : (share + 1) * size], mine)
            ref[layer : layer + 1, :] = mine


def placements(cols):
    windows = cols // WIN
    patches = WIN * cols
    padded = -(-patches // LANES) * LANES
    plain = np.zeros((padded, windows * LANES), np.float32)
    moved = np.zeros((padded, windows * LANES), np.float32)
    for line in range(WIN):
        for col in range(cols):
            source = line * cols + col
            plain[source, (col // WIN) * LANES + line * WIN + col % WIN] = 1
            new_line, new_col = (line - SHIFT) % WIN, (col - SHIFT) % cols
            moved[source, (new_col // WIN) * LANES + new_line * WIN + new_col % WIN] = 1
    return plain.astype(BF), moved.astype(BF)


def swaps():
    on = np.zeros((2 * LANES, LANES), np.float32)
    back = np.zeros((2 * LANES, LANES), np.float32)
    for line in range(SHIFT):
        for col in range(WIN):
            moved, plain = line * WIN + col, (line + SHIFT) * WIN + (col + SHIFT) % WIN
            on[plain + (LANES if col >= SHIFT else 0), moved] = 1
            back[moved + (LANES if col < SHIFT else 0), plain] = 1
    return on.astype(BF), back.astype(BF)


def table_spread():
    size = 2 * WIN - 1
    spread = np.zeros((WIN, 2 * LANES, TABLE), np.float32)
    for key_col in range(WIN):
        for offset in range(size):
            for col in range(WIN):
                spread[key_col, offset * WIN + col, offset * size + col - key_col + WIN - 1] = 1
    spread = spread.reshape(WIN // 2, 2, 2 * LANES, TABLE).swapaxes(1, 2)
    return spread.reshape(WIN * LANES, 2 * TABLE).astype(BF)


def copy_all(*refs):
    *refs, sems = refs
    count = len(refs) // 3
    sources, targets, held = refs[:count], refs[count : 2 * count], refs[2 * count :]
    ways = [*zip(sources, held), *zip(held, targets)]
    copies = [pltpu.make_async_copy(*way, sems.at[number]) for number, way in enumerate(ways)]
    for copy in copies[:count]:
        copy.start()
    for incoming, outgoing in zip(copies[:count], copies[count:]):
        incoming.wait()
        outgoing.start()
    for copy in copies[count:]:
        copy.wait()


def hand_out(values):
    anywhere = pl.BlockSpec(memory_space=pl.ANY)
    return pl.pallas_call(
        copy_all,
        out_shape=[jax.ShapeDtypeStruct(value.shape, value.dtype) for value in values],
        in_specs=[anywhere] * len(values),
        out_specs=[anywhere] * len(values),
        scratch_shapes=[pltpu.VMEM(value.shape, value.dtype) for value in values]
        + [pltpu.SemaphoreType.DMA((2 * len(values),))],
        compiler_params=pltpu.CompilerParams(vmem_limit_bytes=VMEM_LIMIT),
        name="results",
    )(*values)


def per_device(
    page_tokens,
    blank_mask,
    cotangent,
    ln_gain,
    ln_bias,
    qv_bias,
    rel_table,
    w_qkv,
    w_proj,
    proj_bias,
    w_fc1,
    fc1_bias,
    w_fc2,
    fc2_bias,
):
    pages, shares = lax.axis_size(PAGE), lax.axis_size(ROW)
    plan = Plan(pages, shares)
    cols = page_tokens.shape[2]
    windows, lanes = cols // WIN, cols // WIN * LANES
    dense = ((WIN * cols * SPLITS, LANES), F32)
    half_dense = ((WIN * cols * SPLITS // 2, LANES), F32)
    plain, moved = (jnp.asarray(place) for place in placements(cols))
    live_rows = 8 * -(-windows // 8)
    scalar_inputs = dict(blank=blank_mask[0])
    small_inputs = dict(
        table=rel_table,
        ln_gain=ln_gain,
        ln_bias=ln_bias,
        qv_bias=qv_bias,
        proj_bias=proj_bias,
        fc1_bias=fc1_bias,
        fc2_bias=fc2_bias,
    )
    large_inputs = dict(
        in_tokens=page_tokens[0],
        in_grad=cotangent.reshape(dense[0]),
        in_plain=plain,
        in_moved=moved,
        in_swap_on=jnp.asarray(swaps()[0]),
        in_swap_back=jnp.asarray(swaps()[1]),
        in_spread=jnp.asarray(table_spread()),
        in_qkv=w_qkv,
        in_proj=w_proj,
        in_fc1=w_fc1,
        in_fc2=w_fc2,
    )
    saved = dict(
        x=((D, lanes), F32),
        normed=((D, lanes), BF),
        qkv=((3 * D, lanes), BF),
        soft=((windows * HEADS, LANES, LANES), BF),
        merged=((D, lanes), BF),
        hidden=((D, lanes), F32),
        second=((D, lanes), BF),
        active=((FF, lanes), BF),
        slope=((FF, lanes), BF),
    )
    units = ((UNITS,) + plan.sizes[0][0], F32)
    large_outputs = dict(
        out_tokens=dense,
        grad_tokens=dense,
        sum_qkv=((2, D // shares, 3 * D), F32),
        sum_proj=((2, D // shares, D), F32),
        sum_fc1=((2, D // shares, FF), F32),
        sum_fc2=((2, FF // shares, D), F32),
        units_zero=units,
        units_one=units,
        kept_x=((D, lanes), F32),
        kept_normed=((D, lanes), BF),
        kept_qkv=((3 * D, lanes), BF),
        kept_soft=((windows * HEADS, LANES, LANES), BF),
        kept_merged=((D, lanes), BF),
        kept_hidden=((D, lanes), F32),
        kept_second=((D, lanes), BF),
        kept_active=((FF, lanes), BF),
        kept_slope=((FF, lanes), BF),
    )
    small_outputs = dict(
        d_ln_gain=((2, 2 * D // shares), F32),
        d_ln_bias=((2, 2 * D // shares), F32),
        d_qv_bias=((2, 2 * D // shares), F32),
        d_proj_bias=((2, D // shares), F32),
        d_fc1_bias=((2, FF // shares), F32),
        d_fc2_bias=((2, D // shares), F32),
        d_table=((2, HEADS, OFFSETS), F32),
    )
    small = (2, SMALL, D)
    vmem = dict(
        saved,
        tokens=((WIN, cols, D), BF),
        plain=(plain.shape, BF),
        moved=(moved.shape, BF),
        w_qkv=((D, 3 * D), BF),
        w_proj=((D, D), BF),
        w_fc1=((D, FF), BF),
        w_fc2=((FF, D), BF),
        dense=dense,
        upper=half_dense,
        swap_on=((2 * LANES, LANES), BF),
        swap_back=((2 * LANES, LANES), BF),
        grad_upper=half_dense,
        next_upper=half_dense,
        live_upper=((live_rows, LANES), F32),
        live_two=((live_rows, LANES), F32),
        work=((D, lanes), F32),
        grad=((D, lanes), F32),
        low=((D, lanes), BF),
        sums=((VECTORS, D, LANES), F32),
        gains=((2, D, LANES), F32),
        bias=((HEADS, LANES, LANES), F32),
        bias_rows=((HEADS * LANES, LANES), F32),
        regions=((2, LANES, LANES), F32),
        padded_table=((HEADS, TABLE), F32),
        live=((live_rows, LANES), F32),
        vector_rows=((VECTOR_ROWS, D), F32),
        staged=((2 * CHUNK, CHUNK), F32),
        done=((DONE * CLASSES, CHUNK // shares, CHUNK), F32),
        held=((HELD * CLASSES,) + plan.sizes[0][0], F32),
        first_landing=((RING * CLASSES,) + plan.sizes[0][0], F32),
        small_own=(small, F32),
        small_parts=((plan.halvings,) + small, F32),
    )
    semaphores = dict(
        move_sems=pltpu.SemaphoreType.DMA((48,)),
        halo_sems=pltpu.SemaphoreType.DMA((2, 5)),
        send_sems=pltpu.SemaphoreType.DMA((2 * UNITS, plan.phases)),
        recv_sems=pltpu.SemaphoreType.DMA((2 * UNITS, plan.phases)),
        own_sems=pltpu.SemaphoreType.DMA((2 * UNITS, 2)),
        stage_sems=pltpu.SemaphoreType.DMA((2, shares, 2)),
        first_sems=pltpu.SemaphoreType.DMA((2 * UNITS, shares)),
        first_free=pltpu.SemaphoreType.REGULAR((2 * UNITS,)),
        small_sems=pltpu.SemaphoreType.DMA((2, plan.halvings)),
        free_sems=pltpu.SemaphoreType.REGULAR((CLASSES, plan.halvings)),
    )
    landing = [((RING,) + size, F32) for sizes in plan.sizes for size in sizes[1:]]
    layout = [*scalar_inputs, *small_inputs, *large_inputs, *small_outputs, *large_outputs, *vmem, *semaphores]
    in_vmem, anywhere = pl.BlockSpec(memory_space=pltpu.VMEM), pl.BlockSpec(memory_space=pl.ANY)
    outputs = {**small_outputs, **large_outputs}
    results = pl.pallas_call(
        functools.partial(run, plan, layout),
        out_shape=[jax.ShapeDtypeStruct(*shape) for shape in outputs.values()],
        in_specs=[pl.BlockSpec(memory_space=pltpu.SMEM)] + [in_vmem] * len(small_inputs) + [anywhere] * len(large_inputs),
        out_specs=[in_vmem] * len(small_outputs) + [anywhere] * len(large_outputs),
        scratch_shapes=[pltpu.VMEM(*shape) for shape in vmem.values()]
        + list(semaphores.values())
        + [pltpu.VMEM(*shape) for shape in landing],
        compiler_params=pltpu.CompilerParams(
            vmem_limit_bytes=VMEM_LIMIT, collective_id=0, has_side_effects=True
        ),
        name="two_layers",
    )(*scalar_inputs.values(), *small_inputs.values(), *large_inputs.values())
    results = hand_out(results[: len(small_outputs) + 6])
    d_ln_gain, d_ln_bias, d_qv_bias, d_proj_bias, d_fc1_bias, d_fc2_bias, d_table = results[: len(small_outputs)]
    out_tokens, grad_tokens, sum_qkv, sum_proj, sum_fc1, sum_fc2 = results[len(small_outputs) :]
    return (
        out_tokens.reshape(cotangent.shape),
        grad_tokens.reshape(cotangent.shape),
        d_ln_gain,
        d_ln_bias,
        d_qv_bias,
        d_table,
        sum_qkv,
        sum_proj,
        d_proj_bias,
        sum_fc1,
        d_fc1_bias,
        sum_fc2,
        d_fc2_bias,
    )


def solution(mesh):
    tokens, by_row, shares = P(PAGE, ROW, None, None), P(None, ROW), P(None, ROW, None)
    return jax.shard_map(
        per_device,
        mesh=mesh,
        in_specs=(tokens, P(PAGE, ROW, None), tokens) + (P(),) * 11,
        out_specs=(tokens, tokens)
        + (by_row, by_row, by_row, P(), shares, shares, by_row, shares, by_row, shares, by_row),
        check_vma=False,
    )
```

```python
import functools

import jax
import jax.numpy as jnp
import numpy as np
from jax import lax
from jax.experimental import pallas as pl
from jax.experimental.pallas import tpu as pltpu
from jax.sharding import PartitionSpec as P

WIN = 10
SHIFT = 5
AREA = WIN * WIN
LANES = 128
D = 512
HEADS = 16
GROUP = 4
HEAD_DIM = 32
FF = 2048
CHUNK = 512
FEEDS = FF // CHUNK
SPLITS = D // LANES
EPSILON = 1e-05
MASK_VALUE = -100.0
NEVER = -1e30
SCORE_SCALE = HEAD_DIM ** (-0.5)
VMEM_LIMIT = 63 * 1024 * 1024 + 512 * 1024
BF = jnp.bfloat16
F32 = jnp.float32
MESH = pl.DeviceIdType.MESH
PAGE, ROW = "page", "row"

G1, B1, G2, B2, QB, VB, PB, F2B, F1B, VECTORS = 0, 1, 2, 3, 4, 5, 6, 7, 8, 12
VECTOR_ROWS = 16
SMALL = VECTOR_ROWS + HEADS
OFFSETS = (2 * WIN - 1) ** 2
TABLE = 384

UNIT_FC1, UNIT_FC2, UNIT_PROJ, UNIT_QKV, UNITS = 0, 4, 8, 9, 12
CLASSES = 3
GROUPS = UNITS // CLASSES
TRIPLES = 2 * GROUPS
HELD = 4
DONE = 5
RING = 3
QKV, PROJ, FC1, FC2 = range(4)
TARGETS = (
    ((FC1, 0, 0), (FC1, 0, 1), (FC1, 0, 2)),
    ((FC1, 0, 3), (FC2, 0, 0), (FC2, 1, 0)),
    ((FC2, 2, 0), (FC2, 3, 0), (PROJ, 0, 0)),
    ((QKV, 0, 0), (QKV, 0, 1), (QKV, 0, 2)),
)


def mm(left, right, left_dim, right_dim):
    return lax.dot_general(
        left, right, (((left_dim,), (right_dim,)), ((), ())), preferred_element_type=F32
    )


def split(values):
    high = values.astype(BF)
    return high, (values - high.astype(F32)).astype(BF)


def lane_tile(index):
    return pl.ds(pl.multiple_of(index * LANES, LANES), LANES)


def chunk_of(index):
    return pl.ds(pl.multiple_of(index * CHUNK, CHUNK), CHUNK)


def wide(column, count):
    return jnp.concatenate([column] * count, axis=1)


def fold(values):
    total = values[:, :LANES]
    for start in range(LANES, values.shape[1], LANES):
        total = total + values[:, start : start + LANES]
    return total


def norm_parts(values):
    center = values - jnp.sum(values, axis=0, keepdims=True) * (1.0 / D)
    spread = jnp.sum(center * center, axis=0, keepdims=True) * (1.0 / D)
    scale = lax.rsqrt(spread + EPSILON)
    return center * scale, scale


def norm_pull(grad, gain, hat, scale):
    scaled = grad * gain
    mean_one = jnp.sum(scaled, axis=0, keepdims=True) * (1.0 / D)
    mean_two = jnp.sum(scaled * hat, axis=0, keepdims=True) * (1.0 / D)
    return scale * (scaled - mean_one - hat * mean_two)


def gelu_parts(inner):
    step = 1.0 / (1.0 + (0.3275911 * 0.7071067811865476) * jnp.abs(inner))
    bell = jnp.exp(inner * inner * -0.5)
    poly = 0.5 * 1.061405429
    for factor in (-1.453152027, 1.421413741, -0.284496736, 0.254829592):
        poly = poly * step + 0.5 * factor
    tail = poly * step * bell
    below = jnp.where(inner >= 0, 1.0 - tail, tail)
    return inner * below, below + inner * bell * 0.3989422804014327


def to_channels(page_ref, place_ref, out_ref, exact=False):
    def step(index, carry):
        channels = pl.ds(pl.multiple_of(index * 256, 256), 256)
        values = page_ref[:, channels]
        if exact:
            out_ref[channels, :] = mm(values.astype(BF), place_ref[...], 0, 0)
        else:
            high, low = split(values)
            out_ref[channels, :] = mm(high, place_ref[...], 0, 0) + mm(low, place_ref[...], 0, 0)
        return carry

    lax.fori_loop(0, D // 256, step, 0)


def to_dense(values_ref, place_ref, dense_ref, padded):
    count = dense_ref.shape[0] // SPLITS
    for index in range(D // 256):
        high, low = split(values_ref[index * 256 : (index + 1) * 256, :])
        page = mm(place_ref[:padded, :], high, 1, 1) + mm(place_ref[:padded, :], low, 1, 1)
        for part in range(2):
            rows = pl.ds(2 * index + part, count, stride=SPLITS)
            dense_ref[rows, :] = page[:count, part * LANES : (part + 1) * LANES]


def from_dense(dense_ref, page_ref, row):
    count = dense_ref.shape[0] // SPLITS
    for part in range(SPLITS):
        rows = pl.ds(part, count, stride=SPLITS)
        page_ref[pl.ds(row, count), part * LANES : (part + 1) * LANES] = dense_ref[rows, :]


def add_halo(page_ref, place_ref, out_ref, count, padded):
    page_ref[pl.ds(count, padded - count), :] = jnp.zeros((padded - count, D), F32)

    def step(index, carry):
        channels = pl.ds(pl.multiple_of(index * 256, 256), 256)
        high, low = split(page_ref[:padded, channels])
        out_ref[channels, :] += mm(high, place_ref[:padded, :], 0, 0) + mm(low, place_ref[:padded, :], 0, 0)
        return carry

    lax.fori_loop(0, D // 256, step, 0)


def move_own(values_ref, swap_ref, out_ref, windows, first):
    for window in range(windows):
        sources = [(window + first + part) % windows * LANES for part in range(2)]
        values = jnp.concatenate([values_ref[:, start : start + LANES] for start in sources], axis=1)
        high, low = split(values)
        target = slice(window * LANES, (window + 1) * LANES)
        out_ref[:, target] = mm(high, swap_ref[...], 1, 0) + mm(low, swap_ref[...], 1, 0)


def vector_rows(s, layer):
    rows = s.vector_rows
    sources = ((G1, s.ln_gain, 0), (B1, s.ln_bias, 0), (G2, s.ln_gain, 1), (B2, s.ln_bias, 1))
    sources += ((QB, s.qv_bias, 0), (VB, s.qv_bias, 1), (PB, s.proj_bias, 0), (F2B, s.fc2_bias, 0))
    sources += tuple((F1B + part, s.fc1_bias, part) for part in range(FEEDS))
    for index, source, part in sources:
        rows[index : index + 1, :] = source[layer : layer + 1, part * D : (part + 1) * D]
    rows[VECTORS:, :] = jnp.zeros((VECTOR_ROWS - VECTORS, D), F32)
    return rows[...].T


def spread_columns(s, layer):
    columns = vector_rows(s, layer)
    for index in range(VECTORS):
        s.sums[index] = jnp.broadcast_to(columns[:, index : index + 1], (D, LANES))


def spread_gains(s, layer):
    columns = vector_rows(s, layer)
    for index, vector in enumerate((G1, G2)):
        s.gains[index] = jnp.broadcast_to(columns[:, vector : vector + 1], (D, LANES))


def spread_part(col):
    rows, lanes = (col // 2) * 2 * LANES, (col % 2) * TABLE
    return slice(rows, rows + 2 * LANES), slice(lanes, lanes + TABLE)


def spread_bias(s, layer):
    spread_ref, rows_ref, bias_ref = s.spread, s.bias_rows, s.bias
    s.padded_table[...] = jnp.zeros(s.padded_table.shape, F32)
    s.padded_table[:, :OFFSETS] = s.table[layer]
    high, low = split(s.padded_table[...])
    parts = []
    for col in range(WIN):
        chosen = spread_ref[spread_part(col)]
        parts.append(mm(high, chosen, 1, 1) + mm(low, chosen, 1, 1))
    source = jnp.concatenate(parts, axis=0)
    rows_ref[...] = jnp.zeros(rows_ref.shape, F32)
    for row in range(WIN):
        shift = (WIN - 1 - row) * WIN
        moved = source if shift == 0 else pltpu.roll(source, 2 * LANES - shift, axis=1)
        rows_ref[pl.ds(row * WIN * HEADS, WIN * HEADS), :] = moved[:, :LANES]
    for head in range(HEADS):
        bias_ref[head] = rows_ref[pl.ds(head, LANES, stride=HEADS), :]


def gather_bias(grad_ref, spread_ref, rows_ref):
    for head in range(HEADS):
        rows_ref[pl.ds(head, LANES, stride=HEADS), :] = grad_ref[head]
    total = jnp.zeros((WIN * HEADS, 2 * LANES), F32)
    for row in range(WIN):
        shift = (WIN - 1 - row) * WIN
        piece = rows_ref[pl.ds(row * WIN * HEADS, WIN * HEADS), :]
        piece = jnp.concatenate([piece, jnp.zeros_like(piece)], axis=1)
        total = total + (piece if shift == 0 else pltpu.roll(piece, shift, axis=1))
    table = jnp.zeros((HEADS, TABLE), F32)
    for col in range(WIN):
        for part in split(total[col * HEADS : (col + 1) * HEADS]):
            table = table + mm(part, spread_ref[spread_part(col)], 1, 0)
    return table


def region_masks(shifted_layer, out_ref):
    key = lax.broadcasted_iota(jnp.int32, (LANES, LANES), 0)
    query = lax.broadcasted_iota(jnp.int32, (LANES, LANES), 1)
    padding = jnp.where(key < AREA, 0.0, NEVER)
    out_ref[0] = padding
    out_ref[1] = padding
    if shifted_layer:
        last = lax.axis_index(ROW) == lax.axis_size(ROW) - 1
        rows_differ = ((key >= AREA // 2) != (query >= AREA // 2)) & last
        cols_differ = (key % WIN >= SHIFT) != (query % WIN >= SHIFT)
        out_ref[0] += jnp.where(rows_differ, MASK_VALUE, 0.0)
        out_ref[1] += jnp.where(rows_differ | cols_differ, MASK_VALUE, 0.0)


def shifted_live(s, windows):
    place = lax.broadcasted_iota(jnp.int32, (1, LANES), 1)
    for window in range(windows):
        here, after = slice(window, window + 1), slice((window + 1) % windows, (window + 1) % windows + 1)
        beyond = place % WIN >= SHIFT
        own = jnp.where(beyond, s.live[after, :], s.live[here, :])
        upper = jnp.where(beyond, s.live_upper[after, :], s.live_upper[here, :])
        s.live_two[here, :] = jnp.where(place >= AREA // 2, upper, own)


def head_rows(group, part, base=0):
    return pl.ds(pl.multiple_of(base + group * GROUP * HEAD_DIM + part * HEAD_DIM, HEAD_DIM), HEAD_DIM)


def norm_one_forward(s, windows):
    def step(index, carry):
        lanes = lane_tile(index)
        hat, _ = norm_parts(s.x[:, lanes])
        s.normed[:, lanes] = (hat * s.sums[G1] + s.sums[B1]).astype(BF)
        return carry

    lax.fori_loop(0, windows, step, 0)


def project_forward(s, windows):
    def step(index, carry):
        rows = chunk_of(index)
        bias = s.sums[jnp.where(index == 0, QB, VB)] * jnp.where(index == 1, 0.0, 1.0)
        out = mm(s.w_qkv[:, rows], s.normed[...], 0, 0)
        s.qkv[rows, :] = (out + wide(bias, windows)).astype(BF)
        return carry

    lax.fori_loop(0, 3, step, 0)


def attend_forward(s, windows, live_ref):
    def step(index, carry):
        lanes = lane_tile(index)
        live = jnp.broadcast_to(live_ref[pl.ds(index, 1), :], (LANES, LANES)).T
        masked = s.regions[jnp.where(index == windows - 1, 1, 0)] + MASK_VALUE * (1.0 - live)
        s.masked[...] = masked

        def heads(group, carry):
            for part in range(GROUP):
                head = group * GROUP + part
                query = s.qkv[head_rows(group, part), lanes]
                key = s.qkv[head_rows(group, part, D), lanes]
                value = s.qkv[head_rows(group, part, 2 * D), lanes]
                scores = mm(key, query, 0, 0) * SCORE_SCALE + (s.bias[head] + s.masked[...])
                exponent = jnp.exp(scores - jnp.max(scores, axis=0, keepdims=True))
                total = jnp.sum(exponent, axis=0, keepdims=True)
                soft = (exponent * (1.0 / total)).astype(BF)
                s.soft[index * HEADS + head] = soft
                s.merged[head_rows(group, part), lanes] = mm(value, soft, 1, 0).astype(BF)
            return carry

        lax.fori_loop(0, HEADS // GROUP, heads, 0)
        return carry

    lax.fori_loop(0, windows, step, 0)


def norm_two_forward(s, windows, live_ref):
    def step(index, carry):
        lanes = lane_tile(index)
        hidden = s.x[:, lanes] + live_ref[pl.ds(index, 1), :] * (s.work[:, lanes] + s.sums[PB])
        s.hidden[:, lanes] = hidden
        s.work[:, lanes] = hidden + s.sums[F2B]
        hat, _ = norm_parts(hidden)
        s.second[:, lanes] = (hat * s.sums[G2] + s.sums[B2]).astype(BF)
        return carry

    lax.fori_loop(0, windows, step, 0)


def feed_forward(s, windows):
    def step(index, carry):
        rows = chunk_of(index)
        inner = mm(s.w_fc1[:, rows], s.second[...], 0, 0) + wide(s.sums[F1B + index], windows)
        active, slope = gelu_parts(inner)
        active = active.astype(BF)
        s.active[rows, :] = active
        s.slope[rows, :] = slope.astype(BF)
        s.work[...] += mm(s.w_fc2[rows, :], active, 0, 0)
        return carry

    lax.fori_loop(0, FEEDS, step, 0)


def feed_backward(s, sink, times):
    s.sums[...] = jnp.zeros(s.sums.shape, F32)
    s.bias[...] = jnp.zeros(s.bias.shape, F32)
    lowered = s.grad[...].astype(BF)
    s.low[...] = lowered
    s.sums[F2B] = fold(lowered.astype(F32))
    s.work[...] = jnp.zeros(s.work.shape, F32)

    claims = sink.layer == 0
    if claims:
        for unit in range(UNIT_FC2, UNIT_FC2 + FEEDS):
            sink.claim(unit)

    def step(index, carry):
        rows = chunk_of(index)
        if claims:
            sink.claim(UNIT_FC1 + index)
        sink.put(0, mm(s.active[rows, :], s.low[...], 1, 1), feed_pieces(index, sink.shares), index == 0)
        grad_inner = mm(s.w_fc2[rows, :], s.low[...], 1, 0) * s.slope[rows, :].astype(F32)
        grad_inner = grad_inner.astype(BF)
        s.sums[F1B + index] = fold(grad_inner.astype(F32))
        sink.put(1, mm(s.second[...], grad_inner, 1, 1), row_pieces(UNIT_FC1 + index, sink.shares), index == 0)
        s.work[...] += mm(s.w_fc1[:, rows], grad_inner, 1, 0)
        sink.advance_at(index, times)
        return carry

    lax.fori_loop(0, FEEDS, step, 0)
    sink.settle(0)
    sink.settle(1)


def norm_two_backward(s, windows, live_ref):
    def step(index, carry):
        lanes = lane_tile(index)
        hat, scale = norm_parts(s.hidden[:, lanes])
        grad = s.work[:, lanes]
        s.sums[G2] += grad * hat
        s.sums[B2] += grad
        grad = s.grad[:, lanes] + norm_pull(grad, s.gains[1], hat, scale)
        s.grad[:, lanes] = grad
        grad_low = (grad * live_ref[pl.ds(index, 1), :]).astype(BF)
        s.low[:, lanes] = grad_low
        s.sums[PB] += grad_low.astype(F32)
        return carry

    lax.fori_loop(0, windows, step, 0)


def merge_backward(s, sink):
    if sink.layer == 0:
        sink.claim(UNIT_PROJ)
    sink.put(0, mm(s.merged[...], s.low[...], 1, 1), row_pieces(UNIT_PROJ, sink.shares), True)
    s.merged[...] = mm(s.w_proj[...], s.low[...], 1, 0).astype(BF)
    sink.settle(0)


def attend_backward(s, windows, sink, times):
    def step(index, carry):
        lanes = lane_tile(index)

        def heads(group, carry):
            for part in range(GROUP):
                head = group * GROUP + part
                rows = head_rows(group, part)
                key_rows, value_rows = head_rows(group, part, D), head_rows(group, part, 2 * D)
                query, key, value = s.qkv[rows, lanes], s.qkv[key_rows, lanes], s.qkv[value_rows, lanes]
                grad_out = s.merged[rows, lanes]
                soft_low = s.soft[index * HEADS + head]
                soft = soft_low.astype(F32)
                grad_soft = mm(value, grad_out, 0, 0)
                inner = jnp.sum(soft * grad_soft, axis=0, keepdims=True)
                grad_scores = (soft * (grad_soft - inner)).astype(BF)
                s.bias[head] += grad_scores.astype(F32)
                grad_query = (mm(key, grad_scores, 1, 0) * SCORE_SCALE).astype(BF)
                grad_key = (mm(query, grad_scores, 1, 1) * SCORE_SCALE).astype(BF)
                grad_value = mm(grad_out, soft_low, 1, 1).astype(BF)
                s.qkv[rows, lanes] = grad_query
                s.qkv[key_rows, lanes] = grad_key
                s.qkv[value_rows, lanes] = grad_value
                s.sums[QB, rows, :] += grad_query.astype(F32)
                s.sums[VB, rows, :] += grad_value.astype(F32)
            return carry

        lax.fori_loop(0, HEADS // GROUP, heads, 0)
        sink.advance_at(index, times)
        return carry

    lax.fori_loop(0, windows, step, 0)


def project_backward(s, sink):
    def step(index, carry):
        rows = chunk_of(index)
        sink.claim(UNIT_QKV + index)
        sink.put(1, mm(s.normed[...], s.qkv[rows, :], 1, 1), row_pieces(UNIT_QKV + index, sink.shares), index == 0)
        return carry

    lax.fori_loop(0, 3, step, 0)


def input_backward(s):
    s.work[...] = mm(s.w_qkv[...], s.qkv[...], 1, 0)


def norm_one_backward(s, windows):
    def step(index, carry):
        lanes = lane_tile(index)
        hat, scale = norm_parts(s.x[:, lanes])
        grad = s.work[:, lanes]
        s.sums[G1] += grad * hat
        s.sums[B1] += grad
        s.grad[:, lanes] += norm_pull(grad, s.gains[0], hat, scale)
        return carry

    lax.fori_loop(0, windows, step, 0)


def small_gradients(s, small_ref):
    places = lax.broadcasted_iota(jnp.int32, (D, LANES), 1)
    packed = jnp.zeros((D, LANES), F32)
    for index in range(VECTORS):
        packed = jnp.where(places == index, jnp.sum(s.sums[index], axis=1, keepdims=True), packed)
    small_ref[:VECTOR_ROWS, :] = packed.T[:VECTOR_ROWS]
    table = gather_bias(s.bias, s.spread, s.bias_rows)
    small_ref[VECTOR_ROWS:, :] = jnp.concatenate([table, jnp.zeros((HEADS, D - TABLE), F32)], axis=1)


def reversed_bits(value, count):
    turned = 0
    for bit in range(count):
        turned = turned * 2 + (value // 2**bit) % 2
    return turned


def row_pieces(unit, shares):
    rows, count = CHUNK // shares, shares.bit_length() - 1
    return [(share * rows, unit, reversed_bits(share, count)) for share in range(shares)]


def feed_pieces(index, shares):
    rows, count = CHUNK // shares, shares.bit_length() - 1
    pieces = []
    for share in range(shares // FEEDS):
        place = reversed_bits(index * (shares // FEEDS) + share, count)
        for part in range(FEEDS):
            pieces.append(((share * FEEDS + part) * rows, UNIT_FC2 + part, place))
    return pieces


class Plan:
    def __init__(self, pages, shares):
        self.shares, self.rows = shares, CHUNK // shares
        page_bits, row_bits = pages.bit_length() - 1, shares.bit_length() - 1
        others = page_bits - 1
        self.steps = []
        for kind in range(CLASSES):
            turn = kind % 2
            page = [(PAGE, 2 ** (1 + (bit + turn) % others)) for bit in range(others)]
            row = [(ROW, 2**bit) for bit in range(row_bits)]
            self.steps.append([(PAGE, 1)] + (row + page if kind == 2 else page + row))
        self.page_steps = [[0] + [at for at, step in enumerate(steps) if at and step[0] == PAGE] for steps in self.steps]
        self.halvings = page_bits + row_bits
        self.phases = self.halvings + page_bits
        self.sizes, self.axes = [], []
        for steps in self.steps:
            size, sizes, axes = [shares, self.rows, CHUNK], [], []
            for axis, _ in steps:
                axes.append(0 if axis == ROW else 1 if size[1] >= 16 else 2)
                size[axes[-1]] //= 2
                sizes.append(tuple(size))
            self.sizes.append(sizes)
            self.axes.append(axes)
        self.steps_at = self.schedule()

    def schedule(self):
        small = TRIPLES
        free, ready, stage_of, plan, now = {}, {}, {}, [], 0.0
        for triple in range(TRIPLES):
            for kind in range(CLASSES):
                stage_of[triple, kind] = 0
        stage_of[small, 0] = 0

        def link(key, phase):
            triple, kind = key
            if phase < self.halvings:
                axis, stride = self.steps[kind][phase]
                size = 2.0**-phase / 2 if triple != small else 0.125
            else:
                axis, stride = self.steps[kind][self.page_steps[kind][self.phases - 1 - phase]]
                size = 2.0 ** (phase - 2 * self.halvings)
            if axis == PAGE and stride == 1:
                return 0, size * PLAN_CORE
            return (axis, stride if axis == PAGE else 0), size * PLAN_LINK * (1.0 if stride == 1 or axis == PAGE else 1.5)

        def last_stage(key):
            return self.halvings if key[0] == small else self.phases + 1

        def allowed(key, point):
            triple, kind = key
            stage = stage_of[key]
            if stage > last_stage(key):
                return False
            if triple == small:
                return point >= len(PLAN_POINTS) - 1
            if stage == 0 and point < PLAN_THERE[triple]:
                return False
            if triple > 0 and stage_of[triple - 1, kind] <= stage:
                return False
            if triple >= RING and stage < self.halvings and stage_of[triple - RING, kind] <= stage + 1:
                return False
            if stage == 0 and triple >= DONE and stage_of[triple - DONE, kind] <= self.phases + 1:
                return False
            return not (stage == 0 and triple >= HELD and stage_of[triple - HELD, kind] <= self.halvings + 1)

        for point, work in enumerate(PLAN_POINTS):
            now += work
            if point == PLAN_HALO:
                free[ROW, 0] = max(now, free.get((ROW, 0), 0.0)) + PLAN_HALO_TIME
            steps, final = [], point == len(PLAN_POINTS) - 1
            while True:
                keys = [key for key in stage_of if allowed(key, point)]
                needed = PLAN_FORCE.get(point, -1)
                keys = [
                    key
                    for key in keys
                    if final or ready.get(key, 0.0) <= now + PLAN_SLACK or (key[0] <= needed and stage_of[key] <= 1)
                ]
                if not keys:
                    break
                key = min(keys, key=lambda key: (max(ready.get(key, 0.0), now), -stage_of[key], key))
                stage = stage_of[key]
                now = max(now, ready.get(key, 0.0)) + (PLAN_ADD * 2.0**-stage if stage else 0.0)
                if stage == self.phases:
                    ready[key] = now + PLAN_LATENCY
                elif stage < last_stage(key):
                    name, length = link(key, stage)
                    free[name] = max(now, free.get(name, 0.0)) + length
                    ready[key] = free[name] + PLAN_LATENCY
                steps.append((*key, stage))
                stage_of[key] += 1
            plan.append(steps)
        assert all(stage_of[key] > last_stage(key) for key in stage_of)
        return plan

    def partner(self, kind, level):
        axis, stride = self.steps[kind][level]
        page, row = lax.axis_index(PAGE), lax.axis_index(ROW)
        mine = page if axis == PAGE else row
        bit = (mine // stride) % 2
        other = mine + (1 - 2 * bit) * stride
        return bit, ((other, row) if axis == PAGE else (page, other))

    def part(self, kind, level, sent=False):
        starts, sizes = [0, 0, 0], list(self.sizes[kind][0])
        for at in range(1, level + 1):
            axis = self.axes[kind][at]
            sizes[axis] //= 2
            bit, _ = self.partner(kind, at)
            which = 1 - bit if sent and at == level else bit
            starts[axis] = starts[axis] + which * sizes[axis]
        return (
            pl.ds(starts[0], sizes[0]),
            pl.ds(pl.multiple_of(starts[1], 8), sizes[1]),
            pl.ds(pl.multiple_of(starts[2], LANES), sizes[2]),
        )

    def place(self, kind, count):
        starts, sizes = [0, 0], [self.rows, CHUNK]
        for at in self.page_steps[kind][:count]:
            axis = self.axes[kind][at] - 1
            sizes[axis] //= 2
            bit, _ = self.partner(kind, at)
            starts[axis] = starts[axis] + bit * sizes[axis]
        return starts, sizes


class Reducer:
    def __init__(self, plan, s):
        self.plan, self.s = plan, s
        self.shares = plan.shares
        self.layer = 1

    def stage_copies(self, slot, pieces):
        s, plan = self.s, self.plan
        bit, device = plan.partner(0, 0)
        rows = plan.rows // 2
        copies = []
        for number, (start, unit, place) in enumerate(pieces):
            start = slot * CHUNK + start
            number_sems = s.stage_sems.at[slot, number]
            overall = self.first_unit() + unit
            sent = pltpu.make_async_remote_copy(
                src_ref=s.staged.at[pl.ds(pl.multiple_of(start + (1 - bit) * rows, 8), rows)],
                dst_ref=s.first_landing.at[overall % (RING * CLASSES), place],
                send_sem=number_sems.at[0],
                recv_sem=s.first_sems.at[overall, place],
                device_id=device,
                device_id_type=MESH,
            )
            kept = pltpu.make_async_copy(
                s.staged.at[pl.ds(pl.multiple_of(start + bit * rows, 8), rows)],
                s.units[self.layer].at[unit, place],
                number_sems.at[1],
            )
            copies.append((sent, kept))
        return copies

    def first_unit(self):
        return UNITS * (1 - self.layer)

    def claim(self, unit):
        pl.semaphore_wait(self.s.first_free.at[self.first_unit() + unit], 1)

    def put(self, slot, grad, pieces, first):
        if first is not True:

            @pl.when(jnp.logical_not(first))
            def _():
                self.settle(slot)

        self.s.staged[pl.ds(slot * CHUNK, CHUNK), :] = grad
        for sent, kept in self.stage_copies(slot, pieces):
            sent.start()
            kept.start()

    def settle(self, slot):
        for sent, kept in self.stage_copies(slot, row_pieces(0, self.shares)):
            sent.wait_send()
            kept.wait()

    def first_arrived(self, triple, kind):
        s, unit = self.s, CLASSES * triple + kind
        landed = s.first_landing.at[unit % (RING * CLASSES)]
        _, device = self.plan.partner(0, 0)
        for place in range(self.shares):
            pltpu.make_async_remote_copy(
                src_ref=landed.at[place],
                dst_ref=landed.at[place],
                send_sem=s.first_sems.at[unit, place],
                recv_sem=s.first_sems.at[unit, place],
                device_id=device,
                device_id_type=MESH,
            ).wait_recv()

    def remote(self, source, target, unit, phase, device):
        return pltpu.make_async_remote_copy(
            src_ref=source,
            dst_ref=target,
            send_sem=self.s.send_sems.at[unit, phase],
            recv_sem=self.s.recv_sems.at[unit, phase],
            device_id=device,
            device_id_type=MESH,
        )

    def held(self, triple, kind):
        return self.s.held.at[CLASSES * (triple % HELD) + kind]

    def landed(self, triple, kind, level):
        if level == 0:
            return self.s.first_landing.at[(CLASSES * triple + kind) % (RING * CLASSES)]
        return self.s.landing[kind][level - 1].at[triple % RING]

    def halving(self, triple, kind, level):
        _, device = self.plan.partner(kind, level)
        source = self.held(triple, kind).at[self.plan.part(kind, level, True)]
        return self.remote(source, self.landed(triple, kind, level), CLASSES * triple + kind, level, device)

    def own_half(self, triple, kind):
        source = self.s.units[1 - triple // GROUPS].at[CLASSES * (triple % GROUPS) + kind]
        sem = self.s.own_sems.at[CLASSES * triple + kind, 0]
        return pltpu.make_async_copy(source, self.held(triple, kind), sem)

    def finished(self, triple, kind):
        return self.held(triple, kind).at[self.plan.part(kind, self.plan.halvings - 1)].at[0]

    def done(self, triple, kind, count):
        starts, sizes = self.plan.place(kind, count)
        return self.s.done.at[
            CLASSES * (triple % DONE) + kind,
            pl.ds(pl.multiple_of(starts[0], 8), sizes[0]),
            pl.ds(pl.multiple_of(starts[1], LANES), sizes[1]),
        ]

    def gathering(self, triple, kind, phase):
        plan = self.plan
        count = len(plan.page_steps[kind]) - (phase - plan.halvings)
        part = self.done(triple, kind, count)
        _, device = plan.partner(kind, plan.page_steps[kind][count - 1])
        return self.remote(part, part, CLASSES * triple + kind, phase, device)

    def result(self, triple, kind):
        which, row_block, col_block = TARGETS[triple % GROUPS][kind]
        rows = self.plan.rows
        target = self.s.results[which].at[
            1 - triple // GROUPS, pl.ds(row_block * rows, rows), pl.ds(col_block * CHUNK, CHUNK)
        ]
        sem = self.s.own_sems.at[CLASSES * triple + kind, 1]
        return pltpu.make_async_copy(self.done(triple, kind, 0), target, sem)

    def start(self, triple, kind, phase):
        plan = self.plan
        if phase == 0:
            self.own_half(triple, kind).start()
        elif phase < plan.halvings:
            if triple >= RING:
                pl.semaphore_wait(self.s.free_sems.at[kind, phase], 1)
            self.halving(triple, kind, phase).start()
        elif phase < plan.phases:
            if phase == plan.halvings:
                self.done(triple, kind, len(plan.page_steps[kind]))[...] = self.finished(triple, kind)[...]
            self.gathering(triple, kind, phase).start()
        elif phase == plan.phases:
            self.result(triple, kind).start()

    def finish(self, triple, kind, phase):
        plan, s = self.plan, self.s
        if phase < plan.halvings:
            if phase == 0:
                self.first_arrived(triple, kind)
                self.own_half(triple, kind).wait()
            else:
                self.halving(triple, kind, phase).wait()
            landed = self.landed(triple, kind, phase)
            kept = self.held(triple, kind).at[plan.part(kind, phase)]
            for share in range(landed.shape[0]):
                kept[share] += landed[share]
            if triple < TRIPLES - RING:
                _, device = plan.partner(kind, phase)
                free = s.free_sems.at[kind, phase]
                if phase == 0:
                    free = s.first_free.at[CLASSES * (triple + RING) + kind]
                pl.semaphore_signal(free, inc=1, device_id=device, device_id_type=MESH)
        elif phase < plan.phases:
            self.gathering(triple, kind, phase).wait()
        else:
            self.result(triple, kind).wait()

    def advance(self, point):
        for triple, kind, stage in self.plan.steps_at[point]:
            if triple == TRIPLES:
                self.small_step(stage - 1)
                continue
            if stage > 0:
                self.finish(triple, kind, stage - 1)
            self.start(triple, kind, stage)

    def advance_at(self, index, points):
        for number, point in enumerate(points):
            if self.plan.steps_at[point]:

                @pl.when(index == number)
                def _(point=point):
                    self.advance(point)

    def small_copy(self, phase):
        s = self.s
        _, device = self.plan.partner(0, phase)
        return pltpu.make_async_remote_copy(
            src_ref=s.small_own if phase == 0 else s.small_parts.at[phase - 1],
            dst_ref=s.small_parts.at[phase],
            send_sem=s.small_sems.at[0, phase],
            recv_sem=s.small_sems.at[1, phase],
            device_id=device,
            device_id_type=MESH,
        )

    def small_step(self, phase):
        s = self.s
        if phase >= 0:
            self.small_copy(phase).wait()
            s.small_parts[phase] += s.small_own[...] if phase == 0 else s.small_parts[phase - 1]
        if phase + 1 < self.plan.halvings:
            self.small_copy(phase + 1).start()


PLAN_POINTS = (0, 2, 3) + (2.7,) * 6 + (5.2, 3, 3, 6) + (3.2,) * 4 + (0.3, 2, 3) + (2.7,) * 6 + (3, 3, 3, 3)
PLAN_THERE = (0, 0, 2, 10, 17, 17, 19, 26)
PLAN_FORCE = {9: 0, 12: 3, 25: 4}
PLAN_HALO, PLAN_HALO_TIME = 9, 12.3
PLAN_CORE, PLAN_LINK, PLAN_LATENCY, PLAN_ADD, PLAN_SLACK = 1.7, 20.0, 2.0, 0.9, 0.0


class Moves:
    def __init__(self, sems):
        self.sems, self.used = sems, 0

    def __call__(self, source, target):
        number, self.used = self.used, self.used + 1
        make = functools.partial(pltpu.make_async_copy, source, target, self.sems.at[number])
        make().start()
        return lambda: make().wait()


class Refs:
    pass


def run(plan, layout, *refs):
    s = Refs()
    for name, ref in zip(layout, refs):
        setattr(s, name, ref)
    rest = list(refs[len(layout) :])
    s.landing = [[rest.pop(0) for _ in range(1, plan.halvings)] for _ in range(CLASSES)]
    s.results = (s.sum_qkv, s.sum_proj, s.sum_fc1, s.sum_fc2)
    s.units = (s.units_zero, s.units_one)
    s.page = s.staged.at[pl.ds(0, s.plain.shape[0])]
    s.spread = s.qkv.at[pl.ds(0, s.in_spread.shape[0])]
    windows = s.x.shape[1] // LANES
    patches = s.dense.shape[0] // SPLITS
    half, half_rows = patches // 2, s.dense.shape[0] // 2
    padded = 16 * -(-half // 16)
    upper, lower = pl.ds(0, half_rows), pl.ds(half_rows, half_rows)
    reducer = Reducer(plan, s)
    move = Moves(s.move_sems)
    page, row = lax.axis_index(PAGE), lax.axis_index(ROW)
    count = lax.axis_size(ROW)
    above, below = (page, (row + count - 1) % count), (page, (row + 1) % count)

    def halo(number, source, target, device):
        make = functools.partial(
            pltpu.make_async_remote_copy,
            src_ref=source,
            dst_ref=target,
            send_sem=s.halo_sems.at[0, number],
            recv_sem=s.halo_sems.at[1, number],
            device_id=device,
            device_id_type=MESH,
        )
        make().start()
        return lambda: make().wait()

    tokens_there = move(s.in_tokens, s.tokens)
    places_there = (move(s.in_plain, s.plain), move(s.in_moved, s.moved))
    swaps_there = (move(s.in_swap_on, s.swap_on), move(s.in_swap_back, s.swap_back))
    spread_there = move(s.in_spread, s.spread)
    weights = ((s.in_qkv, s.w_qkv), (s.in_proj, s.w_proj), (s.in_fc1, s.w_fc1), (s.in_fc2, s.w_fc2))

    def fetch_weight(which, layer):
        source, target = weights[which]
        return move(source.at[layer], target)

    there = [fetch_weight(which, 0) for which in range(4)]

    barrier = pltpu.get_barrier_semaphore()
    devices = [plan.partner(0, level)[1] for level in range(plan.halvings)] + [above, below]
    for device in devices:
        pl.semaphore_signal(barrier, inc=1, device_id=device, device_id_type=MESH)
    pl.semaphore_wait(barrier, len(devices))

    s.live[...] = jnp.zeros(s.live.shape, F32)
    for window in range(windows):
        s.live[window : window + 1, :] = jnp.full((1, LANES), 1.0 - s.blank[0, window].astype(F32))
    live_there = halo(0, s.live, s.live_upper, above)
    grad_there = halo(1, s.in_grad.at[upper], s.grad_upper, above)
    grad_lower_there = move(s.in_grad.at[lower], s.dense.at[lower])
    s.page[...] = jnp.zeros(s.page.shape, F32)
    tokens_there()
    cols = s.tokens.shape[1]
    for line in range(WIN):
        s.page[pl.ds(line * cols, cols), :] = s.tokens[line].astype(F32)
    places_there[0]()
    to_channels(s.page, s.plain, s.x, True)
    saves = [move(s.x, s.kept_x)]
    spread_columns(s, 0)
    spread_there()
    spread_bias(s, 0)
    region_masks(False, s.regions)
    norm_one_forward(s, windows)
    saves.append(move(s.normed, s.kept_normed))
    there[QKV]()
    project_forward(s, windows)
    qkv_saved = move(s.qkv, s.kept_qkv)
    there[QKV] = fetch_weight(QKV, 1)
    attend_forward(s, windows, s.live)
    saves.append(move(s.soft, s.kept_soft))
    saves.append(move(s.merged, s.kept_merged))
    there[PROJ]()
    s.work[...] = mm(s.w_proj[...], s.merged[...], 0, 0)
    there[PROJ] = fetch_weight(PROJ, 1)
    norm_two_forward(s, windows, s.live)
    saves.append(move(s.hidden, s.kept_hidden))
    saves.append(move(s.second, s.kept_second))
    there[FC1]()
    there[FC2]()
    feed_forward(s, windows)
    saves.append(move(s.active, s.kept_active))
    saves.append(move(s.slope, s.kept_slope))
    there[FC1] = fetch_weight(FC1, 1)
    there[FC2] = fetch_weight(FC2, 1)
    to_dense(s.work, s.plain, s.dense.at[upper], padded)
    upper_there = halo(2, s.dense.at[upper], s.upper, above)

    qkv_saved()
    spread_there = move(s.in_spread, s.spread)
    places_there[1]()
    swaps_there[0]()
    saves.pop(0)()
    move_own(s.work, s.swap_on, s.x, windows, 0)
    spread_columns(s, 1)
    spread_there()
    spread_bias(s, 1)
    region_masks(True, s.regions)
    live_there()
    shifted_live(s, windows)
    grad_there()
    grad_lower_there()
    from_dense(s.grad_upper, s.page, 0)
    from_dense(s.dense.at[lower], s.page, half)
    to_channels(s.page, s.moved, s.grad)
    for saved in saves:
        saved()
    upper_there()
    from_dense(s.upper, s.page, 0)
    add_halo(s.page, s.moved, s.x, half, padded)
    norm_one_forward(s, windows)
    there[QKV]()
    project_forward(s, windows)
    attend_forward(s, windows, s.live_two)
    there[PROJ]()
    s.work[...] = mm(s.w_proj[...], s.merged[...], 0, 0)
    norm_two_forward(s, windows, s.live_two)
    there[FC1]()
    there[FC2]()
    feed_forward(s, windows)
    to_dense(s.work, s.moved, s.dense, s.moved.shape[0])
    out_there = halo(3, s.dense.at[upper], s.out_tokens.at[upper], below)
    out_kept = move(s.dense.at[lower], s.out_tokens.at[lower])

    spread_gains(s, 1)

    def backward(layer, live_ref, fetch, points):
        reducer.layer = layer
        first = 0 if layer else FEEDS
        feed_backward(s, reducer, points[:first])
        reducer.advance(points[first])
        fetch(0)
        norm_two_backward(s, windows, live_ref)
        reducer.advance(points[first + 1])
        fetch(1)
        merge_backward(s, reducer)
        reducer.advance(points[first + 2])
        fetch(2)
        attend_backward(s, windows, reducer, points[first + 3 :])
        fetch(3)

    back = {}

    def refill(point):
        if point == 0:
            back[0] = [move(s.kept_active, s.active), move(s.kept_slope, s.slope), move(s.kept_second, s.second)]
            back[0] += [fetch_weight(FC1, 0), fetch_weight(FC2, 0)]
        elif point == 1:
            back[1] = [move(s.kept_hidden, s.hidden)]
        elif point == 2:
            back[2] = [fetch_weight(PROJ, 0)]
        elif point == 3:
            back[2] += [move(s.kept_merged, s.merged)]
            back[3] = [move(s.kept_soft, s.soft)]
        elif point == 4:
            back[4] = [move(s.kept_x, s.x)]
        else:
            back[3] += [move(s.kept_qkv, s.qkv), move(s.kept_normed, s.normed), fetch_weight(QKV, 0)]

    def needed(point):
        if point in back:
            for arrived in back.pop(point):
                arrived()

    backward(1, s.live_two, refill, range(9))
    input_backward(s)
    norm_one_backward(s, windows)
    refill(4)
    out_there()
    to_dense(s.grad, s.moved, s.dense.at[upper], padded)
    next_there = halo(4, s.dense.at[upper], s.next_upper, below)
    reducer.advance(9)
    project_backward(s, reducer)
    spread_there = move(s.in_spread, s.spread)
    reducer.settle(1)
    reducer.advance(10)

    swaps_there[1]()
    move_own(s.grad, s.swap_back, s.work, windows, -1)
    spread_there()
    small_gradients(s, s.small_own.at[1])
    refill(5)
    spread_gains(s, 0)
    reducer.advance(11)
    next_there()
    from_dense(s.next_upper, s.page, 0)
    s.grad[...] = s.work[...]
    add_halo(s.page, s.plain, s.grad, half, padded)
    reducer.advance(12)
    needed(0)

    def wait_next(point):
        needed(point + 1)

    backward(0, s.live, wait_next, range(13, 26))
    project_backward(s, reducer)
    reducer.settle(1)
    reducer.advance(26)
    input_backward(s)
    spread_there = move(s.in_spread, s.spread)
    reducer.advance(27)
    needed(4)
    norm_one_backward(s, windows)
    out_kept()
    to_dense(s.grad, s.plain, s.dense, s.plain.shape[0])
    grad_kept = move(s.dense, s.grad_tokens)
    reducer.advance(28)
    spread_there()
    small_gradients(s, s.small_own.at[0])
    reducer.advance(29)
    finish_small(s, plan, row)
    grad_kept()


def finish_small(s, plan, row):
    total = s.small_parts.at[plan.halvings - 1]
    outs = (
        (s.d_ln_gain, (G1, G2)),
        (s.d_ln_bias, (B1, B2)),
        (s.d_qv_bias, (QB, VB)),
        (s.d_proj_bias, (PB,)),
        (s.d_fc1_bias, tuple(range(F1B, F1B + FEEDS))),
        (s.d_fc2_bias, (F2B,)),
    )
    for layer in range(2):
        s.d_table[layer] = total[layer, VECTOR_ROWS:, :OFFSETS]
        for ref, indices in outs:
            whole = jnp.concatenate([total[layer, index : index + 1, :] for index in indices], axis=1)
            size = ref.shape[1]
            mine = jnp.zeros((1, size), F32)
            for share in range(plan.shares):
                mine = jnp.where(row == share, whole[:, share * size : (share + 1) * size], mine)
            ref[layer : layer + 1, :] = mine


def placements(cols):
    windows = cols // WIN
    patches = WIN * cols
    padded = -(-patches // LANES) * LANES
    plain = np.zeros((padded, windows * LANES), np.float32)
    moved = np.zeros((padded, windows * LANES), np.float32)
    for line in range(WIN):
        for col in range(cols):
            source = line * cols + col
            plain[source, (col // WIN) * LANES + line * WIN + col % WIN] = 1
            new_line, new_col = (line - SHIFT) % WIN, (col - SHIFT) % cols
            moved[source, (new_col // WIN) * LANES + new_line * WIN + new_col % WIN] = 1
    return plain.astype(BF), moved.astype(BF)


def swaps():
    on = np.zeros((2 * LANES, LANES), np.float32)
    back = np.zeros((2 * LANES, LANES), np.float32)
    for line in range(SHIFT):
        for col in range(WIN):
            moved, plain = line * WIN + col, (line + SHIFT) * WIN + (col + SHIFT) % WIN
            on[plain + (LANES if col >= SHIFT else 0), moved] = 1
            back[moved + (LANES if col < SHIFT else 0), plain] = 1
    return on.astype(BF), back.astype(BF)


def table_spread():
    size = 2 * WIN - 1
    spread = np.zeros((WIN, 2 * LANES, TABLE), np.float32)
    for key_col in range(WIN):
        for offset in range(size):
            for col in range(WIN):
                spread[key_col, offset * WIN + col, offset * size + col - key_col + WIN - 1] = 1
    spread = spread.reshape(WIN // 2, 2, 2 * LANES, TABLE).swapaxes(1, 2)
    return spread.reshape(WIN * LANES, 2 * TABLE).astype(BF)


def copy_all(*refs):
    *refs, sems = refs
    count = len(refs) // 3
    sources, targets, held = refs[:count], refs[count : 2 * count], refs[2 * count :]
    ways = [*zip(sources, held), *zip(held, targets)]
    copies = [pltpu.make_async_copy(*way, sems.at[number]) for number, way in enumerate(ways)]
    for copy in copies[:count]:
        copy.start()
    for incoming, outgoing in zip(copies[:count], copies[count:]):
        incoming.wait()
        outgoing.start()
    for copy in copies[count:]:
        copy.wait()


def hand_out(values):
    anywhere = pl.BlockSpec(memory_space=pl.ANY)
    return pl.pallas_call(
        copy_all,
        out_shape=[jax.ShapeDtypeStruct(value.shape, value.dtype) for value in values],
        in_specs=[anywhere] * len(values),
        out_specs=[anywhere] * len(values),
        scratch_shapes=[pltpu.VMEM(value.shape, value.dtype) for value in values]
        + [pltpu.SemaphoreType.DMA((2 * len(values),))],
        compiler_params=pltpu.CompilerParams(vmem_limit_bytes=VMEM_LIMIT),
        name="results",
    )(*values)


def per_device(
    page_tokens,
    blank_mask,
    cotangent,
    ln_gain,
    ln_bias,
    qv_bias,
    rel_table,
    w_qkv,
    w_proj,
    proj_bias,
    w_fc1,
    fc1_bias,
    w_fc2,
    fc2_bias,
):
    pages, shares = lax.axis_size(PAGE), lax.axis_size(ROW)
    plan = Plan(pages, shares)
    cols = page_tokens.shape[2]
    windows, lanes = cols // WIN, cols // WIN * LANES
    dense = ((WIN * cols * SPLITS, LANES), F32)
    half_dense = ((WIN * cols * SPLITS // 2, LANES), F32)
    plain, moved = (jnp.asarray(place) for place in placements(cols))
    live_rows = 8 * -(-windows // 8)
    scalar_inputs = dict(blank=blank_mask[0])
    small_inputs = dict(
        table=rel_table,
        ln_gain=ln_gain,
        ln_bias=ln_bias,
        qv_bias=qv_bias,
        proj_bias=proj_bias,
        fc1_bias=fc1_bias,
        fc2_bias=fc2_bias,
    )
    large_inputs = dict(
        in_tokens=page_tokens[0],
        in_grad=cotangent.reshape(dense[0]),
        in_plain=plain,
        in_moved=moved,
        in_swap_on=jnp.asarray(swaps()[0]),
        in_swap_back=jnp.asarray(swaps()[1]),
        in_spread=jnp.asarray(table_spread()),
        in_qkv=w_qkv,
        in_proj=w_proj,
        in_fc1=w_fc1,
        in_fc2=w_fc2,
    )
    saved = dict(
        x=((D, lanes), F32),
        normed=((D, lanes), BF),
        qkv=((3 * D, lanes), BF),
        soft=((windows * HEADS, LANES, LANES), BF),
        merged=((D, lanes), BF),
        hidden=((D, lanes), F32),
        second=((D, lanes), BF),
        active=((FF, lanes), BF),
        slope=((FF, lanes), BF),
    )
    units = ((UNITS,) + plan.sizes[0][0], F32)
    large_outputs = dict(
        out_tokens=dense,
        grad_tokens=dense,
        sum_qkv=((2, D // shares, 3 * D), F32),
        sum_proj=((2, D // shares, D), F32),
        sum_fc1=((2, D // shares, FF), F32),
        sum_fc2=((2, FF // shares, D), F32),
        units_zero=units,
        units_one=units,
        kept_x=((D, lanes), F32),
        kept_normed=((D, lanes), BF),
        kept_qkv=((3 * D, lanes), BF),
        kept_soft=((windows * HEADS, LANES, LANES), BF),
        kept_merged=((D, lanes), BF),
        kept_hidden=((D, lanes), F32),
        kept_second=((D, lanes), BF),
        kept_active=((FF, lanes), BF),
        kept_slope=((FF, lanes), BF),
    )
    small_outputs = dict(
        d_ln_gain=((2, 2 * D // shares), F32),
        d_ln_bias=((2, 2 * D // shares), F32),
        d_qv_bias=((2, 2 * D // shares), F32),
        d_proj_bias=((2, D // shares), F32),
        d_fc1_bias=((2, FF // shares), F32),
        d_fc2_bias=((2, D // shares), F32),
        d_table=((2, HEADS, OFFSETS), F32),
    )
    small = (2, SMALL, D)
    vmem = dict(
        saved,
        tokens=((WIN, cols, D), BF),
        plain=(plain.shape, BF),
        moved=(moved.shape, BF),
        w_qkv=((D, 3 * D), BF),
        w_proj=((D, D), BF),
        w_fc1=((D, FF), BF),
        w_fc2=((FF, D), BF),
        dense=dense,
        upper=half_dense,
        swap_on=((2 * LANES, LANES), BF),
        swap_back=((2 * LANES, LANES), BF),
        grad_upper=half_dense,
        next_upper=half_dense,
        live_upper=((live_rows, LANES), F32),
        live_two=((live_rows, LANES), F32),
        work=((D, lanes), F32),
        grad=((D, lanes), F32),
        low=((D, lanes), BF),
        sums=((VECTORS, D, LANES), F32),
        gains=((2, D, LANES), F32),
        bias=((HEADS, LANES, LANES), F32),
        bias_rows=((HEADS * LANES, LANES), F32),
        regions=((2, LANES, LANES), F32),
        masked=((LANES, LANES), F32),
        padded_table=((HEADS, TABLE), F32),
        live=((live_rows, LANES), F32),
        vector_rows=((VECTOR_ROWS, D), F32),
        staged=((2 * CHUNK, CHUNK), F32),
        done=((DONE * CLASSES, CHUNK // shares, CHUNK), F32),
        held=((HELD * CLASSES,) + plan.sizes[0][0], F32),
        first_landing=((RING * CLASSES,) + plan.sizes[0][0], F32),
        small_own=(small, F32),
        small_parts=((plan.halvings,) + small, F32),
    )
    semaphores = dict(
        move_sems=pltpu.SemaphoreType.DMA((48,)),
        halo_sems=pltpu.SemaphoreType.DMA((2, 5)),
        send_sems=pltpu.SemaphoreType.DMA((2 * UNITS, plan.phases)),
        recv_sems=pltpu.SemaphoreType.DMA((2 * UNITS, plan.phases)),
        own_sems=pltpu.SemaphoreType.DMA((2 * UNITS, 2)),
        stage_sems=pltpu.SemaphoreType.DMA((2, shares, 2)),
        first_sems=pltpu.SemaphoreType.DMA((2 * UNITS, shares)),
        first_free=pltpu.SemaphoreType.REGULAR((2 * UNITS,)),
        small_sems=pltpu.SemaphoreType.DMA((2, plan.halvings)),
        free_sems=pltpu.SemaphoreType.REGULAR((CLASSES, plan.halvings)),
    )
    landing = [((RING,) + size, F32) for sizes in plan.sizes for size in sizes[1:]]
    layout = [*scalar_inputs, *small_inputs, *large_inputs, *small_outputs, *large_outputs, *vmem, *semaphores]
    in_vmem, anywhere = pl.BlockSpec(memory_space=pltpu.VMEM), pl.BlockSpec(memory_space=pl.ANY)
    outputs = {**small_outputs, **large_outputs}
    results = pl.pallas_call(
        functools.partial(run, plan, layout),
        out_shape=[jax.ShapeDtypeStruct(*shape) for shape in outputs.values()],
        in_specs=[pl.BlockSpec(memory_space=pltpu.SMEM)] + [in_vmem] * len(small_inputs) + [anywhere] * len(large_inputs),
        out_specs=[in_vmem] * len(small_outputs) + [anywhere] * len(large_outputs),
        scratch_shapes=[pltpu.VMEM(*shape) for shape in vmem.values()]
        + list(semaphores.values())
        + [pltpu.VMEM(*shape) for shape in landing],
        compiler_params=pltpu.CompilerParams(
            vmem_limit_bytes=VMEM_LIMIT, collective_id=0, has_side_effects=True
        ),
        name="two_layers",
    )(*scalar_inputs.values(), *small_inputs.values(), *large_inputs.values())
    results = hand_out(results[: len(small_outputs) + 6])
    d_ln_gain, d_ln_bias, d_qv_bias, d_proj_bias, d_fc1_bias, d_fc2_bias, d_table = results[: len(small_outputs)]
    out_tokens, grad_tokens, sum_qkv, sum_proj, sum_fc1, sum_fc2 = results[len(small_outputs) :]
    return (
        out_tokens.reshape(cotangent.shape),
        grad_tokens.reshape(cotangent.shape),
        d_ln_gain,
        d_ln_bias,
        d_qv_bias,
        d_table,
        sum_qkv,
        sum_proj,
        d_proj_bias,
        sum_fc1,
        d_fc1_bias,
        sum_fc2,
        d_fc2_bias,
    )


def solution(mesh):
    tokens, by_row, shares = P(PAGE, ROW, None, None), P(None, ROW), P(None, ROW, None)
    return jax.shard_map(
        per_device,
        mesh=mesh,
        in_specs=(tokens, P(PAGE, ROW, None), tokens) + (P(),) * 11,
        out_specs=(tokens, tokens)
        + (by_row, by_row, by_row, P(), shares, shares, by_row, shares, by_row, shares, by_row),
        check_vma=False,
    )
```

```python
import functools

import jax
import jax.numpy as jnp
import numpy as np
from jax import lax
from jax.experimental import pallas as pl
from jax.experimental.pallas import tpu as pltpu
from jax.sharding import PartitionSpec as P

WIN = 10
SHIFT = 5
AREA = WIN * WIN
LANES = 128
D = 512
HEADS = 16
HEAD_DIM = 32
FF = 2048
CHUNK = 512
FEEDS = FF // CHUNK
SPLITS = D // LANES
EPSILON = 1e-05
MASK_VALUE = -100.0
NEVER = -1e30
SCORE_SCALE = HEAD_DIM ** (-0.5)
VMEM_LIMIT = 63 * 1024 * 1024 + 512 * 1024
BF = jnp.bfloat16
F32 = jnp.float32
MESH = pl.DeviceIdType.MESH
PAGE, ROW = "page", "row"

G1, B1, G2, B2, QB, VB, PB, F2B, F1B, VECTORS = 0, 1, 2, 3, 4, 5, 6, 7, 8, 12
VECTOR_ROWS = 16
SMALL = VECTOR_ROWS + HEADS
OFFSETS = (2 * WIN - 1) ** 2
TABLE = 384

UNIT_FC1, UNIT_FC2, UNIT_PROJ, UNIT_QKV, UNITS = 0, 4, 8, 9, 12
CLASSES = 3
GROUPS = UNITS // CLASSES
TRIPLES = 2 * GROUPS
HELD = 4
DONE = 5
RING = 3
QKV, PROJ, FC1, FC2 = range(4)
TARGETS = (
    ((FC1, 0, 0), (FC1, 0, 1), (FC1, 0, 2)),
    ((FC1, 0, 3), (FC2, 0, 0), (FC2, 1, 0)),
    ((FC2, 2, 0), (FC2, 3, 0), (PROJ, 0, 0)),
    ((QKV, 0, 0), (QKV, 0, 1), (QKV, 0, 2)),
)


def mm(left, right, left_dim, right_dim):
    return lax.dot_general(
        left, right, (((left_dim,), (right_dim,)), ((), ())), preferred_element_type=F32
    )


def split(values):
    high = values.astype(BF)
    return high, (values - high.astype(F32)).astype(BF)


def lane_tile(index):
    return pl.ds(pl.multiple_of(index * LANES, LANES), LANES)


def chunk_of(index):
    return pl.ds(pl.multiple_of(index * CHUNK, CHUNK), CHUNK)


def wide(column, count):
    return jnp.concatenate([column] * count, axis=1)


def fold(values):
    total = values[:, :LANES]
    for start in range(LANES, values.shape[1], LANES):
        total = total + values[:, start : start + LANES]
    return total


def norm_parts(values):
    center = values - jnp.sum(values, axis=0, keepdims=True) * (1.0 / D)
    spread = jnp.sum(center * center, axis=0, keepdims=True) * (1.0 / D)
    scale = lax.rsqrt(spread + EPSILON)
    return center * scale, scale


def norm_pull(grad, gain, hat, scale):
    scaled = grad * gain
    mean_one = jnp.sum(scaled, axis=0, keepdims=True) * (1.0 / D)
    mean_two = jnp.sum(scaled * hat, axis=0, keepdims=True) * (1.0 / D)
    return scale * (scaled - mean_one - hat * mean_two)


def gelu_parts(inner):
    step = 1.0 / (1.0 + (0.3275911 * 0.7071067811865476) * jnp.abs(inner))
    bell = jnp.exp(inner * inner * -0.5)
    poly = 0.5 * 1.061405429
    for factor in (-1.453152027, 1.421413741, -0.284496736, 0.254829592):
        poly = poly * step + 0.5 * factor
    tail = poly * step * bell
    below = jnp.where(inner >= 0, 1.0 - tail, tail)
    return inner * below, below + inner * bell * 0.3989422804014327


def to_channels(page_ref, place_ref, out_ref, exact=False):
    def step(index, carry):
        channels = pl.ds(pl.multiple_of(index * 256, 256), 256)
        values = page_ref[:, channels]
        if exact:
            out_ref[channels, :] = mm(values.astype(BF), place_ref[...], 0, 0)
        else:
            high, low = split(values)
            out_ref[channels, :] = mm(high, place_ref[...], 0, 0) + mm(low, place_ref[...], 0, 0)
        return carry

    lax.fori_loop(0, D // 256, step, 0)


def to_dense(values_ref, place_ref, dense_ref, padded):
    count = dense_ref.shape[0] // SPLITS
    for index in range(D // 256):
        high, low = split(values_ref[index * 256 : (index + 1) * 256, :])
        page = mm(place_ref[:padded, :], high, 1, 1) + mm(place_ref[:padded, :], low, 1, 1)
        for part in range(2):
            rows = pl.ds(2 * index + part, count, stride=SPLITS)
            dense_ref[rows, :] = page[:count, part * LANES : (part + 1) * LANES]


def from_dense(dense_ref, page_ref, row):
    count = dense_ref.shape[0] // SPLITS
    for part in range(SPLITS):
        rows = pl.ds(part, count, stride=SPLITS)
        page_ref[pl.ds(row, count), part * LANES : (part + 1) * LANES] = dense_ref[rows, :]


def add_halo(page_ref, place_ref, out_ref, count, padded):
    page_ref[pl.ds(count, padded - count), :] = jnp.zeros((padded - count, D), F32)

    def step(index, carry):
        channels = pl.ds(pl.multiple_of(index * 256, 256), 256)
        high, low = split(page_ref[:padded, channels])
        out_ref[channels, :] += mm(high, place_ref[:padded, :], 0, 0) + mm(low, place_ref[:padded, :], 0, 0)
        return carry

    lax.fori_loop(0, D // 256, step, 0)


def move_own(values_ref, swap_ref, out_ref, windows, first):
    for window in range(windows):
        sources = [(window + first + part) % windows * LANES for part in range(2)]
        values = jnp.concatenate([values_ref[:, start : start + LANES] for start in sources], axis=1)
        high, low = split(values)
        target = slice(window * LANES, (window + 1) * LANES)
        out_ref[:, target] = mm(high, swap_ref[...], 1, 0) + mm(low, swap_ref[...], 1, 0)


def vector_rows(s, layer):
    rows = s.vector_rows
    sources = ((G1, s.ln_gain, 0), (B1, s.ln_bias, 0), (G2, s.ln_gain, 1), (B2, s.ln_bias, 1))
    sources += ((QB, s.qv_bias, 0), (VB, s.qv_bias, 1), (PB, s.proj_bias, 0), (F2B, s.fc2_bias, 0))
    sources += tuple((F1B + part, s.fc1_bias, part) for part in range(FEEDS))
    for index, source, part in sources:
        rows[index : index + 1, :] = source[layer : layer + 1, part * D : (part + 1) * D]
    rows[VECTORS:, :] = jnp.zeros((VECTOR_ROWS - VECTORS, D), F32)
    return rows[...].T


def spread_columns(s, layer):
    columns = vector_rows(s, layer)
    for index in range(VECTORS):
        s.sums[index] = jnp.broadcast_to(columns[:, index : index + 1], (D, LANES))


def spread_gains(s, layer):
    columns = vector_rows(s, layer)
    for index, vector in enumerate((G1, G2)):
        s.gains[index] = jnp.broadcast_to(columns[:, vector : vector + 1], (D, LANES))


def spread_part(col):
    rows, lanes = (col // 2) * 2 * LANES, (col % 2) * TABLE
    return slice(rows, rows + 2 * LANES), slice(lanes, lanes + TABLE)


def spread_bias(s, layer):
    spread_ref, rows_ref, bias_ref = s.spread, s.bias_rows, s.bias
    s.padded_table[...] = jnp.zeros(s.padded_table.shape, F32)
    s.padded_table[:, :OFFSETS] = s.table[layer]
    high, low = split(s.padded_table[...])
    parts = []
    for col in range(WIN):
        chosen = spread_ref[spread_part(col)]
        parts.append(mm(high, chosen, 1, 1) + mm(low, chosen, 1, 1))
    source = jnp.concatenate(parts, axis=0)
    rows_ref[...] = jnp.zeros(rows_ref.shape, F32)
    for row in range(WIN):
        shift = (WIN - 1 - row) * WIN
        moved = source if shift == 0 else pltpu.roll(source, 2 * LANES - shift, axis=1)
        rows_ref[pl.ds(row * WIN * HEADS, WIN * HEADS), :] = moved[:, :LANES]
    for head in range(HEADS):
        bias_ref[head] = rows_ref[pl.ds(head, LANES, stride=HEADS), :]


def gather_bias(grad_ref, spread_ref, rows_ref):
    for head in range(HEADS):
        rows_ref[pl.ds(head, LANES, stride=HEADS), :] = grad_ref[head]
    total = jnp.zeros((WIN * HEADS, 2 * LANES), F32)
    for row in range(WIN):
        shift = (WIN - 1 - row) * WIN
        piece = rows_ref[pl.ds(row * WIN * HEADS, WIN * HEADS), :]
        piece = jnp.concatenate([piece, jnp.zeros_like(piece)], axis=1)
        total = total + (piece if shift == 0 else pltpu.roll(piece, shift, axis=1))
    table = jnp.zeros((HEADS, TABLE), F32)
    for col in range(WIN):
        for part in split(total[col * HEADS : (col + 1) * HEADS]):
            table = table + mm(part, spread_ref[spread_part(col)], 1, 0)
    return table


def region_masks(shifted_layer, out_ref):
    key = lax.broadcasted_iota(jnp.int32, (LANES, LANES), 0)
    query = lax.broadcasted_iota(jnp.int32, (LANES, LANES), 1)
    padding = jnp.where(key < AREA, 0.0, NEVER)
    out_ref[0] = padding
    out_ref[1] = padding
    if shifted_layer:
        last = lax.axis_index(ROW) == lax.axis_size(ROW) - 1
        rows_differ = ((key >= AREA // 2) != (query >= AREA // 2)) & last
        cols_differ = (key % WIN >= SHIFT) != (query % WIN >= SHIFT)
        out_ref[0] += jnp.where(rows_differ, MASK_VALUE, 0.0)
        out_ref[1] += jnp.where(rows_differ | cols_differ, MASK_VALUE, 0.0)


def shifted_live(s, windows):
    place = lax.broadcasted_iota(jnp.int32, (1, LANES), 1)
    for window in range(windows):
        here, after = slice(window, window + 1), slice((window + 1) % windows, (window + 1) % windows + 1)
        beyond = place % WIN >= SHIFT
        own = jnp.where(beyond, s.live[after, :], s.live[here, :])
        upper = jnp.where(beyond, s.live_upper[after, :], s.live_upper[here, :])
        s.live_two[here, :] = jnp.where(place >= AREA // 2, upper, own)


def head_rows(head, base=0):
    return pl.ds(base + head * HEAD_DIM, HEAD_DIM)


def norm_one_forward(s, windows):
    def step(index, carry):
        lanes = lane_tile(index)
        hat, _ = norm_parts(s.x[:, lanes])
        s.normed[:, lanes] = (hat * s.sums[G1] + s.sums[B1]).astype(BF)
        return carry

    lax.fori_loop(0, windows, step, 0, unroll=3)


def project_forward(s, windows):
    def step(index, carry):
        rows = chunk_of(index)
        bias = s.sums[jnp.where(index == 0, QB, VB)] * jnp.where(index == 1, 0.0, 1.0)
        out = mm(s.w_qkv[:, rows], s.normed[...], 0, 0)
        s.qkv[rows, :] = (out + wide(bias, windows)).astype(BF)
        return carry

    lax.fori_loop(0, 3, step, 0)


def attend_forward(s, windows, live_ref):
    def step(index, carry):
        lanes = lane_tile(index)
        live = jnp.broadcast_to(live_ref[pl.ds(index, 1), :], (LANES, LANES)).T
        masked = s.regions[jnp.where(index == windows - 1, 1, 0)] + MASK_VALUE * (1.0 - live)
        for head in range(HEADS):
            query = s.qkv[head_rows(head), lanes]
            key = s.qkv[head_rows(head, D), lanes]
            value = s.qkv[head_rows(head, 2 * D), lanes]
            scores = mm(key, query, 0, 0) * SCORE_SCALE + (s.bias[head] + masked)
            exponent = jnp.exp(scores - jnp.max(scores, axis=0, keepdims=True))
            total = jnp.sum(exponent, axis=0, keepdims=True)
            soft = (exponent * (1.0 / total)).astype(BF)
            s.soft[index * HEADS + head] = soft
            s.merged[head_rows(head), lanes] = mm(value, soft, 1, 0).astype(BF)
        return carry

    lax.fori_loop(0, windows, step, 0, unroll=2)


def norm_two_forward(s, windows, live_ref):
    def step(index, carry):
        lanes = lane_tile(index)
        hidden = s.x[:, lanes] + live_ref[pl.ds(index, 1), :] * (s.work[:, lanes] + s.sums[PB])
        s.hidden[:, lanes] = hidden
        s.work[:, lanes] = hidden + s.sums[F2B]
        hat, _ = norm_parts(hidden)
        s.second[:, lanes] = (hat * s.sums[G2] + s.sums[B2]).astype(BF)
        return carry

    lax.fori_loop(0, windows, step, 0, unroll=3)


def feed_forward(s, windows):
    def step(index, carry):
        rows = chunk_of(index)
        inner = mm(s.w_fc1[:, rows], s.second[...], 0, 0) + wide(s.sums[F1B + index], windows)
        active, slope = gelu_parts(inner)
        active = active.astype(BF)
        s.active[rows, :] = active
        s.slope[rows, :] = slope.astype(BF)
        s.work[...] += mm(s.w_fc2[rows, :], active, 0, 0)
        return carry

    lax.fori_loop(0, FEEDS, step, 0)


def feed_backward(s, sink, times):
    s.sums[...] = jnp.zeros(s.sums.shape, F32)
    s.bias[...] = jnp.zeros(s.bias.shape, F32)
    lowered = s.grad[...].astype(BF)
    s.low[...] = lowered
    s.sums[F2B] = fold(lowered.astype(F32))
    s.work[...] = jnp.zeros(s.work.shape, F32)

    claims = sink.layer == 0
    if claims:
        for unit in range(UNIT_FC2, UNIT_FC2 + FEEDS):
            sink.claim(unit)

    def step(index, carry):
        rows = chunk_of(index)
        if claims:
            sink.claim(UNIT_FC1 + index)
        sink.put(0, mm(s.active[rows, :], s.low[...], 1, 1), feed_pieces(index, sink.shares), index == 0)
        grad_inner = mm(s.w_fc2[rows, :], s.low[...], 1, 0) * s.slope[rows, :].astype(F32)
        grad_inner = grad_inner.astype(BF)
        s.sums[F1B + index] = fold(grad_inner.astype(F32))
        sink.put(1, mm(s.second[...], grad_inner, 1, 1), row_pieces(UNIT_FC1 + index, sink.shares), index == 0)
        s.work[...] += mm(s.w_fc1[:, rows], grad_inner, 1, 0)
        sink.advance_at(index, times)
        return carry

    lax.fori_loop(0, FEEDS, step, 0)
    sink.settle(0)
    sink.settle(1)


def norm_two_backward(s, windows, live_ref):
    def step(index, carry):
        lanes = lane_tile(index)
        hat, scale = norm_parts(s.hidden[:, lanes])
        grad = s.work[:, lanes]
        s.sums[G2] += grad * hat
        s.sums[B2] += grad
        grad = s.grad[:, lanes] + norm_pull(grad, s.gains[1], hat, scale)
        s.grad[:, lanes] = grad
        grad_low = (grad * live_ref[pl.ds(index, 1), :]).astype(BF)
        s.low[:, lanes] = grad_low
        s.sums[PB] += grad_low.astype(F32)
        return carry

    lax.fori_loop(0, windows, step, 0, unroll=3)


def merge_backward(s, sink):
    if sink.layer == 0:
        sink.claim(UNIT_PROJ)
    sink.put(0, mm(s.merged[...], s.low[...], 1, 1), row_pieces(UNIT_PROJ, sink.shares), True)
    s.merged[...] = mm(s.w_proj[...], s.low[...], 1, 0).astype(BF)
    sink.settle(0)


def attend_backward(s, windows, sink, times):
    def step(index, carry):
        lanes = lane_tile(index)
        for head in range(HEADS):
            query = s.qkv[head_rows(head), lanes]
            key = s.qkv[head_rows(head, D), lanes]
            value = s.qkv[head_rows(head, 2 * D), lanes]
            grad_out = s.merged[head_rows(head), lanes]
            soft_low = s.soft[index * HEADS + head]
            soft = soft_low.astype(F32)
            grad_soft = mm(value, grad_out, 0, 0)
            inner = jnp.sum(soft * grad_soft, axis=0, keepdims=True)
            grad_scores = (soft * (grad_soft - inner)).astype(BF)
            s.bias[head] += grad_scores.astype(F32)
            grad_query = (mm(key, grad_scores, 1, 0) * SCORE_SCALE).astype(BF)
            grad_key = (mm(query, grad_scores, 1, 1) * SCORE_SCALE).astype(BF)
            grad_value = mm(grad_out, soft_low, 1, 1).astype(BF)
            s.qkv[head_rows(head), lanes] = grad_query
            s.qkv[head_rows(head, D), lanes] = grad_key
            s.qkv[head_rows(head, 2 * D), lanes] = grad_value
            s.sums[QB, head_rows(head), :] += grad_query.astype(F32)
            s.sums[VB, head_rows(head), :] += grad_value.astype(F32)
        sink.advance_at(index, times)
        return carry

    lax.fori_loop(0, windows, step, 0)


def project_backward(s, sink):
    def step(index, carry):
        rows = chunk_of(index)
        sink.claim(UNIT_QKV + index)
        sink.put(1, mm(s.normed[...], s.qkv[rows, :], 1, 1), row_pieces(UNIT_QKV + index, sink.shares), index == 0)
        return carry

    lax.fori_loop(0, 3, step, 0)


def input_backward(s):
    s.work[...] = mm(s.w_qkv[...], s.qkv[...], 1, 0)


def norm_one_backward(s, windows):
    def step(index, carry):
        lanes = lane_tile(index)
        hat, scale = norm_parts(s.x[:, lanes])
        grad = s.work[:, lanes]
        s.sums[G1] += grad * hat
        s.sums[B1] += grad
        s.grad[:, lanes] += norm_pull(grad, s.gains[0], hat, scale)
        return carry

    lax.fori_loop(0, windows, step, 0, unroll=3)


def small_gradients(s, small_ref):
    places = lax.broadcasted_iota(jnp.int32, (D, LANES), 1)
    packed = jnp.zeros((D, LANES), F32)
    for index in range(VECTORS):
        packed = jnp.where(places == index, jnp.sum(s.sums[index], axis=1, keepdims=True), packed)
    small_ref[:VECTOR_ROWS, :] = packed.T[:VECTOR_ROWS]
    table = gather_bias(s.bias, s.spread, s.bias_rows)
    small_ref[VECTOR_ROWS:, :] = jnp.concatenate([table, jnp.zeros((HEADS, D - TABLE), F32)], axis=1)


def reversed_bits(value, count):
    turned = 0
    for bit in range(count):
        turned = turned * 2 + (value // 2**bit) % 2
    return turned


def row_pieces(unit, shares):
    rows, count = CHUNK // shares, shares.bit_length() - 1
    return [(share * rows, unit, reversed_bits(share, count)) for share in range(shares)]


def feed_pieces(index, shares):
    rows, count = CHUNK // shares, shares.bit_length() - 1
    pieces = []
    for share in range(shares // FEEDS):
        place = reversed_bits(index * (shares // FEEDS) + share, count)
        for part in range(FEEDS):
            pieces.append(((share * FEEDS + part) * rows, UNIT_FC2 + part, place))
    return pieces


class Plan:
    def __init__(self, pages, shares):
        self.shares, self.rows = shares, CHUNK // shares
        page_bits, row_bits = pages.bit_length() - 1, shares.bit_length() - 1
        others = page_bits - 1
        self.steps = []
        for kind in range(CLASSES):
            turn = kind % 2
            page = [(PAGE, 2 ** (1 + (bit + turn) % others)) for bit in range(others)]
            row = [(ROW, 2**bit) for bit in range(row_bits)]
            self.steps.append([(PAGE, 1)] + (row + page if kind == 2 else page + row))
        self.page_steps = [[0] + [at for at, step in enumerate(steps) if at and step[0] == PAGE] for steps in self.steps]
        self.halvings = page_bits + row_bits
        self.phases = self.halvings + page_bits
        self.sizes, self.axes = [], []
        for steps in self.steps:
            size, sizes, axes = [shares, self.rows, CHUNK], [], []
            for axis, _ in steps:
                axes.append(0 if axis == ROW else 1 if size[1] >= 16 else 2)
                size[axes[-1]] //= 2
                sizes.append(tuple(size))
            self.sizes.append(sizes)
            self.axes.append(axes)
        self.steps_at = self.schedule()

    def schedule(self):
        small = TRIPLES
        free, ready, stage_of, plan, now = {}, {}, {}, [], 0.0
        for triple in range(TRIPLES):
            for kind in range(CLASSES):
                stage_of[triple, kind] = 0
        stage_of[small, 0] = 0

        def link(key, phase):
            triple, kind = key
            if phase < self.halvings:
                axis, stride = self.steps[kind][phase]
                size = 2.0**-phase / 2 if triple != small else 0.125
            else:
                axis, stride = self.steps[kind][self.page_steps[kind][self.phases - 1 - phase]]
                size = 2.0 ** (phase - 2 * self.halvings)
            if axis == PAGE and stride == 1:
                return 0, size * PLAN_CORE
            return (axis, stride if axis == PAGE else 0), size * PLAN_LINK * (1.0 if stride == 1 or axis == PAGE else 1.5)

        def last_stage(key):
            return self.halvings if key[0] == small else self.phases + 1

        def allowed(key, point):
            triple, kind = key
            stage = stage_of[key]
            if stage > last_stage(key):
                return False
            if triple == small:
                return point >= len(PLAN_POINTS) - 1
            if stage == 0 and point < PLAN_THERE[triple]:
                return False
            if triple > 0 and stage_of[triple - 1, kind] <= stage:
                return False
            if triple >= RING and stage < self.halvings and stage_of[triple - RING, kind] <= stage + 1:
                return False
            if stage == 0 and triple >= DONE and stage_of[triple - DONE, kind] <= self.phases + 1:
                return False
            return not (stage == 0 and triple >= HELD and stage_of[triple - HELD, kind] <= self.halvings + 1)

        for point, work in enumerate(PLAN_POINTS):
            now += work
            if point == PLAN_HALO:
                free[ROW, 0] = max(now, free.get((ROW, 0), 0.0)) + PLAN_HALO_TIME
            steps, final = [], point == len(PLAN_POINTS) - 1
            while True:
                keys = [key for key in stage_of if allowed(key, point)]
                needed = PLAN_FORCE.get(point, -1)
                keys = [
                    key
                    for key in keys
                    if final or ready.get(key, 0.0) <= now + PLAN_SLACK or (key[0] <= needed and stage_of[key] <= 1)
                ]
                if not keys:
                    break
                key = min(keys, key=lambda key: (max(ready.get(key, 0.0), now), -stage_of[key], key))
                stage = stage_of[key]
                now = max(now, ready.get(key, 0.0)) + (PLAN_ADD * 2.0**-stage if stage else 0.0)
                if stage == self.phases:
                    ready[key] = now + PLAN_LATENCY
                elif stage < last_stage(key):
                    name, length = link(key, stage)
                    free[name] = max(now, free.get(name, 0.0)) + length
                    ready[key] = free[name] + PLAN_LATENCY
                steps.append((*key, stage))
                stage_of[key] += 1
            plan.append(steps)
        assert all(stage_of[key] > last_stage(key) for key in stage_of)
        return plan

    def partner(self, kind, level):
        axis, stride = self.steps[kind][level]
        page, row = lax.axis_index(PAGE), lax.axis_index(ROW)
        mine = page if axis == PAGE else row
        bit = (mine // stride) % 2
        other = mine + (1 - 2 * bit) * stride
        return bit, ((other, row) if axis == PAGE else (page, other))

    def part(self, kind, level, sent=False):
        starts, sizes = [0, 0, 0], list(self.sizes[kind][0])
        for at in range(1, level + 1):
            axis = self.axes[kind][at]
            sizes[axis] //= 2
            bit, _ = self.partner(kind, at)
            which = 1 - bit if sent and at == level else bit
            starts[axis] = starts[axis] + which * sizes[axis]
        return (
            pl.ds(starts[0], sizes[0]),
            pl.ds(pl.multiple_of(starts[1], 8), sizes[1]),
            pl.ds(pl.multiple_of(starts[2], LANES), sizes[2]),
        )

    def place(self, kind, count):
        starts, sizes = [0, 0], [self.rows, CHUNK]
        for at in self.page_steps[kind][:count]:
            axis = self.axes[kind][at] - 1
            sizes[axis] //= 2
            bit, _ = self.partner(kind, at)
            starts[axis] = starts[axis] + bit * sizes[axis]
        return starts, sizes


class Reducer:
    def __init__(self, plan, s):
        self.plan, self.s = plan, s
        self.shares = plan.shares
        self.layer = 1

    def stage_copies(self, slot, pieces):
        s, plan = self.s, self.plan
        bit, device = plan.partner(0, 0)
        rows = plan.rows // 2
        copies = []
        for number, (start, unit, place) in enumerate(pieces):
            start = slot * CHUNK + start
            number_sems = s.stage_sems.at[slot, number]
            overall = self.first_unit() + unit
            sent = pltpu.make_async_remote_copy(
                src_ref=s.staged.at[pl.ds(pl.multiple_of(start + (1 - bit) * rows, 8), rows)],
                dst_ref=s.first_landing.at[overall % (RING * CLASSES), place],
                send_sem=number_sems.at[0],
                recv_sem=s.first_sems.at[overall, place],
                device_id=device,
                device_id_type=MESH,
            )
            kept = pltpu.make_async_copy(
                s.staged.at[pl.ds(pl.multiple_of(start + bit * rows, 8), rows)],
                s.units[self.layer].at[unit, place],
                number_sems.at[1],
            )
            copies.append((sent, kept))
        return copies

    def first_unit(self):
        return UNITS * (1 - self.layer)

    def claim(self, unit):
        pl.semaphore_wait(self.s.first_free.at[self.first_unit() + unit], 1)

    def put(self, slot, grad, pieces, first):
        if first is not True:

            @pl.when(jnp.logical_not(first))
            def _():
                self.settle(slot)

        self.s.staged[pl.ds(slot * CHUNK, CHUNK), :] = grad
        for sent, kept in self.stage_copies(slot, pieces):
            sent.start()
            kept.start()

    def settle(self, slot):
        for sent, kept in self.stage_copies(slot, row_pieces(0, self.shares)):
            sent.wait_send()
            kept.wait()

    def first_arrived(self, triple, kind):
        s, unit = self.s, CLASSES * triple + kind
        landed = s.first_landing.at[unit % (RING * CLASSES)]
        _, device = self.plan.partner(0, 0)
        for place in range(self.shares):
            pltpu.make_async_remote_copy(
                src_ref=landed.at[place],
                dst_ref=landed.at[place],
                send_sem=s.first_sems.at[unit, place],
                recv_sem=s.first_sems.at[unit, place],
                device_id=device,
                device_id_type=MESH,
            ).wait_recv()

    def remote(self, source, target, unit, phase, device):
        return pltpu.make_async_remote_copy(
            src_ref=source,
            dst_ref=target,
            send_sem=self.s.send_sems.at[unit, phase],
            recv_sem=self.s.recv_sems.at[unit, phase],
            device_id=device,
            device_id_type=MESH,
        )

    def held(self, triple, kind):
        return self.s.held.at[CLASSES * (triple % HELD) + kind]

    def landed(self, triple, kind, level):
        if level == 0:
            return self.s.first_landing.at[(CLASSES * triple + kind) % (RING * CLASSES)]
        return self.s.landing[kind][level - 1].at[triple % RING]

    def halving(self, triple, kind, level):
        _, device = self.plan.partner(kind, level)
        source = self.held(triple, kind).at[self.plan.part(kind, level, True)]
        return self.remote(source, self.landed(triple, kind, level), CLASSES * triple + kind, level, device)

    def own_half(self, triple, kind):
        source = self.s.units[1 - triple // GROUPS].at[CLASSES * (triple % GROUPS) + kind]
        sem = self.s.own_sems.at[CLASSES * triple + kind, 0]
        return pltpu.make_async_copy(source, self.held(triple, kind), sem)

    def finished(self, triple, kind):
        return self.held(triple, kind).at[self.plan.part(kind, self.plan.halvings - 1)].at[0]

    def done(self, triple, kind, count):
        starts, sizes = self.plan.place(kind, count)
        return self.s.done.at[
            CLASSES * (triple % DONE) + kind,
            pl.ds(pl.multiple_of(starts[0], 8), sizes[0]),
            pl.ds(pl.multiple_of(starts[1], LANES), sizes[1]),
        ]

    def gathering(self, triple, kind, phase):
        plan = self.plan
        count = len(plan.page_steps[kind]) - (phase - plan.halvings)
        part = self.done(triple, kind, count)
        _, device = plan.partner(kind, plan.page_steps[kind][count - 1])
        return self.remote(part, part, CLASSES * triple + kind, phase, device)

    def result(self, triple, kind):
        which, row_block, col_block = TARGETS[triple % GROUPS][kind]
        rows = self.plan.rows
        target = self.s.results[which].at[
            1 - triple // GROUPS, pl.ds(row_block * rows, rows), pl.ds(col_block * CHUNK, CHUNK)
        ]
        sem = self.s.own_sems.at[CLASSES * triple + kind, 1]
        return pltpu.make_async_copy(self.done(triple, kind, 0), target, sem)

    def start(self, triple, kind, phase):
        plan = self.plan
        if phase == 0:
            self.own_half(triple, kind).start()
        elif phase < plan.halvings:
            if triple >= RING:
                pl.semaphore_wait(self.s.free_sems.at[kind, phase], 1)
            self.halving(triple, kind, phase).start()
        elif phase < plan.phases:
            if phase == plan.halvings:
                self.done(triple, kind, len(plan.page_steps[kind]))[...] = self.finished(triple, kind)[...]
            self.gathering(triple, kind, phase).start()
        elif phase == plan.phases:
            self.result(triple, kind).start()

    def finish(self, triple, kind, phase):
        plan, s = self.plan, self.s
        if phase < plan.halvings:
            if phase == 0:
                self.first_arrived(triple, kind)
                self.own_half(triple, kind).wait()
            else:
                self.halving(triple, kind, phase).wait()
            landed = self.landed(triple, kind, phase)
            kept = self.held(triple, kind).at[plan.part(kind, phase)]
            for share in range(landed.shape[0]):
                kept[share] += landed[share]
            if triple < TRIPLES - RING:
                _, device = plan.partner(kind, phase)
                free = s.free_sems.at[kind, phase]
                if phase == 0:
                    free = s.first_free.at[CLASSES * (triple + RING) + kind]
                pl.semaphore_signal(free, inc=1, device_id=device, device_id_type=MESH)
        elif phase < plan.phases:
            self.gathering(triple, kind, phase).wait()
        else:
            self.result(triple, kind).wait()

    def advance(self, point):
        for triple, kind, stage in self.plan.steps_at[point]:
            if triple == TRIPLES:
                self.small_step(stage - 1)
                continue
            if stage > 0:
                self.finish(triple, kind, stage - 1)
            self.start(triple, kind, stage)

    def advance_at(self, index, points):
        for number, point in enumerate(points):
            if self.plan.steps_at[point]:

                @pl.when(index == number)
                def _(point=point):
                    self.advance(point)

    def small_copy(self, phase):
        s = self.s
        _, device = self.plan.partner(0, phase)
        return pltpu.make_async_remote_copy(
            src_ref=s.small_own if phase == 0 else s.small_parts.at[phase - 1],
            dst_ref=s.small_parts.at[phase],
            send_sem=s.small_sems.at[0, phase],
            recv_sem=s.small_sems.at[1, phase],
            device_id=device,
            device_id_type=MESH,
        )

    def small_step(self, phase):
        s = self.s
        if phase >= 0:
            self.small_copy(phase).wait()
            s.small_parts[phase] += s.small_own[...] if phase == 0 else s.small_parts[phase - 1]
        if phase + 1 < self.plan.halvings:
            self.small_copy(phase + 1).start()


PLAN_POINTS = (0, 2, 3) + (2.7,) * 6 + (5.2, 3, 3, 6) + (3.2,) * 4 + (0.3, 2, 3) + (2.7,) * 6 + (3, 3, 3, 3)
PLAN_THERE = (0, 0, 2, 10, 17, 17, 19, 26)
PLAN_FORCE = {9: 0, 12: 3, 25: 4}
PLAN_HALO, PLAN_HALO_TIME = 9, 12.3
PLAN_CORE, PLAN_LINK, PLAN_LATENCY, PLAN_ADD, PLAN_SLACK = 1.7, 20.0, 2.0, 0.9, 0.0


class Moves:
    def __init__(self, sems):
        self.sems, self.used = sems, 0

    def __call__(self, source, target):
        number, self.used = self.used, self.used + 1
        make = functools.partial(pltpu.make_async_copy, source, target, self.sems.at[number])
        make().start()
        return lambda: make().wait()


class Refs:
    pass


def run(plan, layout, *refs):
    s = Refs()
    for name, ref in zip(layout, refs):
        setattr(s, name, ref)
    rest = list(refs[len(layout) :])
    s.landing = [[rest.pop(0) for _ in range(1, plan.halvings)] for _ in range(CLASSES)]
    s.results = (s.sum_qkv, s.sum_proj, s.sum_fc1, s.sum_fc2)
    s.units = (s.units_zero, s.units_one)
    s.page = s.staged.at[pl.ds(0, s.plain.shape[0])]
    s.spread = s.qkv.at[pl.ds(0, s.in_spread.shape[0])]
    windows = s.x.shape[1] // LANES
    patches = s.dense.shape[0] // SPLITS
    half, half_rows = patches // 2, s.dense.shape[0] // 2
    padded = 16 * -(-half // 16)
    upper, lower = pl.ds(0, half_rows), pl.ds(half_rows, half_rows)
    reducer = Reducer(plan, s)
    move = Moves(s.move_sems)
    page, row = lax.axis_index(PAGE), lax.axis_index(ROW)
    count = lax.axis_size(ROW)
    above, below = (page, (row + count - 1) % count), (page, (row + 1) % count)

    def halo(number, source, target, device):
        make = functools.partial(
            pltpu.make_async_remote_copy,
            src_ref=source,
            dst_ref=target,
            send_sem=s.halo_sems.at[0, number],
            recv_sem=s.halo_sems.at[1, number],
            device_id=device,
            device_id_type=MESH,
        )
        make().start()
        return lambda: make().wait()

    tokens_there = move(s.in_tokens, s.tokens)
    places_there = (move(s.in_plain, s.plain), move(s.in_moved, s.moved))
    swaps_there = (move(s.in_swap_on, s.swap_on), move(s.in_swap_back, s.swap_back))
    spread_there = move(s.in_spread, s.spread)
    weights = ((s.in_qkv, s.w_qkv), (s.in_proj, s.w_proj), (s.in_fc1, s.w_fc1), (s.in_fc2, s.w_fc2))

    def fetch_weight(which, layer):
        source, target = weights[which]
        return move(source.at[layer], target)

    there = [fetch_weight(which, 0) for which in range(4)]

    barrier = pltpu.get_barrier_semaphore()
    devices = [plan.partner(0, level)[1] for level in range(plan.halvings)] + [above, below]
    for device in devices:
        pl.semaphore_signal(barrier, inc=1, device_id=device, device_id_type=MESH)
    pl.semaphore_wait(barrier, len(devices))

    s.live[...] = jnp.zeros(s.live.shape, F32)
    for window in range(windows):
        s.live[window : window + 1, :] = jnp.full((1, LANES), 1.0 - s.blank[0, window].astype(F32))
    live_there = halo(0, s.live, s.live_upper, above)
    grad_there = halo(1, s.in_grad.at[upper], s.grad_upper, above)
    grad_lower_there = move(s.in_grad.at[lower], s.dense.at[lower])
    s.page[...] = jnp.zeros(s.page.shape, F32)
    tokens_there()
    cols = s.tokens.shape[1]
    for line in range(WIN):
        s.page[pl.ds(line * cols, cols), :] = s.tokens[line].astype(F32)
    places_there[0]()
    to_channels(s.page, s.plain, s.x, True)
    saves = [move(s.x, s.kept_x)]
    spread_columns(s, 0)
    spread_there()
    spread_bias(s, 0)
    region_masks(False, s.regions)
    norm_one_forward(s, windows)
    saves.append(move(s.normed, s.kept_normed))
    there[QKV]()
    project_forward(s, windows)
    qkv_saved = move(s.qkv, s.kept_qkv)
    there[QKV] = fetch_weight(QKV, 1)
    attend_forward(s, windows, s.live)
    saves.append(move(s.soft, s.kept_soft))
    saves.append(move(s.merged, s.kept_merged))
    there[PROJ]()
    s.work[...] = mm(s.w_proj[...], s.merged[...], 0, 0)
    there[PROJ] = fetch_weight(PROJ, 1)
    norm_two_forward(s, windows, s.live)
    saves.append(move(s.hidden, s.kept_hidden))
    saves.append(move(s.second, s.kept_second))
    there[FC1]()
    there[FC2]()
    feed_forward(s, windows)
    saves.append(move(s.active, s.kept_active))
    saves.append(move(s.slope, s.kept_slope))
    there[FC1] = fetch_weight(FC1, 1)
    there[FC2] = fetch_weight(FC2, 1)
    to_dense(s.work, s.plain, s.dense.at[upper], padded)
    upper_there = halo(2, s.dense.at[upper], s.upper, above)

    qkv_saved()
    spread_there = move(s.in_spread, s.spread)
    places_there[1]()
    swaps_there[0]()
    saves.pop(0)()
    move_own(s.work, s.swap_on, s.x, windows, 0)
    spread_columns(s, 1)
    spread_there()
    spread_bias(s, 1)
    region_masks(True, s.regions)
    live_there()
    shifted_live(s, windows)
    grad_there()
    grad_lower_there()
    from_dense(s.grad_upper, s.page, 0)
    from_dense(s.dense.at[lower], s.page, half)
    to_channels(s.page, s.moved, s.grad)
    for saved in saves:
        saved()
    upper_there()
    from_dense(s.upper, s.page, 0)
    add_halo(s.page, s.moved, s.x, half, padded)
    norm_one_forward(s, windows)
    there[QKV]()
    project_forward(s, windows)
    attend_forward(s, windows, s.live_two)
    there[PROJ]()
    s.work[...] = mm(s.w_proj[...], s.merged[...], 0, 0)
    norm_two_forward(s, windows, s.live_two)
    there[FC1]()
    there[FC2]()
    feed_forward(s, windows)
    to_dense(s.work, s.moved, s.dense, s.moved.shape[0])
    out_there = halo(3, s.dense.at[upper], s.out_tokens.at[upper], below)
    out_kept = move(s.dense.at[lower], s.out_tokens.at[lower])

    spread_gains(s, 1)

    def backward(layer, live_ref, fetch, points):
        reducer.layer = layer
        first = 0 if layer else FEEDS
        feed_backward(s, reducer, points[:first])
        reducer.advance(points[first])
        fetch(0)
        norm_two_backward(s, windows, live_ref)
        reducer.advance(points[first + 1])
        fetch(1)
        merge_backward(s, reducer)
        reducer.advance(points[first + 2])
        fetch(2)
        attend_backward(s, windows, reducer, points[first + 3 :])
        fetch(3)

    back = {}

    def refill(point):
        if point == 0:
            back[0] = [move(s.kept_active, s.active), move(s.kept_slope, s.slope), move(s.kept_second, s.second)]
            back[0] += [fetch_weight(FC1, 0), fetch_weight(FC2, 0)]
        elif point == 1:
            back[1] = [move(s.kept_hidden, s.hidden)]
        elif point == 2:
            back[2] = [fetch_weight(PROJ, 0)]
        elif point == 3:
            back[2] += [move(s.kept_merged, s.merged)]
            back[3] = [move(s.kept_soft, s.soft)]
        elif point == 4:
            back[4] = [move(s.kept_x, s.x)]
        else:
            back[3] += [move(s.kept_qkv, s.qkv), move(s.kept_normed, s.normed), fetch_weight(QKV, 0)]

    def needed(point):
        if point in back:
            for arrived in back.pop(point):
                arrived()

    backward(1, s.live_two, refill, range(9))
    input_backward(s)
    norm_one_backward(s, windows)
    refill(4)
    out_there()
    to_dense(s.grad, s.moved, s.dense.at[upper], padded)
    next_there = halo(4, s.dense.at[upper], s.next_upper, below)
    reducer.advance(9)
    project_backward(s, reducer)
    spread_there = move(s.in_spread, s.spread)
    reducer.settle(1)
    reducer.advance(10)

    swaps_there[1]()
    move_own(s.grad, s.swap_back, s.work, windows, -1)
    spread_there()
    small_gradients(s, s.small_own.at[1])
    refill(5)
    spread_gains(s, 0)
    reducer.advance(11)
    next_there()
    from_dense(s.next_upper, s.page, 0)
    s.grad[...] = s.work[...]
    add_halo(s.page, s.plain, s.grad, half, padded)
    reducer.advance(12)
    needed(0)

    def wait_next(point):
        needed(point + 1)

    backward(0, s.live, wait_next, range(13, 26))
    project_backward(s, reducer)
    reducer.settle(1)
    reducer.advance(26)
    input_backward(s)
    spread_there = move(s.in_spread, s.spread)
    reducer.advance(27)
    needed(4)
    norm_one_backward(s, windows)
    out_kept()
    to_dense(s.grad, s.plain, s.dense, s.plain.shape[0])
    grad_kept = move(s.dense, s.grad_tokens)
    reducer.advance(28)
    spread_there()
    small_gradients(s, s.small_own.at[0])
    reducer.advance(29)
    finish_small(s, plan, row)
    grad_kept()


def finish_small(s, plan, row):
    total = s.small_parts.at[plan.halvings - 1]
    outs = (
        (s.d_ln_gain, (G1, G2)),
        (s.d_ln_bias, (B1, B2)),
        (s.d_qv_bias, (QB, VB)),
        (s.d_proj_bias, (PB,)),
        (s.d_fc1_bias, tuple(range(F1B, F1B + FEEDS))),
        (s.d_fc2_bias, (F2B,)),
    )
    for layer in range(2):
        s.d_table[layer] = total[layer, VECTOR_ROWS:, :OFFSETS]
        for ref, indices in outs:
            whole = jnp.concatenate([total[layer, index : index + 1, :] for index in indices], axis=1)
            size = ref.shape[1]
            mine = jnp.zeros((1, size), F32)
            for share in range(plan.shares):
                mine = jnp.where(row == share, whole[:, share * size : (share + 1) * size], mine)
            ref[layer : layer + 1, :] = mine


def placements(cols):
    windows = cols // WIN
    patches = WIN * cols
    padded = -(-patches // LANES) * LANES
    plain = np.zeros((padded, windows * LANES), np.float32)
    moved = np.zeros((padded, windows * LANES), np.float32)
    for line in range(WIN):
        for col in range(cols):
            source = line * cols + col
            plain[source, (col // WIN) * LANES + line * WIN + col % WIN] = 1
            new_line, new_col = (line - SHIFT) % WIN, (col - SHIFT) % cols
            moved[source, (new_col // WIN) * LANES + new_line * WIN + new_col % WIN] = 1
    return plain.astype(BF), moved.astype(BF)


def swaps():
    on = np.zeros((2 * LANES, LANES), np.float32)
    back = np.zeros((2 * LANES, LANES), np.float32)
    for line in range(SHIFT):
        for col in range(WIN):
            moved, plain = line * WIN + col, (line + SHIFT) * WIN + (col + SHIFT) % WIN
            on[plain + (LANES if col >= SHIFT else 0), moved] = 1
            back[moved + (LANES if col < SHIFT else 0), plain] = 1
    return on.astype(BF), back.astype(BF)


def table_spread():
    size = 2 * WIN - 1
    spread = np.zeros((WIN, 2 * LANES, TABLE), np.float32)
    for key_col in range(WIN):
        for offset in range(size):
            for col in range(WIN):
                spread[key_col, offset * WIN + col, offset * size + col - key_col + WIN - 1] = 1
    spread = spread.reshape(WIN // 2, 2, 2 * LANES, TABLE).swapaxes(1, 2)
    return spread.reshape(WIN * LANES, 2 * TABLE).astype(BF)


def copy_all(*refs):
    *refs, sems = refs
    count = len(refs) // 3
    sources, targets, held = refs[:count], refs[count : 2 * count], refs[2 * count :]
    ways = [*zip(sources, held), *zip(held, targets)]
    copies = [pltpu.make_async_copy(*way, sems.at[number]) for number, way in enumerate(ways)]
    for copy in copies[:count]:
        copy.start()
    for incoming, outgoing in zip(copies[:count], copies[count:]):
        incoming.wait()
        outgoing.start()
    for copy in copies[count:]:
        copy.wait()


def hand_out(values):
    anywhere = pl.BlockSpec(memory_space=pl.ANY)
    return pl.pallas_call(
        copy_all,
        out_shape=[jax.ShapeDtypeStruct(value.shape, value.dtype) for value in values],
        in_specs=[anywhere] * len(values),
        out_specs=[anywhere] * len(values),
        scratch_shapes=[pltpu.VMEM(value.shape, value.dtype) for value in values]
        + [pltpu.SemaphoreType.DMA((2 * len(values),))],
        compiler_params=pltpu.CompilerParams(vmem_limit_bytes=VMEM_LIMIT),
        name="results",
    )(*values)


def per_device(
    page_tokens,
    blank_mask,
    cotangent,
    ln_gain,
    ln_bias,
    qv_bias,
    rel_table,
    w_qkv,
    w_proj,
    proj_bias,
    w_fc1,
    fc1_bias,
    w_fc2,
    fc2_bias,
):
    pages, shares = lax.axis_size(PAGE), lax.axis_size(ROW)
    plan = Plan(pages, shares)
    cols = page_tokens.shape[2]
    windows, lanes = cols // WIN, cols // WIN * LANES
    dense = ((WIN * cols * SPLITS, LANES), F32)
    half_dense = ((WIN * cols * SPLITS // 2, LANES), F32)
    plain, moved = (jnp.asarray(place) for place in placements(cols))
    live_rows = 8 * -(-windows // 8)
    scalar_inputs = dict(blank=blank_mask[0])
    small_inputs = dict(
        table=rel_table,
        ln_gain=ln_gain,
        ln_bias=ln_bias,
        qv_bias=qv_bias,
        proj_bias=proj_bias,
        fc1_bias=fc1_bias,
        fc2_bias=fc2_bias,
    )
    large_inputs = dict(
        in_tokens=page_tokens[0],
        in_grad=cotangent.reshape(dense[0]),
        in_plain=plain,
        in_moved=moved,
        in_swap_on=jnp.asarray(swaps()[0]),
        in_swap_back=jnp.asarray(swaps()[1]),
        in_spread=jnp.asarray(table_spread()),
        in_qkv=w_qkv,
        in_proj=w_proj,
        in_fc1=w_fc1,
        in_fc2=w_fc2,
    )
    saved = dict(
        x=((D, lanes), F32),
        normed=((D, lanes), BF),
        qkv=((3 * D, lanes), BF),
        soft=((windows * HEADS, LANES, LANES), BF),
        merged=((D, lanes), BF),
        hidden=((D, lanes), F32),
        second=((D, lanes), BF),
        active=((FF, lanes), BF),
        slope=((FF, lanes), BF),
    )
    units = ((UNITS,) + plan.sizes[0][0], F32)
    large_outputs = dict(
        out_tokens=dense,
        grad_tokens=dense,
        sum_qkv=((2, D // shares, 3 * D), F32),
        sum_proj=((2, D // shares, D), F32),
        sum_fc1=((2, D // shares, FF), F32),
        sum_fc2=((2, FF // shares, D), F32),
        units_zero=units,
        units_one=units,
        kept_x=((D, lanes), F32),
        kept_normed=((D, lanes), BF),
        kept_qkv=((3 * D, lanes), BF),
        kept_soft=((windows * HEADS, LANES, LANES), BF),
        kept_merged=((D, lanes), BF),
        kept_hidden=((D, lanes), F32),
        kept_second=((D, lanes), BF),
        kept_active=((FF, lanes), BF),
        kept_slope=((FF, lanes), BF),
    )
    small_outputs = dict(
        d_ln_gain=((2, 2 * D // shares), F32),
        d_ln_bias=((2, 2 * D // shares), F32),
        d_qv_bias=((2, 2 * D // shares), F32),
        d_proj_bias=((2, D // shares), F32),
        d_fc1_bias=((2, FF // shares), F32),
        d_fc2_bias=((2, D // shares), F32),
        d_table=((2, HEADS, OFFSETS), F32),
    )
    small = (2, SMALL, D)
    vmem = dict(
        saved,
        tokens=((WIN, cols, D), BF),
        plain=(plain.shape, BF),
        moved=(moved.shape, BF),
        w_qkv=((D, 3 * D), BF),
        w_proj=((D, D), BF),
        w_fc1=((D, FF), BF),
        w_fc2=((FF, D), BF),
        dense=dense,
        upper=half_dense,
        swap_on=((2 * LANES, LANES), BF),
        swap_back=((2 * LANES, LANES), BF),
        grad_upper=half_dense,
        next_upper=half_dense,
        live_upper=((live_rows, LANES), F32),
        live_two=((live_rows, LANES), F32),
        work=((D, lanes), F32),
        grad=((D, lanes), F32),
        low=((D, lanes), BF),
        sums=((VECTORS, D, LANES), F32),
        gains=((2, D, LANES), F32),
        bias=((HEADS, LANES, LANES), F32),
        bias_rows=((HEADS * LANES, LANES), F32),
        regions=((2, LANES, LANES), F32),
        padded_table=((HEADS, TABLE), F32),
        live=((live_rows, LANES), F32),
        vector_rows=((VECTOR_ROWS, D), F32),
        staged=((2 * CHUNK, CHUNK), F32),
        done=((DONE * CLASSES, CHUNK // shares, CHUNK), F32),
        held=((HELD * CLASSES,) + plan.sizes[0][0], F32),
        first_landing=((RING * CLASSES,) + plan.sizes[0][0], F32),
        small_own=(small, F32),
        small_parts=((plan.halvings,) + small, F32),
    )
    semaphores = dict(
        move_sems=pltpu.SemaphoreType.DMA((48,)),
        halo_sems=pltpu.SemaphoreType.DMA((2, 5)),
        send_sems=pltpu.SemaphoreType.DMA((2 * UNITS, plan.phases)),
        recv_sems=pltpu.SemaphoreType.DMA((2 * UNITS, plan.phases)),
        own_sems=pltpu.SemaphoreType.DMA((2 * UNITS, 2)),
        stage_sems=pltpu.SemaphoreType.DMA((2, shares, 2)),
        first_sems=pltpu.SemaphoreType.DMA((2 * UNITS, shares)),
        first_free=pltpu.SemaphoreType.REGULAR((2 * UNITS,)),
        small_sems=pltpu.SemaphoreType.DMA((2, plan.halvings)),
        free_sems=pltpu.SemaphoreType.REGULAR((CLASSES, plan.halvings)),
    )
    landing = [((RING,) + size, F32) for sizes in plan.sizes for size in sizes[1:]]
    layout = [*scalar_inputs, *small_inputs, *large_inputs, *small_outputs, *large_outputs, *vmem, *semaphores]
    in_vmem, anywhere = pl.BlockSpec(memory_space=pltpu.VMEM), pl.BlockSpec(memory_space=pl.ANY)
    outputs = {**small_outputs, **large_outputs}
    results = pl.pallas_call(
        functools.partial(run, plan, layout),
        out_shape=[jax.ShapeDtypeStruct(*shape) for shape in outputs.values()],
        in_specs=[pl.BlockSpec(memory_space=pltpu.SMEM)] + [in_vmem] * len(small_inputs) + [anywhere] * len(large_inputs),
        out_specs=[in_vmem] * len(small_outputs) + [anywhere] * len(large_outputs),
        scratch_shapes=[pltpu.VMEM(*shape) for shape in vmem.values()]
        + list(semaphores.values())
        + [pltpu.VMEM(*shape) for shape in landing],
        compiler_params=pltpu.CompilerParams(
            vmem_limit_bytes=VMEM_LIMIT, collective_id=0, has_side_effects=True
        ),
        name="two_layers",
    )(*scalar_inputs.values(), *small_inputs.values(), *large_inputs.values())
    results = hand_out(results[: len(small_outputs) + 6])
    d_ln_gain, d_ln_bias, d_qv_bias, d_proj_bias, d_fc1_bias, d_fc2_bias, d_table = results[: len(small_outputs)]
    out_tokens, grad_tokens, sum_qkv, sum_proj, sum_fc1, sum_fc2 = results[len(small_outputs) :]
    return (
        out_tokens.reshape(cotangent.shape),
        grad_tokens.reshape(cotangent.shape),
        d_ln_gain,
        d_ln_bias,
        d_qv_bias,
        d_table,
        sum_qkv,
        sum_proj,
        d_proj_bias,
        sum_fc1,
        d_fc1_bias,
        sum_fc2,
        d_fc2_bias,
    )


def solution(mesh):
    tokens, by_row, shares = P(PAGE, ROW, None, None), P(None, ROW), P(None, ROW, None)
    return jax.shard_map(
        per_device,
        mesh=mesh,
        in_specs=(tokens, P(PAGE, ROW, None), tokens) + (P(),) * 11,
        out_specs=(tokens, tokens)
        + (by_row, by_row, by_row, P(), shares, shares, by_row, shares, by_row, shares, by_row),
        check_vma=False,
    )
```

```python
import functools

import jax
import jax.numpy as jnp
import numpy as np
from jax import lax
from jax.experimental import pallas as pl
from jax.experimental.pallas import tpu as pltpu
from jax.sharding import PartitionSpec as P

WIN = 10
SHIFT = 5
AREA = WIN * WIN
LANES = 128
D = 512
HEADS = 16
HEAD_DIM = 32
FF = 2048
CHUNK = 512
FEEDS = FF // CHUNK
SPLITS = D // LANES
EPSILON = 1e-05
MASK_VALUE = -100.0
NEVER = -1e30
SCORE_SCALE = HEAD_DIM ** (-0.5)
VMEM_LIMIT = 63 * 1024 * 1024 + 512 * 1024
BF = jnp.bfloat16
F32 = jnp.float32
MESH = pl.DeviceIdType.MESH
PAGE, ROW = "page", "row"

G1, B1, G2, B2, QB, VB, PB, F2B, F1B, VECTORS = 0, 1, 2, 3, 4, 5, 6, 7, 8, 12
VECTOR_ROWS = 16
SMALL = VECTOR_ROWS + HEADS
OFFSETS = (2 * WIN - 1) ** 2
TABLE = 384

UNIT_FC1, UNIT_FC2, UNIT_PROJ, UNIT_QKV, UNITS = 0, 4, 8, 9, 12
CLASSES = 3
GROUPS = UNITS // CLASSES
TRIPLES = 2 * GROUPS
HELD = 4
DONE = 5
RING = 3
QKV, PROJ, FC1, FC2 = range(4)
TARGETS = (
    ((FC1, 0, 0), (FC1, 0, 1), (FC1, 0, 2)),
    ((FC1, 0, 3), (FC2, 0, 0), (FC2, 1, 0)),
    ((FC2, 2, 0), (FC2, 3, 0), (PROJ, 0, 0)),
    ((QKV, 0, 0), (QKV, 0, 1), (QKV, 0, 2)),
)


def mm(left, right, left_dim, right_dim):
    return lax.dot_general(
        left, right, (((left_dim,), (right_dim,)), ((), ())), preferred_element_type=F32
    )


def split(values):
    high = values.astype(BF)
    return high, (values - high.astype(F32)).astype(BF)


def lane_tile(index):
    return pl.ds(pl.multiple_of(index * LANES, LANES), LANES)


def chunk_of(index):
    return pl.ds(pl.multiple_of(index * CHUNK, CHUNK), CHUNK)


def wide(column, count):
    return jnp.concatenate([column] * count, axis=1)


def fold(values):
    total = values[:, :LANES]
    for start in range(LANES, values.shape[1], LANES):
        total = total + values[:, start : start + LANES]
    return total


def norm_parts(values):
    center = values - jnp.sum(values, axis=0, keepdims=True) * (1.0 / D)
    spread = jnp.sum(center * center, axis=0, keepdims=True) * (1.0 / D)
    scale = lax.rsqrt(spread + EPSILON)
    return center * scale, scale


def norm_pull(grad, gain, hat, scale):
    scaled = grad * gain
    mean_one = jnp.sum(scaled, axis=0, keepdims=True) * (1.0 / D)
    mean_two = jnp.sum(scaled * hat, axis=0, keepdims=True) * (1.0 / D)
    return scale * (scaled - mean_one - hat * mean_two)


def gelu_parts(inner):
    step = 1.0 / (1.0 + (0.3275911 * 0.7071067811865476) * jnp.abs(inner))
    bell = jnp.exp(inner * inner * -0.5)
    poly = 0.5 * 1.061405429
    for factor in (-1.453152027, 1.421413741, -0.284496736, 0.254829592):
        poly = poly * step + 0.5 * factor
    tail = poly * step * bell
    below = jnp.where(inner >= 0, 1.0 - tail, tail)
    return inner * below, below + inner * bell * 0.3989422804014327


def to_channels(page_ref, place_ref, out_ref, exact=False):
    def step(index, carry):
        channels = pl.ds(pl.multiple_of(index * 256, 256), 256)
        values = page_ref[:, channels]
        if exact:
            out_ref[channels, :] = mm(values.astype(BF), place_ref[...], 0, 0)
        else:
            high, low = split(values)
            out_ref[channels, :] = mm(high, place_ref[...], 0, 0) + mm(low, place_ref[...], 0, 0)
        return carry

    lax.fori_loop(0, D // 256, step, 0, unroll=2)


def to_dense(values_ref, place_ref, dense_ref, padded):
    count = dense_ref.shape[0] // SPLITS
    for index in range(D // 256):
        high, low = split(values_ref[index * 256 : (index + 1) * 256, :])
        page = mm(place_ref[:padded, :], high, 1, 1) + mm(place_ref[:padded, :], low, 1, 1)
        for part in range(2):
            rows = pl.ds(2 * index + part, count, stride=SPLITS)
            dense_ref[rows, :] = page[:count, part * LANES : (part + 1) * LANES]


def from_dense(dense_ref, page_ref, row):
    count = dense_ref.shape[0] // SPLITS
    for part in range(SPLITS):
        rows = pl.ds(part, count, stride=SPLITS)
        page_ref[pl.ds(row, count), part * LANES : (part + 1) * LANES] = dense_ref[rows, :]


def add_halo(page_ref, place_ref, out_ref, count, padded):
    page_ref[pl.ds(count, padded - count), :] = jnp.zeros((padded - count, D), F32)

    def step(index, carry):
        channels = pl.ds(pl.multiple_of(index * 256, 256), 256)
        high, low = split(page_ref[:padded, channels])
        out_ref[channels, :] += mm(high, place_ref[:padded, :], 0, 0) + mm(low, place_ref[:padded, :], 0, 0)
        return carry

    lax.fori_loop(0, D // 256, step, 0, unroll=2)


def move_own(values_ref, swap_ref, out_ref, windows, first):
    for window in range(windows):
        sources = [(window + first + part) % windows * LANES for part in range(2)]
        values = jnp.concatenate([values_ref[:, start : start + LANES] for start in sources], axis=1)
        high, low = split(values)
        target = slice(window * LANES, (window + 1) * LANES)
        out_ref[:, target] = mm(high, swap_ref[...], 1, 0) + mm(low, swap_ref[...], 1, 0)


def vector_rows(s, layer):
    rows = s.vector_rows
    sources = ((G1, s.ln_gain, 0), (B1, s.ln_bias, 0), (G2, s.ln_gain, 1), (B2, s.ln_bias, 1))
    sources += ((QB, s.qv_bias, 0), (VB, s.qv_bias, 1), (PB, s.proj_bias, 0), (F2B, s.fc2_bias, 0))
    sources += tuple((F1B + part, s.fc1_bias, part) for part in range(FEEDS))
    for index, source, part in sources:
        rows[index : index + 1, :] = source[layer : layer + 1, part * D : (part + 1) * D]
    rows[VECTORS:, :] = jnp.zeros((VECTOR_ROWS - VECTORS, D), F32)
    return rows[...].T


def spread_columns(s, layer):
    columns = vector_rows(s, layer)
    for index in range(VECTORS):
        s.sums[index] = jnp.broadcast_to(columns[:, index : index + 1], (D, LANES))


def spread_gains(s, layer):
    columns = vector_rows(s, layer)
    for index, vector in enumerate((G1, G2)):
        s.gains[index] = jnp.broadcast_to(columns[:, vector : vector + 1], (D, LANES))


def spread_part(col):
    rows, lanes = (col // 2) * 2 * LANES, (col % 2) * TABLE
    return slice(rows, rows + 2 * LANES), slice(lanes, lanes + TABLE)


def spread_bias(s, layer):
    spread_ref, rows_ref, bias_ref = s.spread, s.bias_rows, s.bias
    s.padded_table[...] = jnp.zeros(s.padded_table.shape, F32)
    s.padded_table[:, :OFFSETS] = s.table[layer]
    high, low = split(s.padded_table[...])
    parts = []
    for col in range(WIN):
        chosen = spread_ref[spread_part(col)]
        parts.append(mm(high, chosen, 1, 1) + mm(low, chosen, 1, 1))
    source = jnp.concatenate(parts, axis=0)
    rows_ref[...] = jnp.zeros(rows_ref.shape, F32)
    for row in range(WIN):
        shift = (WIN - 1 - row) * WIN
        moved = source if shift == 0 else pltpu.roll(source, 2 * LANES - shift, axis=1)
        rows_ref[pl.ds(row * WIN * HEADS, WIN * HEADS), :] = moved[:, :LANES]
    for head in range(HEADS):
        bias_ref[head] = rows_ref[pl.ds(head, LANES, stride=HEADS), :]


def gather_bias(grad_ref, spread_ref, rows_ref):
    for head in range(HEADS):
        rows_ref[pl.ds(head, LANES, stride=HEADS), :] = grad_ref[head]
    total = jnp.zeros((WIN * HEADS, 2 * LANES), F32)
    for row in range(WIN):
        shift = (WIN - 1 - row) * WIN
        piece = rows_ref[pl.ds(row * WIN * HEADS, WIN * HEADS), :]
        piece = jnp.concatenate([piece, jnp.zeros_like(piece)], axis=1)
        total = total + (piece if shift == 0 else pltpu.roll(piece, shift, axis=1))
    table = jnp.zeros((HEADS, TABLE), F32)
    for col in range(WIN):
        for part in split(total[col * HEADS : (col + 1) * HEADS]):
            table = table + mm(part, spread_ref[spread_part(col)], 1, 0)
    return table


def region_masks(shifted_layer, out_ref):
    key = lax.broadcasted_iota(jnp.int32, (LANES, LANES), 0)
    query = lax.broadcasted_iota(jnp.int32, (LANES, LANES), 1)
    padding = jnp.where(key < AREA, 0.0, NEVER)
    out_ref[0] = padding
    out_ref[1] = padding
    if shifted_layer:
        last = lax.axis_index(ROW) == lax.axis_size(ROW) - 1
        rows_differ = ((key >= AREA // 2) != (query >= AREA // 2)) & last
        cols_differ = (key % WIN >= SHIFT) != (query % WIN >= SHIFT)
        out_ref[0] += jnp.where(rows_differ, MASK_VALUE, 0.0)
        out_ref[1] += jnp.where(rows_differ | cols_differ, MASK_VALUE, 0.0)


def shifted_live(s, windows):
    place = lax.broadcasted_iota(jnp.int32, (1, LANES), 1)
    for window in range(windows):
        here, after = slice(window, window + 1), slice((window + 1) % windows, (window + 1) % windows + 1)
        beyond = place % WIN >= SHIFT
        own = jnp.where(beyond, s.live[after, :], s.live[here, :])
        upper = jnp.where(beyond, s.live_upper[after, :], s.live_upper[here, :])
        s.live_two[here, :] = jnp.where(place >= AREA // 2, upper, own)


def head_rows(head, base=0):
    return pl.ds(base + head * HEAD_DIM, HEAD_DIM)


def norm_one_forward(s, windows):
    def step(index, carry):
        lanes = lane_tile(index)
        hat, _ = norm_parts(s.x[:, lanes])
        s.normed[:, lanes] = (hat * s.sums[G1] + s.sums[B1]).astype(BF)
        return carry

    lax.fori_loop(0, windows, step, 0, unroll=3)


def project_forward(s, windows):
    def step(index, carry):
        rows = chunk_of(index)
        bias = s.sums[jnp.where(index == 0, QB, VB)] * jnp.where(index == 1, 0.0, 1.0)
        out = mm(s.w_qkv[:, rows], s.normed[...], 0, 0)
        s.qkv[rows, :] = (out + wide(bias, windows)).astype(BF)
        return carry

    lax.fori_loop(0, 3, step, 0)


def attend_forward(s, windows, live_ref):
    def step(index, carry):
        lanes = lane_tile(index)
        live = jnp.broadcast_to(live_ref[pl.ds(index, 1), :], (LANES, LANES)).T
        masked = s.regions[jnp.where(index == windows - 1, 1, 0)] + MASK_VALUE * (1.0 - live)
        for head in range(HEADS):
            query = s.qkv[head_rows(head), lanes]
            key = s.qkv[head_rows(head, D), lanes]
            value = s.qkv[head_rows(head, 2 * D), lanes]
            scores = mm(key, query, 0, 0) * SCORE_SCALE + (s.bias[head] + masked)
            exponent = jnp.exp(scores - jnp.max(scores, axis=0, keepdims=True))
            total = jnp.sum(exponent, axis=0, keepdims=True)
            soft = (exponent * (1.0 / total)).astype(BF)
            s.soft[index * HEADS + head] = soft
            s.merged[head_rows(head), lanes] = mm(value, soft, 1, 0).astype(BF)
        return carry

    lax.fori_loop(0, windows, step, 0, unroll=2)


def norm_two_forward(s, windows, live_ref):
    def step(index, carry):
        lanes = lane_tile(index)
        hidden = s.x[:, lanes] + live_ref[pl.ds(index, 1), :] * (s.work[:, lanes] + s.sums[PB])
        s.hidden[:, lanes] = hidden
        s.work[:, lanes] = hidden + s.sums[F2B]
        hat, _ = norm_parts(hidden)
        s.second[:, lanes] = (hat * s.sums[G2] + s.sums[B2]).astype(BF)
        return carry

    lax.fori_loop(0, windows, step, 0, unroll=3)


def feed_forward(s, windows):
    def step(index, carry):
        rows = chunk_of(index)
        inner = mm(s.w_fc1[:, rows], s.second[...], 0, 0) + wide(s.sums[F1B + index], windows)
        active, slope = gelu_parts(inner)
        active = active.astype(BF)
        s.active[rows, :] = active
        s.slope[rows, :] = slope.astype(BF)
        s.work[...] += mm(s.w_fc2[rows, :], active, 0, 0)
        return carry

    lax.fori_loop(0, FEEDS, step, 0)


def feed_backward(s, sink, times):
    s.sums[...] = jnp.zeros(s.sums.shape, F32)
    s.bias[...] = jnp.zeros(s.bias.shape, F32)
    lowered = s.grad[...].astype(BF)
    s.low[...] = lowered
    s.sums[F2B] = fold(lowered.astype(F32))
    s.work[...] = jnp.zeros(s.work.shape, F32)

    claims = sink.layer == 0
    if claims:
        for unit in range(UNIT_FC2, UNIT_FC2 + FEEDS):
            sink.claim(unit)

    def step(index, carry):
        rows = chunk_of(index)
        if claims:
            sink.claim(UNIT_FC1 + index)
        sink.put(0, mm(s.active[rows, :], s.low[...], 1, 1), feed_pieces(index, sink.shares), index == 0)
        grad_inner = mm(s.w_fc2[rows, :], s.low[...], 1, 0) * s.slope[rows, :].astype(F32)
        grad_inner = grad_inner.astype(BF)
        s.sums[F1B + index] = fold(grad_inner.astype(F32))
        sink.put(1, mm(s.second[...], grad_inner, 1, 1), row_pieces(UNIT_FC1 + index, sink.shares), index == 0)
        s.work[...] += mm(s.w_fc1[:, rows], grad_inner, 1, 0)
        sink.advance_at(index, times)
        return carry

    lax.fori_loop(0, FEEDS, step, 0)
    sink.settle(0)
    sink.settle(1)


def norm_two_backward(s, windows, live_ref):
    def step(index, carry):
        lanes = lane_tile(index)
        hat, scale = norm_parts(s.hidden[:, lanes])
        grad = s.work[:, lanes]
        s.sums[G2] += grad * hat
        s.sums[B2] += grad
        grad = s.grad[:, lanes] + norm_pull(grad, s.gains[1], hat, scale)
        s.grad[:, lanes] = grad
        grad_low = (grad * live_ref[pl.ds(index, 1), :]).astype(BF)
        s.low[:, lanes] = grad_low
        s.sums[PB] += grad_low.astype(F32)
        return carry

    lax.fori_loop(0, windows, step, 0, unroll=3)


def merge_backward(s, sink):
    if sink.layer == 0:
        sink.claim(UNIT_PROJ)
    sink.put(0, mm(s.merged[...], s.low[...], 1, 1), row_pieces(UNIT_PROJ, sink.shares), True)
    s.merged[...] = mm(s.w_proj[...], s.low[...], 1, 0).astype(BF)
    sink.settle(0)


def attend_backward(s, windows, sink, times):
    def step(index, carry):
        lanes = lane_tile(index)
        for head in range(HEADS):
            query = s.qkv[head_rows(head), lanes]
            key = s.qkv[head_rows(head, D), lanes]
            value = s.qkv[head_rows(head, 2 * D), lanes]
            grad_out = s.merged[head_rows(head), lanes]
            soft_low = s.soft[index * HEADS + head]
            soft = soft_low.astype(F32)
            grad_soft = mm(value, grad_out, 0, 0)
            inner = jnp.sum(soft * grad_soft, axis=0, keepdims=True)
            grad_scores = (soft * (grad_soft - inner)).astype(BF)
            s.bias[head] += grad_scores.astype(F32)
            grad_query = (mm(key, grad_scores, 1, 0) * SCORE_SCALE).astype(BF)
            grad_key = (mm(query, grad_scores, 1, 1) * SCORE_SCALE).astype(BF)
            grad_value = mm(grad_out, soft_low, 1, 1).astype(BF)
            s.qkv[head_rows(head), lanes] = grad_query
            s.qkv[head_rows(head, D), lanes] = grad_key
            s.qkv[head_rows(head, 2 * D), lanes] = grad_value
            s.sums[QB, head_rows(head), :] += grad_query.astype(F32)
            s.sums[VB, head_rows(head), :] += grad_value.astype(F32)
        sink.advance_at(index, times)
        return carry

    lax.fori_loop(0, windows, step, 0)


def project_backward(s, sink):
    def step(index, carry):
        rows = chunk_of(index)
        sink.claim(UNIT_QKV + index)
        sink.put(1, mm(s.normed[...], s.qkv[rows, :], 1, 1), row_pieces(UNIT_QKV + index, sink.shares), index == 0)
        return carry

    lax.fori_loop(0, 3, step, 0)


def input_backward(s):
    s.work[...] = mm(s.w_qkv[...], s.qkv[...], 1, 0)


def norm_one_backward(s, windows):
    def step(index, carry):
        lanes = lane_tile(index)
        hat, scale = norm_parts(s.x[:, lanes])
        grad = s.work[:, lanes]
        s.sums[G1] += grad * hat
        s.sums[B1] += grad
        s.grad[:, lanes] += norm_pull(grad, s.gains[0], hat, scale)
        return carry

    lax.fori_loop(0, windows, step, 0, unroll=3)


def small_gradients(s, small_ref):
    places = lax.broadcasted_iota(jnp.int32, (D, LANES), 1)
    packed = jnp.zeros((D, LANES), F32)
    for index in range(VECTORS):
        packed = jnp.where(places == index, jnp.sum(s.sums[index], axis=1, keepdims=True), packed)
    small_ref[:VECTOR_ROWS, :] = packed.T[:VECTOR_ROWS]
    table = gather_bias(s.bias, s.spread, s.bias_rows)
    small_ref[VECTOR_ROWS:, :] = jnp.concatenate([table, jnp.zeros((HEADS, D - TABLE), F32)], axis=1)


def reversed_bits(value, count):
    turned = 0
    for bit in range(count):
        turned = turned * 2 + (value // 2**bit) % 2
    return turned


def row_pieces(unit, shares):
    rows, count = CHUNK // shares, shares.bit_length() - 1
    return [(share * rows, unit, reversed_bits(share, count)) for share in range(shares)]


def feed_pieces(index, shares):
    rows, count = CHUNK // shares, shares.bit_length() - 1
    pieces = []
    for share in range(shares // FEEDS):
        place = reversed_bits(index * (shares // FEEDS) + share, count)
        for part in range(FEEDS):
            pieces.append(((share * FEEDS + part) * rows, UNIT_FC2 + part, place))
    return pieces


class Plan:
    def __init__(self, pages, shares):
        self.shares, self.rows = shares, CHUNK // shares
        page_bits, row_bits = pages.bit_length() - 1, shares.bit_length() - 1
        others = page_bits - 1
        self.steps = []
        for kind in range(CLASSES):
            turn = kind % 2
            page = [(PAGE, 2 ** (1 + (bit + turn) % others)) for bit in range(others)]
            row = [(ROW, 2**bit) for bit in range(row_bits)]
            self.steps.append([(PAGE, 1)] + (row + page if kind == 2 else page + row))
        self.page_steps = [[0] + [at for at, step in enumerate(steps) if at and step[0] == PAGE] for steps in self.steps]
        self.halvings = page_bits + row_bits
        self.phases = self.halvings + page_bits
        self.sizes, self.axes = [], []
        for steps in self.steps:
            size, sizes, axes = [shares, self.rows, CHUNK], [], []
            for axis, _ in steps:
                axes.append(0 if axis == ROW else 1 if size[1] >= 16 else 2)
                size[axes[-1]] //= 2
                sizes.append(tuple(size))
            self.sizes.append(sizes)
            self.axes.append(axes)
        self.steps_at = self.schedule()

    def schedule(self):
        small = TRIPLES
        free, ready, stage_of, plan, now = {}, {}, {}, [], 0.0
        for triple in range(TRIPLES):
            for kind in range(CLASSES):
                stage_of[triple, kind] = 0
        stage_of[small, 0] = 0

        def link(key, phase):
            triple, kind = key
            if phase < self.halvings:
                axis, stride = self.steps[kind][phase]
                size = 2.0**-phase / 2 if triple != small else 0.125
            else:
                axis, stride = self.steps[kind][self.page_steps[kind][self.phases - 1 - phase]]
                size = 2.0 ** (phase - 2 * self.halvings)
            if axis == PAGE and stride == 1:
                return 0, size * PLAN_CORE
            return (axis, stride if axis == PAGE else 0), size * PLAN_LINK * (1.0 if stride == 1 or axis == PAGE else 1.5)

        def last_stage(key):
            return self.halvings if key[0] == small else self.phases + 1

        def allowed(key, point):
            triple, kind = key
            stage = stage_of[key]
            if stage > last_stage(key):
                return False
            if triple == small:
                return point >= len(PLAN_POINTS) - 1
            if stage == 0 and point < PLAN_THERE[triple]:
                return False
            if triple > 0 and stage_of[triple - 1, kind] <= stage:
                return False
            if triple >= RING and stage < self.halvings and stage_of[triple - RING, kind] <= stage + 1:
                return False
            if stage == 0 and triple >= DONE and stage_of[triple - DONE, kind] <= self.phases + 1:
                return False
            return not (stage == 0 and triple >= HELD and stage_of[triple - HELD, kind] <= self.halvings + 1)

        for point, work in enumerate(PLAN_POINTS):
            now += work
            if point == PLAN_HALO:
                free[ROW, 0] = max(now, free.get((ROW, 0), 0.0)) + PLAN_HALO_TIME
            steps, final = [], point == len(PLAN_POINTS) - 1
            while True:
                keys = [key for key in stage_of if allowed(key, point)]
                needed = PLAN_FORCE.get(point, -1)
                keys = [
                    key
                    for key in keys
                    if final or ready.get(key, 0.0) <= now + PLAN_SLACK or (key[0] <= needed and stage_of[key] <= 1)
                ]
                if not keys:
                    break
                key = min(keys, key=lambda key: (max(ready.get(key, 0.0), now), -stage_of[key], key))
                stage = stage_of[key]
                now = max(now, ready.get(key, 0.0)) + (PLAN_ADD * 2.0**-stage if stage else 0.0)
                if stage == self.phases:
                    ready[key] = now + PLAN_LATENCY
                elif stage < last_stage(key):
                    name, length = link(key, stage)
                    free[name] = max(now, free.get(name, 0.0)) + length
                    ready[key] = free[name] + PLAN_LATENCY
                steps.append((*key, stage))
                stage_of[key] += 1
            plan.append(steps)
        assert all(stage_of[key] > last_stage(key) for key in stage_of)
        return plan

    def partner(self, kind, level):
        axis, stride = self.steps[kind][level]
        page, row = lax.axis_index(PAGE), lax.axis_index(ROW)
        mine = page if axis == PAGE else row
        bit = (mine // stride) % 2
        other = mine + (1 - 2 * bit) * stride
        return bit, ((other, row) if axis == PAGE else (page, other))

    def part(self, kind, level, sent=False):
        starts, sizes = [0, 0, 0], list(self.sizes[kind][0])
        for at in range(1, level + 1):
            axis = self.axes[kind][at]
            sizes[axis] //= 2
            bit, _ = self.partner(kind, at)
            which = 1 - bit if sent and at == level else bit
            starts[axis] = starts[axis] + which * sizes[axis]
        return (
            pl.ds(starts[0], sizes[0]),
            pl.ds(pl.multiple_of(starts[1], 8), sizes[1]),
            pl.ds(pl.multiple_of(starts[2], LANES), sizes[2]),
        )

    def place(self, kind, count):
        starts, sizes = [0, 0], [self.rows, CHUNK]
        for at in self.page_steps[kind][:count]:
            axis = self.axes[kind][at] - 1
            sizes[axis] //= 2
            bit, _ = self.partner(kind, at)
            starts[axis] = starts[axis] + bit * sizes[axis]
        return starts, sizes


class Reducer:
    def __init__(self, plan, s):
        self.plan, self.s = plan, s
        self.shares = plan.shares
        self.layer = 1

    def stage_copies(self, slot, pieces):
        s, plan = self.s, self.plan
        bit, device = plan.partner(0, 0)
        rows = plan.rows // 2
        copies = []
        for number, (start, unit, place) in enumerate(pieces):
            start = slot * CHUNK + start
            number_sems = s.stage_sems.at[slot, number]
            overall = self.first_unit() + unit
            sent = pltpu.make_async_remote_copy(
                src_ref=s.staged.at[pl.ds(pl.multiple_of(start + (1 - bit) * rows, 8), rows)],
                dst_ref=s.first_landing.at[overall % (RING * CLASSES), place],
                send_sem=number_sems.at[0],
                recv_sem=s.first_sems.at[overall, place],
                device_id=device,
                device_id_type=MESH,
            )
            kept = pltpu.make_async_copy(
                s.staged.at[pl.ds(pl.multiple_of(start + bit * rows, 8), rows)],
                s.units[self.layer].at[unit, place],
                number_sems.at[1],
            )
            copies.append((sent, kept))
        return copies

    def first_unit(self):
        return UNITS * (1 - self.layer)

    def claim(self, unit):
        pl.semaphore_wait(self.s.first_free.at[self.first_unit() + unit], 1)

    def put(self, slot, grad, pieces, first):
        if first is not True:

            @pl.when(jnp.logical_not(first))
            def _():
                self.settle(slot)

        self.s.staged[pl.ds(slot * CHUNK, CHUNK), :] = grad
        for sent, kept in self.stage_copies(slot, pieces):
            sent.start()
            kept.start()

    def settle(self, slot):
        for sent, kept in self.stage_copies(slot, row_pieces(0, self.shares)):
            sent.wait_send()
            kept.wait()

    def first_arrived(self, triple, kind):
        s, unit = self.s, CLASSES * triple + kind
        landed = s.first_landing.at[unit % (RING * CLASSES)]
        _, device = self.plan.partner(0, 0)
        for place in range(self.shares):
            pltpu.make_async_remote_copy(
                src_ref=landed.at[place],
                dst_ref=landed.at[place],
                send_sem=s.first_sems.at[unit, place],
                recv_sem=s.first_sems.at[unit, place],
                device_id=device,
                device_id_type=MESH,
            ).wait_recv()

    def remote(self, source, target, unit, phase, device):
        return pltpu.make_async_remote_copy(
            src_ref=source,
            dst_ref=target,
            send_sem=self.s.send_sems.at[unit, phase],
            recv_sem=self.s.recv_sems.at[unit, phase],
            device_id=device,
            device_id_type=MESH,
        )

    def held(self, triple, kind):
        return self.s.held.at[CLASSES * (triple % HELD) + kind]

    def landed(self, triple, kind, level):
        if level == 0:
            return self.s.first_landing.at[(CLASSES * triple + kind) % (RING * CLASSES)]
        return self.s.landing[kind][level - 1].at[triple % RING]

    def halving(self, triple, kind, level):
        _, device = self.plan.partner(kind, level)
        source = self.held(triple, kind).at[self.plan.part(kind, level, True)]
        return self.remote(source, self.landed(triple, kind, level), CLASSES * triple + kind, level, device)

    def own_half(self, triple, kind):
        source = self.s.units[1 - triple // GROUPS].at[CLASSES * (triple % GROUPS) + kind]
        sem = self.s.own_sems.at[CLASSES * triple + kind, 0]
        return pltpu.make_async_copy(source, self.held(triple, kind), sem)

    def finished(self, triple, kind):
        return self.held(triple, kind).at[self.plan.part(kind, self.plan.halvings - 1)].at[0]

    def done(self, triple, kind, count):
        starts, sizes = self.plan.place(kind, count)
        return self.s.done.at[
            CLASSES * (triple % DONE) + kind,
            pl.ds(pl.multiple_of(starts[0], 8), sizes[0]),
            pl.ds(pl.multiple_of(starts[1], LANES), sizes[1]),
        ]

    def gathering(self, triple, kind, phase):
        plan = self.plan
        count = len(plan.page_steps[kind]) - (phase - plan.halvings)
        part = self.done(triple, kind, count)
        _, device = plan.partner(kind, plan.page_steps[kind][count - 1])
        return self.remote(part, part, CLASSES * triple + kind, phase, device)

    def result(self, triple, kind):
        which, row_block, col_block = TARGETS[triple % GROUPS][kind]
        rows = self.plan.rows
        target = self.s.results[which].at[
            1 - triple // GROUPS, pl.ds(row_block * rows, rows), pl.ds(col_block * CHUNK, CHUNK)
        ]
        sem = self.s.own_sems.at[CLASSES * triple + kind, 1]
        return pltpu.make_async_copy(self.done(triple, kind, 0), target, sem)

    def start(self, triple, kind, phase):
        plan = self.plan
        if phase == 0:
            self.own_half(triple, kind).start()
        elif phase < plan.halvings:
            if triple >= RING:
                pl.semaphore_wait(self.s.free_sems.at[kind, phase], 1)
            self.halving(triple, kind, phase).start()
        elif phase < plan.phases:
            if phase == plan.halvings:
                self.done(triple, kind, len(plan.page_steps[kind]))[...] = self.finished(triple, kind)[...]
            self.gathering(triple, kind, phase).start()
        elif phase == plan.phases:
            self.result(triple, kind).start()

    def arrive(self, triple, kind, phase):
        plan = self.plan
        if phase == 0:
            self.first_arrived(triple, kind)
            self.own_half(triple, kind).wait()
        elif phase < plan.halvings:
            self.halving(triple, kind, phase).wait()
        elif phase < plan.phases:
            self.gathering(triple, kind, phase).wait()
        else:
            self.result(triple, kind).wait()

    def take_in(self, triple, kind, phase):
        plan, s = self.plan, self.s
        if phase >= plan.halvings:
            return
        landed = self.landed(triple, kind, phase)
        kept = self.held(triple, kind).at[plan.part(kind, phase)]
        for share in range(landed.shape[0]):
            kept[share] += landed[share]
        if triple < TRIPLES - RING:
            _, device = plan.partner(kind, phase)
            free = s.free_sems.at[kind, phase]
            if phase == 0:
                free = s.first_free.at[CLASSES * (triple + RING) + kind]
            pl.semaphore_signal(free, inc=1, device_id=device, device_id_type=MESH)

    def advance(self, point):
        steps = self.plan.steps_at[point]
        most = 1 if point == len(self.plan.steps_at) - 1 else 6
        groups = []
        for step in steps:
            if groups and len(groups[-1]) < most and all(step[:2] != other[:2] for other in groups[-1]):
                groups[-1].append(step)
            else:
                groups.append([step])
        for group in groups:
            if group[0][0] == TRIPLES:
                self.small_step(group[0][2] - 1)
                continue
            for act in (self.arrive, self.take_in):
                for triple, kind, stage in group:
                    if stage > 0:
                        act(triple, kind, stage - 1)
            for triple, kind, stage in group:
                self.start(triple, kind, stage)

    def advance_at(self, index, points):
        for number, point in enumerate(points):
            if self.plan.steps_at[point]:

                @pl.when(index == number)
                def _(point=point):
                    self.advance(point)

    def small_copy(self, phase):
        s = self.s
        _, device = self.plan.partner(0, phase)
        return pltpu.make_async_remote_copy(
            src_ref=s.small_own if phase == 0 else s.small_parts.at[phase - 1],
            dst_ref=s.small_parts.at[phase],
            send_sem=s.small_sems.at[0, phase],
            recv_sem=s.small_sems.at[1, phase],
            device_id=device,
            device_id_type=MESH,
        )

    def small_step(self, phase):
        s = self.s
        if phase >= 0:
            self.small_copy(phase).wait()
            s.small_parts[phase] += s.small_own[...] if phase == 0 else s.small_parts[phase - 1]
        if phase + 1 < self.plan.halvings:
            self.small_copy(phase + 1).start()


PLAN_POINTS = (0, 2, 3) + (2.7,) * 6 + (5.2, 3, 3, 6) + (3.2,) * 4 + (0.3, 2, 3) + (2.7,) * 6 + (3, 3, 3, 3)
PLAN_THERE = (0, 0, 2, 10, 17, 17, 19, 26)
PLAN_FORCE = {9: 0, 12: 3, 25: 4}
PLAN_HALO, PLAN_HALO_TIME = 9, 12.3
PLAN_CORE, PLAN_LINK, PLAN_LATENCY, PLAN_ADD, PLAN_SLACK = 1.7, 20.0, 2.0, 0.9, 0.0


class Moves:
    def __init__(self, sems):
        self.sems, self.used = sems, 0

    def __call__(self, source, target):
        number, self.used = self.used, self.used + 1
        make = functools.partial(pltpu.make_async_copy, source, target, self.sems.at[number])
        make().start()
        return lambda: make().wait()


class Refs:
    pass


def run(plan, layout, *refs):
    s = Refs()
    for name, ref in zip(layout, refs):
        setattr(s, name, ref)
    rest = list(refs[len(layout) :])
    s.landing = [[rest.pop(0) for _ in range(1, plan.halvings)] for _ in range(CLASSES)]
    s.results = (s.sum_qkv, s.sum_proj, s.sum_fc1, s.sum_fc2)
    s.units = (s.units_zero, s.units_one)
    s.page = s.staged.at[pl.ds(0, s.plain.shape[0])]
    s.spread = s.qkv.at[pl.ds(0, s.in_spread.shape[0])]
    windows = s.x.shape[1] // LANES
    patches = s.dense.shape[0] // SPLITS
    half, half_rows = patches // 2, s.dense.shape[0] // 2
    padded = 16 * -(-half // 16)
    upper, lower = pl.ds(0, half_rows), pl.ds(half_rows, half_rows)
    reducer = Reducer(plan, s)
    move = Moves(s.move_sems)
    page, row = lax.axis_index(PAGE), lax.axis_index(ROW)
    count = lax.axis_size(ROW)
    above, below = (page, (row + count - 1) % count), (page, (row + 1) % count)

    def halo(number, source, target, device):
        make = functools.partial(
            pltpu.make_async_remote_copy,
            src_ref=source,
            dst_ref=target,
            send_sem=s.halo_sems.at[0, number],
            recv_sem=s.halo_sems.at[1, number],
            device_id=device,
            device_id_type=MESH,
        )
        make().start()
        return lambda: make().wait()

    tokens_there = move(s.in_tokens, s.tokens)
    places_there = (move(s.in_plain, s.plain), move(s.in_moved, s.moved))
    swaps_there = (move(s.in_swap_on, s.swap_on), move(s.in_swap_back, s.swap_back))
    spread_there = move(s.in_spread, s.spread)
    weights = ((s.in_qkv, s.w_qkv), (s.in_proj, s.w_proj), (s.in_fc1, s.w_fc1), (s.in_fc2, s.w_fc2))

    def fetch_weight(which, layer):
        source, target = weights[which]
        return move(source.at[layer], target)

    there = [fetch_weight(which, 0) for which in range(4)]

    barrier = pltpu.get_barrier_semaphore()
    devices = [plan.partner(0, level)[1] for level in range(plan.halvings)] + [above, below]
    for device in devices:
        pl.semaphore_signal(barrier, inc=1, device_id=device, device_id_type=MESH)

    s.live[...] = jnp.zeros(s.live.shape, F32)
    for window in range(windows):
        s.live[window : window + 1, :] = jnp.full((1, LANES), 1.0 - s.blank[0, window].astype(F32))
    s.page[...] = jnp.zeros(s.page.shape, F32)
    tokens_there()
    cols = s.tokens.shape[1]
    for line in range(WIN):
        s.page[pl.ds(line * cols, cols), :] = s.tokens[line].astype(F32)
    places_there[0]()
    to_channels(s.page, s.plain, s.x, True)
    saves = [move(s.x, s.kept_x)]
    spread_columns(s, 0)
    spread_there()
    spread_bias(s, 0)
    region_masks(False, s.regions)
    pl.semaphore_wait(barrier, len(devices))
    live_there = halo(0, s.live, s.live_upper, above)
    grad_there = halo(1, s.in_grad.at[upper], s.grad_upper, above)
    grad_lower_there = move(s.in_grad.at[lower], s.dense.at[lower])
    norm_one_forward(s, windows)
    saves.append(move(s.normed, s.kept_normed))
    there[QKV]()
    project_forward(s, windows)
    qkv_saved = move(s.qkv, s.kept_qkv)
    there[QKV] = fetch_weight(QKV, 1)
    attend_forward(s, windows, s.live)
    saves.append(move(s.soft, s.kept_soft))
    saves.append(move(s.merged, s.kept_merged))
    there[PROJ]()
    s.work[...] = mm(s.w_proj[...], s.merged[...], 0, 0)
    there[PROJ] = fetch_weight(PROJ, 1)
    norm_two_forward(s, windows, s.live)
    saves.append(move(s.hidden, s.kept_hidden))
    saves.append(move(s.second, s.kept_second))
    there[FC1]()
    there[FC2]()
    feed_forward(s, windows)
    saves.append(move(s.active, s.kept_active))
    saves.append(move(s.slope, s.kept_slope))
    there[FC1] = fetch_weight(FC1, 1)
    there[FC2] = fetch_weight(FC2, 1)
    to_dense(s.work, s.plain, s.dense.at[upper], padded)
    upper_there = halo(2, s.dense.at[upper], s.upper, above)

    qkv_saved()
    spread_there = move(s.in_spread, s.spread)
    places_there[1]()
    swaps_there[0]()
    saves.pop(0)()
    move_own(s.work, s.swap_on, s.x, windows, 0)
    spread_columns(s, 1)
    spread_there()
    spread_bias(s, 1)
    region_masks(True, s.regions)
    live_there()
    shifted_live(s, windows)
    grad_there()
    grad_lower_there()
    from_dense(s.grad_upper, s.page, 0)
    from_dense(s.dense.at[lower], s.page, half)
    to_channels(s.page, s.moved, s.grad)
    for saved in saves:
        saved()
    upper_there()
    from_dense(s.upper, s.page, 0)
    add_halo(s.page, s.moved, s.x, half, padded)
    norm_one_forward(s, windows)
    there[QKV]()
    project_forward(s, windows)
    attend_forward(s, windows, s.live_two)
    there[PROJ]()
    s.work[...] = mm(s.w_proj[...], s.merged[...], 0, 0)
    norm_two_forward(s, windows, s.live_two)
    there[FC1]()
    there[FC2]()
    feed_forward(s, windows)
    to_dense(s.work, s.moved, s.dense, s.moved.shape[0])
    out_there = halo(3, s.dense.at[upper], s.out_tokens.at[upper], below)
    out_kept = move(s.dense.at[lower], s.out_tokens.at[lower])

    spread_gains(s, 1)

    def backward(layer, live_ref, fetch, points):
        reducer.layer = layer
        first = 0 if layer else FEEDS
        feed_backward(s, reducer, points[:first])
        reducer.advance(points[first])
        fetch(0)
        norm_two_backward(s, windows, live_ref)
        reducer.advance(points[first + 1])
        fetch(1)
        merge_backward(s, reducer)
        reducer.advance(points[first + 2])
        fetch(2)
        attend_backward(s, windows, reducer, points[first + 3 :])
        fetch(3)

    back = {}

    def refill(point):
        if point == 0:
            back[0] = [move(s.kept_active, s.active), move(s.kept_slope, s.slope), move(s.kept_second, s.second)]
            back[0] += [fetch_weight(FC1, 0), fetch_weight(FC2, 0)]
        elif point == 1:
            back[1] = [move(s.kept_hidden, s.hidden)]
        elif point == 2:
            back[2] = [fetch_weight(PROJ, 0)]
        elif point == 3:
            back[2] += [move(s.kept_merged, s.merged)]
            back[3] = [move(s.kept_soft, s.soft)]
        elif point == 4:
            back[4] = [move(s.kept_x, s.x)]
        else:
            back[3] += [move(s.kept_qkv, s.qkv), move(s.kept_normed, s.normed), fetch_weight(QKV, 0)]

    def needed(point):
        if point in back:
            for arrived in back.pop(point):
                arrived()

    backward(1, s.live_two, refill, range(9))
    input_backward(s)
    norm_one_backward(s, windows)
    refill(4)
    out_there()
    to_dense(s.grad, s.moved, s.dense.at[upper], padded)
    next_there = halo(4, s.dense.at[upper], s.next_upper, below)
    reducer.advance(9)
    project_backward(s, reducer)
    spread_there = move(s.in_spread, s.spread)
    reducer.settle(1)
    reducer.advance(10)

    swaps_there[1]()
    move_own(s.grad, s.swap_back, s.work, windows, -1)
    spread_there()
    small_gradients(s, s.small_own.at[1])
    refill(5)
    spread_gains(s, 0)
    reducer.advance(11)
    next_there()
    from_dense(s.next_upper, s.page, 0)
    s.grad[...] = s.work[...]
    add_halo(s.page, s.plain, s.grad, half, padded)
    reducer.advance(12)
    needed(0)

    def wait_next(point):
        needed(point + 1)

    backward(0, s.live, wait_next, range(13, 26))
    project_backward(s, reducer)
    reducer.settle(1)
    reducer.advance(26)
    input_backward(s)
    spread_there = move(s.in_spread, s.spread)
    reducer.advance(27)
    needed(4)
    norm_one_backward(s, windows)
    out_kept()
    to_dense(s.grad, s.plain, s.dense, s.plain.shape[0])
    grad_kept = move(s.dense, s.grad_tokens)
    reducer.advance(28)
    spread_there()
    small_gradients(s, s.small_own.at[0])
    reducer.advance(29)
    finish_small(s, plan, row)
    grad_kept()


def finish_small(s, plan, row):
    total = s.small_parts.at[plan.halvings - 1]
    outs = (
        (s.d_ln_gain, (G1, G2)),
        (s.d_ln_bias, (B1, B2)),
        (s.d_qv_bias, (QB, VB)),
        (s.d_proj_bias, (PB,)),
        (s.d_fc1_bias, tuple(range(F1B, F1B + FEEDS))),
        (s.d_fc2_bias, (F2B,)),
    )
    for layer in range(2):
        s.d_table[layer] = total[layer, VECTOR_ROWS:, :OFFSETS]
        for ref, indices in outs:
            whole = jnp.concatenate([total[layer, index : index + 1, :] for index in indices], axis=1)
            size = ref.shape[1]
            mine = jnp.zeros((1, size), F32)
            for share in range(plan.shares):
                mine = jnp.where(row == share, whole[:, share * size : (share + 1) * size], mine)
            ref[layer : layer + 1, :] = mine


def placements(cols):
    windows = cols // WIN
    patches = WIN * cols
    padded = -(-patches // LANES) * LANES
    plain = np.zeros((padded, windows * LANES), np.float32)
    moved = np.zeros((padded, windows * LANES), np.float32)
    for line in range(WIN):
        for col in range(cols):
            source = line * cols + col
            plain[source, (col // WIN) * LANES + line * WIN + col % WIN] = 1
            new_line, new_col = (line - SHIFT) % WIN, (col - SHIFT) % cols
            moved[source, (new_col // WIN) * LANES + new_line * WIN + new_col % WIN] = 1
    return plain.astype(BF), moved.astype(BF)


def swaps():
    on = np.zeros((2 * LANES, LANES), np.float32)
    back = np.zeros((2 * LANES, LANES), np.float32)
    for line in range(SHIFT):
        for col in range(WIN):
            moved, plain = line * WIN + col, (line + SHIFT) * WIN + (col + SHIFT) % WIN
            on[plain + (LANES if col >= SHIFT else 0), moved] = 1
            back[moved + (LANES if col < SHIFT else 0), plain] = 1
    return on.astype(BF), back.astype(BF)


def table_spread():
    size = 2 * WIN - 1
    spread = np.zeros((WIN, 2 * LANES, TABLE), np.float32)
    for key_col in range(WIN):
        for offset in range(size):
            for col in range(WIN):
                spread[key_col, offset * WIN + col, offset * size + col - key_col + WIN - 1] = 1
    spread = spread.reshape(WIN // 2, 2, 2 * LANES, TABLE).swapaxes(1, 2)
    return spread.reshape(WIN * LANES, 2 * TABLE).astype(BF)


def copy_all(*refs):
    *refs, sems = refs
    count = len(refs) // 3
    sources, targets, held = refs[:count], refs[count : 2 * count], refs[2 * count :]
    ways = [*zip(sources, held), *zip(held, targets)]
    copies = [pltpu.make_async_copy(*way, sems.at[number]) for number, way in enumerate(ways)]
    for copy in copies[:count]:
        copy.start()
    for incoming, outgoing in zip(copies[:count], copies[count:]):
        incoming.wait()
        outgoing.start()
    for copy in copies[count:]:
        copy.wait()


def hand_out(values):
    anywhere = pl.BlockSpec(memory_space=pl.ANY)
    return pl.pallas_call(
        copy_all,
        out_shape=[jax.ShapeDtypeStruct(value.shape, value.dtype) for value in values],
        in_specs=[anywhere] * len(values),
        out_specs=[anywhere] * len(values),
        scratch_shapes=[pltpu.VMEM(value.shape, value.dtype) for value in values]
        + [pltpu.SemaphoreType.DMA((2 * len(values),))],
        compiler_params=pltpu.CompilerParams(vmem_limit_bytes=VMEM_LIMIT),
        name="results",
    )(*values)


def per_device(
    page_tokens,
    blank_mask,
    cotangent,
    ln_gain,
    ln_bias,
    qv_bias,
    rel_table,
    w_qkv,
    w_proj,
    proj_bias,
    w_fc1,
    fc1_bias,
    w_fc2,
    fc2_bias,
):
    pages, shares = lax.axis_size(PAGE), lax.axis_size(ROW)
    plan = Plan(pages, shares)
    cols = page_tokens.shape[2]
    windows, lanes = cols // WIN, cols // WIN * LANES
    dense = ((WIN * cols * SPLITS, LANES), F32)
    half_dense = ((WIN * cols * SPLITS // 2, LANES), F32)
    plain, moved = (jnp.asarray(place) for place in placements(cols))
    live_rows = 8 * -(-windows // 8)
    scalar_inputs = dict(blank=blank_mask[0])
    small_inputs = dict(
        table=rel_table,
        ln_gain=ln_gain,
        ln_bias=ln_bias,
        qv_bias=qv_bias,
        proj_bias=proj_bias,
        fc1_bias=fc1_bias,
        fc2_bias=fc2_bias,
    )
    large_inputs = dict(
        in_tokens=page_tokens[0],
        in_grad=cotangent.reshape(dense[0]),
        in_plain=plain,
        in_moved=moved,
        in_swap_on=jnp.asarray(swaps()[0]),
        in_swap_back=jnp.asarray(swaps()[1]),
        in_spread=jnp.asarray(table_spread()),
        in_qkv=w_qkv,
        in_proj=w_proj,
        in_fc1=w_fc1,
        in_fc2=w_fc2,
    )
    saved = dict(
        x=((D, lanes), F32),
        normed=((D, lanes), BF),
        qkv=((3 * D, lanes), BF),
        soft=((windows * HEADS, LANES, LANES), BF),
        merged=((D, lanes), BF),
        hidden=((D, lanes), F32),
        second=((D, lanes), BF),
        active=((FF, lanes), BF),
        slope=((FF, lanes), BF),
    )
    units = ((UNITS,) + plan.sizes[0][0], F32)
    large_outputs = dict(
        out_tokens=dense,
        grad_tokens=dense,
        sum_qkv=((2, D // shares, 3 * D), F32),
        sum_proj=((2, D // shares, D), F32),
        sum_fc1=((2, D // shares, FF), F32),
        sum_fc2=((2, FF // shares, D), F32),
        units_zero=units,
        units_one=units,
        kept_x=((D, lanes), F32),
        kept_normed=((D, lanes), BF),
        kept_qkv=((3 * D, lanes), BF),
        kept_soft=((windows * HEADS, LANES, LANES), BF),
        kept_merged=((D, lanes), BF),
        kept_hidden=((D, lanes), F32),
        kept_second=((D, lanes), BF),
        kept_active=((FF, lanes), BF),
        kept_slope=((FF, lanes), BF),
    )
    small_outputs = dict(
        d_ln_gain=((2, 2 * D // shares), F32),
        d_ln_bias=((2, 2 * D // shares), F32),
        d_qv_bias=((2, 2 * D // shares), F32),
        d_proj_bias=((2, D // shares), F32),
        d_fc1_bias=((2, FF // shares), F32),
        d_fc2_bias=((2, D // shares), F32),
        d_table=((2, HEADS, OFFSETS), F32),
    )
    small = (2, SMALL, D)
    vmem = dict(
        saved,
        tokens=((WIN, cols, D), BF),
        plain=(plain.shape, BF),
        moved=(moved.shape, BF),
        w_qkv=((D, 3 * D), BF),
        w_proj=((D, D), BF),
        w_fc1=((D, FF), BF),
        w_fc2=((FF, D), BF),
        dense=dense,
        upper=half_dense,
        swap_on=((2 * LANES, LANES), BF),
        swap_back=((2 * LANES, LANES), BF),
        grad_upper=half_dense,
        next_upper=half_dense,
        live_upper=((live_rows, LANES), F32),
        live_two=((live_rows, LANES), F32),
        work=((D, lanes), F32),
        grad=((D, lanes), F32),
        low=((D, lanes), BF),
        sums=((VECTORS, D, LANES), F32),
        gains=((2, D, LANES), F32),
        bias=((HEADS, LANES, LANES), F32),
        bias_rows=((HEADS * LANES, LANES), F32),
        regions=((2, LANES, LANES), F32),
        padded_table=((HEADS, TABLE), F32),
        live=((live_rows, LANES), F32),
        vector_rows=((VECTOR_ROWS, D), F32),
        staged=((2 * CHUNK, CHUNK), F32),
        done=((DONE * CLASSES, CHUNK // shares, CHUNK), F32),
        held=((HELD * CLASSES,) + plan.sizes[0][0], F32),
        first_landing=((RING * CLASSES,) + plan.sizes[0][0], F32),
        small_own=(small, F32),
        small_parts=((plan.halvings,) + small, F32),
    )
    semaphores = dict(
        move_sems=pltpu.SemaphoreType.DMA((48,)),
        halo_sems=pltpu.SemaphoreType.DMA((2, 5)),
        send_sems=pltpu.SemaphoreType.DMA((2 * UNITS, plan.phases)),
        recv_sems=pltpu.SemaphoreType.DMA((2 * UNITS, plan.phases)),
        own_sems=pltpu.SemaphoreType.DMA((2 * UNITS, 2)),
        stage_sems=pltpu.SemaphoreType.DMA((2, shares, 2)),
        first_sems=pltpu.SemaphoreType.DMA((2 * UNITS, shares)),
        first_free=pltpu.SemaphoreType.REGULAR((2 * UNITS,)),
        small_sems=pltpu.SemaphoreType.DMA((2, plan.halvings)),
        free_sems=pltpu.SemaphoreType.REGULAR((CLASSES, plan.halvings)),
    )
    landing = [((RING,) + size, F32) for sizes in plan.sizes for size in sizes[1:]]
    layout = [*scalar_inputs, *small_inputs, *large_inputs, *small_outputs, *large_outputs, *vmem, *semaphores]
    in_vmem, anywhere = pl.BlockSpec(memory_space=pltpu.VMEM), pl.BlockSpec(memory_space=pl.ANY)
    outputs = {**small_outputs, **large_outputs}
    results = pl.pallas_call(
        functools.partial(run, plan, layout),
        out_shape=[jax.ShapeDtypeStruct(*shape) for shape in outputs.values()],
        in_specs=[pl.BlockSpec(memory_space=pltpu.SMEM)] + [in_vmem] * len(small_inputs) + [anywhere] * len(large_inputs),
        out_specs=[in_vmem] * len(small_outputs) + [anywhere] * len(large_outputs),
        scratch_shapes=[pltpu.VMEM(*shape) for shape in vmem.values()]
        + list(semaphores.values())
        + [pltpu.VMEM(*shape) for shape in landing],
        compiler_params=pltpu.CompilerParams(
            vmem_limit_bytes=VMEM_LIMIT, collective_id=0, has_side_effects=True
        ),
        name="two_layers",
    )(*scalar_inputs.values(), *small_inputs.values(), *large_inputs.values())
    results = hand_out(results[: len(small_outputs) + 6])
    d_ln_gain, d_ln_bias, d_qv_bias, d_proj_bias, d_fc1_bias, d_fc2_bias, d_table = results[: len(small_outputs)]
    out_tokens, grad_tokens, sum_qkv, sum_proj, sum_fc1, sum_fc2 = results[len(small_outputs) :]
    return (
        out_tokens.reshape(cotangent.shape),
        grad_tokens.reshape(cotangent.shape),
        d_ln_gain,
        d_ln_bias,
        d_qv_bias,
        d_table,
        sum_qkv,
        sum_proj,
        d_proj_bias,
        sum_fc1,
        d_fc1_bias,
        sum_fc2,
        d_fc2_bias,
    )


def solution(mesh):
    tokens, by_row, shares = P(PAGE, ROW, None, None), P(None, ROW), P(None, ROW, None)
    return jax.shard_map(
        per_device,
        mesh=mesh,
        in_specs=(tokens, P(PAGE, ROW, None), tokens) + (P(),) * 11,
        out_specs=(tokens, tokens)
        + (by_row, by_row, by_row, P(), shares, shares, by_row, shares, by_row, shares, by_row),
        check_vma=False,
    )
```

```python
import functools

import jax
import jax.numpy as jnp
import numpy as np
from jax import lax
from jax.experimental import pallas as pl
from jax.experimental.pallas import tpu as pltpu
from jax.sharding import PartitionSpec as P

WIN = 10
SHIFT = 5
AREA = WIN * WIN
LANES = 128
D = 512
HEADS = 16
HEAD_DIM = 32
FF = 2048
CHUNK = 512
FEEDS = FF // CHUNK
SPLITS = D // LANES
EPSILON = 1e-05
MASK_VALUE = -100.0
NEVER = -1e30
SCORE_SCALE = HEAD_DIM ** (-0.5)
VMEM_LIMIT = 63 * 1024 * 1024 + 512 * 1024
BF = jnp.bfloat16
F32 = jnp.float32
MESH = pl.DeviceIdType.MESH
PAGE, ROW = "page", "row"

G1, B1, G2, B2, QB, VB, PB, F2B, F1B, VECTORS = 0, 1, 2, 3, 4, 5, 6, 7, 8, 12
VECTOR_ROWS = 16
SMALL = VECTOR_ROWS + HEADS
OFFSETS = (2 * WIN - 1) ** 2
TABLE = 384

UNIT_FC1, UNIT_FC2, UNIT_PROJ, UNIT_QKV, UNITS = 0, 4, 8, 9, 12
CLASSES = 3
GROUPS = UNITS // CLASSES
TRIPLES = 2 * GROUPS
HELD = 4
DONE = 5
RING = 3
QKV, PROJ, FC1, FC2 = range(4)
TARGETS = (
    ((FC1, 0, 0), (FC1, 0, 1), (FC1, 0, 2)),
    ((FC1, 0, 3), (FC2, 0, 0), (FC2, 1, 0)),
    ((FC2, 2, 0), (FC2, 3, 0), (PROJ, 0, 0)),
    ((QKV, 0, 0), (QKV, 0, 1), (QKV, 0, 2)),
)


def mm(left, right, left_dim, right_dim):
    return lax.dot_general(
        left, right, (((left_dim,), (right_dim,)), ((), ())), preferred_element_type=F32
    )


def split(values):
    high = values.astype(BF)
    return high, (values - high.astype(F32)).astype(BF)


def lane_tile(index):
    return pl.ds(pl.multiple_of(index * LANES, LANES), LANES)


def chunk_of(index):
    return pl.ds(pl.multiple_of(index * CHUNK, CHUNK), CHUNK)


def wide(column, count):
    return jnp.concatenate([column] * count, axis=1)


def fold(values):
    total = values[:, :LANES]
    for start in range(LANES, values.shape[1], LANES):
        total = total + values[:, start : start + LANES]
    return total


def norm_parts(values):
    center = values - jnp.sum(values, axis=0, keepdims=True) * (1.0 / D)
    spread = jnp.sum(center * center, axis=0, keepdims=True) * (1.0 / D)
    scale = lax.rsqrt(spread + EPSILON)
    return center * scale, scale


def norm_pull(grad, gain, hat, scale):
    scaled = grad * gain
    mean_one = jnp.sum(scaled, axis=0, keepdims=True) * (1.0 / D)
    mean_two = jnp.sum(scaled * hat, axis=0, keepdims=True) * (1.0 / D)
    return scale * (scaled - mean_one - hat * mean_two)


def gelu_parts(inner):
    step = 1.0 / (1.0 + (0.3275911 * 0.7071067811865476) * jnp.abs(inner))
    bell = jnp.exp(inner * inner * -0.5)
    poly = 0.5 * 1.061405429
    for factor in (-1.453152027, 1.421413741, -0.284496736, 0.254829592):
        poly = poly * step + 0.5 * factor
    tail = poly * step * bell
    below = jnp.where(inner >= 0, 1.0 - tail, tail)
    return inner * below, below + inner * bell * 0.3989422804014327


def to_channels(page_ref, place_ref, out_ref, exact=False):
    def step(index, carry):
        channels = pl.ds(pl.multiple_of(index * 256, 256), 256)
        values = page_ref[:, channels]
        if exact:
            out_ref[channels, :] = mm(values.astype(BF), place_ref[...], 0, 0)
        else:
            high, low = split(values)
            out_ref[channels, :] = mm(high, place_ref[...], 0, 0) + mm(low, place_ref[...], 0, 0)
        return carry

    lax.fori_loop(0, D // 256, step, 0, unroll=2)


def to_dense(values_ref, place_ref, dense_ref, padded):
    count = dense_ref.shape[0] // SPLITS
    for index in range(D // 256):
        high, low = split(values_ref[index * 256 : (index + 1) * 256, :])
        page = mm(place_ref[:padded, :], high, 1, 1) + mm(place_ref[:padded, :], low, 1, 1)
        for part in range(2):
            rows = pl.ds(2 * index + part, count, stride=SPLITS)
            dense_ref[rows, :] = page[:count, part * LANES : (part + 1) * LANES]


def from_dense(dense_ref, page_ref, row):
    count = dense_ref.shape[0] // SPLITS
    for part in range(SPLITS):
        rows = pl.ds(part, count, stride=SPLITS)
        page_ref[pl.ds(row, count), part * LANES : (part + 1) * LANES] = dense_ref[rows, :]


def add_halo(page_ref, place_ref, out_ref, count, padded):
    page_ref[pl.ds(count, padded - count), :] = jnp.zeros((padded - count, D), F32)

    def step(index, carry):
        channels = pl.ds(pl.multiple_of(index * 256, 256), 256)
        high, low = split(page_ref[:padded, channels])
        out_ref[channels, :] += mm(high, place_ref[:padded, :], 0, 0) + mm(low, place_ref[:padded, :], 0, 0)
        return carry

    lax.fori_loop(0, D // 256, step, 0, unroll=2)


def move_own(values_ref, swap_ref, out_ref, windows, first):
    for window in range(windows):
        sources = [(window + first + part) % windows * LANES for part in range(2)]
        values = jnp.concatenate([values_ref[:, start : start + LANES] for start in sources], axis=1)
        high, low = split(values)
        target = slice(window * LANES, (window + 1) * LANES)
        out_ref[:, target] = mm(high, swap_ref[...], 1, 0) + mm(low, swap_ref[...], 1, 0)


def vector_rows(s, layer):
    rows = s.vector_rows
    sources = ((G1, s.ln_gain, 0), (B1, s.ln_bias, 0), (G2, s.ln_gain, 1), (B2, s.ln_bias, 1))
    sources += ((QB, s.qv_bias, 0), (VB, s.qv_bias, 1), (PB, s.proj_bias, 0), (F2B, s.fc2_bias, 0))
    sources += tuple((F1B + part, s.fc1_bias, part) for part in range(FEEDS))
    for index, source, part in sources:
        rows[index : index + 1, :] = source[layer : layer + 1, part * D : (part + 1) * D]
    rows[VECTORS:, :] = jnp.zeros((VECTOR_ROWS - VECTORS, D), F32)
    return rows[...].T


def spread_columns(s, layer):
    columns = vector_rows(s, layer)
    for index in range(VECTORS):
        s.sums[index] = jnp.broadcast_to(columns[:, index : index + 1], (D, LANES))


def spread_gains(s, layer):
    columns = vector_rows(s, layer)
    for index, vector in enumerate((G1, G2)):
        s.gains[index] = jnp.broadcast_to(columns[:, vector : vector + 1], (D, LANES))


def spread_part(col):
    rows, lanes = (col // 2) * 2 * LANES, (col % 2) * TABLE
    return slice(rows, rows + 2 * LANES), slice(lanes, lanes + TABLE)


def spread_bias(s, layer):
    spread_ref, rows_ref, bias_ref = s.spread, s.bias_rows, s.bias
    s.padded_table[...] = jnp.zeros(s.padded_table.shape, F32)
    s.padded_table[:, :OFFSETS] = s.table[layer]
    high, low = split(s.padded_table[...])
    parts = []
    for col in range(WIN):
        chosen = spread_ref[spread_part(col)]
        parts.append(mm(high, chosen, 1, 1) + mm(low, chosen, 1, 1))
    source = jnp.concatenate(parts, axis=0)
    rows_ref[...] = jnp.zeros(rows_ref.shape, F32)
    for row in range(WIN):
        shift = (WIN - 1 - row) * WIN
        moved = source if shift == 0 else pltpu.roll(source, 2 * LANES - shift, axis=1)
        rows_ref[pl.ds(row * WIN * HEADS, WIN * HEADS), :] = moved[:, :LANES]
    for head in range(HEADS):
        bias_ref[head] = rows_ref[pl.ds(head, LANES, stride=HEADS), :]


def gather_bias(grad_ref, spread_ref, rows_ref):
    for head in range(HEADS):
        rows_ref[pl.ds(head, LANES, stride=HEADS), :] = grad_ref[head]
    total = jnp.zeros((WIN * HEADS, 2 * LANES), F32)
    for row in range(WIN):
        shift = (WIN - 1 - row) * WIN
        piece = rows_ref[pl.ds(row * WIN * HEADS, WIN * HEADS), :]
        piece = jnp.concatenate([piece, jnp.zeros_like(piece)], axis=1)
        total = total + (piece if shift == 0 else pltpu.roll(piece, shift, axis=1))
    table = jnp.zeros((HEADS, TABLE), F32)
    for col in range(WIN):
        for part in split(total[col * HEADS : (col + 1) * HEADS]):
            table = table + mm(part, spread_ref[spread_part(col)], 1, 0)
    return table


def region_masks(shifted_layer, out_ref):
    key = lax.broadcasted_iota(jnp.int32, (LANES, LANES), 0)
    query = lax.broadcasted_iota(jnp.int32, (LANES, LANES), 1)
    padding = jnp.where(key < AREA, 0.0, NEVER)
    out_ref[0] = padding
    out_ref[1] = padding
    if shifted_layer:
        last = lax.axis_index(ROW) == lax.axis_size(ROW) - 1
        rows_differ = ((key >= AREA // 2) != (query >= AREA // 2)) & last
        cols_differ = (key % WIN >= SHIFT) != (query % WIN >= SHIFT)
        out_ref[0] += jnp.where(rows_differ, MASK_VALUE, 0.0)
        out_ref[1] += jnp.where(rows_differ | cols_differ, MASK_VALUE, 0.0)


def shifted_live(s, windows):
    place = lax.broadcasted_iota(jnp.int32, (1, LANES), 1)
    for window in range(windows):
        here, after = slice(window, window + 1), slice((window + 1) % windows, (window + 1) % windows + 1)
        beyond = place % WIN >= SHIFT
        own = jnp.where(beyond, s.live[after, :], s.live[here, :])
        upper = jnp.where(beyond, s.live_upper[after, :], s.live_upper[here, :])
        s.live_two[here, :] = jnp.where(place >= AREA // 2, upper, own)


def head_rows(head, base=0):
    return pl.ds(base + head * HEAD_DIM, HEAD_DIM)


def norm_one_forward(s, windows):
    def step(index, carry):
        lanes = lane_tile(index)
        hat, _ = norm_parts(s.x[:, lanes])
        s.normed[:, lanes] = (hat * s.sums[G1] + s.sums[B1]).astype(BF)
        return carry

    lax.fori_loop(0, windows, step, 0, unroll=3)


def project_forward(s, windows):
    def step(index, carry):
        rows = chunk_of(index)
        bias = s.sums[jnp.where(index == 0, QB, VB)] * jnp.where(index == 1, 0.0, 1.0)
        out = mm(s.w_qkv[:, rows], s.normed[...], 0, 0)
        s.qkv[rows, :] = (out + wide(bias, windows)).astype(BF)
        return carry

    lax.fori_loop(0, 3, step, 0)


def attend_forward(s, windows, live_ref):
    def step(index, carry):
        lanes = lane_tile(index)
        live = jnp.broadcast_to(live_ref[pl.ds(index, 1), :], (LANES, LANES)).T
        masked = s.regions[jnp.where(index == windows - 1, 1, 0)] + MASK_VALUE * (1.0 - live)
        for head in range(HEADS):
            query = s.qkv[head_rows(head), lanes]
            key = s.qkv[head_rows(head, D), lanes]
            value = s.qkv[head_rows(head, 2 * D), lanes]
            scores = mm(key, query, 0, 0) * SCORE_SCALE + (s.bias[head] + masked)
            exponent = jnp.exp(scores - jnp.max(scores, axis=0, keepdims=True))
            total = jnp.sum(exponent, axis=0, keepdims=True)
            soft = (exponent * (1.0 / total)).astype(BF)
            s.soft[index * HEADS + head] = soft
            s.merged[head_rows(head), lanes] = mm(value, soft, 1, 0).astype(BF)
        return carry

    lax.fori_loop(0, windows, step, 0, unroll=2)


def norm_two_forward(s, windows, live_ref):
    def step(index, carry):
        lanes = lane_tile(index)
        hidden = s.x[:, lanes] + live_ref[pl.ds(index, 1), :] * (s.work[:, lanes] + s.sums[PB])
        s.hidden[:, lanes] = hidden
        s.work[:, lanes] = hidden + s.sums[F2B]
        hat, _ = norm_parts(hidden)
        s.second[:, lanes] = (hat * s.sums[G2] + s.sums[B2]).astype(BF)
        return carry

    lax.fori_loop(0, windows, step, 0, unroll=3)


def feed_forward(s, windows):
    def step(index, carry):
        rows = chunk_of(index)
        inner = mm(s.w_fc1[:, rows], s.second[...], 0, 0) + wide(s.sums[F1B + index], windows)
        active, slope = gelu_parts(inner)
        active = active.astype(BF)
        s.active[rows, :] = active
        s.slope[rows, :] = slope.astype(BF)
        s.work[...] += mm(s.w_fc2[rows, :], active, 0, 0)
        return carry

    lax.fori_loop(0, FEEDS, step, 0)


def feed_backward(s, sink, times):
    s.sums[...] = jnp.zeros(s.sums.shape, F32)
    s.bias[...] = jnp.zeros(s.bias.shape, F32)
    lowered = s.grad[...].astype(BF)
    s.low[...] = lowered
    s.sums[F2B] = fold(lowered.astype(F32))
    s.work[...] = jnp.zeros(s.work.shape, F32)

    claims = sink.layer == 0
    if claims:
        for unit in range(UNIT_FC2, UNIT_FC2 + FEEDS):
            sink.claim(unit)

    def step(index, carry):
        rows = chunk_of(index)
        if claims:
            sink.claim(UNIT_FC1 + index)
        sink.put(0, mm(s.active[rows, :], s.low[...], 1, 1), feed_pieces(index, sink.shares), index == 0)
        grad_inner = mm(s.w_fc2[rows, :], s.low[...], 1, 0) * s.slope[rows, :].astype(F32)
        grad_inner = grad_inner.astype(BF)
        s.sums[F1B + index] = fold(grad_inner.astype(F32))
        sink.put(1, mm(s.second[...], grad_inner, 1, 1), row_pieces(UNIT_FC1 + index, sink.shares), index == 0)
        s.work[...] += mm(s.w_fc1[:, rows], grad_inner, 1, 0)
        sink.advance_at(index, times)
        return carry

    lax.fori_loop(0, FEEDS, step, 0)
    sink.settle(0)
    sink.settle(1)


def norm_two_backward(s, windows, live_ref):
    def step(index, carry):
        lanes = lane_tile(index)
        hat, scale = norm_parts(s.hidden[:, lanes])
        grad = s.work[:, lanes]
        s.sums[G2] += grad * hat
        s.sums[B2] += grad
        grad = s.grad[:, lanes] + norm_pull(grad, s.gains[1], hat, scale)
        s.grad[:, lanes] = grad
        grad_low = (grad * live_ref[pl.ds(index, 1), :]).astype(BF)
        s.low[:, lanes] = grad_low
        s.sums[PB] += grad_low.astype(F32)
        return carry

    lax.fori_loop(0, windows, step, 0, unroll=3)


def merge_backward(s, sink):
    if sink.layer == 0:
        sink.claim(UNIT_PROJ)
    sink.put(0, mm(s.merged[...], s.low[...], 1, 1), row_pieces(UNIT_PROJ, sink.shares), True)
    s.merged[...] = mm(s.w_proj[...], s.low[...], 1, 0).astype(BF)
    sink.settle(0)


def attend_backward(s, windows, sink, times):
    def step(index, carry):
        lanes = lane_tile(index)
        for head in range(HEADS):
            query = s.qkv[head_rows(head), lanes]
            key = s.qkv[head_rows(head, D), lanes]
            value = s.qkv[head_rows(head, 2 * D), lanes]
            grad_out = s.merged[head_rows(head), lanes]
            soft_low = s.soft[index * HEADS + head]
            soft = soft_low.astype(F32)
            grad_soft = mm(value, grad_out, 0, 0)
            inner = jnp.sum(soft * grad_soft, axis=0, keepdims=True)
            grad_scores = (soft * (grad_soft - inner)).astype(BF)
            s.bias[head] += grad_scores.astype(F32)
            grad_query = (mm(key, grad_scores, 1, 0) * SCORE_SCALE).astype(BF)
            grad_key = (mm(query, grad_scores, 1, 1) * SCORE_SCALE).astype(BF)
            grad_value = mm(grad_out, soft_low, 1, 1).astype(BF)
            s.qkv[head_rows(head), lanes] = grad_query
            s.qkv[head_rows(head, D), lanes] = grad_key
            s.qkv[head_rows(head, 2 * D), lanes] = grad_value
            s.sums[QB, head_rows(head), :] += grad_query.astype(F32)
            s.sums[VB, head_rows(head), :] += grad_value.astype(F32)
        sink.advance_at(index, times)
        return carry

    lax.fori_loop(0, windows, step, 0)


def project_backward(s, sink):
    def step(index, carry):
        rows = chunk_of(index)
        sink.claim(UNIT_QKV + index)
        sink.put(index % 2, mm(s.normed[...], s.qkv[rows, :], 1, 1), row_pieces(UNIT_QKV + index, sink.shares), index < 2)
        return carry

    lax.fori_loop(0, 3, step, 0)


def input_backward(s):
    s.work[...] = mm(s.w_qkv[...], s.qkv[...], 1, 0)


def norm_one_backward(s, windows):
    def step(index, carry):
        lanes = lane_tile(index)
        hat, scale = norm_parts(s.x[:, lanes])
        grad = s.work[:, lanes]
        s.sums[G1] += grad * hat
        s.sums[B1] += grad
        s.grad[:, lanes] += norm_pull(grad, s.gains[0], hat, scale)
        return carry

    lax.fori_loop(0, windows, step, 0, unroll=3)


def small_gradients(s, small_ref):
    places = lax.broadcasted_iota(jnp.int32, (D, LANES), 1)
    packed = jnp.zeros((D, LANES), F32)
    for index in range(VECTORS):
        packed = jnp.where(places == index, jnp.sum(s.sums[index], axis=1, keepdims=True), packed)
    small_ref[:VECTOR_ROWS, :] = packed.T[:VECTOR_ROWS]
    table = gather_bias(s.bias, s.spread, s.bias_rows)
    small_ref[VECTOR_ROWS:, :] = jnp.concatenate([table, jnp.zeros((HEADS, D - TABLE), F32)], axis=1)


def reversed_bits(value, count):
    turned = 0
    for bit in range(count):
        turned = turned * 2 + (value // 2**bit) % 2
    return turned


def row_pieces(unit, shares):
    rows, count = CHUNK // shares, shares.bit_length() - 1
    return [(share * rows, unit, reversed_bits(share, count)) for share in range(shares)]


def feed_pieces(index, shares):
    rows, count = CHUNK // shares, shares.bit_length() - 1
    pieces = []
    for share in range(shares // FEEDS):
        place = reversed_bits(index * (shares // FEEDS) + share, count)
        for part in range(FEEDS):
            pieces.append(((share * FEEDS + part) * rows, UNIT_FC2 + part, place))
    return pieces


class Plan:
    def __init__(self, pages, shares):
        self.shares, self.rows = shares, CHUNK // shares
        page_bits, row_bits = pages.bit_length() - 1, shares.bit_length() - 1
        others = page_bits - 1
        self.steps = []
        for kind in range(CLASSES):
            turn = kind % 2
            page = [(PAGE, 2 ** (1 + (bit + turn) % others)) for bit in range(others)]
            row = [(ROW, 2**bit) for bit in range(row_bits)]
            self.steps.append([(PAGE, 1)] + (row + page if kind == 2 else page + row))
        self.page_steps = [[0] + [at for at, step in enumerate(steps) if at and step[0] == PAGE] for steps in self.steps]
        self.halvings = page_bits + row_bits
        self.phases = self.halvings + page_bits
        self.sizes, self.axes = [], []
        for steps in self.steps:
            size, sizes, axes = [shares, self.rows, CHUNK], [], []
            for axis, _ in steps:
                axes.append(0 if axis == ROW else 1 if size[1] >= 16 else 2)
                size[axes[-1]] //= 2
                sizes.append(tuple(size))
            self.sizes.append(sizes)
            self.axes.append(axes)
        self.steps_at = self.schedule()

    def schedule(self):
        small = TRIPLES
        free, ready, stage_of, plan, now = {}, {}, {}, [], 0.0
        for triple in range(TRIPLES):
            for kind in range(CLASSES):
                stage_of[triple, kind] = 0
        stage_of[small, 0] = 0

        def link(key, phase):
            triple, kind = key
            if phase < self.halvings:
                axis, stride = self.steps[kind][phase]
                size = 2.0**-phase / 2 if triple != small else 0.125
            else:
                axis, stride = self.steps[kind][self.page_steps[kind][self.phases - 1 - phase]]
                size = 2.0 ** (phase - 2 * self.halvings)
            if axis == PAGE and stride == 1:
                return 0, size * PLAN_CORE
            return (axis, stride if axis == PAGE else 0), size * PLAN_LINK * (1.0 if stride == 1 or axis == PAGE else 1.5)

        def last_stage(key):
            return self.halvings if key[0] == small else self.phases + 1

        def allowed(key, point):
            triple, kind = key
            stage = stage_of[key]
            if stage > last_stage(key):
                return False
            if triple == small:
                return point >= len(PLAN_POINTS) - 1
            if stage == 0 and point < PLAN_THERE[triple]:
                return False
            if triple > 0 and stage_of[triple - 1, kind] <= stage:
                return False
            if triple >= RING and stage < self.halvings and stage_of[triple - RING, kind] <= stage + 1:
                return False
            if stage == 0 and triple >= DONE and stage_of[triple - DONE, kind] <= self.phases + 1:
                return False
            return not (stage == 0 and triple >= HELD and stage_of[triple - HELD, kind] <= self.halvings + 1)

        for point, work in enumerate(PLAN_POINTS):
            now += work
            if point == PLAN_HALO:
                free[ROW, 0] = max(now, free.get((ROW, 0), 0.0)) + PLAN_HALO_TIME
            steps, final = [], point == len(PLAN_POINTS) - 1
            while True:
                keys = [key for key in stage_of if allowed(key, point)]
                needed = PLAN_FORCE.get(point, -1)
                keys = [
                    key
                    for key in keys
                    if final or ready.get(key, 0.0) <= now + PLAN_SLACK or (key[0] <= needed and stage_of[key] <= 1)
                ]
                if not keys:
                    break
                key = min(keys, key=lambda key: (max(ready.get(key, 0.0), now), -stage_of[key], key))
                stage = stage_of[key]
                now = max(now, ready.get(key, 0.0)) + (PLAN_ADD * 2.0**-stage if stage else 0.0)
                if stage == self.phases:
                    ready[key] = now + PLAN_LATENCY
                elif stage < last_stage(key):
                    name, length = link(key, stage)
                    free[name] = max(now, free.get(name, 0.0)) + length
                    ready[key] = free[name] + PLAN_LATENCY
                steps.append((*key, stage))
                stage_of[key] += 1
            plan.append(steps)
        assert all(stage_of[key] > last_stage(key) for key in stage_of)
        return plan

    def partner(self, kind, level):
        axis, stride = self.steps[kind][level]
        page, row = lax.axis_index(PAGE), lax.axis_index(ROW)
        mine = page if axis == PAGE else row
        bit = (mine // stride) % 2
        other = mine + (1 - 2 * bit) * stride
        return bit, ((other, row) if axis == PAGE else (page, other))

    def part(self, kind, level, sent=False):
        starts, sizes = [0, 0, 0], list(self.sizes[kind][0])
        for at in range(1, level + 1):
            axis = self.axes[kind][at]
            sizes[axis] //= 2
            bit, _ = self.partner(kind, at)
            which = 1 - bit if sent and at == level else bit
            starts[axis] = starts[axis] + which * sizes[axis]
        return (
            pl.ds(starts[0], sizes[0]),
            pl.ds(pl.multiple_of(starts[1], 8), sizes[1]),
            pl.ds(pl.multiple_of(starts[2], LANES), sizes[2]),
        )

    def place(self, kind, count):
        starts, sizes = [0, 0], [self.rows, CHUNK]
        for at in self.page_steps[kind][:count]:
            axis = self.axes[kind][at] - 1
            sizes[axis] //= 2
            bit, _ = self.partner(kind, at)
            starts[axis] = starts[axis] + bit * sizes[axis]
        return starts, sizes


class Reducer:
    def __init__(self, plan, s):
        self.plan, self.s = plan, s
        self.shares = plan.shares
        self.layer = 1

    def stage_copies(self, slot, pieces):
        s, plan = self.s, self.plan
        bit, device = plan.partner(0, 0)
        rows = plan.rows // 2
        copies = []
        for number, (start, unit, place) in enumerate(pieces):
            start = slot * CHUNK + start
            number_sems = s.stage_sems.at[slot, number]
            overall = self.first_unit() + unit
            sent = pltpu.make_async_remote_copy(
                src_ref=s.staged.at[pl.ds(pl.multiple_of(start + (1 - bit) * rows, 8), rows)],
                dst_ref=s.first_landing.at[overall % (RING * CLASSES), place],
                send_sem=number_sems.at[0],
                recv_sem=s.first_sems.at[overall, place],
                device_id=device,
                device_id_type=MESH,
            )
            kept = pltpu.make_async_copy(
                s.staged.at[pl.ds(pl.multiple_of(start + bit * rows, 8), rows)],
                s.units[self.layer].at[unit, place],
                number_sems.at[1],
            )
            copies.append((sent, kept))
        return copies

    def first_unit(self):
        return UNITS * (1 - self.layer)

    def claim(self, unit):
        pl.semaphore_wait(self.s.first_free.at[self.first_unit() + unit], 1)

    def put(self, slot, grad, pieces, first):
        if first is not True:

            @pl.when(jnp.logical_not(first))
            def _():
                self.settle(slot)

        self.s.staged[pl.ds(pl.multiple_of(slot * CHUNK, CHUNK), CHUNK), :] = grad
        for sent, kept in self.stage_copies(slot, pieces):
            sent.start()
            kept.start()

    def settle(self, slot):
        for sent, kept in self.stage_copies(slot, row_pieces(0, self.shares)):
            sent.wait_send()
            kept.wait()

    def first_arrived(self, triple, kind):
        s, unit = self.s, CLASSES * triple + kind
        landed = s.first_landing.at[unit % (RING * CLASSES)]
        _, device = self.plan.partner(0, 0)
        for place in range(self.shares):
            pltpu.make_async_remote_copy(
                src_ref=landed.at[place],
                dst_ref=landed.at[place],
                send_sem=s.first_sems.at[unit, place],
                recv_sem=s.first_sems.at[unit, place],
                device_id=device,
                device_id_type=MESH,
            ).wait_recv()

    def remote(self, source, target, unit, phase, device):
        return pltpu.make_async_remote_copy(
            src_ref=source,
            dst_ref=target,
            send_sem=self.s.send_sems.at[unit, phase],
            recv_sem=self.s.recv_sems.at[unit, phase],
            device_id=device,
            device_id_type=MESH,
        )

    def held(self, triple, kind):
        return self.s.held.at[CLASSES * (triple % HELD) + kind]

    def landed(self, triple, kind, level):
        if level == 0:
            return self.s.first_landing.at[(CLASSES * triple + kind) % (RING * CLASSES)]
        return self.s.landing[kind][level - 1].at[triple % RING]

    def halving(self, triple, kind, level):
        _, device = self.plan.partner(kind, level)
        source = self.held(triple, kind).at[self.plan.part(kind, level, True)]
        return self.remote(source, self.landed(triple, kind, level), CLASSES * triple + kind, level, device)

    def own_half(self, triple, kind):
        source = self.s.units[1 - triple // GROUPS].at[CLASSES * (triple % GROUPS) + kind]
        sem = self.s.own_sems.at[CLASSES * triple + kind, 0]
        return pltpu.make_async_copy(source, self.held(triple, kind), sem)

    def finished(self, triple, kind):
        return self.held(triple, kind).at[self.plan.part(kind, self.plan.halvings - 1)].at[0]

    def done(self, triple, kind, count):
        starts, sizes = self.plan.place(kind, count)
        return self.s.done.at[
            CLASSES * (triple % DONE) + kind,
            pl.ds(pl.multiple_of(starts[0], 8), sizes[0]),
            pl.ds(pl.multiple_of(starts[1], LANES), sizes[1]),
        ]

    def gathering(self, triple, kind, phase):
        plan = self.plan
        count = len(plan.page_steps[kind]) - (phase - plan.halvings)
        part = self.done(triple, kind, count)
        _, device = plan.partner(kind, plan.page_steps[kind][count - 1])
        return self.remote(part, part, CLASSES * triple + kind, phase, device)

    def result(self, triple, kind):
        which, row_block, col_block = TARGETS[triple % GROUPS][kind]
        rows = self.plan.rows
        target = self.s.results[which].at[
            1 - triple // GROUPS, pl.ds(row_block * rows, rows), pl.ds(col_block * CHUNK, CHUNK)
        ]
        sem = self.s.own_sems.at[CLASSES * triple + kind, 1]
        return pltpu.make_async_copy(self.done(triple, kind, 0), target, sem)

    def start(self, triple, kind, phase):
        plan = self.plan
        if phase == 0:
            self.own_half(triple, kind).start()
        elif phase < plan.halvings:
            if triple >= RING:
                pl.semaphore_wait(self.s.free_sems.at[kind, phase], 1)
            self.halving(triple, kind, phase).start()
        elif phase < plan.phases:
            if phase == plan.halvings:
                self.done(triple, kind, len(plan.page_steps[kind]))[...] = self.finished(triple, kind)[...]
            self.gathering(triple, kind, phase).start()
        elif phase == plan.phases:
            self.result(triple, kind).start()

    def arrive(self, triple, kind, phase):
        plan = self.plan
        if phase == 0:
            self.first_arrived(triple, kind)
            self.own_half(triple, kind).wait()
        elif phase < plan.halvings:
            self.halving(triple, kind, phase).wait()
        elif phase < plan.phases:
            self.gathering(triple, kind, phase).wait()
        else:
            self.result(triple, kind).wait()

    def take_in(self, triple, kind, phase):
        plan, s = self.plan, self.s
        if phase >= plan.halvings:
            return
        landed = self.landed(triple, kind, phase)
        kept = self.held(triple, kind).at[plan.part(kind, phase)]
        for share in range(landed.shape[0]):
            kept[share] += landed[share]
        if triple < TRIPLES - RING:
            _, device = plan.partner(kind, phase)
            free = s.free_sems.at[kind, phase]
            if phase == 0:
                free = s.first_free.at[CLASSES * (triple + RING) + kind]
            pl.semaphore_signal(free, inc=1, device_id=device, device_id_type=MESH)

    def advance(self, point):
        steps = self.plan.steps_at[point]
        most = 1 if point == len(self.plan.steps_at) - 1 else 6
        groups = []
        for step in steps:
            if groups and len(groups[-1]) < most and all(step[:2] != other[:2] for other in groups[-1]):
                groups[-1].append(step)
            else:
                groups.append([step])
        for group in groups:
            if group[0][0] == TRIPLES:
                self.small_step(group[0][2] - 1)
                continue
            for act in (self.arrive, self.take_in):
                for triple, kind, stage in group:
                    if stage > 0:
                        act(triple, kind, stage - 1)
            for triple, kind, stage in group:
                self.start(triple, kind, stage)

    def advance_at(self, index, points):
        for number, point in enumerate(points):
            if self.plan.steps_at[point]:

                @pl.when(index == number)
                def _(point=point):
                    self.advance(point)

    def small_copy(self, phase):
        s = self.s
        _, device = self.plan.partner(0, phase)
        return pltpu.make_async_remote_copy(
            src_ref=s.small_own if phase == 0 else s.small_parts.at[phase - 1],
            dst_ref=s.small_parts.at[phase],
            send_sem=s.small_sems.at[0, phase],
            recv_sem=s.small_sems.at[1, phase],
            device_id=device,
            device_id_type=MESH,
        )

    def small_step(self, phase):
        s = self.s
        if phase >= 0:
            self.small_copy(phase).wait()
            s.small_parts[phase] += s.small_own[...] if phase == 0 else s.small_parts[phase - 1]
        if phase + 1 < self.plan.halvings:
            self.small_copy(phase + 1).start()


PLAN_POINTS = (0, 2, 3) + (2.7,) * 6 + (5.2, 3, 3, 6) + (3.2,) * 4 + (0.3, 2, 3) + (2.7,) * 6 + (3, 3, 3, 3)
PLAN_THERE = (0, 0, 2, 10, 17, 17, 19, 26)
PLAN_FORCE = {9: 0, 12: 3, 25: 4}
PLAN_HALO, PLAN_HALO_TIME = 9, 12.3
PLAN_CORE, PLAN_LINK, PLAN_LATENCY, PLAN_ADD, PLAN_SLACK = 1.7, 20.0, 2.0, 0.9, 0.0


class Moves:
    def __init__(self, sems):
        self.sems, self.used = sems, 0

    def __call__(self, source, target):
        number, self.used = self.used, self.used + 1
        make = functools.partial(pltpu.make_async_copy, source, target, self.sems.at[number])
        make().start()
        return lambda: make().wait()


class Refs:
    pass


def run(plan, layout, *refs):
    s = Refs()
    for name, ref in zip(layout, refs):
        setattr(s, name, ref)
    rest = list(refs[len(layout) :])
    s.landing = [[rest.pop(0) for _ in range(1, plan.halvings)] for _ in range(CLASSES)]
    s.results = (s.sum_qkv, s.sum_proj, s.sum_fc1, s.sum_fc2)
    s.units = (s.units_zero, s.units_one)
    s.page = s.staged.at[pl.ds(0, s.plain.shape[0])]
    s.spread = s.qkv.at[pl.ds(0, s.in_spread.shape[0])]
    windows = s.x.shape[1] // LANES
    patches = s.dense.shape[0] // SPLITS
    half, half_rows = patches // 2, s.dense.shape[0] // 2
    padded = 16 * -(-half // 16)
    upper, lower = pl.ds(0, half_rows), pl.ds(half_rows, half_rows)
    reducer = Reducer(plan, s)
    move = Moves(s.move_sems)
    page, row = lax.axis_index(PAGE), lax.axis_index(ROW)
    count = lax.axis_size(ROW)
    above, below = (page, (row + count - 1) % count), (page, (row + 1) % count)

    def halo(number, source, target, device):
        make = functools.partial(
            pltpu.make_async_remote_copy,
            src_ref=source,
            dst_ref=target,
            send_sem=s.halo_sems.at[0, number],
            recv_sem=s.halo_sems.at[1, number],
            device_id=device,
            device_id_type=MESH,
        )
        make().start()
        return lambda: make().wait()

    tokens_there = move(s.in_tokens, s.tokens)
    places_there = (move(s.in_plain, s.plain), move(s.in_moved, s.moved))
    swaps_there = (move(s.in_swap_on, s.swap_on), move(s.in_swap_back, s.swap_back))
    spread_there = move(s.in_spread, s.spread)
    weights = ((s.in_qkv, s.w_qkv), (s.in_proj, s.w_proj), (s.in_fc1, s.w_fc1), (s.in_fc2, s.w_fc2))

    def fetch_weight(which, layer):
        source, target = weights[which]
        return move(source.at[layer], target)

    there = [fetch_weight(which, 0) for which in range(4)]

    barrier = pltpu.get_barrier_semaphore()
    devices = [plan.partner(0, level)[1] for level in range(plan.halvings)] + [above, below]
    for device in devices:
        pl.semaphore_signal(barrier, inc=1, device_id=device, device_id_type=MESH)

    s.live[...] = jnp.zeros(s.live.shape, F32)
    for window in range(windows):
        s.live[window : window + 1, :] = jnp.full((1, LANES), 1.0 - s.blank[0, window].astype(F32))
    s.page[...] = jnp.zeros(s.page.shape, F32)
    tokens_there()
    cols = s.tokens.shape[1]
    for line in range(WIN):
        s.page[pl.ds(line * cols, cols), :] = s.tokens[line].astype(F32)
    places_there[0]()
    to_channels(s.page, s.plain, s.x, True)
    saves = [move(s.x, s.kept_x)]
    spread_columns(s, 0)
    spread_there()
    spread_bias(s, 0)
    region_masks(False, s.regions)
    pl.semaphore_wait(barrier, len(devices))
    live_there = halo(0, s.live, s.live_upper, above)
    grad_there = halo(1, s.in_grad.at[upper], s.grad_upper, above)
    grad_lower_there = move(s.in_grad.at[lower], s.dense.at[lower])
    norm_one_forward(s, windows)
    saves.append(move(s.normed, s.kept_normed))
    there[QKV]()
    project_forward(s, windows)
    qkv_saved = move(s.qkv, s.kept_qkv)
    there[QKV] = fetch_weight(QKV, 1)
    attend_forward(s, windows, s.live)
    saves.append(move(s.soft, s.kept_soft))
    saves.append(move(s.merged, s.kept_merged))
    there[PROJ]()
    s.work[...] = mm(s.w_proj[...], s.merged[...], 0, 0)
    there[PROJ] = fetch_weight(PROJ, 1)
    norm_two_forward(s, windows, s.live)
    saves.append(move(s.hidden, s.kept_hidden))
    saves.append(move(s.second, s.kept_second))
    there[FC1]()
    there[FC2]()
    feed_forward(s, windows)
    saves.append(move(s.active, s.kept_active))
    saves.append(move(s.slope, s.kept_slope))
    there[FC1] = fetch_weight(FC1, 1)
    there[FC2] = fetch_weight(FC2, 1)
    to_dense(s.work, s.plain, s.dense.at[upper], padded)
    upper_there = halo(2, s.dense.at[upper], s.upper, above)

    qkv_saved()
    spread_there = move(s.in_spread, s.spread)
    places_there[1]()
    swaps_there[0]()
    saves.pop(0)()
    move_own(s.work, s.swap_on, s.x, windows, 0)
    spread_columns(s, 1)
    spread_there()
    spread_bias(s, 1)
    region_masks(True, s.regions)
    live_there()
    shifted_live(s, windows)
    grad_there()
    grad_lower_there()
    from_dense(s.grad_upper, s.page, 0)
    from_dense(s.dense.at[lower], s.page, half)
    to_channels(s.page, s.moved, s.grad)
    for saved in saves:
        saved()
    upper_there()
    from_dense(s.upper, s.page, 0)
    add_halo(s.page, s.moved, s.x, half, padded)
    norm_one_forward(s, windows)
    there[QKV]()
    project_forward(s, windows)
    attend_forward(s, windows, s.live_two)
    there[PROJ]()
    s.work[...] = mm(s.w_proj[...], s.merged[...], 0, 0)
    norm_two_forward(s, windows, s.live_two)
    there[FC1]()
    there[FC2]()
    feed_forward(s, windows)
    to_dense(s.work, s.moved, s.dense, s.moved.shape[0])
    out_there = halo(3, s.dense.at[upper], s.out_tokens.at[upper], below)
    out_kept = move(s.dense.at[lower], s.out_tokens.at[lower])

    spread_gains(s, 1)

    def backward(layer, live_ref, fetch, points):
        reducer.layer = layer
        first = 0 if layer else FEEDS
        feed_backward(s, reducer, points[:first])
        reducer.advance(points[first])
        fetch(0)
        norm_two_backward(s, windows, live_ref)
        reducer.advance(points[first + 1])
        fetch(1)
        merge_backward(s, reducer)
        reducer.advance(points[first + 2])
        fetch(2)
        attend_backward(s, windows, reducer, points[first + 3 :])
        fetch(3)

    back = {}

    def refill(point):
        if point == 0:
            back[0] = [move(s.kept_active, s.active), move(s.kept_slope, s.slope), move(s.kept_second, s.second)]
            back[0] += [fetch_weight(FC1, 0), fetch_weight(FC2, 0)]
        elif point == 1:
            back[1] = [move(s.kept_hidden, s.hidden)]
        elif point == 2:
            back[2] = [fetch_weight(PROJ, 0)]
        elif point == 3:
            back[2] += [move(s.kept_merged, s.merged)]
            back[3] = [move(s.kept_soft, s.soft)]
        elif point == 4:
            back[4] = [move(s.kept_x, s.x)]
        else:
            back[3] += [move(s.kept_qkv, s.qkv), move(s.kept_normed, s.normed), fetch_weight(QKV, 0)]

    def needed(point):
        if point in back:
            for arrived in back.pop(point):
                arrived()

    backward(1, s.live_two, refill, range(9))
    input_backward(s)
    norm_one_backward(s, windows)
    refill(4)
    out_there()
    to_dense(s.grad, s.moved, s.dense.at[upper], padded)
    next_there = halo(4, s.dense.at[upper], s.next_upper, below)
    reducer.advance(9)
    project_backward(s, reducer)
    spread_there = move(s.in_spread, s.spread)
    swaps_there[1]()
    move_own(s.grad, s.swap_back, s.work, windows, -1)
    reducer.settle(0)
    reducer.settle(1)
    reducer.advance(10)

    spread_there()
    small_gradients(s, s.small_own.at[1])
    refill(5)
    spread_gains(s, 0)
    reducer.advance(11)
    next_there()
    from_dense(s.next_upper, s.page, 0)
    s.grad[...] = s.work[...]
    add_halo(s.page, s.plain, s.grad, half, padded)
    reducer.advance(12)
    needed(0)

    def wait_next(point):
        needed(point + 1)

    backward(0, s.live, wait_next, range(13, 26))
    project_backward(s, reducer)
    input_backward(s)
    spread_there = move(s.in_spread, s.spread)
    reducer.settle(0)
    reducer.settle(1)
    reducer.advance(26)
    reducer.advance(27)
    needed(4)
    norm_one_backward(s, windows)
    out_kept()
    to_dense(s.grad, s.plain, s.dense, s.plain.shape[0])
    grad_kept = move(s.dense, s.grad_tokens)
    reducer.advance(28)
    spread_there()
    small_gradients(s, s.small_own.at[0])
    reducer.advance(29)
    finish_small(s, plan, row)
    grad_kept()


def finish_small(s, plan, row):
    total = s.small_parts.at[plan.halvings - 1]
    outs = (
        (s.d_ln_gain, (G1, G2)),
        (s.d_ln_bias, (B1, B2)),
        (s.d_qv_bias, (QB, VB)),
        (s.d_proj_bias, (PB,)),
        (s.d_fc1_bias, tuple(range(F1B, F1B + FEEDS))),
        (s.d_fc2_bias, (F2B,)),
    )
    for layer in range(2):
        s.d_table[layer] = total[layer, VECTOR_ROWS:, :OFFSETS]
        for ref, indices in outs:
            whole = jnp.concatenate([total[layer, index : index + 1, :] for index in indices], axis=1)
            size = ref.shape[1]
            mine = jnp.zeros((1, size), F32)
            for share in range(plan.shares):
                mine = jnp.where(row == share, whole[:, share * size : (share + 1) * size], mine)
            ref[layer : layer + 1, :] = mine


def placements(cols):
    windows = cols // WIN
    patches = WIN * cols
    padded = -(-patches // LANES) * LANES
    plain = np.zeros((padded, windows * LANES), np.float32)
    moved = np.zeros((padded, windows * LANES), np.float32)
    for line in range(WIN):
        for col in range(cols):
            source = line * cols + col
            plain[source, (col // WIN) * LANES + line * WIN + col % WIN] = 1
            new_line, new_col = (line - SHIFT) % WIN, (col - SHIFT) % cols
            moved[source, (new_col // WIN) * LANES + new_line * WIN + new_col % WIN] = 1
    return plain.astype(BF), moved.astype(BF)


def swaps():
    on = np.zeros((2 * LANES, LANES), np.float32)
    back = np.zeros((2 * LANES, LANES), np.float32)
    for line in range(SHIFT):
        for col in range(WIN):
            moved, plain = line * WIN + col, (line + SHIFT) * WIN + (col + SHIFT) % WIN
            on[plain + (LANES if col >= SHIFT else 0), moved] = 1
            back[moved + (LANES if col < SHIFT else 0), plain] = 1
    return on.astype(BF), back.astype(BF)


def table_spread():
    size = 2 * WIN - 1
    spread = np.zeros((WIN, 2 * LANES, TABLE), np.float32)
    for key_col in range(WIN):
        for offset in range(size):
            for col in range(WIN):
                spread[key_col, offset * WIN + col, offset * size + col - key_col + WIN - 1] = 1
    spread = spread.reshape(WIN // 2, 2, 2 * LANES, TABLE).swapaxes(1, 2)
    return spread.reshape(WIN * LANES, 2 * TABLE).astype(BF)


def copy_all(*refs):
    *refs, sems = refs
    count = len(refs) // 3
    sources, targets, held = refs[:count], refs[count : 2 * count], refs[2 * count :]
    ways = [*zip(sources, held), *zip(held, targets)]
    copies = [pltpu.make_async_copy(*way, sems.at[number]) for number, way in enumerate(ways)]
    for copy in copies[:count]:
        copy.start()
    for incoming, outgoing in zip(copies[:count], copies[count:]):
        incoming.wait()
        outgoing.start()
    for copy in copies[count:]:
        copy.wait()


def hand_out(values):
    anywhere = pl.BlockSpec(memory_space=pl.ANY)
    return pl.pallas_call(
        copy_all,
        out_shape=[jax.ShapeDtypeStruct(value.shape, value.dtype) for value in values],
        in_specs=[anywhere] * len(values),
        out_specs=[anywhere] * len(values),
        scratch_shapes=[pltpu.VMEM(value.shape, value.dtype) for value in values]
        + [pltpu.SemaphoreType.DMA((2 * len(values),))],
        compiler_params=pltpu.CompilerParams(vmem_limit_bytes=VMEM_LIMIT),
        name="results",
    )(*values)


def per_device(
    page_tokens,
    blank_mask,
    cotangent,
    ln_gain,
    ln_bias,
    qv_bias,
    rel_table,
    w_qkv,
    w_proj,
    proj_bias,
    w_fc1,
    fc1_bias,
    w_fc2,
    fc2_bias,
):
    pages, shares = lax.axis_size(PAGE), lax.axis_size(ROW)
    plan = Plan(pages, shares)
    cols = page_tokens.shape[2]
    windows, lanes = cols // WIN, cols // WIN * LANES
    dense = ((WIN * cols * SPLITS, LANES), F32)
    half_dense = ((WIN * cols * SPLITS // 2, LANES), F32)
    plain, moved = (jnp.asarray(place) for place in placements(cols))
    live_rows = 8 * -(-windows // 8)
    scalar_inputs = dict(blank=blank_mask[0])
    small_inputs = dict(
        table=rel_table,
        ln_gain=ln_gain,
        ln_bias=ln_bias,
        qv_bias=qv_bias,
        proj_bias=proj_bias,
        fc1_bias=fc1_bias,
        fc2_bias=fc2_bias,
    )
    large_inputs = dict(
        in_tokens=page_tokens[0],
        in_grad=cotangent.reshape(dense[0]),
        in_plain=plain,
        in_moved=moved,
        in_swap_on=jnp.asarray(swaps()[0]),
        in_swap_back=jnp.asarray(swaps()[1]),
        in_spread=jnp.asarray(table_spread()),
        in_qkv=w_qkv,
        in_proj=w_proj,
        in_fc1=w_fc1,
        in_fc2=w_fc2,
    )
    saved = dict(
        x=((D, lanes), F32),
        normed=((D, lanes), BF),
        qkv=((3 * D, lanes), BF),
        soft=((windows * HEADS, LANES, LANES), BF),
        merged=((D, lanes), BF),
        hidden=((D, lanes), F32),
        second=((D, lanes), BF),
        active=((FF, lanes), BF),
        slope=((FF, lanes), BF),
    )
    units = ((UNITS,) + plan.sizes[0][0], F32)
    large_outputs = dict(
        out_tokens=dense,
        grad_tokens=dense,
        sum_qkv=((2, D // shares, 3 * D), F32),
        sum_proj=((2, D // shares, D), F32),
        sum_fc1=((2, D // shares, FF), F32),
        sum_fc2=((2, FF // shares, D), F32),
        units_zero=units,
        units_one=units,
        kept_x=((D, lanes), F32),
        kept_normed=((D, lanes), BF),
        kept_qkv=((3 * D, lanes), BF),
        kept_soft=((windows * HEADS, LANES, LANES), BF),
        kept_merged=((D, lanes), BF),
        kept_hidden=((D, lanes), F32),
        kept_second=((D, lanes), BF),
        kept_active=((FF, lanes), BF),
        kept_slope=((FF, lanes), BF),
    )
    small_outputs = dict(
        d_ln_gain=((2, 2 * D // shares), F32),
        d_ln_bias=((2, 2 * D // shares), F32),
        d_qv_bias=((2, 2 * D // shares), F32),
        d_proj_bias=((2, D // shares), F32),
        d_fc1_bias=((2, FF // shares), F32),
        d_fc2_bias=((2, D // shares), F32),
        d_table=((2, HEADS, OFFSETS), F32),
    )
    small = (2, SMALL, D)
    vmem = dict(
        saved,
        tokens=((WIN, cols, D), BF),
        plain=(plain.shape, BF),
        moved=(moved.shape, BF),
        w_qkv=((D, 3 * D), BF),
        w_proj=((D, D), BF),
        w_fc1=((D, FF), BF),
        w_fc2=((FF, D), BF),
        dense=dense,
        upper=half_dense,
        swap_on=((2 * LANES, LANES), BF),
        swap_back=((2 * LANES, LANES), BF),
        grad_upper=half_dense,
        next_upper=half_dense,
        live_upper=((live_rows, LANES), F32),
        live_two=((live_rows, LANES), F32),
        work=((D, lanes), F32),
        grad=((D, lanes), F32),
        low=((D, lanes), BF),
        sums=((VECTORS, D, LANES), F32),
        gains=((2, D, LANES), F32),
        bias=((HEADS, LANES, LANES), F32),
        bias_rows=((HEADS * LANES, LANES), F32),
        regions=((2, LANES, LANES), F32),
        padded_table=((HEADS, TABLE), F32),
        live=((live_rows, LANES), F32),
        vector_rows=((VECTOR_ROWS, D), F32),
        staged=((2 * CHUNK, CHUNK), F32),
        done=((DONE * CLASSES, CHUNK // shares, CHUNK), F32),
        held=((HELD * CLASSES,) + plan.sizes[0][0], F32),
        first_landing=((RING * CLASSES,) + plan.sizes[0][0], F32),
        small_own=(small, F32),
        small_parts=((plan.halvings,) + small, F32),
    )
    semaphores = dict(
        move_sems=pltpu.SemaphoreType.DMA((48,)),
        halo_sems=pltpu.SemaphoreType.DMA((2, 5)),
        send_sems=pltpu.SemaphoreType.DMA((2 * UNITS, plan.phases)),
        recv_sems=pltpu.SemaphoreType.DMA((2 * UNITS, plan.phases)),
        own_sems=pltpu.SemaphoreType.DMA((2 * UNITS, 2)),
        stage_sems=pltpu.SemaphoreType.DMA((2, shares, 2)),
        first_sems=pltpu.SemaphoreType.DMA((2 * UNITS, shares)),
        first_free=pltpu.SemaphoreType.REGULAR((2 * UNITS,)),
        small_sems=pltpu.SemaphoreType.DMA((2, plan.halvings)),
        free_sems=pltpu.SemaphoreType.REGULAR((CLASSES, plan.halvings)),
    )
    landing = [((RING,) + size, F32) for sizes in plan.sizes for size in sizes[1:]]
    layout = [*scalar_inputs, *small_inputs, *large_inputs, *small_outputs, *large_outputs, *vmem, *semaphores]
    in_vmem, anywhere = pl.BlockSpec(memory_space=pltpu.VMEM), pl.BlockSpec(memory_space=pl.ANY)
    outputs = {**small_outputs, **large_outputs}
    results = pl.pallas_call(
        functools.partial(run, plan, layout),
        out_shape=[jax.ShapeDtypeStruct(*shape) for shape in outputs.values()],
        in_specs=[pl.BlockSpec(memory_space=pltpu.SMEM)] + [in_vmem] * len(small_inputs) + [anywhere] * len(large_inputs),
        out_specs=[in_vmem] * len(small_outputs) + [anywhere] * len(large_outputs),
        scratch_shapes=[pltpu.VMEM(*shape) for shape in vmem.values()]
        + list(semaphores.values())
        + [pltpu.VMEM(*shape) for shape in landing],
        compiler_params=pltpu.CompilerParams(
            vmem_limit_bytes=VMEM_LIMIT, collective_id=0, has_side_effects=True
        ),
        name="two_layers",
    )(*scalar_inputs.values(), *small_inputs.values(), *large_inputs.values())
    results = hand_out(results[: len(small_outputs) + 6])
    d_ln_gain, d_ln_bias, d_qv_bias, d_proj_bias, d_fc1_bias, d_fc2_bias, d_table = results[: len(small_outputs)]
    out_tokens, grad_tokens, sum_qkv, sum_proj, sum_fc1, sum_fc2 = results[len(small_outputs) :]
    return (
        out_tokens.reshape(cotangent.shape),
        grad_tokens.reshape(cotangent.shape),
        d_ln_gain,
        d_ln_bias,
        d_qv_bias,
        d_table,
        sum_qkv,
        sum_proj,
        d_proj_bias,
        sum_fc1,
        d_fc1_bias,
        sum_fc2,
        d_fc2_bias,
    )


def solution(mesh):
    tokens, by_row, shares = P(PAGE, ROW, None, None), P(None, ROW), P(None, ROW, None)
    return jax.shard_map(
        per_device,
        mesh=mesh,
        in_specs=(tokens, P(PAGE, ROW, None), tokens) + (P(),) * 11,
        out_specs=(tokens, tokens)
        + (by_row, by_row, by_row, P(), shares, shares, by_row, shares, by_row, shares, by_row),
        check_vma=False,
    )
```

```python
import functools

import jax
import jax.numpy as jnp
import numpy as np
from jax import lax
from jax.experimental import pallas as pl
from jax.experimental.pallas import tpu as pltpu
from jax.sharding import PartitionSpec as P

WIN = 10
SHIFT = 5
AREA = WIN * WIN
LANES = 128
D = 512
HEADS = 16
HEAD_DIM = 32
FF = 2048
CHUNK = 512
FEEDS = FF // CHUNK
SPLITS = D // LANES
EPSILON = 1e-05
MASK_VALUE = -100.0
NEVER = -1e30
SCORE_SCALE = HEAD_DIM ** (-0.5)
VMEM_LIMIT = 63 * 1024 * 1024 + 512 * 1024
BF = jnp.bfloat16
F32 = jnp.float32
MESH = pl.DeviceIdType.MESH
PAGE, ROW = "page", "row"

G1, B1, G2, B2, QB, VB, PB, F2B, F1B, VECTORS = 0, 1, 2, 3, 4, 5, 6, 7, 8, 12
VECTOR_ROWS = 16
SMALL = VECTOR_ROWS + HEADS
OFFSETS = (2 * WIN - 1) ** 2
TABLE = 384

UNIT_FC1, UNIT_FC2, UNIT_PROJ, UNIT_QKV, UNITS = 0, 4, 8, 9, 12
CLASSES = 3
GROUPS = UNITS // CLASSES
TRIPLES = 2 * GROUPS
HELD = 4
DONE = 5
RING = 3
QKV, PROJ, FC1, FC2 = range(4)
TARGETS = (
    ((FC1, 0, 0), (FC1, 0, 1), (FC1, 0, 2)),
    ((FC1, 0, 3), (FC2, 0, 0), (FC2, 1, 0)),
    ((FC2, 2, 0), (FC2, 3, 0), (PROJ, 0, 0)),
    ((QKV, 0, 0), (QKV, 0, 1), (QKV, 0, 2)),
)


def mm(left, right, left_dim, right_dim):
    return lax.dot_general(
        left, right, (((left_dim,), (right_dim,)), ((), ())), preferred_element_type=F32
    )


def split(values):
    high = values.astype(BF)
    return high, (values - high.astype(F32)).astype(BF)


def lane_tile(index):
    return pl.ds(pl.multiple_of(index * LANES, LANES), LANES)


def chunk_of(index):
    return pl.ds(pl.multiple_of(index * CHUNK, CHUNK), CHUNK)


def wide(column, count):
    return jnp.concatenate([column] * count, axis=1)


def fold(values):
    total = values[:, :LANES]
    for start in range(LANES, values.shape[1], LANES):
        total = total + values[:, start : start + LANES]
    return total


def norm_parts(values):
    center = values - jnp.sum(values, axis=0, keepdims=True) * (1.0 / D)
    spread = jnp.sum(center * center, axis=0, keepdims=True) * (1.0 / D)
    scale = lax.rsqrt(spread + EPSILON)
    return center * scale, scale


def norm_pull(grad, gain, hat, scale):
    scaled = grad * gain
    mean_one = jnp.sum(scaled, axis=0, keepdims=True) * (1.0 / D)
    mean_two = jnp.sum(scaled * hat, axis=0, keepdims=True) * (1.0 / D)
    return scale * (scaled - mean_one - hat * mean_two)


def gelu_parts(inner):
    step = 1.0 / (1.0 + (0.3275911 * 0.7071067811865476) * jnp.abs(inner))
    bell = jnp.exp(inner * inner * -0.5)
    poly = 0.5 * 1.061405429
    for factor in (-1.453152027, 1.421413741, -0.284496736, 0.254829592):
        poly = poly * step + 0.5 * factor
    tail = poly * step * bell
    below = jnp.where(inner >= 0, 1.0 - tail, tail)
    return inner * below, below + inner * bell * 0.3989422804014327


def to_channels(page_ref, place_ref, out_ref, exact=False):
    def step(index, carry):
        channels = pl.ds(pl.multiple_of(index * 256, 256), 256)
        values = page_ref[:, channels]
        if exact:
            out_ref[channels, :] = mm(values.astype(BF), place_ref[...], 0, 0)
        else:
            high, low = split(values)
            out_ref[channels, :] = mm(high, place_ref[...], 0, 0) + mm(low, place_ref[...], 0, 0)
        return carry

    lax.fori_loop(0, D // 256, step, 0, unroll=2)


def to_dense(values_ref, place_ref, dense_ref, padded):
    count = dense_ref.shape[0] // SPLITS
    for index in range(D // 256):
        high, low = split(values_ref[index * 256 : (index + 1) * 256, :])
        page = mm(place_ref[:padded, :], high, 1, 1) + mm(place_ref[:padded, :], low, 1, 1)
        for part in range(2):
            rows = pl.ds(2 * index + part, count, stride=SPLITS)
            dense_ref[rows, :] = page[:count, part * LANES : (part + 1) * LANES]


def from_dense(dense_ref, page_ref, row):
    count = dense_ref.shape[0] // SPLITS
    for part in range(SPLITS):
        rows = pl.ds(part, count, stride=SPLITS)
        page_ref[pl.ds(row, count), part * LANES : (part + 1) * LANES] = dense_ref[rows, :]


def add_halo(page_ref, place_ref, out_ref, count, padded):
    page_ref[pl.ds(count, padded - count), :] = jnp.zeros((padded - count, D), F32)

    def step(index, carry):
        channels = pl.ds(pl.multiple_of(index * 256, 256), 256)
        high, low = split(page_ref[:padded, channels])
        out_ref[channels, :] += mm(high, place_ref[:padded, :], 0, 0) + mm(low, place_ref[:padded, :], 0, 0)
        return carry

    lax.fori_loop(0, D // 256, step, 0, unroll=2)


def move_own(values_ref, swap_ref, out_ref, windows, first):
    for window in range(windows):
        sources = [(window + first + part) % windows * LANES for part in range(2)]
        values = jnp.concatenate([values_ref[:, start : start + LANES] for start in sources], axis=1)
        high, low = split(values)
        target = slice(window * LANES, (window + 1) * LANES)
        out_ref[:, target] = mm(high, swap_ref[...], 1, 0) + mm(low, swap_ref[...], 1, 0)


def vector_rows(s, layer):
    rows = s.vector_rows
    sources = ((G1, s.ln_gain, 0), (B1, s.ln_bias, 0), (G2, s.ln_gain, 1), (B2, s.ln_bias, 1))
    sources += ((QB, s.qv_bias, 0), (VB, s.qv_bias, 1), (PB, s.proj_bias, 0), (F2B, s.fc2_bias, 0))
    sources += tuple((F1B + part, s.fc1_bias, part) for part in range(FEEDS))
    for index, source, part in sources:
        rows[index : index + 1, :] = source[layer : layer + 1, part * D : (part + 1) * D]
    rows[VECTORS:, :] = jnp.zeros((VECTOR_ROWS - VECTORS, D), F32)
    return rows[...].T


def spread_columns(s, layer):
    columns = vector_rows(s, layer)
    for index in range(VECTORS):
        s.sums[index] = jnp.broadcast_to(columns[:, index : index + 1], (D, LANES))


def spread_gains(s, layer):
    columns = vector_rows(s, layer)
    for index, vector in enumerate((G1, G2)):
        s.gains[index] = jnp.broadcast_to(columns[:, vector : vector + 1], (D, LANES))


def spread_part(col):
    rows, lanes = (col // 2) * 2 * LANES, (col % 2) * TABLE
    return slice(rows, rows + 2 * LANES), slice(lanes, lanes + TABLE)


def spread_bias(s, layer):
    spread_ref, rows_ref, bias_ref = s.spread, s.bias_rows, s.bias
    s.padded_table[...] = jnp.zeros(s.padded_table.shape, F32)
    s.padded_table[:, :OFFSETS] = s.table[layer]
    high, low = split(s.padded_table[...])
    parts = []
    for col in range(WIN):
        chosen = spread_ref[spread_part(col)]
        parts.append(mm(high, chosen, 1, 1) + mm(low, chosen, 1, 1))
    source = jnp.concatenate(parts, axis=0)
    rows_ref[...] = jnp.zeros(rows_ref.shape, F32)
    for row in range(WIN):
        shift = (WIN - 1 - row) * WIN
        moved = source if shift == 0 else pltpu.roll(source, 2 * LANES - shift, axis=1)
        rows_ref[pl.ds(row * WIN * HEADS, WIN * HEADS), :] = moved[:, :LANES]
    for head in range(HEADS):
        bias_ref[head] = rows_ref[pl.ds(head, LANES, stride=HEADS), :]


def gather_bias(grad_ref, spread_ref, rows_ref):
    for head in range(HEADS):
        rows_ref[pl.ds(head, LANES, stride=HEADS), :] = grad_ref[head]
    total = jnp.zeros((WIN * HEADS, 2 * LANES), F32)
    for row in range(WIN):
        shift = (WIN - 1 - row) * WIN
        piece = rows_ref[pl.ds(row * WIN * HEADS, WIN * HEADS), :]
        piece = jnp.concatenate([piece, jnp.zeros_like(piece)], axis=1)
        total = total + (piece if shift == 0 else pltpu.roll(piece, shift, axis=1))
    table = jnp.zeros((HEADS, TABLE), F32)
    for col in range(WIN):
        for part in split(total[col * HEADS : (col + 1) * HEADS]):
            table = table + mm(part, spread_ref[spread_part(col)], 1, 0)
    return table


def region_masks(shifted_layer, out_ref):
    key = lax.broadcasted_iota(jnp.int32, (LANES, LANES), 0)
    query = lax.broadcasted_iota(jnp.int32, (LANES, LANES), 1)
    padding = jnp.where(key < AREA, 0.0, NEVER)
    out_ref[0] = padding
    out_ref[1] = padding
    if shifted_layer:
        last = lax.axis_index(ROW) == lax.axis_size(ROW) - 1
        rows_differ = ((key >= AREA // 2) != (query >= AREA // 2)) & last
        cols_differ = (key % WIN >= SHIFT) != (query % WIN >= SHIFT)
        out_ref[0] += jnp.where(rows_differ, MASK_VALUE, 0.0)
        out_ref[1] += jnp.where(rows_differ | cols_differ, MASK_VALUE, 0.0)


def shifted_live(s, windows):
    place = lax.broadcasted_iota(jnp.int32, (1, LANES), 1)
    for window in range(windows):
        here, after = slice(window, window + 1), slice((window + 1) % windows, (window + 1) % windows + 1)
        beyond = place % WIN >= SHIFT
        own = jnp.where(beyond, s.live[after, :], s.live[here, :])
        upper = jnp.where(beyond, s.live_upper[after, :], s.live_upper[here, :])
        s.live_two[here, :] = jnp.where(place >= AREA // 2, upper, own)


def head_rows(head, base=0):
    return pl.ds(base + head * HEAD_DIM, HEAD_DIM)


def norm_one_forward(s, windows):
    def step(index, carry):
        lanes = lane_tile(index)
        hat, _ = norm_parts(s.x[:, lanes])
        s.normed[:, lanes] = (hat * s.sums[G1] + s.sums[B1]).astype(BF)
        return carry

    lax.fori_loop(0, windows, step, 0, unroll=3)


def project_forward(s, windows):
    def step(index, carry):
        rows = chunk_of(index)
        bias = s.sums[jnp.where(index == 0, QB, VB)] * jnp.where(index == 1, 0.0, 1.0)
        out = mm(s.w_qkv[:, rows], s.normed[...], 0, 0)
        s.qkv[rows, :] = (out + wide(bias, windows)).astype(BF)
        return carry

    lax.fori_loop(0, 3, step, 0)


def attend_forward(s, windows, live_ref):
    def step(index, carry):
        lanes = lane_tile(index)
        live = jnp.broadcast_to(live_ref[pl.ds(index, 1), :], (LANES, LANES)).T
        masked = s.regions[jnp.where(index == windows - 1, 1, 0)] + MASK_VALUE * (1.0 - live)
        for head in range(HEADS):
            query = s.qkv[head_rows(head), lanes]
            key = s.qkv[head_rows(head, D), lanes]
            value = s.qkv[head_rows(head, 2 * D), lanes]
            scores = mm(key, query, 0, 0) * SCORE_SCALE + (s.bias[head] + masked)
            exponent = jnp.exp(scores - jnp.max(scores, axis=0, keepdims=True))
            total = jnp.sum(exponent, axis=0, keepdims=True)
            soft = (exponent * (1.0 / total)).astype(BF)
            s.soft[index * HEADS + head] = soft
            s.merged[head_rows(head), lanes] = mm(value, soft, 1, 0).astype(BF)
        return carry

    lax.fori_loop(0, windows, step, 0, unroll=2)


def norm_two_forward(s, windows, live_ref):
    def step(index, carry):
        lanes = lane_tile(index)
        hidden = s.x[:, lanes] + live_ref[pl.ds(index, 1), :] * (s.work[:, lanes] + s.sums[PB])
        s.hidden[:, lanes] = hidden
        s.work[:, lanes] = hidden + s.sums[F2B]
        hat, _ = norm_parts(hidden)
        s.second[:, lanes] = (hat * s.sums[G2] + s.sums[B2]).astype(BF)
        return carry

    lax.fori_loop(0, windows, step, 0, unroll=3)


def feed_forward(s, windows):
    def step(index, carry):
        rows = chunk_of(index)
        inner = mm(s.w_fc1[:, rows], s.second[...], 0, 0) + wide(s.sums[F1B + index], windows)
        active, slope = gelu_parts(inner)
        active = active.astype(BF)
        s.active[rows, :] = active
        s.slope[rows, :] = slope.astype(BF)
        s.work[...] += mm(s.w_fc2[rows, :], active, 0, 0)
        return carry

    lax.fori_loop(0, FEEDS, step, 0)


def feed_backward(s, sink, times):
    s.sums[...] = jnp.zeros(s.sums.shape, F32)
    s.bias[...] = jnp.zeros(s.bias.shape, F32)
    lowered = s.grad[...].astype(BF)
    s.low[...] = lowered
    s.sums[F2B] = fold(lowered.astype(F32))
    s.work[...] = jnp.zeros(s.work.shape, F32)

    claims = sink.layer == 0
    if claims:
        for unit in range(UNIT_FC2, UNIT_FC2 + FEEDS):
            sink.claim(unit)

    def step(index, carry):
        rows = chunk_of(index)
        if claims:
            sink.claim(UNIT_FC1 + index)
        sink.put(0, mm(s.active[rows, :], s.low[...], 1, 1), feed_pieces(index, sink.shares), index == 0)
        grad_inner = mm(s.w_fc2[rows, :], s.low[...], 1, 0) * s.slope[rows, :].astype(F32)
        grad_inner = grad_inner.astype(BF)
        s.sums[F1B + index] = fold(grad_inner.astype(F32))
        sink.put(1, mm(s.second[...], grad_inner, 1, 1), row_pieces(UNIT_FC1 + index, sink.shares), index == 0)
        s.work[...] += mm(s.w_fc1[:, rows], grad_inner, 1, 0)
        sink.advance_at(index, times)
        return carry

    lax.fori_loop(0, FEEDS, step, 0)
    sink.settle(0)
    sink.settle(1)


def norm_two_backward(s, windows, live_ref):
    def step(index, carry):
        lanes = lane_tile(index)
        hat, scale = norm_parts(s.hidden[:, lanes])
        grad = s.work[:, lanes]
        s.sums[G2] += grad * hat
        s.sums[B2] += grad
        grad = s.grad[:, lanes] + norm_pull(grad, s.gains[1], hat, scale)
        s.grad[:, lanes] = grad
        grad_low = (grad * live_ref[pl.ds(index, 1), :]).astype(BF)
        s.low[:, lanes] = grad_low
        s.sums[PB] += grad_low.astype(F32)
        return carry

    lax.fori_loop(0, windows, step, 0, unroll=3)


def merge_backward(s, sink):
    if sink.layer == 0:
        sink.claim(UNIT_PROJ)
    sink.put(0, mm(s.merged[...], s.low[...], 1, 1), row_pieces(UNIT_PROJ, sink.shares), True)
    s.merged[...] = mm(s.w_proj[...], s.low[...], 1, 0).astype(BF)
    sink.settle(0)


def attend_backward(s, windows, sink, times):
    def step(index, carry):
        lanes = lane_tile(index)
        for head in range(HEADS):
            query = s.qkv[head_rows(head), lanes]
            key = s.qkv[head_rows(head, D), lanes]
            value = s.qkv[head_rows(head, 2 * D), lanes]
            grad_out = s.merged[head_rows(head), lanes]
            soft_low = s.soft[index * HEADS + head]
            soft = soft_low.astype(F32)
            grad_soft = mm(value, grad_out, 0, 0)
            inner = jnp.sum(soft * grad_soft, axis=0, keepdims=True)
            grad_scores = (soft * (grad_soft - inner)).astype(BF)
            s.bias[head] += grad_scores.astype(F32)
            grad_query = (mm(key, grad_scores, 1, 0) * SCORE_SCALE).astype(BF)
            grad_key = (mm(query, grad_scores, 1, 1) * SCORE_SCALE).astype(BF)
            grad_value = mm(grad_out, soft_low, 1, 1).astype(BF)
            s.qkv[head_rows(head), lanes] = grad_query
            s.qkv[head_rows(head, D), lanes] = grad_key
            s.qkv[head_rows(head, 2 * D), lanes] = grad_value
            s.sums[QB, head_rows(head), :] += grad_query.astype(F32)
            s.sums[VB, head_rows(head), :] += grad_value.astype(F32)
        sink.advance_at(index, times)
        return carry

    lax.fori_loop(0, windows, step, 0)


def project_backward(s, sink):
    def step(index, carry):
        rows = chunk_of(index)
        sink.claim(UNIT_QKV + index)
        sink.put(index % 2, mm(s.normed[...], s.qkv[rows, :], 1, 1), row_pieces(UNIT_QKV + index, sink.shares), index < 2)
        return carry

    lax.fori_loop(0, 3, step, 0)


def input_backward(s):
    s.work[...] = mm(s.w_qkv[...], s.qkv[...], 1, 0)


def norm_one_backward(s, windows):
    def step(index, carry):
        lanes = lane_tile(index)
        hat, scale = norm_parts(s.x[:, lanes])
        grad = s.work[:, lanes]
        s.sums[G1] += grad * hat
        s.sums[B1] += grad
        s.grad[:, lanes] += norm_pull(grad, s.gains[0], hat, scale)
        return carry

    lax.fori_loop(0, windows, step, 0, unroll=3)


def small_gradients(s, small_ref):
    places = lax.broadcasted_iota(jnp.int32, (D, LANES), 1)
    packed = jnp.zeros((D, LANES), F32)
    for index in range(VECTORS):
        packed = jnp.where(places == index, jnp.sum(s.sums[index], axis=1, keepdims=True), packed)
    small_ref[:VECTOR_ROWS, :] = packed.T[:VECTOR_ROWS]
    table = gather_bias(s.bias, s.spread, s.bias_rows)
    small_ref[VECTOR_ROWS:, :] = jnp.concatenate([table, jnp.zeros((HEADS, D - TABLE), F32)], axis=1)


def reversed_bits(value, count):
    turned = 0
    for bit in range(count):
        turned = turned * 2 + (value // 2**bit) % 2
    return turned


def row_pieces(unit, shares):
    rows, count = CHUNK // shares, shares.bit_length() - 1
    return [(share * rows, unit, reversed_bits(share, count)) for share in range(shares)]


def feed_pieces(index, shares):
    rows, count = CHUNK // shares, shares.bit_length() - 1
    pieces = []
    for share in range(shares // FEEDS):
        place = reversed_bits(index * (shares // FEEDS) + share, count)
        for part in range(FEEDS):
            pieces.append(((share * FEEDS + part) * rows, UNIT_FC2 + part, place))
    return pieces


class Plan:
    def __init__(self, pages, shares):
        self.shares, self.rows = shares, CHUNK // shares
        page_bits, row_bits = pages.bit_length() - 1, shares.bit_length() - 1
        others = page_bits - 1
        self.steps = []
        for kind in range(CLASSES):
            turn = kind % 2
            page = [(PAGE, 2 ** (1 + (bit + turn) % others)) for bit in range(others)]
            row = [(ROW, 2**bit) for bit in range(row_bits)]
            self.steps.append([(PAGE, 1)] + (row + page if kind == 2 else page + row))
        self.page_steps = [[0] + [at for at, step in enumerate(steps) if at and step[0] == PAGE] for steps in self.steps]
        self.halvings = page_bits + row_bits
        self.phases = self.halvings + page_bits
        self.sizes, self.axes = [], []
        for steps in self.steps:
            size, sizes, axes = [shares, self.rows, CHUNK], [], []
            for axis, _ in steps:
                axes.append(0 if axis == ROW else 1 if size[1] >= 16 else 2)
                size[axes[-1]] //= 2
                sizes.append(tuple(size))
            self.sizes.append(sizes)
            self.axes.append(axes)
        self.steps_at = self.schedule()

    def schedule(self):
        small = TRIPLES
        free, ready, stage_of, plan, now = {}, {}, {}, [], 0.0
        for triple in range(TRIPLES):
            for kind in range(CLASSES):
                stage_of[triple, kind] = 0
        stage_of[small, 0] = 0

        def link(key, phase):
            triple, kind = key
            if phase < self.halvings:
                axis, stride = self.steps[kind][phase]
                size = 2.0**-phase / 2 if triple != small else 0.125
            else:
                axis, stride = self.steps[kind][self.page_steps[kind][self.phases - 1 - phase]]
                size = 2.0 ** (phase - 2 * self.halvings)
            if axis == PAGE and stride == 1:
                return 0, size * PLAN_CORE
            return (axis, stride if axis == PAGE else 0), size * PLAN_LINK * (1.0 if stride == 1 or axis == PAGE else 1.5)

        def last_stage(key):
            return self.halvings if key[0] == small else self.phases + 1

        def allowed(key, point):
            triple, kind = key
            stage = stage_of[key]
            if stage > last_stage(key):
                return False
            if triple == small:
                return point >= len(PLAN_POINTS) - 1
            if stage == 0 and point < PLAN_THERE[triple]:
                return False
            if triple > 0 and stage_of[triple - 1, kind] <= stage:
                return False
            if triple >= RING and stage < self.halvings and stage_of[triple - RING, kind] <= stage + 1:
                return False
            if stage == 0 and triple >= DONE and stage_of[triple - DONE, kind] <= self.phases + 1:
                return False
            return not (stage == 0 and triple >= HELD and stage_of[triple - HELD, kind] <= self.halvings + 1)

        for point, work in enumerate(PLAN_POINTS):
            now += work
            if point == PLAN_HALO:
                free[ROW, 0] = max(now, free.get((ROW, 0), 0.0)) + PLAN_HALO_TIME
            steps, final = [], point == len(PLAN_POINTS) - 1
            while True:
                keys = [key for key in stage_of if allowed(key, point)]
                needed = PLAN_FORCE.get(point, -1)
                keys = [
                    key
                    for key in keys
                    if final or ready.get(key, 0.0) <= now + PLAN_SLACK or (key[0] <= needed and stage_of[key] <= 1)
                ]
                if not keys:
                    break
                key = min(keys, key=lambda key: (max(ready.get(key, 0.0), now), -stage_of[key], key))
                stage = stage_of[key]
                now = max(now, ready.get(key, 0.0)) + (PLAN_ADD * 2.0**-stage if stage else 0.0)
                if stage == self.phases:
                    ready[key] = now + PLAN_LATENCY
                elif stage < last_stage(key):
                    name, length = link(key, stage)
                    free[name] = max(now, free.get(name, 0.0)) + length
                    ready[key] = free[name] + PLAN_LATENCY
                steps.append((*key, stage))
                stage_of[key] += 1
            plan.append(steps)
        assert all(stage_of[key] > last_stage(key) for key in stage_of)
        return plan

    def partner(self, kind, level):
        axis, stride = self.steps[kind][level]
        page, row = lax.axis_index(PAGE), lax.axis_index(ROW)
        mine = page if axis == PAGE else row
        bit = (mine // stride) % 2
        other = mine + (1 - 2 * bit) * stride
        return bit, ((other, row) if axis == PAGE else (page, other))

    def part(self, kind, level, sent=False):
        starts, sizes = [0, 0, 0], list(self.sizes[kind][0])
        for at in range(1, level + 1):
            axis = self.axes[kind][at]
            sizes[axis] //= 2
            bit, _ = self.partner(kind, at)
            which = 1 - bit if sent and at == level else bit
            starts[axis] = starts[axis] + which * sizes[axis]
        return (
            pl.ds(starts[0], sizes[0]),
            pl.ds(pl.multiple_of(starts[1], 8), sizes[1]),
            pl.ds(pl.multiple_of(starts[2], LANES), sizes[2]),
        )

    def place(self, kind, count):
        starts, sizes = [0, 0], [self.rows, CHUNK]
        for at in self.page_steps[kind][:count]:
            axis = self.axes[kind][at] - 1
            sizes[axis] //= 2
            bit, _ = self.partner(kind, at)
            starts[axis] = starts[axis] + bit * sizes[axis]
        return starts, sizes


class Reducer:
    def __init__(self, plan, s):
        self.plan, self.s = plan, s
        self.shares = plan.shares
        self.layer = 1

    def stage_copies(self, slot, pieces):
        s, plan = self.s, self.plan
        bit, device = plan.partner(0, 0)
        rows = plan.rows // 2
        copies = []
        for number, (start, unit, place) in enumerate(pieces):
            start = slot * CHUNK + start
            number_sems = s.stage_sems.at[slot, number]
            overall = self.first_unit() + unit
            sent = pltpu.make_async_remote_copy(
                src_ref=s.staged.at[pl.ds(pl.multiple_of(start + (1 - bit) * rows, 8), rows)],
                dst_ref=s.first_landing.at[overall % (RING * CLASSES), place],
                send_sem=number_sems.at[0],
                recv_sem=s.first_sems.at[overall, place],
                device_id=device,
                device_id_type=MESH,
            )
            kept = pltpu.make_async_copy(
                s.staged.at[pl.ds(pl.multiple_of(start + bit * rows, 8), rows)],
                s.units[self.layer].at[unit, place],
                number_sems.at[1],
            )
            copies.append((sent, kept))
        return copies

    def first_unit(self):
        return UNITS * (1 - self.layer)

    def claim(self, unit):
        pl.semaphore_wait(self.s.first_free.at[self.first_unit() + unit], 1)

    def put(self, slot, grad, pieces, first):
        if first is not True:

            @pl.when(jnp.logical_not(first))
            def _():
                self.settle(slot)

        self.s.staged[pl.ds(pl.multiple_of(slot * CHUNK, CHUNK), CHUNK), :] = grad
        for sent, kept in self.stage_copies(slot, pieces):
            sent.start()
            kept.start()

    def settle(self, slot):
        for sent, kept in self.stage_copies(slot, row_pieces(0, self.shares)):
            sent.wait_send()
            kept.wait()

    def first_arrived(self, triple, kind):
        s, unit = self.s, CLASSES * triple + kind
        landed = s.first_landing.at[unit % (RING * CLASSES)]
        _, device = self.plan.partner(0, 0)
        for place in range(self.shares):
            pltpu.make_async_remote_copy(
                src_ref=landed.at[place],
                dst_ref=landed.at[place],
                send_sem=s.first_sems.at[unit, place],
                recv_sem=s.first_sems.at[unit, place],
                device_id=device,
                device_id_type=MESH,
            ).wait_recv()

    def remote(self, source, target, unit, phase, device):
        return pltpu.make_async_remote_copy(
            src_ref=source,
            dst_ref=target,
            send_sem=self.s.send_sems.at[unit, phase],
            recv_sem=self.s.recv_sems.at[unit, phase],
            device_id=device,
            device_id_type=MESH,
        )

    def held(self, triple, kind):
        return self.s.held.at[CLASSES * (triple % HELD) + kind]

    def landed(self, triple, kind, level):
        if level == 0:
            return self.s.first_landing.at[(CLASSES * triple + kind) % (RING * CLASSES)]
        return self.s.landing[kind][level - 1].at[triple % RING]

    def halving(self, triple, kind, level):
        _, device = self.plan.partner(kind, level)
        source = self.held(triple, kind).at[self.plan.part(kind, level, True)]
        return self.remote(source, self.landed(triple, kind, level), CLASSES * triple + kind, level, device)

    def own_half(self, triple, kind):
        source = self.s.units[1 - triple // GROUPS].at[CLASSES * (triple % GROUPS) + kind]
        sem = self.s.own_sems.at[CLASSES * triple + kind, 0]
        return pltpu.make_async_copy(source, self.held(triple, kind), sem)

    def finished(self, triple, kind):
        return self.held(triple, kind).at[self.plan.part(kind, self.plan.halvings - 1)].at[0]

    def done(self, triple, kind, count):
        starts, sizes = self.plan.place(kind, count)
        return self.s.done.at[
            CLASSES * (triple % DONE) + kind,
            pl.ds(pl.multiple_of(starts[0], 8), sizes[0]),
            pl.ds(pl.multiple_of(starts[1], LANES), sizes[1]),
        ]

    def gathering(self, triple, kind, phase):
        plan = self.plan
        count = len(plan.page_steps[kind]) - (phase - plan.halvings)
        part = self.done(triple, kind, count)
        _, device = plan.partner(kind, plan.page_steps[kind][count - 1])
        return self.remote(part, part, CLASSES * triple + kind, phase, device)

    def result(self, triple, kind):
        which, row_block, col_block = TARGETS[triple % GROUPS][kind]
        rows = self.plan.rows
        target = self.s.results[which].at[
            1 - triple // GROUPS, pl.ds(row_block * rows, rows), pl.ds(col_block * CHUNK, CHUNK)
        ]
        sem = self.s.own_sems.at[CLASSES * triple + kind, 1]
        return pltpu.make_async_copy(self.done(triple, kind, 0), target, sem)

    def start(self, triple, kind, phase):
        plan = self.plan
        if phase == 0:
            self.own_half(triple, kind).start()
        elif phase < plan.halvings:
            if triple >= RING:
                pl.semaphore_wait(self.s.free_sems.at[kind, phase], 1)
            self.halving(triple, kind, phase).start()
        elif phase < plan.phases:
            if phase == plan.halvings:
                self.done(triple, kind, len(plan.page_steps[kind]))[...] = self.finished(triple, kind)[...]
            self.gathering(triple, kind, phase).start()
        elif phase == plan.phases:
            self.result(triple, kind).start()

    def arrive(self, triple, kind, phase):
        plan = self.plan
        if phase == 0:
            self.first_arrived(triple, kind)
            self.own_half(triple, kind).wait()
        elif phase < plan.halvings:
            self.halving(triple, kind, phase).wait()
        elif phase < plan.phases:
            self.gathering(triple, kind, phase).wait()
        else:
            self.result(triple, kind).wait()

    def take_in(self, triple, kind, phase):
        plan, s = self.plan, self.s
        if phase >= plan.halvings:
            return
        landed = self.landed(triple, kind, phase)
        kept = self.held(triple, kind).at[plan.part(kind, phase)]
        for share in range(landed.shape[0]):
            kept[share] += landed[share]
        if triple < TRIPLES - RING:
            _, device = plan.partner(kind, phase)
            free = s.free_sems.at[kind, phase]
            if phase == 0:
                free = s.first_free.at[CLASSES * (triple + RING) + kind]
            pl.semaphore_signal(free, inc=1, device_id=device, device_id_type=MESH)

    def advance(self, point):
        steps, last = self.plan.steps_at[point], point == len(self.plan.steps_at) - 1
        groups = []
        for step in steps:
            fits = groups and len(groups[-1]) < (3 if last else 6) and step[0] != TRIPLES != groups[-1][0][0]
            if fits and last:
                fits = step[2] == groups[-1][0][2]
            if fits and all(step[:2] != other[:2] for other in groups[-1]):
                groups[-1].append(step)
            else:
                groups.append([step])
        for group in groups:
            if group[0][0] == TRIPLES:
                self.small_step(group[0][2] - 1)
                continue
            for act in (self.arrive, self.take_in):
                for triple, kind, stage in group:
                    if stage > 0:
                        act(triple, kind, stage - 1)
            for triple, kind, stage in group:
                self.start(triple, kind, stage)

    def advance_at(self, index, points):
        for number, point in enumerate(points):
            if self.plan.steps_at[point]:

                @pl.when(index == number)
                def _(point=point):
                    self.advance(point)

    def small_copy(self, phase):
        s = self.s
        _, device = self.plan.partner(0, phase)
        return pltpu.make_async_remote_copy(
            src_ref=s.small_own if phase == 0 else s.small_parts.at[phase - 1],
            dst_ref=s.small_parts.at[phase],
            send_sem=s.small_sems.at[0, phase],
            recv_sem=s.small_sems.at[1, phase],
            device_id=device,
            device_id_type=MESH,
        )

    def small_step(self, phase):
        s = self.s
        if phase >= 0:
            self.small_copy(phase).wait()
            s.small_parts[phase] += s.small_own[...] if phase == 0 else s.small_parts[phase - 1]
        if phase + 1 < self.plan.halvings:
            self.small_copy(phase + 1).start()


PLAN_POINTS = (0, 2, 3) + (2.7,) * 6 + (5.2, 3, 3, 6) + (3.2,) * 4 + (0.3, 2, 3) + (2.7,) * 6 + (3, 3, 3, 3)
PLAN_THERE = (0, 0, 2, 10, 17, 17, 19, 26)
PLAN_FORCE = {9: 0, 12: 3, 25: 4}
PLAN_HALO, PLAN_HALO_TIME = 9, 12.3
PLAN_CORE, PLAN_LINK, PLAN_LATENCY, PLAN_ADD, PLAN_SLACK = 1.7, 20.0, 2.0, 0.9, 0.0


class Moves:
    def __init__(self, sems):
        self.sems, self.used = sems, 0

    def __call__(self, source, target):
        number, self.used = self.used, self.used + 1
        make = functools.partial(pltpu.make_async_copy, source, target, self.sems.at[number])
        make().start()
        return lambda: make().wait()


class Refs:
    pass


def run(plan, layout, *refs):
    s = Refs()
    for name, ref in zip(layout, refs):
        setattr(s, name, ref)
    rest = list(refs[len(layout) :])
    s.landing = [[rest.pop(0) for _ in range(1, plan.halvings)] for _ in range(CLASSES)]
    s.results = (s.sum_qkv, s.sum_proj, s.sum_fc1, s.sum_fc2)
    s.units = (s.units_zero, s.units_one)
    s.page = s.staged.at[pl.ds(0, s.plain.shape[0])]
    s.spread = s.qkv.at[pl.ds(0, s.in_spread.shape[0])]
    windows = s.x.shape[1] // LANES
    patches = s.dense.shape[0] // SPLITS
    half, half_rows = patches // 2, s.dense.shape[0] // 2
    padded = 16 * -(-half // 16)
    upper, lower = pl.ds(0, half_rows), pl.ds(half_rows, half_rows)
    reducer = Reducer(plan, s)
    move = Moves(s.move_sems)
    page, row = lax.axis_index(PAGE), lax.axis_index(ROW)
    count = lax.axis_size(ROW)
    above, below = (page, (row + count - 1) % count), (page, (row + 1) % count)

    def halo(number, source, target, device):
        make = functools.partial(
            pltpu.make_async_remote_copy,
            src_ref=source,
            dst_ref=target,
            send_sem=s.halo_sems.at[0, number],
            recv_sem=s.halo_sems.at[1, number],
            device_id=device,
            device_id_type=MESH,
        )
        make().start()
        return lambda: make().wait()

    tokens_there = move(s.in_tokens, s.tokens)
    places_there = (move(s.in_plain, s.plain), move(s.in_moved, s.moved))
    swaps_there = (move(s.in_swap_on, s.swap_on), move(s.in_swap_back, s.swap_back))
    spread_there = move(s.in_spread, s.spread)
    weights = ((s.in_qkv, s.w_qkv), (s.in_proj, s.w_proj), (s.in_fc1, s.w_fc1), (s.in_fc2, s.w_fc2))

    def fetch_weight(which, layer):
        source, target = weights[which]
        return move(source.at[layer], target)

    there = [fetch_weight(which, 0) for which in range(4)]

    barrier = pltpu.get_barrier_semaphore()
    devices = [plan.partner(0, level)[1] for level in range(plan.halvings)] + [above, below]
    for device in devices:
        pl.semaphore_signal(barrier, inc=1, device_id=device, device_id_type=MESH)

    s.live[...] = jnp.zeros(s.live.shape, F32)
    for window in range(windows):
        s.live[window : window + 1, :] = jnp.full((1, LANES), 1.0 - s.blank[0, window].astype(F32))
    s.page[...] = jnp.zeros(s.page.shape, F32)
    tokens_there()
    cols = s.tokens.shape[1]
    for line in range(WIN):
        s.page[pl.ds(line * cols, cols), :] = s.tokens[line].astype(F32)
    places_there[0]()
    to_channels(s.page, s.plain, s.x, True)
    saves = [move(s.x, s.kept_x)]
    spread_columns(s, 0)
    spread_there()
    spread_bias(s, 0)
    region_masks(False, s.regions)
    pl.semaphore_wait(barrier, len(devices))
    live_there = halo(0, s.live, s.live_upper, above)
    grad_there = halo(1, s.in_grad.at[upper], s.grad_upper, above)
    grad_lower_there = move(s.in_grad.at[lower], s.dense.at[lower])
    norm_one_forward(s, windows)
    saves.append(move(s.normed, s.kept_normed))
    there[QKV]()
    project_forward(s, windows)
    qkv_saved = move(s.qkv, s.kept_qkv)
    there[QKV] = fetch_weight(QKV, 1)
    attend_forward(s, windows, s.live)
    saves.append(move(s.soft, s.kept_soft))
    saves.append(move(s.merged, s.kept_merged))
    there[PROJ]()
    s.work[...] = mm(s.w_proj[...], s.merged[...], 0, 0)
    there[PROJ] = fetch_weight(PROJ, 1)
    norm_two_forward(s, windows, s.live)
    saves.append(move(s.hidden, s.kept_hidden))
    saves.append(move(s.second, s.kept_second))
    there[FC1]()
    there[FC2]()
    feed_forward(s, windows)
    saves.append(move(s.active, s.kept_active))
    saves.append(move(s.slope, s.kept_slope))
    there[FC1] = fetch_weight(FC1, 1)
    there[FC2] = fetch_weight(FC2, 1)
    to_dense(s.work, s.plain, s.dense.at[upper], padded)
    upper_there = halo(2, s.dense.at[upper], s.upper, above)

    qkv_saved()
    spread_there = move(s.in_spread, s.spread)
    places_there[1]()
    swaps_there[0]()
    saves.pop(0)()
    move_own(s.work, s.swap_on, s.x, windows, 0)
    spread_columns(s, 1)
    spread_there()
    spread_bias(s, 1)
    region_masks(True, s.regions)
    live_there()
    shifted_live(s, windows)
    grad_there()
    grad_lower_there()
    from_dense(s.grad_upper, s.page, 0)
    from_dense(s.dense.at[lower], s.page, half)
    to_channels(s.page, s.moved, s.grad)
    for saved in saves:
        saved()
    upper_there()
    from_dense(s.upper, s.page, 0)
    add_halo(s.page, s.moved, s.x, half, padded)
    norm_one_forward(s, windows)
    there[QKV]()
    project_forward(s, windows)
    attend_forward(s, windows, s.live_two)
    there[PROJ]()
    s.work[...] = mm(s.w_proj[...], s.merged[...], 0, 0)
    norm_two_forward(s, windows, s.live_two)
    there[FC1]()
    there[FC2]()
    feed_forward(s, windows)
    to_dense(s.work, s.moved, s.dense, s.moved.shape[0])
    out_there = halo(3, s.dense.at[upper], s.out_tokens.at[upper], below)
    out_kept = move(s.dense.at[lower], s.out_tokens.at[lower])

    spread_gains(s, 1)

    def backward(layer, live_ref, fetch, points):
        reducer.layer = layer
        first = 0 if layer else FEEDS
        feed_backward(s, reducer, points[:first])
        reducer.advance(points[first])
        fetch(0)
        norm_two_backward(s, windows, live_ref)
        reducer.advance(points[first + 1])
        fetch(1)
        merge_backward(s, reducer)
        reducer.advance(points[first + 2])
        fetch(2)
        attend_backward(s, windows, reducer, points[first + 3 :])
        fetch(3)

    back = {}

    def refill(point):
        if point == 0:
            back[0] = [move(s.kept_active, s.active), move(s.kept_slope, s.slope), move(s.kept_second, s.second)]
            back[0] += [fetch_weight(FC1, 0), fetch_weight(FC2, 0)]
        elif point == 1:
            back[1] = [move(s.kept_hidden, s.hidden)]
        elif point == 2:
            back[2] = [fetch_weight(PROJ, 0)]
        elif point == 3:
            back[2] += [move(s.kept_merged, s.merged)]
            back[3] = [move(s.kept_soft, s.soft)]
        elif point == 4:
            back[4] = [move(s.kept_x, s.x)]
        else:
            back[3] += [move(s.kept_qkv, s.qkv), move(s.kept_normed, s.normed), fetch_weight(QKV, 0)]

    def needed(point):
        if point in back:
            for arrived in back.pop(point):
                arrived()

    backward(1, s.live_two, refill, range(9))
    input_backward(s)
    norm_one_backward(s, windows)
    refill(4)
    out_there()
    to_dense(s.grad, s.moved, s.dense.at[upper], padded)
    next_there = halo(4, s.dense.at[upper], s.next_upper, below)
    reducer.advance(9)
    project_backward(s, reducer)
    spread_there = move(s.in_spread, s.spread)
    swaps_there[1]()
    move_own(s.grad, s.swap_back, s.work, windows, -1)
    reducer.settle(0)
    reducer.settle(1)
    reducer.advance(10)

    spread_there()
    small_gradients(s, s.small_own.at[1])
    refill(5)
    spread_gains(s, 0)
    reducer.advance(11)
    next_there()
    from_dense(s.next_upper, s.page, 0)
    s.grad[...] = s.work[...]
    add_halo(s.page, s.plain, s.grad, half, padded)
    reducer.advance(12)
    needed(0)

    def wait_next(point):
        needed(point + 1)

    backward(0, s.live, wait_next, range(13, 26))
    project_backward(s, reducer)
    input_backward(s)
    spread_there = move(s.in_spread, s.spread)
    reducer.settle(0)
    reducer.settle(1)
    reducer.advance(26)
    reducer.advance(27)
    needed(4)
    norm_one_backward(s, windows)
    out_kept()
    to_dense(s.grad, s.plain, s.dense, s.plain.shape[0])
    grad_kept = move(s.dense, s.grad_tokens)
    reducer.advance(28)
    spread_there()
    small_gradients(s, s.small_own.at[0])
    reducer.advance(29)
    finish_small(s, plan, row)
    grad_kept()


def finish_small(s, plan, row):
    total = s.small_parts.at[plan.halvings - 1]
    outs = (
        (s.d_ln_gain, (G1, G2)),
        (s.d_ln_bias, (B1, B2)),
        (s.d_qv_bias, (QB, VB)),
        (s.d_proj_bias, (PB,)),
        (s.d_fc1_bias, tuple(range(F1B, F1B + FEEDS))),
        (s.d_fc2_bias, (F2B,)),
    )
    for layer in range(2):
        s.d_table[layer] = total[layer, VECTOR_ROWS:, :OFFSETS]
        for ref, indices in outs:
            whole = jnp.concatenate([total[layer, index : index + 1, :] for index in indices], axis=1)
            size = ref.shape[1]
            mine = jnp.zeros((1, size), F32)
            for share in range(plan.shares):
                mine = jnp.where(row == share, whole[:, share * size : (share + 1) * size], mine)
            ref[layer : layer + 1, :] = mine


def placements(cols):
    windows = cols // WIN
    patches = WIN * cols
    padded = -(-patches // LANES) * LANES
    plain = np.zeros((padded, windows * LANES), np.float32)
    moved = np.zeros((padded, windows * LANES), np.float32)
    for line in range(WIN):
        for col in range(cols):
            source = line * cols + col
            plain[source, (col // WIN) * LANES + line * WIN + col % WIN] = 1
            new_line, new_col = (line - SHIFT) % WIN, (col - SHIFT) % cols
            moved[source, (new_col // WIN) * LANES + new_line * WIN + new_col % WIN] = 1
    return plain.astype(BF), moved.astype(BF)


def swaps():
    on = np.zeros((2 * LANES, LANES), np.float32)
    back = np.zeros((2 * LANES, LANES), np.float32)
    for line in range(SHIFT):
        for col in range(WIN):
            moved, plain = line * WIN + col, (line + SHIFT) * WIN + (col + SHIFT) % WIN
            on[plain + (LANES if col >= SHIFT else 0), moved] = 1
            back[moved + (LANES if col < SHIFT else 0), plain] = 1
    return on.astype(BF), back.astype(BF)


def table_spread():
    size = 2 * WIN - 1
    spread = np.zeros((WIN, 2 * LANES, TABLE), np.float32)
    for key_col in range(WIN):
        for offset in range(size):
            for col in range(WIN):
                spread[key_col, offset * WIN + col, offset * size + col - key_col + WIN - 1] = 1
    spread = spread.reshape(WIN // 2, 2, 2 * LANES, TABLE).swapaxes(1, 2)
    return spread.reshape(WIN * LANES, 2 * TABLE).astype(BF)


def copy_all(*refs):
    *refs, sems = refs
    count = len(refs) // 3
    sources, targets, held = refs[:count], refs[count : 2 * count], refs[2 * count :]
    ways = [*zip(sources, held), *zip(held, targets)]
    copies = [pltpu.make_async_copy(*way, sems.at[number]) for number, way in enumerate(ways)]
    for copy in copies[:count]:
        copy.start()
    for incoming, outgoing in zip(copies[:count], copies[count:]):
        incoming.wait()
        outgoing.start()
    for copy in copies[count:]:
        copy.wait()


def hand_out(values):
    anywhere = pl.BlockSpec(memory_space=pl.ANY)
    return pl.pallas_call(
        copy_all,
        out_shape=[jax.ShapeDtypeStruct(value.shape, value.dtype) for value in values],
        in_specs=[anywhere] * len(values),
        out_specs=[anywhere] * len(values),
        scratch_shapes=[pltpu.VMEM(value.shape, value.dtype) for value in values]
        + [pltpu.SemaphoreType.DMA((2 * len(values),))],
        compiler_params=pltpu.CompilerParams(vmem_limit_bytes=VMEM_LIMIT),
        name="results",
    )(*values)


def per_device(
    page_tokens,
    blank_mask,
    cotangent,
    ln_gain,
    ln_bias,
    qv_bias,
    rel_table,
    w_qkv,
    w_proj,
    proj_bias,
    w_fc1,
    fc1_bias,
    w_fc2,
    fc2_bias,
):
    pages, shares = lax.axis_size(PAGE), lax.axis_size(ROW)
    plan = Plan(pages, shares)
    cols = page_tokens.shape[2]
    windows, lanes = cols // WIN, cols // WIN * LANES
    dense = ((WIN * cols * SPLITS, LANES), F32)
    half_dense = ((WIN * cols * SPLITS // 2, LANES), F32)
    plain, moved = (jnp.asarray(place) for place in placements(cols))
    live_rows = 8 * -(-windows // 8)
    scalar_inputs = dict(blank=blank_mask[0])
    small_inputs = dict(
        table=rel_table,
        ln_gain=ln_gain,
        ln_bias=ln_bias,
        qv_bias=qv_bias,
        proj_bias=proj_bias,
        fc1_bias=fc1_bias,
        fc2_bias=fc2_bias,
    )
    large_inputs = dict(
        in_tokens=page_tokens[0],
        in_grad=cotangent.reshape(dense[0]),
        in_plain=plain,
        in_moved=moved,
        in_swap_on=jnp.asarray(swaps()[0]),
        in_swap_back=jnp.asarray(swaps()[1]),
        in_spread=jnp.asarray(table_spread()),
        in_qkv=w_qkv,
        in_proj=w_proj,
        in_fc1=w_fc1,
        in_fc2=w_fc2,
    )
    saved = dict(
        x=((D, lanes), F32),
        normed=((D, lanes), BF),
        qkv=((3 * D, lanes), BF),
        soft=((windows * HEADS, LANES, LANES), BF),
        merged=((D, lanes), BF),
        hidden=((D, lanes), F32),
        second=((D, lanes), BF),
        active=((FF, lanes), BF),
        slope=((FF, lanes), BF),
    )
    units = ((UNITS,) + plan.sizes[0][0], F32)
    large_outputs = dict(
        out_tokens=dense,
        grad_tokens=dense,
        sum_qkv=((2, D // shares, 3 * D), F32),
        sum_proj=((2, D // shares, D), F32),
        sum_fc1=((2, D // shares, FF), F32),
        sum_fc2=((2, FF // shares, D), F32),
        units_zero=units,
        units_one=units,
        kept_x=((D, lanes), F32),
        kept_normed=((D, lanes), BF),
        kept_qkv=((3 * D, lanes), BF),
        kept_soft=((windows * HEADS, LANES, LANES), BF),
        kept_merged=((D, lanes), BF),
        kept_hidden=((D, lanes), F32),
        kept_second=((D, lanes), BF),
        kept_active=((FF, lanes), BF),
        kept_slope=((FF, lanes), BF),
    )
    small_outputs = dict(
        d_ln_gain=((2, 2 * D // shares), F32),
        d_ln_bias=((2, 2 * D // shares), F32),
        d_qv_bias=((2, 2 * D // shares), F32),
        d_proj_bias=((2, D // shares), F32),
        d_fc1_bias=((2, FF // shares), F32),
        d_fc2_bias=((2, D // shares), F32),
        d_table=((2, HEADS, OFFSETS), F32),
    )
    small = (2, SMALL, D)
    vmem = dict(
        saved,
        tokens=((WIN, cols, D), BF),
        plain=(plain.shape, BF),
        moved=(moved.shape, BF),
        w_qkv=((D, 3 * D), BF),
        w_proj=((D, D), BF),
        w_fc1=((D, FF), BF),
        w_fc2=((FF, D), BF),
        dense=dense,
        upper=half_dense,
        swap_on=((2 * LANES, LANES), BF),
        swap_back=((2 * LANES, LANES), BF),
        grad_upper=half_dense,
        next_upper=half_dense,
        live_upper=((live_rows, LANES), F32),
        live_two=((live_rows, LANES), F32),
        work=((D, lanes), F32),
        grad=((D, lanes), F32),
        low=((D, lanes), BF),
        sums=((VECTORS, D, LANES), F32),
        gains=((2, D, LANES), F32),
        bias=((HEADS, LANES, LANES), F32),
        bias_rows=((HEADS * LANES, LANES), F32),
        regions=((2, LANES, LANES), F32),
        padded_table=((HEADS, TABLE), F32),
        live=((live_rows, LANES), F32),
        vector_rows=((VECTOR_ROWS, D), F32),
        staged=((2 * CHUNK, CHUNK), F32),
        done=((DONE * CLASSES, CHUNK // shares, CHUNK), F32),
        held=((HELD * CLASSES,) + plan.sizes[0][0], F32),
        first_landing=((RING * CLASSES,) + plan.sizes[0][0], F32),
        small_own=(small, F32),
        small_parts=((plan.halvings,) + small, F32),
    )
    semaphores = dict(
        move_sems=pltpu.SemaphoreType.DMA((48,)),
        halo_sems=pltpu.SemaphoreType.DMA((2, 5)),
        send_sems=pltpu.SemaphoreType.DMA((2 * UNITS, plan.phases)),
        recv_sems=pltpu.SemaphoreType.DMA((2 * UNITS, plan.phases)),
        own_sems=pltpu.SemaphoreType.DMA((2 * UNITS, 2)),
        stage_sems=pltpu.SemaphoreType.DMA((2, shares, 2)),
        first_sems=pltpu.SemaphoreType.DMA((2 * UNITS, shares)),
        first_free=pltpu.SemaphoreType.REGULAR((2 * UNITS,)),
        small_sems=pltpu.SemaphoreType.DMA((2, plan.halvings)),
        free_sems=pltpu.SemaphoreType.REGULAR((CLASSES, plan.halvings)),
    )
    landing = [((RING,) + size, F32) for sizes in plan.sizes for size in sizes[1:]]
    layout = [*scalar_inputs, *small_inputs, *large_inputs, *small_outputs, *large_outputs, *vmem, *semaphores]
    in_vmem, anywhere = pl.BlockSpec(memory_space=pltpu.VMEM), pl.BlockSpec(memory_space=pl.ANY)
    outputs = {**small_outputs, **large_outputs}
    results = pl.pallas_call(
        functools.partial(run, plan, layout),
        out_shape=[jax.ShapeDtypeStruct(*shape) for shape in outputs.values()],
        in_specs=[pl.BlockSpec(memory_space=pltpu.SMEM)] + [in_vmem] * len(small_inputs) + [anywhere] * len(large_inputs),
        out_specs=[in_vmem] * len(small_outputs) + [anywhere] * len(large_outputs),
        scratch_shapes=[pltpu.VMEM(*shape) for shape in vmem.values()]
        + list(semaphores.values())
        + [pltpu.VMEM(*shape) for shape in landing],
        compiler_params=pltpu.CompilerParams(
            vmem_limit_bytes=VMEM_LIMIT, collective_id=0, has_side_effects=True
        ),
        name="two_layers",
    )(*scalar_inputs.values(), *small_inputs.values(), *large_inputs.values())
    results = hand_out(results[: len(small_outputs) + 6])
    d_ln_gain, d_ln_bias, d_qv_bias, d_proj_bias, d_fc1_bias, d_fc2_bias, d_table = results[: len(small_outputs)]
    out_tokens, grad_tokens, sum_qkv, sum_proj, sum_fc1, sum_fc2 = results[len(small_outputs) :]
    return (
        out_tokens.reshape(cotangent.shape),
        grad_tokens.reshape(cotangent.shape),
        d_ln_gain,
        d_ln_bias,
        d_qv_bias,
        d_table,
        sum_qkv,
        sum_proj,
        d_proj_bias,
        sum_fc1,
        d_fc1_bias,
        sum_fc2,
        d_fc2_bias,
    )


def solution(mesh):
    tokens, by_row, shares = P(PAGE, ROW, None, None), P(None, ROW), P(None, ROW, None)
    return jax.shard_map(
        per_device,
        mesh=mesh,
        in_specs=(tokens, P(PAGE, ROW, None), tokens) + (P(),) * 11,
        out_specs=(tokens, tokens)
        + (by_row, by_row, by_row, P(), shares, shares, by_row, shares, by_row, shares, by_row),
        check_vma=False,
    )
```
